128 devices in a mesh: fsdp: 16 (over x, z), ctx: 2 (over core), tp: 4 (over y).
Axes of the slice: x: 4, y: 4, z: 4, core: 2. Of those that a mesh axis runs over, the one named last changes fastest.
Arguments:
- inputs: bfloat16 [16384, 2048], P(('fsdp', 'ctx', 'tp')), may hold values from -6 to 6
- seq_lengths: int32 [16], P('fsdp'), may hold values from 513 to 1024, as said below
- carried_state: float32 [16, 8, 256, 432], P('fsdp', 'tp'), may hold values from -3 to 3
- attn_gain: float32 [2048], replicated, may hold values from 0.1 to 1.9
- query_weight: bfloat16 [2048, 2048], P(('fsdp', 'ctx'), 'tp'), may hold values from -0.125 to 0.125
- key_weight: bfloat16 [2048, 2048], P(('fsdp', 'ctx'), 'tp'), may hold values from -0.125 to 0.125
- value_weight: bfloat16 [2048, 3456], P(('fsdp', 'ctx'), 'tp'), may hold values from -0.125 to 0.125
- swish_weight: bfloat16 [2048, 3456], P(('fsdp', 'ctx'), 'tp'), may hold values from -0.125 to 0.125
- out_weight: bfloat16 [3456, 2048], P('tp', ('fsdp', 'ctx')), may hold values from -0.21875 to 0.21875
- mlp_gain: float32 [2048], replicated, may hold values from 0.1 to 1.9
- gate_weight: bfloat16 [2048, 3456], P(('fsdp', 'ctx'), 'tp'), may hold values from -0.125 to 0.125
- up_weight: bfloat16 [2048, 3456], P(('fsdp', 'ctx'), 'tp'), may hold values from -0.125 to 0.125
- down_weight: bfloat16 [3456, 2048], P('tp', ('fsdp', 'ctx')), may hold values from -0.15625 to 0.15625
- output_grad: bfloat16 [16384, 2048], P(('fsdp', 'ctx')), may hold values from -6 to 6
Outputs:
- outputs: bfloat16 [16384, 2048], P(('fsdp', 'ctx', 'tp'))
- input_grad: float32 [16384, 2048], P(('fsdp', 'ctx', 'tp'))
- attn_gain_grad: float32 [2048], replicated
- query_weight_gradient: float32 [2048, 2048], P(('fsdp', 'ctx'), 'tp')
- key_grad: float32 [2048, 2048], P(('fsdp', 'ctx'), 'tp')
- value_grad: float32 [2048, 3456], P(('fsdp', 'ctx'), 'tp')
- swish_grad: float32 [2048, 3456], P(('fsdp', 'ctx'), 'tp')
- out_weight_grad: float32 [3456, 2048], P('tp', ('fsdp', 'ctx'))
- mlp_gain_grad: float32 [2048], replicated
- gate_grad: float32 [2048, 3456], P(('fsdp', 'ctx'), 'tp')
- up_grad: float32 [2048, 3456], P(('fsdp', 'ctx'), 'tp')
- down_grad: float32 [3456, 2048], P('tp', ('fsdp', 'ctx'))
The draws below stay inside these ranges and needn't reach their ends.
Inputs may be any that keep to these rules, and one draw needn't show every extreme that they name: `seq_lengths`: one sequence fills all 1024 positions of its slot and one has exactly 513; positions at or past a sequence's length are padding.
All inputs are finite; a program needn't handle non-finite values.
Results may differ from the reference program's by a relative error of at most 0.02.
Values may be sent and summed in bfloat16 or wider, within the bound.
A program may use at most 192 MiB of HBM per device.

```python
import jax
import jax.numpy as jnp
from jax import lax

D = 2048
HEADS = 8
KDIM = 256
VDIM = 432
FF = 3456
SEQ = 1024
SEQS = 16
TOKENS = 16384
QK = 2048
VD = 3456
N_CTX = 2


def draw_seq_lengths(key, part):
    key = jax.random.fold_in(key, 11)
    length_key, order_key = jax.random.split(key)
    least = SEQ // 2 + 1
    drawn = jax.random.randint(length_key, (SEQS,), least, SEQ + 1)
    order = jax.random.permutation(order_key, SEQS)
    drawn = jnp.where(order == 0, SEQ, drawn)
    drawn = jnp.where(order == 1, least, drawn)
    return drawn.astype(jnp.int32)


def shard_levels(key, dims, cuts, low, high):
    def one(dim, blocks):
        heights = jax.random.uniform(jax.random.fold_in(jax.random.fold_in(key, 6), dim), (blocks,), jnp.float32, low / len(cuts), high / len(cuts))
        return jnp.repeat(jnp.exp(heights), dims[dim] // blocks).reshape((-1,) + (1,) * (len(dims) - dim - 1))

    level = one(*cuts[0])
    for cut in cuts[1:]:
        level = level * one(*cut)
    return level


def normal_values(stream_key, dims, deviation, most, cuts=(), kind=jnp.bfloat16):
    array = jax.random.normal(stream_key, dims, jnp.float32) * deviation
    if len(cuts) > 0:
        array = shard_levels(stream_key, dims, cuts, -0.22, 0.18) * array
    return jnp.clip(array, min=-most, max=most).astype(kind)


def setup_inputs(seed: int = 0) -> dict:
    key_of = jax.random.split(jax.random.key(seed), 15)
    return {
        "inputs": normal_values(key_of[0], (TOKENS, D), 1.0, 6.0, ((0, 128),)),
        "seq_lengths": draw_seq_lengths(jax.random.fold_in(key_of[14], 71), 0),
        "carried_state": normal_values(key_of[2], (SEQS, HEADS, KDIM, VDIM), 0.5, 3.0, ((0, 16), (1, 4)), jnp.float32),
        "attn_gain": jnp.clip(1.0 + 0.18 * jax.random.normal(key_of[3], (D,), jnp.float32), 0.1, 1.9),
        "query_weight": normal_values(key_of[4], (D, QK), D ** -0.5, 0.125, ((0, 32), (1, 4))),
        "key_weight": normal_values(key_of[5], (D, QK), D ** -0.5, 0.125, ((0, 32), (1, 4))),
        "value_weight": normal_values(key_of[6], (D, VD), D ** -0.5, 0.125, ((0, 32), (1, 4))),
        "swish_weight": normal_values(key_of[7], (D, VD), D ** -0.5, 0.125, ((0, 32), (1, 4))),
        "out_weight": normal_values(key_of[8], (VD, D), (VD // 4) ** -0.5, 0.21875, ((0, 4), (1, 32))),
        "mlp_gain": jnp.clip(1.0 + 0.18 * jax.random.normal(key_of[9], (D,), jnp.float32), 0.1, 1.9),
        "gate_weight": normal_values(key_of[10], (D, FF), D ** -0.5, 0.125, ((0, 32), (1, 4))),
        "up_weight": normal_values(key_of[11], (D, FF), D ** -0.5, 0.125, ((0, 32), (1, 4))),
        "down_weight": normal_values(key_of[12], (FF, D), (FF // 2) ** -0.5, 0.15625, ((0, 4), (1, 32))),
        "output_grad": normal_values(key_of[13], (TOKENS, D), 1.0, 6.0, ((0, 32),)),
    }


HIGH = lax.Precision.HIGHEST
EPSILON = 1e-05

@jax.custom_vjp
def low(v):
    return lax.optimization_barrier(v.astype(jnp.bfloat16)).astype(jnp.float32)

@jax.custom_vjp
def lowered_reverse(v):
    return v

def low_keep(v):
    return (low(v), None)

def low_pass(kept, grad):
    return (grad,)

def back_keep(v):
    return (v, None)

def back_low(kept, grad):
    return (low(grad),)
low.defvjp(low_keep, low_pass)
lowered_reverse.defvjp(back_keep, back_low)

def layer_norm(rows_in, gain):
    centre = lax.optimization_barrier(jnp.mean(rows_in, axis=-1, keepdims=True))
    centred = rows_in - centre
    spread = lax.optimization_barrier(jnp.mean(centred * centred, axis=-1, keepdims=True))
    return centred * lax.rsqrt(spread + EPSILON) * gain

def group_norm(values_in, head_count):
    shaped = values_in.reshape(values_in.shape[0], head_count, -1)
    centre = lax.optimization_barrier(jnp.mean(shaped, axis=-1, keepdims=True))
    centred = shaped - centre
    spread = lax.optimization_barrier(jnp.mean(centred * centred, axis=-1, keepdims=True))
    return (centred * lax.rsqrt(spread + EPSILON)).reshape(values_in.shape)

def rotate(field, angles, head_count):
    row_count = field.shape[0]
    half_width = angles.shape[1]
    shaped = field.reshape(row_count, head_count, 2, half_width)
    cosine = jnp.cos(angles)[:, None, :]
    sine = jnp.sin(angles)[:, None, :]
    former = shaped[:, :, 0]
    latter = shaped[:, :, 1]
    turned = jnp.stack([former * cosine - latter * sine, former * sine + latter * cosine], axis=2)
    return turned.reshape(field.shape)

def decay_mask(first_row, row_count, key_count, decays):
    query_pos = (first_row + jnp.arange(row_count)).astype(jnp.float32)
    key_pos = jnp.arange(key_count).astype(jnp.float32)
    distance = query_pos[:, None] - key_pos[None, :]
    factor = jnp.exp(jnp.maximum(distance, 0.0)[None] * decays[:, None, None])
    return jnp.where(distance[None] >= 0.0, factor, 0.0)

def head_decays(head_ids, seq_len):
    return -jnp.power(2.0, 5.0 - head_ids.astype(jnp.float32)) / seq_len

def retention_one(pieces):
    queries, keys_in, values_in, carried = pieces
    rows_ctx = SEQ // N_CTX
    decays = head_decays(jnp.arange(HEADS), SEQ)
    query_four = queries.reshape(N_CTX, rows_ctx, HEADS, KDIM).transpose(0, 2, 1, 3)
    key_four = keys_in.reshape(N_CTX, rows_ctx, HEADS, KDIM).transpose(0, 2, 1, 3)
    value_four = values_in.reshape(N_CTX, rows_ctx, HEADS, VDIM).transpose(0, 2, 1, 3)
    scores = lowered_reverse(jnp.einsum('chrk,chsk->chrs', query_four, key_four, precision=HIGH))
    mixing = low(scores * decay_mask(0, rows_ctx, rows_ctx, decays)[None])
    inner = jnp.einsum('chrs,chsv->chrv', mixing, value_four, precision=HIGH)
    local_pos = jnp.arange(rows_ctx).astype(jnp.float32)
    tail_fac = jnp.exp((rows_ctx - 1.0 - local_pos)[None, :] * decays[:, None])
    head_fac = jnp.exp((local_pos + 1.0)[None, :] * decays[:, None])
    local_state = lowered_reverse(jnp.einsum('chrk,chrv->chkv', key_four * tail_fac[None, :, :, None], value_four, precision=HIGH))
    span = jnp.exp(rows_ctx * decays)[:, None, None]

    def carry_step(carry, state_in):
        return (span * carry + state_in, carry)
    _, prior = lax.scan(carry_step, carried, local_state)
    prior = low(prior)
    cross = jnp.einsum('chrk,chkv->chrv', query_four, prior, precision=HIGH) * head_fac[None, :, :, None]
    return (inner + cross).transpose(0, 2, 1, 3).reshape(SEQ, HEADS * VDIM)

def reference(inputs, seq_lengths, carried_state, attn_gain, query_weight, key_weight, value_weight, swish_weight, out_weight, mlp_gain, gate_weight, up_weight, down_weight, output_grad):
    token_ids = jnp.arange(TOKENS, dtype=jnp.int32)
    position = token_ids % SEQ
    seq_ids = token_ids // SEQ
    row_mask = (position < seq_lengths[seq_ids]).astype(jnp.float32)[:, None]
    half_width = KDIM // 2
    frequency = jnp.power(10000.0, -jnp.arange(half_width).astype(jnp.float32) / half_width)
    angles = position.astype(jnp.float32)[:, None] * frequency[None, :]
    carried_wide = carried_state.astype(jnp.float32)

    def forward(inputs_wide, gain_one, w_query, w_key, w_value, w_swish, w_out, gain_two, w_gate, w_up, w_down):
        normed_one = low(layer_norm(inputs_wide, gain_one))
        query_raw = lowered_reverse(jnp.dot(normed_one, w_query, precision=HIGH))
        key_raw = lowered_reverse(jnp.dot(normed_one, w_key, precision=HIGH))
        value_raw = lowered_reverse(jnp.dot(normed_one, w_value, precision=HIGH))
        swish_raw = lowered_reverse(jnp.dot(normed_one, w_swish, precision=HIGH))
        queries = low(rotate(query_raw, angles, HEADS))
        keys_rot = low(rotate(key_raw, angles, HEADS))
        values_kept = low(value_raw * row_mask)
        retained = lax.map(jax.checkpoint(retention_one), (queries.reshape(SEQS, SEQ, QK), keys_rot.reshape(SEQS, SEQ, QK), values_kept.reshape(SEQS, SEQ, VD), carried_wide))
        retained = lowered_reverse(retained.reshape(TOKENS, VD))
        mixed = low(row_mask * jax.nn.silu(swish_raw) * group_norm(retained, HEADS))
        attn_out = lowered_reverse(jnp.dot(mixed, w_out, precision=HIGH))
        hidden = inputs_wide + attn_out
        normed_two = low(layer_norm(hidden, gain_two))
        gate_pre = lowered_reverse(jnp.dot(normed_two, w_gate, precision=HIGH))
        up_pre = lowered_reverse(jnp.dot(normed_two, w_up, precision=HIGH))
        activated = low(jax.nn.gelu(gate_pre, approximate=False) * up_pre)
        return hidden + jnp.dot(activated, w_down, precision=HIGH)
    result, pull = jax.vjp(forward, inputs.astype(jnp.float32), attn_gain.astype(jnp.float32), query_weight.astype(jnp.float32), key_weight.astype(jnp.float32), value_weight.astype(jnp.float32), swish_weight.astype(jnp.float32), out_weight.astype(jnp.float32), mlp_gain.astype(jnp.float32), gate_weight.astype(jnp.float32), up_weight.astype(jnp.float32), down_weight.astype(jnp.float32))
    grads = pull(output_grad.astype(jnp.float32))
    return (result.astype(jnp.bfloat16), grads[0], grads[1], grads[2], grads[3], grads[4], grads[5], grads[6], grads[7], grads[8], grads[9], grads[10])
```

```python
import functools

import jax
import jax.numpy as jnp
from jax import lax
from jax.experimental import pallas as pl
from jax.experimental.pallas import tpu as pltpu
from jax.sharding import PartitionSpec as P

D = 2048
KDIM = 256
VDIM = 432
SEQ = 1024
HALF = 512
SIZES = (256, 256, 432, 432, 432, 432, 432, 432)
STARTS = (0, 256, 512, 944, 1376, 1808, 2240, 2672)
ROWS = 3104
EPSILON = 1e-05
MESH = pl.DeviceIdType.MESH
BF = jnp.bfloat16
F32 = jnp.float32


def even(rows):
    return rows // 32 * 16


class Net:
    def __init__(self, send, recv):
        group = lax.axis_index("fsdp")
        self.c = lax.axis_index("ctx")
        self.t = lax.axis_index("tp")
        self.x = group // 4
        self.z = group % 4
        self.send, self.recv, self.used = send, recv, 0

    def dev(self, dx=0, dz=0, dt=0, dc=0):
        x, z, t = ((at + d + 4) % 4 if d else at for at, d in ((self.x, dx), (self.z, dz), (self.t, dt)))
        c = 1 - self.c if dc else self.c
        return (x * 4 + z, c, t)

    def greet(self, hops):
        barrier = pltpu.get_barrier_semaphore()
        for hop in hops:
            pl.semaphore_signal(barrier, inc=1, device_id=self.dev(**hop), device_id_type=MESH)
        pl.semaphore_wait(barrier, len(hops))

    def copy(self, src, dst, **hop):
        at = self.used
        self.used += 1
        return pltpu.make_async_remote_copy(
            src_ref=src,
            dst_ref=dst,
            send_sem=self.send.at[at],
            recv_sem=self.recv.at[at],
            device_id=self.dev(**hop),
            device_id_type=MESH,
        )


XZ_HOPS = (dict(dx=1), dict(dx=-1), dict(dz=1), dict(dz=-1))
Y_HOPS = (dict(dt=1), dict(dt=-1), dict(dc=1))


def lanes(piece):
    return pl.ds(pl.multiple_of(piece * 128, 128), 128)


def ring_views(net, axis):
    x, z = net.x, net.z
    if axis == "x":
        first = lambda ref, d, rows: ref.at[(x + d + 4) % 4, rows, lanes(z)]
        second = lambda ref, d, rows: ref.at[:, rows, lanes((z + d + 4) % 4)]
        return first, second, "dx", "dz"
    first = lambda ref, d, rows: ref.at[x, rows, lanes((z + d + 4) % 4)]
    second = lambda ref, d, rows: ref.at[(x + d + 4) % 4, rows, :]
    return first, second, "dz", "dx"


def gather_weights(net, ref, start, stop):
    cut = start + even(stop - start)
    plans = []
    for axis, lo, hi in (("z", start, cut), ("x", cut, stop)):
        mid = lo + even(hi - lo)
        whole, head, tail = pl.ds(lo, hi - lo), pl.ds(lo, mid - lo), pl.ds(mid, hi - mid)
        first, second, hop_a, hop_b = ring_views(net, axis)
        plan = []
        for view, hop in ((first, hop_a), (second, hop_b)):
            mine = view(ref, 0, whole)
            plan.append(
                (
                    net.copy(mine, mine, **{hop: 1}),
                    net.copy(mine, mine, **{hop: -1}),
                    net.copy(view(ref, -1, head), view(ref, -1, head), **{hop: 1}),
                    net.copy(view(ref, 1, tail), view(ref, 1, tail), **{hop: -1}),
                )
            )
        plans.append(plan)

    def near(phase):
        for plan in plans:
            plan[phase][0].start()
            plan[phase][1].start()

    def far(phase):
        for k in (0, 1):
            for plan in plans:
                plan[phase][k].wait_recv()
                plan[phase][2 + k].start()

    def land(phase):
        for plan in plans:
            plan[phase][2].wait_recv()
            plan[phase][3].wait_recv()

    def done():
        land(1)
        for plan in plans:
            for phase in plan:
                for copy in phase:
                    copy.wait_send()

    return [
        lambda: near(0),
        lambda: far(0),
        lambda: (land(0), near(1)),
        lambda: far(1),
        done,
    ]


def add_rows(refs, out, count):
    step = 16

    def body(i, carry):
        at = pl.ds(pl.multiple_of(i * step, step), step)
        total = refs[0](at).astype(F32)
        for ref in refs[1:]:
            total = total + ref(at).astype(F32)
        out(at, total)
        return carry

    lax.fori_loop(0, count // step, body, 0)


def scatter_shapes(rows):
    shapes = []
    cut = even(rows)
    for axis, count in (("z", cut), ("x", rows - cut)):
        head = even(count)
        for slab in ((4, 128), (1, 128)) if axis == "z" else ((1, 512), (1, 128)):
            for n in (head, count - head, count, count):
                shape = (n, slab[1]) if slab[0] == 1 else (slab[0], n, slab[1])
                shapes.append(pltpu.VMEM(shape, BF))
    return shapes


def scatter_weights(net, ref, start, stop, bufs, out):
    cut = start + even(stop - start)
    plans = []
    bufs = list(bufs)
    for axis, lo, hi in (("z", start, cut), ("x", cut, stop)):
        mid = lo + even(hi - lo)
        parts = (lo, mid - lo), (mid, hi - mid), (lo, hi - lo)
        head, tail, whole = (pl.ds(*part) for part in parts)
        far_view, near_view, hop_a, hop_b = ring_views(net, axis)
        plan = []
        if axis == "z":
            wide = lambda r, d, rows: r.at[:, rows, lanes((net.z + d + 4) % 4)]
            thin = lambda r, d, rows: r.at[(net.x + d + 4) % 4, rows, lanes(net.z)]
        else:
            wide = lambda r, d, rows: r.at[(net.x + d + 4) % 4, rows, :]
            thin = lambda r, d, rows: r.at[net.x, rows, lanes((net.z + d + 4) % 4)]
        for view, hop in ((wide, hop_a), (thin, hop_b)):
            fa, fb, ma, mb = bufs[:4]
            bufs = bufs[4:]
            plan.append(
                dict(
                    view=view,
                    bufs=(fa, fb, ma, mb),
                    copies=(
                        net.copy(view(ref, 2, head), fa, **{hop: 1}),
                        net.copy(view(ref, 2, tail), fb, **{hop: -1}),
                        net.copy(view(ref, 1, whole), ma, **{hop: 1}),
                        net.copy(view(ref, -1, whole), mb, **{hop: -1}),
                    ),
                )
            )
        plans.append((plan, parts))

    def at_rows(view, d, lo):
        def read(at):
            return view(ref, d, pl.ds(lo + at.start, at.size))[...]

        def write(at, value):
            view(ref, d, pl.ds(lo + at.start, at.size))[...] = value.astype(BF)

        return read, write

    def buf_rows(buf):
        if len(buf.shape) == 3:
            return lambda at: buf[:, at, :]
        return lambda at: buf[at, :]

    def far(phase):
        for plan, _ in plans:
            plan[phase]["copies"][0].start()
            plan[phase]["copies"][1].start()

    def near(phase):
        for k, d in ((0, 1), (1, -1)):
            for plan, parts in plans:
                step = plan[phase]
                lo, count = parts[k]
                step["copies"][k].wait_recv()
                read, write = at_rows(step["view"], d, lo)
                add_rows((read, buf_rows(step["bufs"][k])), write, count)
                step["copies"][2 + k].start()

    def total(phase, last):
        for plan, parts in plans:
            step = plan[phase]
            lo, count = parts[2]
            step["copies"][2].wait_recv()
            step["copies"][3].wait_recv()
            read, write = at_rows(step["view"], 0, lo)
            if last:
                write = lambda at, value, lo=lo: out(pl.ds(lo + at.start, at.size), value)
            add_rows((read, buf_rows(step["bufs"][2]), buf_rows(step["bufs"][3])), write, count)

    def done():
        total(1, True)
        for plan, _ in plans:
            for step in plan:
                for copy in step["copies"]:
                    copy.wait_send()

    return [
        lambda: far(0),
        lambda: near(0),
        lambda: (total(0, False), far(1)),
        lambda: near(1),
        done,
    ]


def gather_rows(net, ref):
    def block(c, t, lo=0, n=128):
        return ref.at[pl.ds(pl.multiple_of(c * 512 + t * 128 + lo, 16), n), :]

    c, t = net.c, net.t
    before, after, across = (t + 3) % 4, (t + 1) % 4, (t + 2) % 4
    own = block(c, t)
    up = net.copy(own, own, dt=1)
    down = net.copy(own, own, dt=-1)
    side = net.copy(own, own, dc=1)
    fore = net.copy(block(c, before, 0, 64), block(c, before, 0, 64), dt=1)
    back = net.copy(block(c, after, 64, 64), block(c, after, 64, 64), dt=-1)
    over = [
        net.copy(block(c, before), block(c, before), dc=1),
        net.copy(block(c, after), block(c, after), dc=1),
        net.copy(block(c, across, 0, 64), block(c, across, 0, 64), dc=1),
        net.copy(block(c, across, 64, 64), block(c, across, 64, 64), dc=1),
    ]

    def start():
        up.start()
        down.start()
        side.start()

    def forward():
        up.wait_recv()
        fore.start()
        over[0].start()
        down.wait_recv()
        back.start()
        over[1].start()

    def finish():
        fore.wait_recv()
        over[2].start()
        back.wait_recv()
        over[3].start()
        side.wait_recv()
        for copy in over:
            copy.wait_recv()
        for copy in (up, down, side, fore, back, *over):
            copy.wait_send()

    return [start, forward, finish]


ROW_BUFS = [
    pltpu.VMEM((512, D), BF),
    pltpu.VMEM((64, D), BF),
    pltpu.VMEM((64, D), BF),
    pltpu.VMEM((128, D), BF),
    pltpu.VMEM((128, D), BF),
]


def scatter_rows(net, ref, bufs, out):
    c, t = net.c, net.t
    other, far_a, far_b, near_a, near_b = bufs
    side = net.copy(ref.at[pl.ds(pl.multiple_of((1 - c) * 512, 512), 512), :], other, dc=1)

    def row(d, lo=0):
        return c * 512 + (t + d + 4) % 4 * 128 + lo

    def block(d, lo=0, n=128):
        return ref.at[pl.ds(pl.multiple_of(row(d, lo), 16), n), :]

    copies = (
        net.copy(block(2, 0, 64), far_a, dt=1),
        net.copy(block(2, 64, 64), far_b, dt=-1),
        net.copy(block(1), near_a, dt=1),
        net.copy(block(-1), near_b, dt=-1),
    )

    def read(source, base):
        return lambda at: source[pl.ds(pl.multiple_of(base + at.start, 16), at.size), :]

    def write(base):
        def store(at, value):
            ref[pl.ds(pl.multiple_of(base + at.start, 16), at.size), :] = value.astype(BF)

        return store

    def other_row(d, lo=0):
        return (t + d + 4) % 4 * 128 + lo

    def start():
        side.start()

    def far():
        side.wait_recv()
        for d, lo, k in ((2, 0, 0), (2, 64, 1)):
            add_rows((read(ref, row(d, lo)), read(other, other_row(d, lo))), write(row(d, lo)), 64)
            copies[k].start()
        for d in (1, -1, 0):
            add_rows((read(ref, row(d)), read(other, other_row(d))), write(row(d)), 128)

    def near():
        for k, d, lo, buf in ((0, 1, 0, far_a), (1, -1, 64, far_b)):
            copies[k].wait_recv()
            add_rows((read(ref, row(d, lo)), read(buf, 0)), write(row(d, lo)), 64)
            copies[2 + k].start()

    def finish():
        copies[2].wait_recv()
        copies[3].wait_recv()
        add_rows((read(ref, row(0)), read(near_a, 0), read(near_b, 0)), out, 128)
        for copy in (side, *copies):
            copy.wait_send()

    return [start, far, near, finish]


def call(kernel, outs, ins, scratch, copies, cid):
    any_spec = pl.BlockSpec(memory_space=pl.ANY)
    vmem_spec = pl.BlockSpec(memory_space=pltpu.VMEM)
    return pl.pallas_call(
        kernel,
        out_shape=[shape for shape, _ in outs],
        in_specs=[vmem_spec if v else any_spec for _, v in ins],
        out_specs=[vmem_spec if v else any_spec for _, v in outs],
        scratch_shapes=list(scratch)
        + [pltpu.SemaphoreType.DMA((copies,)), pltpu.SemaphoreType.DMA((copies,)), pltpu.SemaphoreType.DMA((40,))],
        compiler_params=pltpu.CompilerParams(
            collective_id=cid, has_side_effects=True, vmem_limit_bytes=56 * 2**20
        ),
    )(*[array for array, _ in ins])


def weights_in(piece, cid):
    def kernel(piece_ref, out_ref, send, recv, local):
        net = Net(send, recv)
        own = pltpu.make_async_copy(piece_ref, out_ref.at[net.x, :, lanes(net.z)], local.at[0])
        own.start()
        net.greet(XZ_HOPS)
        own.wait()
        for stage in gather_weights(net, out_ref, 0, ROWS):
            stage()

    (out,) = call(
        kernel, [(jax.ShapeDtypeStruct((4, ROWS, 512), BF), False)], [(piece, False)], [], 16, cid
    )
    return out


def grads_out(parts, cid):
    def kernel(*refs):
        parts_refs, out_ref, total = refs[:8], refs[8], refs[9]
        bufs, (send, recv, local) = refs[10:-3], refs[-3:]
        net = Net(send, recv)
        loads = []
        for k, ref in enumerate(parts_refs):
            for x in range(4):
                loads.append(
                    pltpu.make_async_copy(
                        ref.at[:, pl.ds(x * 512, 512)],
                        total.at[x, pl.ds(STARTS[k], SIZES[k]), :],
                        local.at[4 * k + x],
                    )
                )
        for load in loads:
            load.start()
        net.greet(XZ_HOPS)
        for load in loads:
            load.wait()

        def out(at, value):
            out_ref[at, :] = value

        for stage in scatter_weights(net, total, 0, ROWS, bufs, out):
            stage()

    (out,) = call(
        kernel,
        [(jax.ShapeDtypeStruct((ROWS, 128), F32), True)],
        [(part, False) for part in parts],
        [pltpu.VMEM((4, ROWS, 512), BF)] + scatter_shapes(ROWS),
        16,
        cid,
    )
    return out


def rows_in(own, cid):
    def kernel(own_ref, out_ref, send, recv, local):
        net = Net(send, recv)
        at = pl.ds(pl.multiple_of(net.c * 512 + net.t * 128, 128), 128)
        load = pltpu.make_async_copy(own_ref, out_ref.at[at, :], local.at[0])
        load.start()
        net.greet(Y_HOPS)
        load.wait()
        for stage in gather_rows(net, out_ref):
            stage()

    (out,) = call(kernel, [(jax.ShapeDtypeStruct((SEQ, D), BF), False)], [(own, False)], [], 9, cid)
    return out


def rows_out(part, cid):
    def kernel(part_ref, out_ref, total, *rest):
        bufs, (send, recv, local) = rest[:5], rest[5:]
        net = Net(send, recv)
        load = pltpu.make_async_copy(part_ref, total, local.at[0])
        load.start()
        net.greet(Y_HOPS)
        load.wait()

        def out(at, value):
            out_ref[at, :] = value

        for stage in scatter_rows(net, total, bufs, out):
            stage()

    (out,) = call(
        kernel,
        [(jax.ShapeDtypeStruct((128, D), F32), True)],
        [(part, False)],
        [pltpu.VMEM((SEQ, D), BF)] + ROW_BUFS,
        5,
        cid,
    )
    return out


def dot(a, b, dims):
    return lax.dot_general(a, b, (dims, ((), ())), preferred_element_type=F32)


NN = ((1,), (0,))
NT = ((1,), (1,))
TN = ((0,), (0,))


def layer_norm(rows_in, gain):
    centre = jnp.mean(rows_in, axis=-1, keepdims=True)
    centred = rows_in - centre
    spread = jnp.mean(centred * centred, axis=-1, keepdims=True)
    return centred * lax.rsqrt(spread + EPSILON) * gain


def group_norm(values_in):
    centre = jnp.mean(values_in, axis=-1, keepdims=True)
    centred = values_in - centre
    spread = jnp.mean(centred * centred, axis=-1, keepdims=True)
    return centred * lax.rsqrt(spread + EPSILON)


def rotate(field, cosine, sine):
    former, latter = field[:, :128], field[:, 128:]
    return jnp.concatenate([former * cosine - latter * sine, former * sine + latter * cosine], axis=1)


def swap_cores(array):
    return lax.ppermute(array, "ctx", [(0, 1), (1, 0)])


def on_device(
    inputs,
    seq_lengths,
    carried_state,
    attn_gain,
    query_weight,
    key_weight,
    value_weight,
    swish_weight,
    out_weight,
    mlp_gain,
    gate_weight,
    up_weight,
    down_weight,
    output_grad,
):
    core = lax.axis_index("ctx")
    head = lax.axis_index("tp") * 2 + core

    def for_core(which):
        parts = []
        for k, weight in enumerate(
            (query_weight, key_weight, value_weight, swish_weight, out_weight, gate_weight, up_weight, down_weight)
        ):
            n = SIZES[k]
            if k in (4, 7):
                parts.append(lax.dynamic_slice_in_dim(weight, which * n, n, 0))
            else:
                parts.append(lax.dynamic_slice_in_dim(weight, which * n, n, 1).T)
        return jnp.concatenate(parts, axis=0)

    mine, got = for_core(core), swap_cores(for_core(1 - core))
    piece = jnp.where(core == 0, jnp.concatenate([mine, got], axis=1), jnp.concatenate([got, mine], axis=1))
    weights = weights_in(piece, 1)
    weights = weights.transpose(1, 0, 2).reshape(ROWS, D)
    w_query, w_key, w_value, w_swish, w_out, w_gate, w_up, w_down = (
        weights[s : s + n] for s, n in zip(STARTS, SIZES)
    )
    position = jnp.arange(SEQ, dtype=jnp.int32)
    row_mask = (position < seq_lengths[0]).astype(F32)[:, None]
    frequency = jnp.power(10000.0, -jnp.arange(128).astype(F32) / 128)
    angles = position.astype(F32)[:, None] * frequency[None, :]
    cosine, sine = jnp.cos(angles), jnp.sin(angles)
    decay = -jnp.power(2.0, 5.0 - head.astype(F32)) / SEQ
    local_pos = jnp.arange(HALF).astype(F32)
    tail_fac = jnp.exp((HALF - 1.0 - local_pos) * decay)[:, None]
    head_fac = jnp.exp((local_pos + 1.0) * decay)[:, None]
    span = jnp.exp(HALF * decay)
    distance = local_pos[:, None] - local_pos[None, :]
    decay_mask = jnp.where(distance >= 0.0, jnp.exp(jnp.maximum(distance, 0.0) * decay), 0.0)
    carried = lax.dynamic_index_in_dim(carried_state[0], core, 0, keepdims=False)

    inputs_wide = inputs.astype(F32)
    rows_one = rows_in(layer_norm(inputs_wide, attn_gain).astype(BF), 2)
    queries = rotate(dot(rows_one, w_query, NT), cosine, sine).astype(BF)
    keys_rot = rotate(dot(rows_one, w_key, NT), cosine, sine).astype(BF)
    values_kept = (dot(rows_one, w_value, NT) * row_mask).astype(BF)
    swish_raw = dot(rows_one, w_swish, NT)
    stretch = lambda a: (a[:HALF], a[HALF:])
    qs, ks, vs = stretch(queries), stretch(keys_rot), stretch(values_kept)
    mixing = [(dot(q, k, NT) * decay_mask).astype(BF) for q, k in zip(qs, ks)]
    local_state = dot((ks[0] * tail_fac).astype(BF), vs[0], TN)
    prior = [carried.astype(BF), (span * carried + local_state).astype(BF)]
    retained = jnp.concatenate(
        [dot(m, v, NN) + dot(q, p, NN) * head_fac for m, v, q, p in zip(mixing, vs, qs, prior)], axis=0
    )

    def gate_piece(swish_in, retained_in):
        return row_mask * jax.nn.silu(swish_in) * group_norm(retained_in)

    mixed = gate_piece(swish_raw, retained).astype(BF)
    hidden = inputs_wide + rows_out(dot(mixed, w_out, NN).astype(BF), 3)
    rows_two = rows_in(layer_norm(hidden, mlp_gain).astype(BF), 4)
    gate_pre = dot(rows_two, w_gate, NT)
    up_pre = dot(rows_two, w_up, NT)

    def mlp_piece(gate_in, up_in):
        return jax.nn.gelu(gate_in, approximate=False) * up_in

    activated = mlp_piece(gate_pre, up_pre).astype(BF)
    outputs = (hidden + rows_out(dot(activated, w_down, NN).astype(BF), 5)).astype(BF)
    grad_all = lax.all_gather(output_grad, "ctx", axis=0, tiled=True)
    grad_own = lax.dynamic_slice_in_dim(output_grad, lax.axis_index("tp") * 128, 128, 0).astype(F32)
    down_part = dot(activated, grad_all, TN)
    grad_act = dot(grad_all, w_down, NT)
    _, mlp_pull = jax.vjp(mlp_piece, gate_pre, up_pre)
    grad_gate, grad_up = (g.astype(BF) for g in mlp_pull(grad_act))
    gate_part = dot(grad_gate, rows_two, TN)
    up_part = dot(grad_up, rows_two, TN)
    grad_norm_two = rows_out((dot(grad_gate, w_gate, NN) + dot(grad_up, w_up, NN)).astype(BF), 6)
    _, norm_two_pull = jax.vjp(layer_norm, hidden, mlp_gain)
    grad_hidden_norm, mlp_gain_part = norm_two_pull(grad_norm_two)
    grad_hidden = grad_own + grad_hidden_norm
    mid_rows = rows_in(grad_hidden.astype(BF), 7)
    out_part = dot(mixed, mid_rows, TN)
    grad_mixed = dot(mid_rows, w_out, NT)
    _, gate_pull = jax.vjp(gate_piece, swish_raw, retained)
    grad_swish, grad_retained = (g.astype(BF) for g in gate_pull(grad_mixed))
    rs = stretch(grad_retained)
    grad_local = dot((qs[1] * head_fac).astype(BF), rs[1], TN).astype(BF)
    gq, gk, gv = [], [], []
    for at in (0, 1):
        grad_scores = (dot(rs[at], vs[at], NT) * decay_mask).astype(BF)
        gq.append(dot(grad_scores, ks[at], NN) + dot(rs[at], prior[at], NT) * head_fac)
        gk.append(dot(grad_scores, qs[at], TN))
        gv.append(dot(mixing[at], rs[at], TN))
    gk[0] = gk[0] + dot(vs[0], grad_local, NT) * tail_fac
    gv[0] = gv[0] + dot(ks[0], grad_local, NN) * tail_fac
    grad_query = rotate(jnp.concatenate(gq, axis=0), cosine, -sine).astype(BF)
    grad_key = rotate(jnp.concatenate(gk, axis=0), cosine, -sine).astype(BF)
    grad_value = (jnp.concatenate(gv, axis=0) * row_mask).astype(BF)
    four = (grad_query, grad_key, grad_value, grad_swish)
    sums = [dot(g, rows_one, TN) for g in four]
    total_rows = sum(dot(g, w, NN) for g, w in zip(four, (w_query, w_key, w_value, w_swish)))
    grad_norm_one = rows_out(total_rows.astype(BF), 8)
    _, norm_one_pull = jax.vjp(layer_norm, inputs_wide, attn_gain)
    grad_inputs_norm, attn_gain_part = norm_one_pull(grad_norm_one)
    input_grad = grad_hidden + grad_inputs_norm
    attn_gain_grad, mlp_gain_grad = lax.psum((attn_gain_part, mlp_gain_part), ("fsdp", "ctx", "tp"))

    summed = grads_out([part.astype(BF) for part in (*sums, out_part, gate_part, up_part, down_part)], 9)
    left, right = summed[:, :64], summed[:, 64:]
    mine = jnp.where(core == 0, left, right)
    got = swap_cores(jnp.where(core == 0, right, left))
    first, second = jnp.where(core == 0, mine, got), jnp.where(core == 0, got, mine)
    grads = []
    for k, (s, n) in enumerate(zip(STARTS, SIZES)):
        both = jnp.concatenate([first[s : s + n], second[s : s + n]], axis=0)
        grads.append(both if k in (4, 7) else both.T)
    return (
        outputs,
        input_grad,
        attn_gain_grad,
        grads[0],
        grads[1],
        grads[2],
        grads[3],
        grads[4],
        mlp_gain_grad,
        grads[5],
        grads[6],
        grads[7],
    )


def solution(mesh):
    placed = (
        P(("fsdp", "ctx", "tp"), None),
        P("fsdp"),
        P("fsdp", "tp", None, None),
        P(),
        P(("fsdp", "ctx"), "tp"),
        P(("fsdp", "ctx"), "tp"),
        P(("fsdp", "ctx"), "tp"),
        P(("fsdp", "ctx"), "tp"),
        P("tp", ("fsdp", "ctx")),
        P(),
        P(("fsdp", "ctx"), "tp"),
        P(("fsdp", "ctx"), "tp"),
        P("tp", ("fsdp", "ctx")),
        P(("fsdp", "ctx"), None),
    )
    return jax.shard_map(
        on_device,
        mesh=mesh,
        in_specs=placed,
        out_specs=(
            P(("fsdp", "ctx", "tp"), None),
            P(("fsdp", "ctx", "tp"), None),
            P(),
            P(("fsdp", "ctx"), "tp"),
            P(("fsdp", "ctx"), "tp"),
            P(("fsdp", "ctx"), "tp"),
            P(("fsdp", "ctx"), "tp"),
            P("tp", ("fsdp", "ctx")),
            P(),
            P(("fsdp", "ctx"), "tp"),
            P(("fsdp", "ctx"), "tp"),
            P("tp", ("fsdp", "ctx")),
        ),
        check_vma=False,
    )
```

```python
import functools

import jax
import jax.numpy as jnp
from jax import lax
from jax.experimental import pallas as pl
from jax.experimental.pallas import tpu as pltpu
from jax.sharding import PartitionSpec as P

D = 2048
KDIM = 256
VDIM = 432
SEQ = 1024
HALF = 512
SIZES = (256, 256, 432, 432, 432, 432, 432, 432)
STARTS = (0, 256, 512, 944, 1376, 1808, 2240, 2672)
ROWS = 3104
EPSILON = 1e-05
MESH = pl.DeviceIdType.MESH
BF = jnp.bfloat16
F32 = jnp.float32


def even(rows):
    return rows // 32 * 16


class Net:
    def __init__(self, send, recv):
        group = lax.axis_index("fsdp")
        self.c = lax.axis_index("ctx")
        self.t = lax.axis_index("tp")
        self.x = group // 4
        self.z = group % 4
        self.send, self.recv, self.used = send, recv, 0

    def dev(self, dx=0, dz=0, dt=0, dc=0):
        x, z, t = ((at + d + 4) % 4 if d else at for at, d in ((self.x, dx), (self.z, dz), (self.t, dt)))
        c = 1 - self.c if dc else self.c
        return (x * 4 + z, c, t)

    def greet(self, hops):
        barrier = pltpu.get_barrier_semaphore()
        for hop in hops:
            pl.semaphore_signal(barrier, inc=1, device_id=self.dev(**hop), device_id_type=MESH)
        pl.semaphore_wait(barrier, len(hops))

    def copy(self, src, dst, **hop):
        at = self.used
        self.used += 1
        return pltpu.make_async_remote_copy(
            src_ref=src,
            dst_ref=dst,
            send_sem=self.send.at[at],
            recv_sem=self.recv.at[at],
            device_id=self.dev(**hop),
            device_id_type=MESH,
        )


XZ_HOPS = (dict(dx=1), dict(dx=-1), dict(dz=1), dict(dz=-1))
Y_HOPS = (dict(dt=1), dict(dt=-1), dict(dc=1))


def lanes(piece):
    return pl.ds(pl.multiple_of(piece * 128, 128), 128)


def ring_views(net, axis):
    x, z = net.x, net.z
    if axis == "x":
        first = lambda ref, d, rows: ref.at[(x + d + 4) % 4, rows, lanes(z)]
        second = lambda ref, d, rows: ref.at[:, rows, lanes((z + d + 4) % 4)]
        return first, second, "dx", "dz"
    first = lambda ref, d, rows: ref.at[x, rows, lanes((z + d + 4) % 4)]
    second = lambda ref, d, rows: ref.at[(x + d + 4) % 4, rows, :]
    return first, second, "dz", "dx"


def gather_weights(net, ref, start, stop):
    cut = start + even(stop - start)
    plans = []
    for axis, lo, hi in (("z", start, cut), ("x", cut, stop)):
        mid = lo + even(hi - lo)
        whole, head, tail = pl.ds(lo, hi - lo), pl.ds(lo, mid - lo), pl.ds(mid, hi - mid)
        first, second, hop_a, hop_b = ring_views(net, axis)
        plan = []
        for view, hop in ((first, hop_a), (second, hop_b)):
            mine = view(ref, 0, whole)
            plan.append(
                (
                    net.copy(mine, mine, **{hop: 1}),
                    net.copy(mine, mine, **{hop: -1}),
                    net.copy(view(ref, -1, head), view(ref, -1, head), **{hop: 1}),
                    net.copy(view(ref, 1, tail), view(ref, 1, tail), **{hop: -1}),
                )
            )
        plans.append(plan)

    def near(phase):
        for plan in plans:
            plan[phase][0].start()
            plan[phase][1].start()

    def far(phase):
        for k in (0, 1):
            for plan in plans:
                plan[phase][k].wait_recv()
                plan[phase][2 + k].start()

    def land(phase):
        for plan in plans:
            plan[phase][2].wait_recv()
            plan[phase][3].wait_recv()

    def done():
        land(1)
        for plan in plans:
            for phase in plan:
                for copy in phase:
                    copy.wait_send()

    return [
        lambda: near(0),
        lambda: far(0),
        lambda: (land(0), near(1)),
        lambda: far(1),
        done,
    ]


def add_rows(refs, out, count):
    step = 16

    def body(i, carry):
        at = pl.ds(pl.multiple_of(i * step, step), step)
        total = refs[0](at).astype(F32)
        for ref in refs[1:]:
            total = total + ref(at).astype(F32)
        out(at, total)
        return carry

    lax.fori_loop(0, count // step, body, 0)


def scatter_shapes(rows):
    shapes = []
    cut = even(rows)
    for axis, count in (("z", cut), ("x", rows - cut)):
        head = even(count)
        for slab in ((4, 128), (1, 128)) if axis == "z" else ((1, 512), (1, 128)):
            for n in (head, count - head, count, count):
                shape = (n, slab[1]) if slab[0] == 1 else (slab[0], n, slab[1])
                shapes.append(pltpu.VMEM(shape, BF))
    return shapes


def scatter_weights(net, ref, start, stop, bufs, out):
    cut = start + even(stop - start)
    plans = []
    bufs = list(bufs)
    for axis, lo, hi in (("z", start, cut), ("x", cut, stop)):
        mid = lo + even(hi - lo)
        parts = (lo, mid - lo), (mid, hi - mid), (lo, hi - lo)
        head, tail, whole = (pl.ds(*part) for part in parts)
        far_view, near_view, hop_a, hop_b = ring_views(net, axis)
        plan = []
        if axis == "z":
            wide = lambda r, d, rows: r.at[:, rows, lanes((net.z + d + 4) % 4)]
            thin = lambda r, d, rows: r.at[(net.x + d + 4) % 4, rows, lanes(net.z)]
        else:
            wide = lambda r, d, rows: r.at[(net.x + d + 4) % 4, rows, :]
            thin = lambda r, d, rows: r.at[net.x, rows, lanes((net.z + d + 4) % 4)]
        for view, hop in ((wide, hop_a), (thin, hop_b)):
            fa, fb, ma, mb = bufs[:4]
            bufs = bufs[4:]
            plan.append(
                dict(
                    view=view,
                    bufs=(fa, fb, ma, mb),
                    copies=(
                        net.copy(view(ref, 2, head), fa, **{hop: 1}),
                        net.copy(view(ref, 2, tail), fb, **{hop: -1}),
                        net.copy(view(ref, 1, whole), ma, **{hop: 1}),
                        net.copy(view(ref, -1, whole), mb, **{hop: -1}),
                    ),
                )
            )
        plans.append((plan, parts))

    def at_rows(view, d, lo):
        def read(at):
            return view(ref, d, pl.ds(lo + at.start, at.size))[...]

        def write(at, value):
            view(ref, d, pl.ds(lo + at.start, at.size))[...] = value.astype(BF)

        return read, write

    def buf_rows(buf):
        if len(buf.shape) == 3:
            return lambda at: buf[:, at, :]
        return lambda at: buf[at, :]

    def far(phase):
        for plan, _ in plans:
            plan[phase]["copies"][0].start()
            plan[phase]["copies"][1].start()

    def near(phase):
        for k, d in ((0, 1), (1, -1)):
            for plan, parts in plans:
                step = plan[phase]
                lo, count = parts[k]
                step["copies"][k].wait_recv()
                read, write = at_rows(step["view"], d, lo)
                add_rows((read, buf_rows(step["bufs"][k])), write, count)
                step["copies"][2 + k].start()

    def total(phase, last):
        for plan, parts in plans:
            step = plan[phase]
            lo, count = parts[2]
            step["copies"][2].wait_recv()
            step["copies"][3].wait_recv()
            read, write = at_rows(step["view"], 0, lo)
            if last:
                write = lambda at, value, lo=lo: out(pl.ds(lo + at.start, at.size), value)
            add_rows((read, buf_rows(step["bufs"][2]), buf_rows(step["bufs"][3])), write, count)

    def done():
        total(1, True)
        for plan, _ in plans:
            for step in plan:
                for copy in step["copies"]:
                    copy.wait_send()

    return [
        lambda: far(0),
        lambda: near(0),
        lambda: (total(0, False), far(1)),
        lambda: near(1),
        done,
    ]


def gather_rows(net, ref):
    def block(c, t, lo=0, n=128):
        return ref.at[pl.ds(pl.multiple_of(c * 512 + t * 128 + lo, 16), n), :]

    c, t = net.c, net.t
    before, after, across = (t + 3) % 4, (t + 1) % 4, (t + 2) % 4
    own = block(c, t)
    up = net.copy(own, own, dt=1)
    down = net.copy(own, own, dt=-1)
    side = net.copy(own, own, dc=1)
    fore = net.copy(block(c, before, 0, 64), block(c, before, 0, 64), dt=1)
    back = net.copy(block(c, after, 64, 64), block(c, after, 64, 64), dt=-1)
    over = [
        net.copy(block(c, before), block(c, before), dc=1),
        net.copy(block(c, after), block(c, after), dc=1),
        net.copy(block(c, across, 0, 64), block(c, across, 0, 64), dc=1),
        net.copy(block(c, across, 64, 64), block(c, across, 64, 64), dc=1),
    ]

    def start():
        up.start()
        down.start()
        side.start()

    def forward():
        up.wait_recv()
        fore.start()
        over[0].start()
        down.wait_recv()
        back.start()
        over[1].start()

    def finish():
        fore.wait_recv()
        over[2].start()
        back.wait_recv()
        over[3].start()
        side.wait_recv()
        for copy in over:
            copy.wait_recv()
        for copy in (up, down, side, fore, back, *over):
            copy.wait_send()

    return [start, forward, finish]


ROW_BUFS = [
    pltpu.VMEM((512, D), BF),
    pltpu.VMEM((64, D), BF),
    pltpu.VMEM((64, D), BF),
    pltpu.VMEM((128, D), BF),
    pltpu.VMEM((128, D), BF),
]


def scatter_rows(net, ref, bufs, out):
    c, t = net.c, net.t
    other, far_a, far_b, near_a, near_b = bufs
    side = net.copy(ref.at[pl.ds(pl.multiple_of((1 - c) * 512, 512), 512), :], other, dc=1)

    def row(d, lo=0):
        return c * 512 + (t + d + 4) % 4 * 128 + lo

    def block(d, lo=0, n=128):
        return ref.at[pl.ds(pl.multiple_of(row(d, lo), 16), n), :]

    copies = (
        net.copy(block(2, 0, 64), far_a, dt=1),
        net.copy(block(2, 64, 64), far_b, dt=-1),
        net.copy(block(1), near_a, dt=1),
        net.copy(block(-1), near_b, dt=-1),
    )

    def read(source, base):
        return lambda at: source[pl.ds(pl.multiple_of(base + at.start, 16), at.size), :]

    def write(base):
        def store(at, value):
            ref[pl.ds(pl.multiple_of(base + at.start, 16), at.size), :] = value.astype(BF)

        return store

    def other_row(d, lo=0):
        return (t + d + 4) % 4 * 128 + lo

    def start():
        side.start()

    def far():
        side.wait_recv()
        for d, lo, k in ((2, 0, 0), (2, 64, 1)):
            add_rows((read(ref, row(d, lo)), read(other, other_row(d, lo))), write(row(d, lo)), 64)
            copies[k].start()
        for d in (1, -1, 0):
            add_rows((read(ref, row(d)), read(other, other_row(d))), write(row(d)), 128)

    def near():
        for k, d, lo, buf in ((0, 1, 0, far_a), (1, -1, 64, far_b)):
            copies[k].wait_recv()
            add_rows((read(ref, row(d, lo)), read(buf, 0)), write(row(d, lo)), 64)
            copies[2 + k].start()

    def finish():
        copies[2].wait_recv()
        copies[3].wait_recv()
        add_rows((read(ref, row(0)), read(near_a, 0), read(near_b, 0)), out, 128)
        for copy in (side, *copies):
            copy.wait_send()

    return [start, far, near, finish]


def call(kernel, outs, ins, scratch, copies, cid):
    any_spec = pl.BlockSpec(memory_space=pl.ANY)
    vmem_spec = pl.BlockSpec(memory_space=pltpu.VMEM)
    return pl.pallas_call(
        kernel,
        out_shape=[shape for shape, _ in outs],
        in_specs=[vmem_spec if v else any_spec for _, v in ins],
        out_specs=[vmem_spec if v else any_spec for _, v in outs],
        scratch_shapes=list(scratch)
        + [pltpu.SemaphoreType.DMA((copies,)), pltpu.SemaphoreType.DMA((copies,)), pltpu.SemaphoreType.DMA((40,))],
        compiler_params=pltpu.CompilerParams(
            collective_id=cid, has_side_effects=True, vmem_limit_bytes=56 * 2**20
        ),
    )(*[array for array, _ in ins])


def grads_out(parts, cid):
    def kernel(*refs):
        parts_refs, out_ref, total = refs[:8], refs[8], refs[9]
        bufs, (send, recv, local) = refs[10:-3], refs[-3:]
        net = Net(send, recv)
        loads = []
        for k, ref in enumerate(parts_refs):
            for x in range(4):
                loads.append(
                    pltpu.make_async_copy(
                        ref.at[:, pl.ds(x * 512, 512)],
                        total.at[x, pl.ds(STARTS[k], SIZES[k]), :],
                        local.at[4 * k + x],
                    )
                )
        for load in loads:
            load.start()
        net.greet(XZ_HOPS)
        for load in loads:
            load.wait()

        def out(at, value):
            out_ref[at, :] = value

        for stage in scatter_weights(net, total, 0, ROWS, bufs, out):
            stage()

    (out,) = call(
        kernel,
        [(jax.ShapeDtypeStruct((ROWS, 128), F32), True)],
        [(part, False) for part in parts],
        [pltpu.VMEM((4, ROWS, 512), BF)] + scatter_shapes(ROWS),
        16,
        cid,
    )
    return out


def rows_in(own, cid):
    def kernel(own_ref, out_ref, rows, send, recv, local):
        net = Net(send, recv)
        at = pl.ds(pl.multiple_of(net.c * 512 + net.t * 128, 128), 128)
        load = pltpu.make_async_copy(own_ref, rows.at[at, :], local.at[0])
        load.start()
        net.greet(Y_HOPS)
        load.wait()
        for stage in gather_rows(net, rows):
            stage()
        store = pltpu.make_async_copy(rows, out_ref, local.at[0])
        store.start()
        store.wait()

    (out,) = call(
        kernel, [(jax.ShapeDtypeStruct((SEQ, D), BF), False)], [(own, False)], [pltpu.VMEM((SEQ, D), BF)], 9, cid
    )
    return out


def rows_out(part, cid):
    def kernel(part_ref, out_ref, total, *rest):
        bufs, (send, recv, local) = rest[:5], rest[5:]
        net = Net(send, recv)
        load = pltpu.make_async_copy(part_ref, total, local.at[0])
        load.start()
        net.greet(Y_HOPS)
        load.wait()

        def out(at, value):
            out_ref[at, :] = value

        for stage in scatter_rows(net, total, bufs, out):
            stage()

    (out,) = call(
        kernel,
        [(jax.ShapeDtypeStruct((128, D), F32), True)],
        [(part, False)],
        [pltpu.VMEM((SEQ, D), BF)] + ROW_BUFS,
        5,
        cid,
    )
    return out


def dot(a, b, dims):
    return lax.dot_general(a, b, (dims, ((), ())), preferred_element_type=F32)


NN = ((1,), (0,))
NT = ((1,), (1,))
TN = ((0,), (0,))


def normal(rows, width):
    centred = rows - jnp.sum(rows, axis=-1, keepdims=True) * (1.0 / width)
    spread = jnp.sum(centred * centred, axis=-1, keepdims=True) * (1.0 / width)
    return centred, lax.rsqrt(spread + EPSILON)


def loop(count, step, body):
    def turn(i, carry):
        body(pl.ds(pl.multiple_of(i * step, step), step))
        return carry

    lax.fori_loop(0, count // step, turn, 0)


def times(rows_ref, rows, weights, k):
    total = None
    for x in range(4):
        part = dot(rows_ref[rows, x * 512 : x * 512 + 512], weights[x, STARTS[k] : STARTS[k] + SIZES[k], :], NT)
        total = part if total is None else total + part
    return total


def forward(piece, inputs, carried_state, attn_gain, mlp_gain, cosine, sine, row_mask, lam, cid):
    def kernel(
        piece_ref, in_ref, carried_ref, gain_one, gain_two, cos_ref, sin_ref, mask_ref, lam_ref,
        weights_out, one_out, two_out, q_ref, k_ref, v_ref, s_ref, mix_ref, norm_ref, dev_ref, mixed_ref, prior_ref,
        hidden_ref,
        weights, one, two, carried, part, *rest,
    ):
        bufs, (send, recv, local) = rest[:5], rest[5:]
        net = Net(send, recv)
        c, t = net.c, net.t
        load = pltpu.make_async_copy(piece_ref, weights.at[net.x, :, lanes(net.z)], local.at[0])
        load.start()
        load_state = pltpu.make_async_copy(carried_ref.at[0, c], carried, local.at[1])
        load_state.start()
        own = c * 512 + t * 128

        def norm_rows(source, gain, rows_ref):
            def body(at):
                centred, dev = normal(source[at, :].astype(F32), D)
                to = pl.ds(pl.multiple_of(own + at.start, 16), at.size)
                rows_ref[to, :] = (centred * dev * gain[...]).astype(BF)

            loop(128, 32, body)

        norm_rows(in_ref, gain_one, one)
        net.greet(XZ_HOPS + Y_HOPS)
        y1 = gather_rows(net, one)
        g1, g2, g3, g4 = (
            gather_weights(net, weights, lo, hi) for lo, hi in ((0, 1376), (1376, 1808), (1808, 2672), (2672, 3104))
        )
        load.wait()
        g1[0]()
        y1[0]()
        g1[1]()
        g1[2]()
        y1[1]()
        g2[0]()
        y1[2]()
        g2[1]()
        g1[3]()
        g2[2]()
        g1[4]()

        def project(at):
            cs, sn = cos_ref[at, :], sin_ref[at, :]
            for k, ref in ((0, q_ref), (1, k_ref)):
                raw = times(one, at, weights, k)
                former, latter = raw[:, :128], raw[:, 128:]
                ref[at, :128] = (former * cs - latter * sn).astype(BF)
                ref[at, 128:] = (former * sn + latter * cs).astype(BF)
            v_ref[at, :] = (times(one, at, weights, 2) * mask_ref[at, :]).astype(BF)
            s_ref[at, :] = times(one, at, weights, 3)

        loop(SEQ, 256, project)
        g2[3]()
        g3[0]()

        decay = lam_ref[0:1, 0:1]
        load_state.wait()
        prior_ref[0] = carried[...].astype(BF)
        far = lax.broadcasted_iota(jnp.int32, (HALF, 1), 0).astype(F32)
        tail = jnp.exp((HALF - 1.0 - far) * decay)
        local_state = dot((k_ref[:HALF, :].astype(F32) * tail).astype(BF), v_ref[:HALF, :], TN)
        prior_ref[1] = (jnp.exp(HALF * decay) * carried[...] + local_state).astype(BF)

        for stretch in range(2):
            keys = pl.ds(stretch * HALF, HALF)

            def retain(rows, stretch=stretch, keys=keys):
                at = pl.ds(pl.multiple_of(stretch * HALF + rows.start, rows.size), rows.size)
                n = lax.broadcasted_iota(jnp.int32, (rows.size, HALF), 0) + rows.start
                distance = (n - lax.broadcasted_iota(jnp.int32, (rows.size, HALF), 1)).astype(F32)
                fade = jnp.where(distance >= 0.0, jnp.exp(jnp.maximum(distance, 0.0) * decay), 0.0)
                mixing = (dot(q_ref[at, :], k_ref[keys, :], NT) * fade).astype(BF)
                mix_ref[at, :] = mixing
                ahead = lax.broadcasted_iota(jnp.int32, (rows.size, 1), 0) + rows.start + 1
                head = jnp.exp(ahead.astype(F32) * decay)
                retained = dot(mixing, v_ref[keys, :], NN) + dot(q_ref[at, :], prior_ref[stretch], NN) * head
                centred, dev = normal(retained, VDIM)
                normed = centred * dev
                norm_ref[at, :] = normed
                dev_ref[at, :] = dev
                swish = s_ref[at, :]
                mixed_ref[at, :] = (mask_ref[at, :] * (swish * jax.nn.sigmoid(swish)) * normed).astype(BF)

            loop(HALF, 128, retain)

        g2[4]()
        g3[1]()

        def out_rows(base):
            def body(rows):
                at = pl.ds(pl.multiple_of(base + rows.start, rows.size), rows.size)
                for x in range(4):
                    got = dot(mixed_ref[at, :], weights[x, STARTS[4] : STARTS[4] + VDIM, :], NN)
                    part[at, x * 512 : x * 512 + 512] = got.astype(BF)

            loop(HALF, 256, body)

        def take(at, value):
            hidden_ref[at, :] = in_ref[at, :].astype(F32) + value

        r1 = scatter_rows(net, part, bufs, take)
        out_rows((1 - c) * HALF)
        r1[0]()
        out_rows(c * HALF)
        g3[2]()
        r1[1]()
        g4[0]()
        r1[2]()
        g3[3]()
        g4[1]()
        r1[3]()
        norm_rows(hidden_ref, gain_two, two)
        y2 = gather_rows(net, two)
        y2[0]()
        g3[4]()
        g4[2]()
        store_one = pltpu.make_async_copy(one, one_out, local.at[2])
        store_one.start()
        y2[1]()
        g4[3]()
        y2[2]()
        store_two = pltpu.make_async_copy(two, two_out, local.at[3])
        store_two.start()
        g4[4]()
        stores = [store_one, store_two]
        for x in range(4):
            store = pltpu.make_async_copy(weights.at[x], weights_out.at[:, pl.ds(x * 512, 512)], local.at[4 + x])
            store.start()
            stores.append(store)
        for store in stores:
            store.wait()

    def shape(*dims, kind=BF):
        return jax.ShapeDtypeStruct(dims, kind)

    return call(
        kernel,
        [
            (shape(ROWS, D), False),
            (shape(SEQ, D), False),
            (shape(SEQ, D), False),
            (shape(SEQ, KDIM), True),
            (shape(SEQ, KDIM), True),
            (shape(SEQ, VDIM), True),
            (shape(SEQ, VDIM, kind=F32), True),
            (shape(SEQ, HALF), True),
            (shape(SEQ, VDIM, kind=F32), True),
            (shape(SEQ, 1, kind=F32), True),
            (shape(SEQ, VDIM), True),
            (shape(2, KDIM, VDIM), True),
            (shape(128, D, kind=F32), True),
        ],
        [
            (piece, False),
            (inputs, True),
            (carried_state, False),
            (attn_gain, True),
            (mlp_gain, True),
            (cosine, True),
            (sine, True),
            (row_mask, True),
            (lam, True),
        ],
        [
            pltpu.VMEM((4, ROWS, 512), BF),
            pltpu.VMEM((SEQ, D), BF),
            pltpu.VMEM((SEQ, D), BF),
            pltpu.VMEM((KDIM, VDIM), F32),
            pltpu.VMEM((SEQ, D), BF),
        ]
        + ROW_BUFS,
        100,
        cid,
    )


def layer_norm(rows_in, gain):
    centre = jnp.mean(rows_in, axis=-1, keepdims=True)
    centred = rows_in - centre
    spread = jnp.mean(centred * centred, axis=-1, keepdims=True)
    return centred * lax.rsqrt(spread + EPSILON) * gain


def rotate(field, cosine, sine):
    former, latter = field[:, :128], field[:, 128:]
    return jnp.concatenate([former * cosine - latter * sine, former * sine + latter * cosine], axis=1)


def swap_cores(array):
    return lax.ppermute(array, "ctx", [(0, 1), (1, 0)])


def on_device(
    inputs,
    seq_lengths,
    carried_state,
    attn_gain,
    query_weight,
    key_weight,
    value_weight,
    swish_weight,
    out_weight,
    mlp_gain,
    gate_weight,
    up_weight,
    down_weight,
    output_grad,
):
    core = lax.axis_index("ctx")
    head = lax.axis_index("tp") * 2 + core

    def for_core(which):
        parts = []
        for k, weight in enumerate(
            (query_weight, key_weight, value_weight, swish_weight, out_weight, gate_weight, up_weight, down_weight)
        ):
            n = SIZES[k]
            if k in (4, 7):
                parts.append(lax.dynamic_slice_in_dim(weight, which * n, n, 0))
            else:
                parts.append(lax.dynamic_slice_in_dim(weight, which * n, n, 1).T)
        return jnp.concatenate(parts, axis=0)

    mine, got = for_core(core), swap_cores(for_core(1 - core))
    piece = jnp.where(core == 0, jnp.concatenate([mine, got], axis=1), jnp.concatenate([got, mine], axis=1))
    position = jnp.arange(SEQ, dtype=jnp.int32)
    row_mask = (position < seq_lengths[0]).astype(F32)[:, None]
    frequency = jnp.power(10000.0, -jnp.arange(128).astype(F32) / 128)
    angles = position.astype(F32)[:, None] * frequency[None, :]
    cosine, sine = jnp.cos(angles), jnp.sin(angles)
    decay = -jnp.power(2.0, 5.0 - head.astype(F32)) / SEQ
    (
        weights, rows_one, rows_two, queries, keys_rot, values_kept, swish_raw, mix, normed, dev, mixed, prior, hidden
    ) = forward(
        piece, inputs, carried_state, attn_gain[None, :], mlp_gain[None, :], cosine, sine, row_mask,
        jnp.full((8, 128), decay, F32), 1
    )
    w_query, w_key, w_value, w_swish, w_out, w_gate, w_up, w_down = (
        weights[s : s + n] for s, n in zip(STARTS, SIZES)
    )
    local_pos = jnp.arange(HALF).astype(F32)
    tail_fac = jnp.exp((HALF - 1.0 - local_pos) * decay)[:, None]
    head_fac = jnp.exp((local_pos + 1.0) * decay)[:, None]
    distance = local_pos[:, None] - local_pos[None, :]
    decay_mask = jnp.where(distance >= 0.0, jnp.exp(jnp.maximum(distance, 0.0) * decay), 0.0)
    inputs_wide = inputs.astype(F32)
    stretch = lambda a: (a[:HALF], a[HALF:])
    qs, ks, vs, mixing = stretch(queries), stretch(keys_rot), stretch(values_kept), stretch(mix)
    gate_pre = dot(rows_two, w_gate, NT)
    up_pre = dot(rows_two, w_up, NT)

    def mlp_piece(gate_in, up_in):
        return jax.nn.gelu(gate_in, approximate=False) * up_in

    activated = mlp_piece(gate_pre, up_pre).astype(BF)
    outputs = (hidden + rows_out(dot(activated, w_down, NN).astype(BF), 5)).astype(BF)
    grad_all = lax.all_gather(output_grad, "ctx", axis=0, tiled=True)
    grad_own = lax.dynamic_slice_in_dim(output_grad, lax.axis_index("tp") * 128, 128, 0).astype(F32)
    down_part = dot(activated, grad_all, TN)
    grad_act = dot(grad_all, w_down, NT)
    _, mlp_pull = jax.vjp(mlp_piece, gate_pre, up_pre)
    grad_gate, grad_up = (g.astype(BF) for g in mlp_pull(grad_act))
    gate_part = dot(grad_gate, rows_two, TN)
    up_part = dot(grad_up, rows_two, TN)
    grad_norm_two = rows_out((dot(grad_gate, w_gate, NN) + dot(grad_up, w_up, NN)).astype(BF), 6)
    _, norm_two_pull = jax.vjp(layer_norm, hidden, mlp_gain)
    grad_hidden_norm, mlp_gain_part = norm_two_pull(grad_norm_two)
    grad_hidden = grad_own + grad_hidden_norm
    mid_rows = rows_in(grad_hidden.astype(BF), 7)
    out_part = dot(mixed, mid_rows, TN)
    grad_mixed = dot(mid_rows, w_out, NT)
    sig = jax.nn.sigmoid(swish_raw)
    grad_swish = (row_mask * grad_mixed * normed * (sig * (1.0 + swish_raw * (1.0 - sig)))).astype(BF)
    grad_normed = row_mask * grad_mixed * (swish_raw * sig)
    grad_normed = grad_normed - jnp.mean(grad_normed, axis=-1, keepdims=True) - normed * jnp.mean(
        grad_normed * normed, axis=-1, keepdims=True
    )
    grad_retained = (grad_normed * dev).astype(BF)
    rs = stretch(grad_retained)
    grad_local = dot((qs[1] * head_fac).astype(BF), rs[1], TN).astype(BF)
    gq, gk, gv = [], [], []
    for at in (0, 1):
        grad_scores = (dot(rs[at], vs[at], NT) * decay_mask).astype(BF)
        gq.append(dot(grad_scores, ks[at], NN) + dot(rs[at], prior[at], NT) * head_fac)
        gk.append(dot(grad_scores, qs[at], TN))
        gv.append(dot(mixing[at], rs[at], TN))
    gk[0] = gk[0] + dot(vs[0], grad_local, NT) * tail_fac
    gv[0] = gv[0] + dot(ks[0], grad_local, NN) * tail_fac
    grad_query = rotate(jnp.concatenate(gq, axis=0), cosine, -sine).astype(BF)
    grad_key = rotate(jnp.concatenate(gk, axis=0), cosine, -sine).astype(BF)
    grad_value = (jnp.concatenate(gv, axis=0) * row_mask).astype(BF)
    four = (grad_query, grad_key, grad_value, grad_swish)
    sums = [dot(g, rows_one, TN) for g in four]
    total_rows = sum(dot(g, w, NN) for g, w in zip(four, (w_query, w_key, w_value, w_swish)))
    grad_norm_one = rows_out(total_rows.astype(BF), 8)
    _, norm_one_pull = jax.vjp(layer_norm, inputs_wide, attn_gain)
    grad_inputs_norm, attn_gain_part = norm_one_pull(grad_norm_one)
    input_grad = grad_hidden + grad_inputs_norm
    attn_gain_grad, mlp_gain_grad = lax.psum((attn_gain_part, mlp_gain_part), ("fsdp", "ctx", "tp"))

    summed = grads_out([part.astype(BF) for part in (*sums, out_part, gate_part, up_part, down_part)], 9)
    left, right = summed[:, :64], summed[:, 64:]
    mine = jnp.where(core == 0, left, right)
    got = swap_cores(jnp.where(core == 0, right, left))
    first, second = jnp.where(core == 0, mine, got), jnp.where(core == 0, got, mine)
    grads = []
    for k, (s, n) in enumerate(zip(STARTS, SIZES)):
        both = jnp.concatenate([first[s : s + n], second[s : s + n]], axis=0)
        grads.append(both if k in (4, 7) else both.T)
    return (
        outputs,
        input_grad,
        attn_gain_grad,
        grads[0],
        grads[1],
        grads[2],
        grads[3],
        grads[4],
        mlp_gain_grad,
        grads[5],
        grads[6],
        grads[7],
    )


def solution(mesh):
    placed = (
        P(("fsdp", "ctx", "tp"), None),
        P("fsdp"),
        P("fsdp", "tp", None, None),
        P(),
        P(("fsdp", "ctx"), "tp"),
        P(("fsdp", "ctx"), "tp"),
        P(("fsdp", "ctx"), "tp"),
        P(("fsdp", "ctx"), "tp"),
        P("tp", ("fsdp", "ctx")),
        P(),
        P(("fsdp", "ctx"), "tp"),
        P(("fsdp", "ctx"), "tp"),
        P("tp", ("fsdp", "ctx")),
        P(("fsdp", "ctx"), None),
    )
    return jax.shard_map(
        on_device,
        mesh=mesh,
        in_specs=placed,
        out_specs=(
            P(("fsdp", "ctx", "tp"), None),
            P(("fsdp", "ctx", "tp"), None),
            P(),
            P(("fsdp", "ctx"), "tp"),
            P(("fsdp", "ctx"), "tp"),
            P(("fsdp", "ctx"), "tp"),
            P(("fsdp", "ctx"), "tp"),
            P("tp", ("fsdp", "ctx")),
            P(),
            P(("fsdp", "ctx"), "tp"),
            P(("fsdp", "ctx"), "tp"),
            P("tp", ("fsdp", "ctx")),
        ),
        check_vma=False,
    )
```

```python
import functools

import jax
import jax.numpy as jnp
from jax import lax
from jax.experimental import pallas as pl
from jax.experimental.pallas import tpu as pltpu
from jax.sharding import PartitionSpec as P

D = 2048
KDIM = 256
VDIM = 432
SEQ = 1024
HALF = 512
SIZES = (256, 256, 432, 432, 432, 432, 432, 432)
STARTS = (0, 256, 512, 944, 1376, 1808, 2240, 2672)
ROWS = 3104
EPSILON = 1e-05
MESH = pl.DeviceIdType.MESH
BF = jnp.bfloat16
F32 = jnp.float32


def even(rows):
    return rows // 32 * 16


class Net:
    def __init__(self, send, recv):
        group = lax.axis_index("fsdp")
        self.c = lax.axis_index("ctx")
        self.t = lax.axis_index("tp")
        self.x = group // 4
        self.z = group % 4
        self.send, self.recv, self.used = send, recv, 0

    def dev(self, dx=0, dz=0, dt=0, dc=0):
        x, z, t = ((at + d + 4) % 4 if d else at for at, d in ((self.x, dx), (self.z, dz), (self.t, dt)))
        c = 1 - self.c if dc else self.c
        return (x * 4 + z, c, t)

    def greet(self, hops):
        barrier = pltpu.get_barrier_semaphore()
        for hop in hops:
            pl.semaphore_signal(barrier, inc=1, device_id=self.dev(**hop), device_id_type=MESH)
        pl.semaphore_wait(barrier, len(hops))

    def copy(self, src, dst, **hop):
        at = self.used
        self.used += 1
        return pltpu.make_async_remote_copy(
            src_ref=src,
            dst_ref=dst,
            send_sem=self.send.at[at],
            recv_sem=self.recv.at[at],
            device_id=self.dev(**hop),
            device_id_type=MESH,
        )


XZ_HOPS = (dict(dx=1), dict(dx=-1), dict(dz=1), dict(dz=-1))
Y_HOPS = (dict(dt=1), dict(dt=-1), dict(dc=1))


def lanes(piece):
    return pl.ds(pl.multiple_of(piece * 128, 128), 128)


def ring_views(net, axis):
    x, z = net.x, net.z
    if axis == "x":
        first = lambda ref, d, rows: ref.at[(x + d + 4) % 4, rows, lanes(z)]
        second = lambda ref, d, rows: ref.at[:, rows, lanes((z + d + 4) % 4)]
        return first, second, "dx", "dz"
    first = lambda ref, d, rows: ref.at[x, rows, lanes((z + d + 4) % 4)]
    second = lambda ref, d, rows: ref.at[(x + d + 4) % 4, rows, :]
    return first, second, "dz", "dx"


def gather_weights(net, ref, start, stop):
    cut = start + even(stop - start)
    plans = []
    for axis, lo, hi in (("z", start, cut), ("x", cut, stop)):
        mid = lo + even(hi - lo)
        whole, head, tail = pl.ds(lo, hi - lo), pl.ds(lo, mid - lo), pl.ds(mid, hi - mid)
        first, second, hop_a, hop_b = ring_views(net, axis)
        plan = []
        for view, hop in ((first, hop_a), (second, hop_b)):
            mine = view(ref, 0, whole)
            plan.append(
                (
                    net.copy(mine, mine, **{hop: 1}),
                    net.copy(mine, mine, **{hop: -1}),
                    net.copy(view(ref, -1, head), view(ref, -1, head), **{hop: 1}),
                    net.copy(view(ref, 1, tail), view(ref, 1, tail), **{hop: -1}),
                )
            )
        plans.append(plan)

    def near(phase):
        for plan in plans:
            plan[phase][0].start()
            plan[phase][1].start()

    def far(phase):
        for k in (0, 1):
            for plan in plans:
                plan[phase][k].wait_recv()
                plan[phase][2 + k].start()

    def land(phase):
        for plan in plans:
            plan[phase][2].wait_recv()
            plan[phase][3].wait_recv()

    def done():
        land(1)
        for plan in plans:
            for phase in plan:
                for copy in phase:
                    copy.wait_send()

    return [
        lambda: near(0),
        lambda: far(0),
        lambda: (land(0), near(1)),
        lambda: far(1),
        done,
    ]


def add_rows(refs, out, count):
    step = 16

    def body(i, carry):
        at = pl.ds(pl.multiple_of(i * step, step), step)
        total = refs[0](at).astype(F32)
        for ref in refs[1:]:
            total = total + ref(at).astype(F32)
        out(at, total)
        return carry

    lax.fori_loop(0, count // step, body, 0)


def scatter_shapes(rows):
    shapes = []
    cut = even(rows)
    for axis, count in (("z", cut), ("x", rows - cut)):
        head = even(count)
        for slab in ((4, 128), (1, 128)) if axis == "z" else ((1, 512), (1, 128)):
            for n in (head, count - head, count, count):
                shape = (n, slab[1]) if slab[0] == 1 else (slab[0], n, slab[1])
                shapes.append(pltpu.VMEM(shape, BF))
    return shapes


def scatter_weights(net, ref, start, stop, bufs, out):
    cut = start + even(stop - start)
    plans = []
    bufs = list(bufs)
    for axis, lo, hi in (("z", start, cut), ("x", cut, stop)):
        mid = lo + even(hi - lo)
        parts = (lo, mid - lo), (mid, hi - mid), (lo, hi - lo)
        head, tail, whole = (pl.ds(*part) for part in parts)
        far_view, near_view, hop_a, hop_b = ring_views(net, axis)
        plan = []
        if axis == "z":
            wide = lambda r, d, rows: r.at[:, rows, lanes((net.z + d + 4) % 4)]
            thin = lambda r, d, rows: r.at[(net.x + d + 4) % 4, rows, lanes(net.z)]
        else:
            wide = lambda r, d, rows: r.at[(net.x + d + 4) % 4, rows, :]
            thin = lambda r, d, rows: r.at[net.x, rows, lanes((net.z + d + 4) % 4)]
        for view, hop in ((wide, hop_a), (thin, hop_b)):
            fa, fb, ma, mb = bufs[:4]
            bufs = bufs[4:]
            plan.append(
                dict(
                    view=view,
                    bufs=(fa, fb, ma, mb),
                    copies=(
                        net.copy(view(ref, 2, head), fa, **{hop: 1}),
                        net.copy(view(ref, 2, tail), fb, **{hop: -1}),
                        net.copy(view(ref, 1, whole), ma, **{hop: 1}),
                        net.copy(view(ref, -1, whole), mb, **{hop: -1}),
                    ),
                )
            )
        plans.append((plan, parts))

    def at_rows(view, d, lo):
        def read(at):
            return view(ref, d, pl.ds(lo + at.start, at.size))[...]

        def write(at, value):
            view(ref, d, pl.ds(lo + at.start, at.size))[...] = value.astype(BF)

        return read, write

    def buf_rows(buf):
        if len(buf.shape) == 3:
            return lambda at: buf[:, at, :]
        return lambda at: buf[at, :]

    def far(phase):
        for plan, _ in plans:
            plan[phase]["copies"][0].start()
            plan[phase]["copies"][1].start()

    def near(phase):
        for k, d in ((0, 1), (1, -1)):
            for plan, parts in plans:
                step = plan[phase]
                lo, count = parts[k]
                step["copies"][k].wait_recv()
                read, write = at_rows(step["view"], d, lo)
                add_rows((read, buf_rows(step["bufs"][k])), write, count)
                step["copies"][2 + k].start()

    def total(phase, last):
        for plan, parts in plans:
            step = plan[phase]
            lo, count = parts[2]
            step["copies"][2].wait_recv()
            step["copies"][3].wait_recv()
            read, write = at_rows(step["view"], 0, lo)
            if last:
                write = lambda at, value, lo=lo: out(pl.ds(lo + at.start, at.size), value)
            add_rows((read, buf_rows(step["bufs"][2]), buf_rows(step["bufs"][3])), write, count)

    def done():
        total(1, True)
        for plan, _ in plans:
            for step in plan:
                for copy in step["copies"]:
                    copy.wait_send()

    return [
        lambda: far(0),
        lambda: near(0),
        lambda: (total(0, False), far(1)),
        lambda: near(1),
        done,
    ]


def gather_rows(net, ref):
    def block(c, t, lo=0, n=128):
        return ref.at[pl.ds(pl.multiple_of(c * 512 + t * 128 + lo, 16), n), :]

    c, t = net.c, net.t
    before, after, across = (t + 3) % 4, (t + 1) % 4, (t + 2) % 4
    own = block(c, t)
    up = net.copy(own, own, dt=1)
    down = net.copy(own, own, dt=-1)
    side = net.copy(own, own, dc=1)
    fore = net.copy(block(c, before, 0, 64), block(c, before, 0, 64), dt=1)
    back = net.copy(block(c, after, 64, 64), block(c, after, 64, 64), dt=-1)
    over = [
        net.copy(block(c, before), block(c, before), dc=1),
        net.copy(block(c, after), block(c, after), dc=1),
        net.copy(block(c, across, 0, 64), block(c, across, 0, 64), dc=1),
        net.copy(block(c, across, 64, 64), block(c, across, 64, 64), dc=1),
    ]

    def start():
        up.start()
        down.start()
        side.start()

    def forward():
        up.wait_recv()
        fore.start()
        over[0].start()
        down.wait_recv()
        back.start()
        over[1].start()

    def finish():
        fore.wait_recv()
        over[2].start()
        back.wait_recv()
        over[3].start()
        side.wait_recv()
        for copy in over:
            copy.wait_recv()
        for copy in (up, down, side, fore, back, *over):
            copy.wait_send()

    return [start, forward, finish]


ROW_BUFS = [
    pltpu.VMEM((512, D), BF),
    pltpu.VMEM((64, D), BF),
    pltpu.VMEM((64, D), BF),
    pltpu.VMEM((128, D), BF),
    pltpu.VMEM((128, D), BF),
]


def scatter_rows(net, ref, bufs, out, source=None):
    c, t = net.c, net.t
    other, far_a, far_b, near_a, near_b = bufs
    source = ref if source is None else source
    side = net.copy(source.at[pl.ds(pl.multiple_of((1 - c) * 512, 512), 512), :], other, dc=1)

    def row(d, lo=0):
        return c * 512 + (t + d + 4) % 4 * 128 + lo

    def block(d, lo=0, n=128):
        return ref.at[pl.ds(pl.multiple_of(row(d, lo), 16), n), :]

    copies = (
        net.copy(block(2, 0, 64), far_a, dt=1),
        net.copy(block(2, 64, 64), far_b, dt=-1),
        net.copy(block(1), near_a, dt=1),
        net.copy(block(-1), near_b, dt=-1),
    )

    def read(source, base):
        return lambda at: source[pl.ds(pl.multiple_of(base + at.start, 16), at.size), :]

    def write(base):
        def store(at, value):
            ref[pl.ds(pl.multiple_of(base + at.start, 16), at.size), :] = value.astype(BF)

        return store

    def other_row(d, lo=0):
        return (t + d + 4) % 4 * 128 + lo

    def start():
        side.start()

    def far():
        side.wait_recv()
        for d, lo, k in ((2, 0, 0), (2, 64, 1)):
            add_rows((read(ref, row(d, lo)), read(other, other_row(d, lo))), write(row(d, lo)), 64)
            copies[k].start()
        for d in (1, -1, 0):
            add_rows((read(ref, row(d)), read(other, other_row(d))), write(row(d)), 128)

    def near():
        for k, d, lo, buf in ((0, 1, 0, far_a), (1, -1, 64, far_b)):
            copies[k].wait_recv()
            add_rows((read(ref, row(d, lo)), read(buf, 0)), write(row(d, lo)), 64)
            copies[2 + k].start()

    def finish():
        copies[2].wait_recv()
        copies[3].wait_recv()
        add_rows((read(ref, row(0)), read(near_a, 0), read(near_b, 0)), out, 128)
        for copy in (side, *copies):
            copy.wait_send()

    return [start, far, near, finish]


def call(kernel, outs, ins, scratch, copies, cid):
    any_spec = pl.BlockSpec(memory_space=pl.ANY)
    vmem_spec = pl.BlockSpec(memory_space=pltpu.VMEM)
    return pl.pallas_call(
        kernel,
        out_shape=[shape for shape, _ in outs],
        in_specs=[vmem_spec if v else any_spec for _, v in ins],
        out_specs=[vmem_spec if v else any_spec for _, v in outs],
        scratch_shapes=list(scratch)
        + [pltpu.SemaphoreType.DMA((copies,)), pltpu.SemaphoreType.DMA((copies,)), pltpu.SemaphoreType.DMA((40,))],
        compiler_params=pltpu.CompilerParams(
            collective_id=cid, has_side_effects=True, vmem_limit_bytes=61 * 2**20
        ),
    )(*[array for array, _ in ins])


def dot(a, b, dims):
    return lax.dot_general(a, b, (dims, ((), ())), preferred_element_type=F32)


NN = ((1,), (0,))
NT = ((1,), (1,))
TN = ((0,), (0,))


def normal(rows, width):
    centred = rows - jnp.sum(rows, axis=-1, keepdims=True) * (1.0 / width)
    spread = jnp.sum(centred * centred, axis=-1, keepdims=True) * (1.0 / width)
    return centred, lax.rsqrt(spread + EPSILON)


def loop(count, step, body):
    def turn(i, carry):
        body(pl.ds(pl.multiple_of(i * step, step), step))
        return carry

    lax.fori_loop(0, count // step, turn, 0)


def times(rows_ref, rows, weights, k):
    total = None
    for x in range(4):
        part = dot(rows_ref[rows, x * 512 : x * 512 + 512], weights[x, STARTS[k] : STARTS[k] + SIZES[k], :], NT)
        total = part if total is None else total + part
    return total


def forward(piece, inputs, carried_state, attn_gain, mlp_gain, cosine, sine, row_mask, lam, output_grad, cid):
    def kernel(
        piece_ref, in_ref, carried_ref, gain_one, gain_two, cos_ref, sin_ref, mask_ref, lam_ref, grad_ref,
        weights_out, one_out, two_out, q_ref, k_ref, v_ref, s_ref, mix_ref, norm_ref, dev_ref, mixed_ref, prior_ref,
        hidden_ref, grad_out,
        weights, one, two, carried, part, *rest,
    ):
        bufs, (send, recv, local) = rest[:5], rest[5:]
        net = Net(send, recv)
        c, t = net.c, net.t
        load = pltpu.make_async_copy(piece_ref, weights.at[net.x, :, lanes(net.z)], local.at[0])
        load.start()
        load_state = pltpu.make_async_copy(carried_ref.at[0, c], carried, local.at[1])
        load_state.start()
        own = c * 512 + t * 128

        def norm_rows(source, gain, rows_ref):
            def body(at):
                centred, dev = normal(source[at, :].astype(F32), D)
                to = pl.ds(pl.multiple_of(own + at.start, 16), at.size)
                rows_ref[to, :] = (centred * dev * gain[...]).astype(BF)

            loop(128, 32, body)

        norm_rows(in_ref, gain_one, one)
        net.greet(XZ_HOPS + Y_HOPS)
        swap = net.copy(grad_ref, grad_out, dc=1)
        y1 = gather_rows(net, one)
        g1, g2, g3, g4 = (
            gather_weights(net, weights, lo, hi) for lo, hi in ((0, 1376), (1376, 1808), (1808, 2672), (2672, 3104))
        )
        load.wait()
        g1[0]()
        y1[0]()
        g1[1]()
        g1[2]()
        y1[1]()
        swap.start()
        g2[0]()
        y1[2]()
        g2[1]()
        g1[3]()
        g2[2]()
        g1[4]()

        def project(at):
            cs, sn = cos_ref[at, :], sin_ref[at, :]
            for k, ref in ((0, q_ref), (1, k_ref)):
                raw = times(one, at, weights, k)
                former, latter = raw[:, :128], raw[:, 128:]
                ref[at, :128] = (former * cs - latter * sn).astype(BF)
                ref[at, 128:] = (former * sn + latter * cs).astype(BF)
            v_ref[at, :] = (times(one, at, weights, 2) * mask_ref[at, :]).astype(BF)
            s_ref[at, :] = times(one, at, weights, 3).astype(BF)

        loop(SEQ, 256, project)
        g2[3]()
        g3[0]()

        decay = lam_ref[0:1, 0:1]
        load_state.wait()
        prior_ref[0] = carried[...].astype(BF)
        far = lax.broadcasted_iota(jnp.int32, (HALF, 1), 0).astype(F32)
        tail = jnp.exp((HALF - 1.0 - far) * decay)
        local_state = dot((k_ref[:HALF, :].astype(F32) * tail).astype(BF), v_ref[:HALF, :], TN)
        prior_ref[1] = (jnp.exp(HALF * decay) * carried[...] + local_state).astype(BF)

        for stretch in range(2):
            keys = pl.ds(stretch * HALF, HALF)

            def retain(rows, stretch=stretch, keys=keys):
                at = pl.ds(pl.multiple_of(stretch * HALF + rows.start, rows.size), rows.size)
                n = lax.broadcasted_iota(jnp.int32, (rows.size, HALF), 0) + rows.start
                distance = (n - lax.broadcasted_iota(jnp.int32, (rows.size, HALF), 1)).astype(F32)
                fade = jnp.where(distance >= 0.0, jnp.exp(jnp.maximum(distance, 0.0) * decay), 0.0)
                mixing = (dot(q_ref[at, :], k_ref[keys, :], NT) * fade).astype(BF)
                mix_ref[at, :] = mixing
                ahead = lax.broadcasted_iota(jnp.int32, (rows.size, 1), 0) + rows.start + 1
                head = jnp.exp(ahead.astype(F32) * decay)
                retained = dot(mixing, v_ref[keys, :], NN) + dot(q_ref[at, :], prior_ref[stretch], NN) * head
                centred, dev = normal(retained, VDIM)
                normed = centred * dev
                norm_ref[at, :] = normed.astype(BF)
                dev_ref[at, :] = dev
                swish = s_ref[at, :].astype(F32)
                mixed_ref[at, :] = (mask_ref[at, :] * (swish * jax.nn.sigmoid(swish)) * normed).astype(BF)

            loop(HALF, 128, retain)

        g2[4]()
        g3[1]()

        def out_rows(base):
            def body(rows):
                at = pl.ds(pl.multiple_of(base + rows.start, rows.size), rows.size)
                for x in range(4):
                    got = dot(mixed_ref[at, :], weights[x, STARTS[4] : STARTS[4] + VDIM, :], NN)
                    part[at, x * 512 : x * 512 + 512] = got.astype(BF)

            loop(HALF, 256, body)

        def take(at, value):
            hidden_ref[at, :] = in_ref[at, :].astype(F32) + value

        r1 = scatter_rows(net, part, bufs, take)
        out_rows((1 - c) * HALF)
        r1[0]()
        out_rows(c * HALF)
        g3[2]()
        r1[1]()
        g4[0]()
        r1[2]()
        g3[3]()
        g4[1]()
        r1[3]()
        norm_rows(hidden_ref, gain_two, two)
        y2 = gather_rows(net, two)
        y2[0]()
        g3[4]()
        g4[2]()
        store_one = pltpu.make_async_copy(one, one_out, local.at[2])
        store_one.start()
        y2[1]()
        g4[3]()
        y2[2]()
        store_two = pltpu.make_async_copy(two, two_out, local.at[3])
        store_two.start()
        g4[4]()
        swap.wait()
        stores = [store_one, store_two]
        for x in range(4):
            store = pltpu.make_async_copy(weights.at[x], weights_out.at[:, pl.ds(x * 512, 512)], local.at[4 + x])
            store.start()
            stores.append(store)
        for store in stores:
            store.wait()

    def shape(*dims, kind=BF):
        return jax.ShapeDtypeStruct(dims, kind)

    return call(
        kernel,
        [
            (shape(ROWS, D), False),
            (shape(SEQ, D), False),
            (shape(SEQ, D), False),
            (shape(SEQ, KDIM), True),
            (shape(SEQ, KDIM), True),
            (shape(SEQ, VDIM), True),
            (shape(SEQ, VDIM), True),
            (shape(SEQ, HALF), True),
            (shape(SEQ, VDIM), True),
            (shape(SEQ, 1, kind=F32), True),
            (shape(SEQ, VDIM), True),
            (shape(2, KDIM, VDIM), True),
            (shape(128, D, kind=F32), True),
            (shape(HALF, D), False),
        ],
        [
            (piece, False),
            (inputs, True),
            (carried_state, False),
            (attn_gain, True),
            (mlp_gain, True),
            (cosine, True),
            (sine, True),
            (row_mask, True),
            (lam, True),
            (output_grad, False),
        ],
        [
            pltpu.VMEM((4, ROWS, 512), BF),
            pltpu.VMEM((SEQ, D), BF),
            pltpu.VMEM((SEQ, D), BF),
            pltpu.VMEM((KDIM, VDIM), F32),
            pltpu.VMEM((SEQ, D), BF),
        ]
        + ROW_BUFS,
        100,
        cid,
    )


def transpose_to(ref, source):
    for lo in range(0, SEQ, 256):
        ref[:, lo : lo + 256] = source[lo : lo + 256, :].astype(F32).T.astype(BF)


def weight_grad(flipped, rows_ref, out, start, count):
    for x in range(4):

        def body(cols, x=x):
            at = pl.ds(pl.multiple_of(x * 512 + cols.start, 256), 256)
            out[x, start : start + count, cols] = dot(flipped[...], rows_ref[:, at], NN).astype(BF)

        loop(512, 256, body)


def times_plain(pairs, x):
    total = None
    for rows, weights, start, count in pairs:
        part = dot(rows, weights[x, start : start + count, :], NN)
        total = part if total is None else total + part
    return total


def times_flipped(rows_ref, at, weights, start, count):
    total = None
    for x in range(4):
        part = dot(rows_ref[at, x * 512 : x * 512 + 512], weights[x, start : start + count, :], NT)
        total = part if total is None else total + part
    return total


def load_weights(source, weights, local, base, pieces):
    loads = []
    for k, (lo, to, rows) in enumerate(pieces):
        for x in range(4):
            loads.append(
                pltpu.make_async_copy(
                    source.at[pl.ds(lo, rows), pl.ds(x * 512, 512)],
                    weights.at[x, pl.ds(to, rows), :],
                    local.at[base + 4 * k + x],
                )
            )
    for load in loads:
        load.start()
    return [loads[4 * k : 4 * k + 4] for k in range(len(pieces))]


def wait_all(copies):
    for copy in copies:
        copy.wait()


def norm_back(source, gain, grad, out):
    def body(i, total):
        at = pl.ds(pl.multiple_of(i * 32, 32), 32)
        centred, dev = normal(source(at), D)
        normed = centred * dev
        back = grad(at)
        scaled = back * gain[...]
        mean = jnp.sum(scaled, axis=-1, keepdims=True) * (1.0 / D)
        along = jnp.sum(scaled * normed, axis=-1, keepdims=True) * (1.0 / D)
        out(at, dev * (scaled - mean - normed * along))
        return total + jnp.sum(back * normed, axis=0, keepdims=True)

    return lax.fori_loop(0, 4, body, jnp.zeros((1, D), F32))


def mlp_back(weights_all, rows_two, grad_own, grad_other, hidden, mlp_gain, cid):
    def kernel(
        w_ref, two_ref, own_ref, other_ref, hidden_ref, gain,
        mid_out, down_out, grad_hidden, gain_out, sums_out,
        weights, two, grads, mid, part, act, gate_grad, up_grad, flipped, total,
        *rest,
    ):
        row_bufs, (send, recv, local) = rest[:5], rest[-3:]
        bufs = rest[5:-3]
        net = Net(send, recv)
        c, t = net.c, net.t
        load_two = pltpu.make_async_copy(two_ref, two, local.at[0])
        load_two.start()
        load_g, load_u, load_d = load_weights(
            w_ref, weights, local, 4, ((STARTS[5], 0, 432), (STARTS[6], 432, 432), (STARTS[7], 864, 432))
        )
        mine, theirs = (pl.ds(pl.multiple_of(k * HALF, HALF), HALF) for k in (c, 1 - c))
        load_own = pltpu.make_async_copy(own_ref, grads.at[mine, :], local.at[1])
        load_other = pltpu.make_async_copy(other_ref, grads.at[theirs, :], local.at[2])
        load_own.start()
        load_other.start()
        net.greet(XZ_HOPS + Y_HOPS)
        wait_all([load_two, *load_g, *load_u, *load_d, load_own, load_other])

        def mlp_rows(base):
            def body(rows):
                at = pl.ds(pl.multiple_of(base + rows.start, rows.size), rows.size)
                gate = times_flipped(two, at, weights, 0, 432)
                up = times_flipped(two, at, weights, 432, 432)
                back = times_flipped(grads, at, weights, 864, 432)
                share = 0.5 + 0.5 * lax.erf(gate * 0.7071067811865476)
                slope = share + gate * (0.3989422804014327 * jnp.exp(-0.5 * gate * gate))
                gelu = gate * share
                act[at, :] = (gelu * up).astype(BF)
                gate_grad[at, :] = (back * up * slope).astype(BF)
                up_grad[at, :] = (back * gelu).astype(BF)
                for x in range(4):
                    pairs = ((gate_grad[at, :], weights, 0, 432), (up_grad[at, :], weights, 432, 432))
                    part[at, x * 512 : x * 512 + 512] = times_plain(pairs, x).astype(BF)

            loop(HALF, 256, body)

        def take(at, value):
            total[at, :] = value

        r1 = scatter_rows(net, part, row_bufs, take)
        mid_stages = gather_rows(net, mid)
        split = len(scatter_shapes(864))
        sums = [
            scatter_weights(
                net, weights, lo, hi, some, lambda at, value: sums_out.__setitem__((at, slice(None)), value)
            )
            for lo, hi, some in ((0, 864, bufs[:split]), (864, 1296, bufs[split:]))
        ]
        mlp_rows((1 - c) * HALF)
        r1[0]()
        mlp_rows(c * HALF)
        r1[1]()
        transpose_to(flipped, gate_grad)
        weight_grad(flipped, two, weights, 0, 432)
        transpose_to(flipped, up_grad)
        weight_grad(flipped, two, weights, 432, 432)
        sums[0][0]()
        r1[2]()
        sums[0][1]()
        r1[3]()

        own = c * 512 + t * 128
        def store(at, value):
            to = pl.ds(pl.multiple_of(own + at.start, 32), 32)
            whole = grads[to, :].astype(F32) + value
            grad_hidden[at, :] = whole
            mid[to, :] = whole.astype(BF)

        gain_out[...] = norm_back(lambda at: hidden_ref[at, :], gain, lambda at: total[at, :], store)
        mid_stages[0]()

        def down_rows(at):
            for x in range(4):
                part[at, x * 512 : x * 512 + 512] = times_plain(((act[at, :], weights, 864, 432),), x).astype(BF)

        loop(SEQ, 256, down_rows)
        save_down = pltpu.make_async_copy(part, down_out, local.at[3])
        save_down.start()
        transpose_to(flipped, act)
        weight_grad(flipped, grads, weights, 864, 432)
        sums[1][0]()
        sums[0][2]()
        mid_stages[1]()
        sums[1][1]()
        sums[0][3]()
        sums[1][2]()
        sums[0][4]()
        mid_stages[2]()
        save_mid = pltpu.make_async_copy(mid, mid_out, local.at[1])
        save_mid.start()
        sums[1][3]()
        sums[1][4]()
        save_down.wait()
        save_mid.wait()

    def shape(*dims, kind=BF):
        return jax.ShapeDtypeStruct(dims, kind)

    return call(
        kernel,
        [
            (shape(SEQ, D), False),
            (shape(SEQ, D), False),
            (shape(128, D, kind=F32), True),
            (shape(1, D, kind=F32), True),
            (shape(1296, 128, kind=F32), True),
        ],
        [
            (weights_all, False),
            (rows_two, False),
            (grad_own, False),
            (grad_other, False),
            (hidden, True),
            (mlp_gain, True),
        ],
        [
            pltpu.VMEM((4, 1296, 512), BF),
            pltpu.VMEM((SEQ, D), BF),
            pltpu.VMEM((SEQ, D), BF),
            pltpu.VMEM((SEQ, D), BF),
            pltpu.VMEM((SEQ, D), BF),
            pltpu.VMEM((SEQ, VDIM), BF),
            pltpu.VMEM((SEQ, VDIM), BF),
            pltpu.VMEM((SEQ, VDIM), BF),
            pltpu.VMEM((VDIM, SEQ), BF),
            pltpu.VMEM((128, D), F32),
        ]
        + ROW_BUFS
        + scatter_shapes(864)
        + scatter_shapes(432),
        64,
        cid,
    )


GRAD_HOPS = (dict(dx=2), dict(dz=2), dict(dt=2))


def retention_back(
    weights_all, rows_mid, rows_one, down_part, mixed, q, k, v, s, normed, dev, mix, prior, hidden, grad_hidden, inputs,
    attn_gain, cosine, sine, row_mask, lam, mlp_gain_part, sums_mlp, cid
):
    places = ((STARTS[4], 0, 432), (STARTS[3], 432, 432), (STARTS[2], 864, 432), (0, 1296, 256), (256, 1552, 256))

    def kernel(
        w_ref, mid_ref, one_ref, down_ref, mixed_ref, q_ref, k_ref, v_ref, s_ref, norm_ref, dev_ref, mix_ref,
        prior_ref, hidden_ref, gh_ref, in_ref, gain, cos_ref, sin_ref, mask_ref, lam_ref, mlp_gain_ref, sums_mlp_ref,
        out_ref, in_grad, gains_out, sums_out, sums_got, mlp_got,
        weights, one, mid, down, swish_grad, ret_grad, q_grad, k_grad, v_grad, score_grad, flipped, total,
        by_core, by_t, by_x, by_z,
        *rest,
    ):
        first_bufs, second_bufs, (send, recv, local) = rest[:5], rest[5:10], rest[-3:]
        bufs = rest[10:-3]
        net = Net(send, recv)
        c, t = net.c, net.t
        load_mid = pltpu.make_async_copy(mid_ref, mid, local.at[0])
        load_mid.start()
        load_o, load_s, load_v, load_q, load_k = load_weights(w_ref, weights, local, 8, places)
        mine = pl.ds(pl.multiple_of(c * HALF, HALF), HALF)
        load_down = pltpu.make_async_copy(down_ref.at[mine, :], down.at[mine, :], local.at[1])
        load_down.start()
        load_one = pltpu.make_async_copy(one_ref, one, local.at[2])
        load_one.start()
        net.greet(XZ_HOPS + Y_HOPS + GRAD_HOPS)
        send_mlp = net.copy(sums_mlp_ref, mlp_got, dc=1)
        send_mlp.start()

        def take_out(at, value):
            out_ref[at, :] = (hidden_ref[at, :] + value).astype(BF)

        def take(at, value):
            total[at, :] = value

        r1 = scatter_rows(net, down, first_bufs, take_out, source=down_ref)
        r1[0]()
        load_down.wait()
        wait_all([load_mid, *load_o])

        def gate_back(at):
            back = times_flipped(mid, at, weights, 0, 432) * mask_ref[at, :]
            swish = s_ref[at, :].astype(F32)
            normed = norm_ref[at, :].astype(F32)
            share = jax.nn.sigmoid(swish)
            swish_grad[at, :] = (back * normed * (share * (1.0 + swish * (1.0 - share)))).astype(BF)
            back = back * (swish * share)
            mean = jnp.sum(back, axis=-1, keepdims=True) * (1.0 / VDIM)
            along = jnp.sum(back * normed, axis=-1, keepdims=True) * (1.0 / VDIM)
            ret_grad[at, :] = ((back - mean - normed * along) * dev_ref[at, :]).astype(BF)

        loop(SEQ, 256, gate_back)
        r1[1]()
        split = [0]
        for rows in (432, 864, 512):
            split.append(split[-1] + len(scatter_shapes(rows)))

        def put(at, value):
            sums_out[at, :] = value

        wait_all(load_s)
        sums = [
            scatter_weights(net, weights, lo, hi, bufs[split[i] : split[i + 1]], put)
            for i, (lo, hi) in enumerate(((0, 432), (432, 1296), (1296, 1808)))
        ]
        transpose_to(flipped, mixed_ref)
        weight_grad(flipped, mid, weights, 0, 432)
        sums[0][0]()

        decay = lam_ref[0:1, 0:1]
        far = lax.broadcasted_iota(jnp.int32, (HALF, 1), 0).astype(F32)
        tail = jnp.exp((HALF - 1.0 - far) * decay)
        head_all = jnp.exp((far + 1.0) * decay)
        ahead = (q_ref[HALF:, :].astype(F32) * head_all).astype(BF)
        grad_local = dot(ahead, ret_grad[HALF:, :], TN).astype(BF)

        def turn_back(at, raw):
            cs, sn = cos_ref[at, :], sin_ref[at, :]
            former, latter = raw[:, :128], raw[:, 128:]
            return (former * cs + latter * sn).astype(BF), (latter * cs - former * sn).astype(BF)

        for stretch in range(2):
            keys = slice(stretch * HALF, stretch * HALF + HALF)

            def score_rows(rows, stretch=stretch, keys=keys):
                at = pl.ds(pl.multiple_of(stretch * HALF + rows.start, rows.size), rows.size)
                n = lax.broadcasted_iota(jnp.int32, (rows.size, HALF), 0) + rows.start
                distance = (n - lax.broadcasted_iota(jnp.int32, (rows.size, HALF), 1)).astype(F32)
                fade = jnp.where(distance >= 0.0, jnp.exp(jnp.maximum(distance, 0.0) * decay), 0.0)
                scores = (dot(ret_grad[at, :], v_ref[keys, :], NT) * fade).astype(BF)
                score_grad[rows, :] = scores
                step = lax.broadcasted_iota(jnp.int32, (rows.size, 1), 0) + rows.start + 1
                head = jnp.exp(step.astype(F32) * decay)
                raw = dot(scores, k_ref[keys, :], NN) + dot(ret_grad[at, :], prior_ref[stretch], NT) * head
                q_grad[at, :128], q_grad[at, 128:] = turn_back(at, raw)

            loop(HALF, 128, score_rows)
            raw = dot(score_grad[...], q_ref[keys, :], TN)
            value = dot(mix_ref[keys, :], ret_grad[keys, :], TN)
            if stretch == 0:
                raw = raw + dot(v_ref[keys, :], grad_local, NT) * tail
                value = value + dot(k_ref[keys, :], grad_local, NN) * tail
            k_grad[keys, :128], k_grad[keys, 128:] = turn_back(keys, raw)
            v_grad[keys, :] = (value * mask_ref[keys, :]).astype(BF)

        r1[2]()
        sums[0][1]()
        wait_all(load_v + load_q + load_k)
        part = mid

        def back_rows(base):
            def body(rows):
                at = pl.ds(pl.multiple_of(base + rows.start, rows.size), rows.size)
                pairs = (
                    (swish_grad[at, :], weights, 432, 432),
                    (v_grad[at, :], weights, 864, 432),
                    (q_grad[at, :], weights, 1296, 256),
                    (k_grad[at, :], weights, 1552, 256),
                )
                for x in range(4):
                    part[at, x * 512 : x * 512 + 512] = times_plain(pairs, x).astype(BF)

            loop(HALF, 256, body)

        r2 = scatter_rows(net, part, second_bufs, take)
        back_rows((1 - c) * HALF)
        r2[0]()
        back_rows(c * HALF)
        r1[3]()
        load_one.wait()
        transpose_to(flipped, swish_grad)
        weight_grad(flipped, one, weights, 432, 432)
        r2[1]()
        sums[0][2]()
        transpose_to(flipped, v_grad)
        weight_grad(flipped, one, weights, 864, 432)
        sums[1][0]()
        sums[0][3]()
        transpose_to(flipped.at[0:256], q_grad)
        weight_grad(flipped.at[0:256], one, weights, 1296, 256)
        transpose_to(flipped.at[0:256], k_grad)
        weight_grad(flipped.at[0:256], one, weights, 1552, 256)
        sums[2][0]()
        r2[2]()
        sums[1][1]()
        sums[0][4]()
        sums[2][1]()
        r2[3]()

        def store(at, value):
            in_grad[at, :] = gh_ref[at, :] + value

        first = norm_back(lambda at: in_ref[at, :].astype(F32), gain, lambda at: total[at, :], store)

        by_core[c, 0:1, :] = first
        by_core[c, 1:2, :] = mlp_gain_ref[...]

        def spread(ref, place, hops, axis):
            copies = [net.copy(ref.at[place], ref.at[place], **{axis: hop}) for hop in hops]
            for copy in copies:
                copy.start()
            return copies

        def gathered(ref, copies, count):
            for copy in copies:
                copy.wait()
            value = ref[0]
            for k in range(1, count):
                value = value + ref[k]
            return value

        near = spread(by_core, c, (1,), "dc")
        by_t[t] = gathered(by_core, near, 2)
        near = spread(by_t, t, (1, -1, 2), "dt")
        sums[1][2]()
        by_x[net.x] = gathered(by_t, near, 4)
        near = spread(by_x, net.x, (1, -1, 2), "dx")
        sums[2][2]()
        by_z[net.z] = gathered(by_x, near, 4)
        near = spread(by_z, net.z, (1, -1, 2), "dz")
        sums[1][3]()
        gains_out[...] = gathered(by_z, near, 4)
        sums[2][3]()
        sums[1][4]()
        sums[2][4]()
        send_sums = net.copy(sums_out, sums_got, dc=1)
        send_sums.start()
        send_mlp.wait()
        send_sums.wait()

    def shape(*dims, kind=BF):
        return jax.ShapeDtypeStruct(dims, kind)

    return call(
        kernel,
        [
            (shape(128, D), True),
            (shape(128, D, kind=F32), True),
            (shape(2, D, kind=F32), True),
            (shape(1808, 128, kind=F32), True),
            (shape(1808, 128, kind=F32), True),
            (shape(1296, 128, kind=F32), False),
        ],
        [
            (weights_all, False),
            (rows_mid, False),
            (rows_one, False),
            (down_part, False),
            (mixed, True),
            (q, True),
            (k, True),
            (v, True),
            (s, True),
            (normed, True),
            (dev, True),
            (mix, True),
            (prior, True),
            (hidden, True),
            (grad_hidden, True),
            (inputs, True),
            (attn_gain, True),
            (cosine, True),
            (sine, True),
            (row_mask, True),
            (lam, True),
            (mlp_gain_part, True),
            (sums_mlp, False),
        ],
        [
            pltpu.VMEM((4, 1808, 512), BF),
            pltpu.VMEM((SEQ, D), BF),
            pltpu.VMEM((SEQ, D), BF),
            pltpu.VMEM((SEQ, D), BF),
            pltpu.VMEM((SEQ, VDIM), BF),
            pltpu.VMEM((SEQ, VDIM), BF),
            pltpu.VMEM((SEQ, KDIM), BF),
            pltpu.VMEM((SEQ, KDIM), BF),
            pltpu.VMEM((SEQ, VDIM), BF),
            pltpu.VMEM((HALF, HALF), BF),
            pltpu.VMEM((VDIM, SEQ), BF),
            pltpu.VMEM((128, D), F32),
            pltpu.VMEM((2, 2, D), F32),
            pltpu.VMEM((4, 2, D), F32),
            pltpu.VMEM((4, 2, D), F32),
            pltpu.VMEM((4, 2, D), F32),
        ]
        + ROW_BUFS
        + ROW_BUFS
        + scatter_shapes(432)
        + scatter_shapes(864)
        + scatter_shapes(512),
        80,
        cid,
    )


def swap_cores(array):
    return lax.ppermute(array, "ctx", [(0, 1), (1, 0)])


def on_device(
    inputs,
    seq_lengths,
    carried_state,
    attn_gain,
    query_weight,
    key_weight,
    value_weight,
    swish_weight,
    out_weight,
    mlp_gain,
    gate_weight,
    up_weight,
    down_weight,
    output_grad,
):
    core = lax.axis_index("ctx")
    head = lax.axis_index("tp") * 2 + core

    def for_core(which):
        parts = []
        for k, weight in enumerate(
            (query_weight, key_weight, value_weight, swish_weight, out_weight, gate_weight, up_weight, down_weight)
        ):
            n = SIZES[k]
            if k in (4, 7):
                parts.append(lax.dynamic_slice_in_dim(weight, which * n, n, 0))
            else:
                parts.append(lax.dynamic_slice_in_dim(weight, which * n, n, 1).T)
        return jnp.concatenate(parts, axis=0)

    mine, got = for_core(core), swap_cores(for_core(1 - core))
    piece = jnp.where(core == 0, jnp.concatenate([mine, got], axis=1), jnp.concatenate([got, mine], axis=1))
    position = jnp.arange(SEQ, dtype=jnp.int32)
    row_mask = (position < seq_lengths[0]).astype(F32)[:, None]
    frequency = jnp.power(10000.0, -jnp.arange(128).astype(F32) / 128)
    angles = position.astype(F32)[:, None] * frequency[None, :]
    cosine, sine = jnp.cos(angles), jnp.sin(angles)
    decay = -jnp.power(2.0, 5.0 - head.astype(F32)) / SEQ
    gains = attn_gain[None, :], mlp_gain[None, :]
    lam = jnp.full((8, 128), decay, F32)
    weights, rows_one, rows_two, q, k, v, s, mix, normed, dev, mixed, prior, hidden, grad_other = forward(
        piece, inputs, carried_state, *gains, cosine, sine, row_mask, lam, output_grad, 1
    )
    rows_mid, down_part, grad_hidden, mlp_gain_part, sums_mlp = mlp_back(
        weights, rows_two, output_grad, grad_other, hidden, gains[1], 2
    )
    outputs, input_grad, gain_grads, sums, got_sums, got_mlp = retention_back(
        weights, rows_mid, rows_one, down_part, mixed, q, k, v, s, normed, dev, mix, prior, hidden, grad_hidden, inputs,
        gains[0], cosine, sine, row_mask, lam, mlp_gain_part, sums_mlp, 3
    )
    own = jnp.where(core == 0, sums[:, :64], sums[:, 64:]), jnp.where(core == 0, sums_mlp[:, :64], sums_mlp[:, 64:])
    got = jnp.where(core == 0, got_sums[:, :64], got_sums[:, 64:]), jnp.where(core == 0, got_mlp[:, :64], got_mlp[:, 64:])
    places = ((0, 1296, 256), (0, 1552, 256), (0, 864, 432), (0, 432, 432), (0, 0, 432), (1, 0, 432), (1, 432, 432), (1, 864, 432))
    grads = []
    for at, (which, lo, n) in enumerate(places):
        a, b = own[which][lo : lo + n], got[which][lo : lo + n]
        both = jnp.where(core == 0, jnp.concatenate([a, b], axis=0), jnp.concatenate([b, a], axis=0))
        grads.append(both if at in (4, 7) else both.T)
    return (
        outputs,
        input_grad,
        gain_grads[0],
        grads[0],
        grads[1],
        grads[2],
        grads[3],
        grads[4],
        gain_grads[1],
        grads[5],
        grads[6],
        grads[7],
    )


def solution(mesh):
    placed = (
        P(("fsdp", "ctx", "tp"), None),
        P("fsdp"),
        P("fsdp", "tp", None, None),
        P(),
        P(("fsdp", "ctx"), "tp"),
        P(("fsdp", "ctx"), "tp"),
        P(("fsdp", "ctx"), "tp"),
        P(("fsdp", "ctx"), "tp"),
        P("tp", ("fsdp", "ctx")),
        P(),
        P(("fsdp", "ctx"), "tp"),
        P(("fsdp", "ctx"), "tp"),
        P("tp", ("fsdp", "ctx")),
        P(("fsdp", "ctx"), None),
    )
    return jax.shard_map(
        on_device,
        mesh=mesh,
        in_specs=placed,
        out_specs=(
            P(("fsdp", "ctx", "tp"), None),
            P(("fsdp", "ctx", "tp"), None),
            P(),
            P(("fsdp", "ctx"), "tp"),
            P(("fsdp", "ctx"), "tp"),
            P(("fsdp", "ctx"), "tp"),
            P(("fsdp", "ctx"), "tp"),
            P("tp", ("fsdp", "ctx")),
            P(),
            P(("fsdp", "ctx"), "tp"),
            P(("fsdp", "ctx"), "tp"),
            P("tp", ("fsdp", "ctx")),
        ),
        check_vma=False,
    )
```

```python
import jax
import jax.numpy as jnp
import numpy as np
from jax import lax
from jax.experimental import pallas as pl
from jax.experimental.pallas import tpu as pltpu
from jax.sharding import PartitionSpec as P

D = 2048
KDIM = 256
VDIM = 432
SEQ = 1024
HALF = 512
SIZES = (256, 256, 432, 432, 432, 432, 432, 432)
STARTS = (0, 256, 512, 944, 1376, 1808, 2240, 2672)
ROWS = 3104
EPSILON = 1e-05
MESH = pl.DeviceIdType.MESH
BF = jnp.bfloat16
F32 = jnp.float32


def even(rows):
    return rows // 32 * 16


class Net:
    def __init__(self, send, recv, local):
        group = lax.axis_index("fsdp")
        self.c = lax.axis_index("ctx")
        self.t = lax.axis_index("tp")
        self.x = group // 4
        self.z = group % 4
        self.send, self.recv, self.local = send, recv, local
        self.copies, self.moves = [], 0

    def dev(self, dx=0, dz=0, dt=0, dc=0):
        x, z, t = ((at + d + 4) % 4 if d else at for at, d in ((self.x, dx), (self.z, dz), (self.t, dt)))
        c = 1 - self.c if dc else self.c
        return (x * 4 + z, c, t)

    def greet(self, hops):
        barrier = pltpu.get_barrier_semaphore()
        for hop in hops:
            pl.semaphore_signal(barrier, inc=1, device_id=self.dev(**hop), device_id_type=MESH)
        pl.semaphore_wait(barrier, len(hops))

    def copy(self, src, dst, **hop):
        at = len(self.copies)
        self.copies.append(
            pltpu.make_async_remote_copy(
                src_ref=src,
                dst_ref=dst,
                send_sem=self.send.at[at],
                recv_sem=self.recv.at[at],
                device_id=self.dev(**hop),
                device_id_type=MESH,
            )
        )
        return self.copies[-1]

    def move(self, src, dst):
        copy = pltpu.make_async_copy(src, dst, self.local.at[self.moves])
        self.moves += 1
        copy.start()
        return copy

    def flush(self):
        for copy in self.copies:
            copy.wait_send()


XZ_HOPS = (dict(dx=1), dict(dx=-1), dict(dz=1), dict(dz=-1))
Y_HOPS = (dict(dt=1), dict(dt=-1), dict(dc=1))


def ring_views(net, axis):
    x, z = net.x, net.z
    along_x = lambda ref, d, rows: ref.at[(x + d + 4) % 4, z, rows, :]
    along_z = lambda ref, d, rows: ref.at[x, (z + d + 4) % 4, rows, :]
    all_z = lambda ref, d, rows: ref.at[(x + d + 4) % 4, :, rows, :]
    all_x = lambda ref, d, rows: ref.at[:, (z + d + 4) % 4, rows, :]
    if axis == "x":
        return along_x, all_x, "dx", "dz"
    return along_z, all_z, "dz", "dx"


def gather_weights(net, ref, start, stop):
    cut = start + even(stop - start)
    plans = []
    for axis, lo, hi in (("z", start, cut), ("x", cut, stop)):
        mid = lo + even(hi - lo)
        whole, head, tail = pl.ds(lo, hi - lo), pl.ds(lo, mid - lo), pl.ds(mid, hi - mid)
        first, second, hop_a, hop_b = ring_views(net, axis)
        plan = []
        for view, hop in ((first, hop_a), (second, hop_b)):
            mine = view(ref, 0, whole)
            plan.append(
                (
                    net.copy(mine, mine, **{hop: 1}),
                    net.copy(mine, mine, **{hop: -1}),
                    net.copy(view(ref, -1, head), view(ref, -1, head), **{hop: 1}),
                    net.copy(view(ref, 1, tail), view(ref, 1, tail), **{hop: -1}),
                )
            )
        plans.append(plan)

    def near(phase):
        for plan in plans:
            plan[phase][0].start()
            plan[phase][1].start()

    def far(phase):
        for k in (0, 1):
            for plan in plans:
                plan[phase][k].wait_recv()
                plan[phase][2 + k].start()

    def land(phase):
        for plan in plans:
            plan[phase][2].wait_recv()
            plan[phase][3].wait_recv()

    return [
        lambda: near(0),
        lambda: far(0),
        lambda: (land(0), near(1)),
        lambda: far(1),
        lambda: land(1),
    ]


def add_rows(refs, out, count):
    step = 16

    def body(i, carry):
        at = pl.ds(pl.multiple_of(i * step, step), step)
        total = refs[0](at).astype(F32)
        for ref in refs[1:]:
            total = total + ref(at).astype(F32)
        out(at, total)
        return carry

    lax.fori_loop(0, count // step, body, 0)


def scatter_shapes(rows):
    shapes = []
    cut = even(rows)
    for axis, count in (("z", cut), ("x", rows - cut)):
        head = even(count)
        for pieces in ((4,), ()):
            for n in (head, count - head, count, count):
                shapes.append(pltpu.VMEM((*pieces, n, 128), BF))
    return shapes


def scatter_weights(net, ref, start, stop, bufs, out):
    cut = start + even(stop - start)
    plans = []
    bufs = list(bufs)
    for axis, lo, hi in (("z", start, cut), ("x", cut, stop)):
        mid = lo + even(hi - lo)
        parts = (lo, mid - lo), (mid, hi - mid), (lo, hi - lo)
        head, tail, whole = (pl.ds(*part) for part in parts)
        plan = []
        _, wide, hop_b, hop_a = ring_views(net, "x" if axis == "z" else "z")
        thin = ring_views(net, "z" if axis == "x" else "x")[0]
        for view, hop in ((wide, hop_a), (thin, hop_b)):
            fa, fb, ma, mb = bufs[:4]
            bufs = bufs[4:]
            plan.append(
                dict(
                    view=view,
                    bufs=(fa, fb, ma, mb),
                    copies=(
                        net.copy(view(ref, 2, head), fa, **{hop: 1}),
                        net.copy(view(ref, 2, tail), fb, **{hop: -1}),
                        net.copy(view(ref, 1, whole), ma, **{hop: 1}),
                        net.copy(view(ref, -1, whole), mb, **{hop: -1}),
                    ),
                )
            )
        plans.append((plan, parts))

    def at_rows(view, d, lo):
        def read(at):
            return view(ref, d, pl.ds(lo + at.start, at.size))[...]

        def write(at, value):
            view(ref, d, pl.ds(lo + at.start, at.size))[...] = value.astype(BF)

        return read, write

    def buf_rows(buf):
        if len(buf.shape) == 3:
            return lambda at: buf[:, at, :]
        return lambda at: buf[at, :]

    def far(phase):
        for plan, _ in plans:
            plan[phase]["copies"][0].start()
            plan[phase]["copies"][1].start()

    def near(phase):
        for k, d in ((0, 1), (1, -1)):
            for plan, parts in plans:
                step = plan[phase]
                lo, count = parts[k]
                step["copies"][k].wait_recv()
                read, write = at_rows(step["view"], d, lo)
                add_rows((read, buf_rows(step["bufs"][k])), write, count)
                step["copies"][2 + k].start()

    def total(phase, last):
        for plan, parts in plans:
            step = plan[phase]
            lo, count = parts[2]
            step["copies"][2].wait_recv()
            step["copies"][3].wait_recv()
            read, write = at_rows(step["view"], 0, lo)
            if last:
                write = lambda at, value, lo=lo: out(pl.ds(lo + at.start, at.size), value)
            add_rows((read, buf_rows(step["bufs"][2]), buf_rows(step["bufs"][3])), write, count)

    return [
        lambda: far(0),
        lambda: near(0),
        lambda: (total(0, False), far(1)),
        lambda: near(1),
        lambda: total(1, True),
    ]


def gather_rows(net, ref):
    def block(c, t, lo=0, n=128):
        return ref.at[pl.ds(pl.multiple_of(c * 512 + t * 128 + lo, 16), n), :]

    c, t = net.c, net.t
    before, after, across = (t + 3) % 4, (t + 1) % 4, (t + 2) % 4
    own = block(c, t)
    up = net.copy(own, own, dt=1)
    down = net.copy(own, own, dt=-1)
    side = net.copy(own, own, dc=1)
    fore = net.copy(block(c, before, 0, 64), block(c, before, 0, 64), dt=1)
    back = net.copy(block(c, after, 64, 64), block(c, after, 64, 64), dt=-1)
    over = [
        net.copy(block(c, before), block(c, before), dc=1),
        net.copy(block(c, after), block(c, after), dc=1),
        net.copy(block(c, across, 0, 64), block(c, across, 0, 64), dc=1),
        net.copy(block(c, across, 64, 64), block(c, across, 64, 64), dc=1),
    ]

    def start():
        up.start()
        down.start()
        side.start()

    def forward():
        up.wait_recv()
        fore.start()
        over[0].start()
        down.wait_recv()
        back.start()
        over[1].start()

    def beside():
        side.wait_recv()

    def near():
        over[0].wait_recv()
        over[1].wait_recv()

    def far():
        fore.wait_recv()
        over[2].start()
        back.wait_recv()
        over[3].start()

    def last():
        over[2].wait_recv()
        over[3].wait_recv()

    return start, forward, beside, near, far, last


ROW_BUFS = [
    pltpu.VMEM((512, D), BF),
    pltpu.VMEM((64, D), BF),
    pltpu.VMEM((64, D), BF),
    pltpu.VMEM((128, D), BF),
    pltpu.VMEM((128, D), BF),
]


class RowSums:
    def __init__(self, net, ref, bufs, out, source=None, first=None):
        c, t = net.c, net.t
        self.t, self.ref, self.out = t, ref, out
        self.first = c * HALF if first is None else first
        self.other, self.far_a, self.far_b, self.near_a, self.near_b = bufs
        source = ref if source is None else source
        self.sides = {}
        for d in (2, 1, -1, 0):
            lo = (t + d + 4) % 4 * 128
            self.sides[d] = net.copy(
                source.at[pl.ds(pl.multiple_of((1 - c) * HALF + lo, 128), 128), :],
                self.other.at[pl.ds(pl.multiple_of(lo, 128), 128), :],
                dc=1,
            )
        self.hops = (
            net.copy(self.block(2, 0, 64), self.far_a, dt=1),
            net.copy(self.block(2, 64, 64), self.far_b, dt=-1),
            net.copy(self.block(1), self.near_a, dt=1),
            net.copy(self.block(-1), self.near_b, dt=-1),
        )

    def row(self, d, lo=0):
        return (self.t + d + 4) % 4 * 128 + lo

    def block(self, d, lo=0, n=128):
        return self.ref.at[pl.ds(pl.multiple_of(self.first + self.row(d, lo), 16), n), :]

    def mine(self, d, lo=0):
        return self.read(self.ref, self.first + self.row(d, lo)), self.read(self.other, self.row(d, lo))

    @staticmethod
    def read(source, base):
        return lambda at: source[pl.ds(pl.multiple_of(base + at.start, 16), at.size), :]

    def keep(self, d, lo=0):
        base = self.first + self.row(d, lo)

        def store(at, value):
            self.ref[pl.ds(pl.multiple_of(base + at.start, 16), at.size), :] = value.astype(BF)

        return store

    def side(self, d):
        self.sides[d].start()

    def far(self):
        self.sides[2].wait_recv()
        for lo, k in ((0, 0), (64, 1)):
            add_rows(self.mine(2, lo), self.keep(2, lo), 64)
            self.hops[k].start()

    def near(self):
        for k, d, lo, buf in ((0, 1, 0, self.far_a), (1, -1, 64, self.far_b)):
            self.sides[d].wait_recv()
            add_rows(self.mine(d, 64 - lo), self.keep(d, 64 - lo), 64)
            self.hops[k].wait_recv()
            add_rows((*self.mine(d, lo), self.read(buf, 0)), self.keep(d, lo), 64)
            self.hops[2 + k].start()

    def finish(self):
        self.sides[0].wait_recv()
        self.hops[2].wait_recv()
        self.hops[3].wait_recv()
        add_rows((*self.mine(0), self.read(self.near_a, 0), self.read(self.near_b, 0)), self.out, 128)


def call(kernel, outs, ins, scratch, copies, moves, cid):
    any_spec = pl.BlockSpec(memory_space=pl.ANY)
    vmem_spec = pl.BlockSpec(memory_space=pltpu.VMEM)
    return pl.pallas_call(
        kernel,
        out_shape=[shape for shape, _ in outs],
        in_specs=[vmem_spec if v else any_spec for _, v in ins],
        out_specs=[vmem_spec if v else any_spec for _, v in outs],
        scratch_shapes=list(scratch)
        + [
            pltpu.SemaphoreType.DMA((copies,)),
            pltpu.SemaphoreType.DMA((copies,)),
            pltpu.SemaphoreType.DMA((moves,)),
        ],
        compiler_params=pltpu.CompilerParams(
            collective_id=cid, has_side_effects=True, vmem_limit_bytes=61 * 2**20
        ),
    )(*[array for array, _ in ins])


def shape(*dims, kind=BF):
    return jax.ShapeDtypeStruct(dims, kind)


def dot(a, b, dims):
    return lax.dot_general(a, b, (dims, ((), ())), preferred_element_type=F32)


NN = ((1,), (0,))
NT = ((1,), (1,))
TN = ((0,), (0,))


def normal(rows, width):
    centred = rows - jnp.sum(rows, axis=-1, keepdims=True) * (1.0 / width)
    spread = jnp.sum(centred * centred, axis=-1, keepdims=True) * (1.0 / width)
    return centred, lax.rsqrt(spread + EPSILON)


def loop(count, step, body):
    def turn(i, carry):
        body(pl.ds(pl.multiple_of(i * step, step), step))
        return carry

    lax.fori_loop(0, count // step, turn, 0)


def pair(net, d):
    lo = (net.t + d + 4) % 4 * 128
    return tuple(pl.ds(pl.multiple_of(c * HALF + lo, 128), 128) for c in (1 - net.c, net.c))


def of(ref, rows, cols=slice(None)):
    if isinstance(rows, tuple):
        return jnp.concatenate([ref[at, cols] for at in rows], axis=0)
    return ref[rows, cols]


def put(ref, rows, value, cols=slice(None)):
    if isinstance(rows, tuple):
        for k, at in enumerate(rows):
            ref[at, cols] = value[k * 128 : k * 128 + 128].astype(ref.dtype)
    else:
        ref[rows, cols] = value.astype(ref.dtype)


def wide(weights, x, start, count):
    return jnp.concatenate([weights[x, z, start : start + count, :] for z in range(4)], axis=1)


def times_flipped(ref, rows, weights, start, count):
    total = None
    for x in range(4):
        part = dot(of(ref, rows, slice(x * 512, x * 512 + 512)), wide(weights, x, start, count), NT)
        total = part if total is None else total + part
    return total


def times_plain(terms, out, rows):
    for x in range(4):
        total = None
        for value, weights, start, count in terms:
            part = dot(value, wide(weights, x, start, count), NN)
            total = part if total is None else total + part
        put(out, rows, total, slice(x * 512, x * 512 + 512))


def weight_grad(cols, rows, out, start, count):
    for x in range(4):
        grad = dot(cols[...], rows[:, x * 512 : x * 512 + 512], TN).astype(BF)
        for z in range(4):
            out[x, z, start : start + count, :] = grad[:, z * 128 : z * 128 + 128]


def wait_all(copies):
    for copy in copies:
        copy.wait()


def masked(facts, start, rows):
    place = lax.broadcasted_iota(jnp.int32, (rows, 1), 0) + start
    return jnp.where(place.astype(F32) < facts[1:2, 0:1], 1.0, 0.0)


def fades(decay, start, rows):
    n = lax.broadcasted_iota(jnp.int32, (rows, HALF), 0) + start
    distance = (n - lax.broadcasted_iota(jnp.int32, (rows, HALF), 1)).astype(F32)
    fade = jnp.where(distance >= 0.0, jnp.exp(jnp.maximum(distance, 0.0) * decay), 0.0)
    ahead = lax.broadcasted_iota(jnp.int32, (rows, 1), 0) + start + 1
    return fade, jnp.exp(ahead.astype(F32) * decay)


def forward(shards, inputs, carried_state, attn_gain, mlp_gain, cosine, sine, facts, output_grad, cid):
    def kernel(
        wq, wk, wv, ws, wo, wg, wu, wd, in_ref, carried_in, gain_one, gain_two, cos_in, sin_in, facts, grad_ref,
        weights_out, one_out, two_out, q_out, k_out, v_out, s_out, mix_out, norm_out, dev_out, mixed_out, prior_out,
        hidden_out, grad_out,
        weights, one, two, part, packs, got, carried, cos_ref, sin_ref,
        q_ref, k_ref, v_ref, s_ref, mix_ref, norm_ref, dev_ref, mixed_ref, prior_ref, hidden_ref,
        *rest,
    ):
        bufs, sems = rest[:5], rest[5:]
        net = Net(*sems)
        c, t = net.c, net.t
        load_cos, load_sin = net.move(cos_in, cos_ref), net.move(sin_in, sin_ref)
        load_state = net.move(carried_in.at[0, c], carried)
        own = c * 512 + t * 128
        stores = []

        def norm_rows(source, gain, rows_ref):
            def body(at):
                centred, dev = normal(source[at, :].astype(F32), D)
                to = pl.ds(pl.multiple_of(own + at.start, 16), at.size)
                rows_ref[to, :] = (centred * dev * gain[...]).astype(BF)

            loop(128, 32, body)

        norm_rows(in_ref, gain_one, one)
        spot = lax.broadcasted_iota(jnp.int32, (64, 128), 0) + c * 64
        place = jnp.where(spot == lax.broadcasted_iota(jnp.int32, (64, 128), 1), 1.0, 0.0).astype(BF)
        for k, ref in enumerate((wq, wk, wv, ws, wo, wg, wu, wd)):
            flat = dot(ref[...], place, TN).astype(BF)
            for core in range(2):
                packs[core, STARTS[k] : STARTS[k] + SIZES[k], :] = flat[core * SIZES[k] : (core + 1) * SIZES[k]]

        net.greet(XZ_HOPS + Y_HOPS)
        y1 = gather_rows(net, one)
        y1[0]()
        bounds = (0, 512, 944, 1376, 1808, 2240, 2672, 3104)
        swaps = [
            net.copy(packs.at[1 - c, pl.ds(lo, hi - lo), :], got.at[pl.ds(lo, hi - lo), :], dc=1)
            for lo, hi in ((0, 512), (512, 944), (944, 1376), (1376, ROWS))
        ]
        swaps[0].start()
        grad_swap = net.copy(grad_ref, grad_out, dc=1)
        g_qk, g_v, g_s, g_o, g_g, g_u, g_d = (
            gather_weights(net, weights, lo, hi) for lo, hi in zip(bounds, bounds[1:])
        )

        def join(lo, hi):
            for at in range(lo, hi, 432 if hi > 512 else 256):
                rows = slice(at, at + (432 if hi > 512 else 256))
                weights[net.x, net.z, rows, :] = packs[c, rows, :] + got[rows, :]

        def keep_weights(lo, hi):
            rows = pl.ds(lo, hi - lo)
            stores.append(net.move(weights.at[:, :, rows, :], weights_out.at[:, :, rows, :]))

        swaps[0].wait_recv()
        join(0, 512)
        g_qk[0]()
        swaps[1].start()
        y1[2]()
        swaps[1].wait_recv()
        join(512, 944)
        g_v[0]()
        swaps[2].start()
        g_qk[1]()
        swaps[2].wait_recv()
        join(944, 1376)
        g_s[0]()
        grad_swap.start()
        g_v[1]()
        swaps[3].start()
        g_qk[2]()
        swaps[3].wait_recv()
        join(1376, ROWS)
        g_o[0]()
        g_v[2]()
        y1[1]()
        g_qk[3]()
        y1[4]()
        g_s[1]()
        y1[5]()
        g_s[2]()
        g_qk[4]()
        keep_weights(0, 512)
        y1[3]()
        stores.append(net.move(one, one_out))
        g_o[1]()
        g_v[3]()
        wait_all([load_cos, load_sin])

        def project_qk(at):
            cs, sn = cos_ref[at, :], sin_ref[at, :]
            for k, ref in ((0, q_ref), (1, k_ref)):
                raw = times_flipped(one, at, weights, STARTS[k], SIZES[k])
                former, latter = raw[:, :128], raw[:, 128:]
                ref[at, :128] = (former * cs - latter * sn).astype(BF)
                ref[at, 128:] = (former * sn + latter * cs).astype(BF)

        loop(SEQ, 256, project_qk)
        stores += [net.move(q_ref, q_out), net.move(k_ref, k_out)]
        decay = facts[0:1, 0:1]
        for stretch in range(2):

            def mix(rows, stretch=stretch):
                at = pl.ds(pl.multiple_of(stretch * HALF + rows.start, rows.size), rows.size)
                fade, _ = fades(decay, rows.start, rows.size)
                keys = k_ref[stretch * HALF : stretch * HALF + HALF, :]
                mix_ref[at, :] = (dot(q_ref[at, :], keys, NT) * fade).astype(BF)

            loop(HALF, 128, mix)
        stores.append(net.move(mix_ref, mix_out))
        g_o[2]()
        g_v[4]()
        keep_weights(512, 944)

        def project_v(at):
            v_ref[at, :] = (
                times_flipped(one, at, weights, STARTS[2], VDIM) * masked(facts, at.start, at.size)
            ).astype(BF)

        loop(SEQ, 256, project_v)
        stores.append(net.move(v_ref, v_out))
        load_state.wait()
        before = carried[...].T
        prior_ref[0] = before.astype(BF)
        far = lax.broadcasted_iota(jnp.int32, (HALF, 1), 0).astype(F32)
        tail = jnp.exp((HALF - 1.0 - far) * decay)
        local_state = dot((k_ref[:HALF, :].astype(F32) * tail).astype(BF), v_ref[:HALF, :], TN)
        prior_ref[1] = (jnp.exp(HALF * decay) * before + local_state).astype(BF)
        stores.append(net.move(prior_ref, prior_out))
        g_s[3]()
        for stretch in range(2):

            def retain(rows, stretch=stretch):
                at = pl.ds(pl.multiple_of(stretch * HALF + rows.start, rows.size), rows.size)
                _, head = fades(decay, rows.start, rows.size)
                values = v_ref[stretch * HALF : stretch * HALF + HALF, :]
                retained = dot(mix_ref[at, :], values, NN) + dot(q_ref[at, :], prior_ref[stretch], NN) * head
                centred, dev = normal(retained, VDIM)
                norm_ref[at, :] = (centred * dev).astype(BF)
                dev_ref[at, :] = dev

            loop(HALF, 128, retain)
        stores += [net.move(norm_ref, norm_out), net.move(dev_ref, dev_out)]
        g_o[3]()
        g_s[4]()
        keep_weights(944, 1376)

        def gate(at):
            swish = times_flipped(one, at, weights, STARTS[3], VDIM)
            s_ref[at, :] = swish.astype(BF)
            share = masked(facts, at.start, at.size) * (swish * jax.nn.sigmoid(swish))
            mixed_ref[at, :] = (share * norm_ref[at, :].astype(F32)).astype(BF)

        loop(SEQ, 256, gate)
        stores += [net.move(s_ref, s_out), net.move(mixed_ref, mixed_out)]
        g_g[0]()
        g_o[4]()
        keep_weights(1376, 1808)

        def take(at, value):
            hidden_ref[at, :] = in_ref[at, :].astype(F32) + value

        r1 = RowSums(net, part, bufs, take)

        def out_rows(d):
            rows = pair(net, d)
            times_plain(((of(mixed_ref, rows), weights, STARTS[4], VDIM),), part, rows)
            r1.side(d)

        out_rows(2)
        out_rows(1)
        r1.far()
        g_u[0]()
        g_g[1]()
        out_rows(-1)
        out_rows(0)
        g_g[2]()
        g_d[0]()
        g_u[1]()
        r1.near()
        g_u[2]()
        g_d[1]()
        g_u[3]()
        r1.finish()
        stores.append(net.move(hidden_ref, hidden_out))
        norm_rows(hidden_ref, gain_two, two)
        y2 = gather_rows(net, two)
        y2[0]()
        g_d[2]()
        g_u[4]()
        keep_weights(2240, 2672)
        g_g[3]()
        y2[1]()
        g_d[3]()
        y2[4]()
        g_g[4]()
        keep_weights(1808, 2240)
        g_d[4]()
        keep_weights(2672, 3104)
        y2[3]()
        y2[2]()
        y2[5]()
        stores.append(net.move(two, two_out))
        grad_swap.wait_recv()
        net.flush()
        wait_all(stores)

    outs = [
        (shape(4, 4, ROWS, 128), False),
        (shape(SEQ, D), False),
        (shape(SEQ, D), False),
        (shape(SEQ, KDIM), False),
        (shape(SEQ, KDIM), False),
        (shape(SEQ, VDIM), False),
        (shape(SEQ, VDIM), False),
        (shape(SEQ, HALF), False),
        (shape(SEQ, VDIM), False),
        (shape(SEQ, 1, kind=F32), False),
        (shape(SEQ, VDIM), False),
        (shape(2, KDIM, VDIM), False),
        (shape(128, D, kind=F32), False),
        (shape(HALF, D), False),
    ]
    return call(
        kernel,
        outs,
        [(shard, True) for shard in shards]
        + [
            (inputs, True),
            (carried_state, False),
            (attn_gain, True),
            (mlp_gain, True),
            (cosine, False),
            (sine, False),
            (facts, True),
            (output_grad, False),
        ],
        [
            pltpu.VMEM((4, 4, ROWS, 128), BF),
            pltpu.VMEM((SEQ, D), BF),
            pltpu.VMEM((SEQ, D), BF),
            pltpu.VMEM((SEQ, D), BF),
            pltpu.VMEM((2, ROWS, 128), BF),
            pltpu.VMEM((ROWS, 128), BF),
            pltpu.VMEM((VDIM, KDIM), F32),
            pltpu.VMEM((SEQ, 128), F32),
            pltpu.VMEM((SEQ, 128), F32),
        ]
        + [pltpu.VMEM(out.shape, out.dtype) for out, _ in outs[3:13]]
        + ROW_BUFS,
        144,
        48,
        cid,
    )


def norm_back(source, gain, grad, out):
    def body(i, total):
        at = pl.ds(pl.multiple_of(i * 32, 32), 32)
        centred, dev = normal(source(at), D)
        normed = centred * dev
        back = grad(at)
        scaled = back * gain[...]
        mean = jnp.sum(scaled, axis=-1, keepdims=True) * (1.0 / D)
        along = jnp.sum(scaled * normed, axis=-1, keepdims=True) * (1.0 / D)
        out(at, dev * (scaled - mean - normed * along))
        return total + jnp.sum(back * normed, axis=0, keepdims=True)

    return lax.fori_loop(0, 4, body, jnp.zeros((1, D), F32))


def load_weights(net, source, weights, lo, to, rows):
    return [net.move(source.at[:, :, pl.ds(lo, rows), :], weights.at[:, :, pl.ds(to, rows), :])]


def mlp_back(weights_all, rows_two, grad_own, grad_other, hidden, mlp_gain, s, normed, dev, mixed, facts, cid):
    def kernel(
        w_ref, two_ref, own_ref, other_ref, hidden_in, gain, s_in, norm_in, dev_in, mixed_in, facts,
        down_out, grad_hidden, gain_out, sums_out, swish_out, ret_out, out_grad_out,
        weights, two, grads, mid, part, down, act, gate_grad, up_grad, swish_grad, ret_grad,
        hidden_ref, s_ref, norm_ref, dev_ref, mixed_ref, total,
        *rest,
    ):
        row_bufs, bufs, sems = rest[:5], rest[5:-3], rest[-3:]
        net = Net(*sems)
        c, t = net.c, net.t
        stores = []
        load_w = []
        for k in (1, 2, 3):
            load_w += load_weights(net, w_ref, weights, STARTS[4 + k], 432 * k, 432)
        load_rows = {}
        for d in (2, 1, -1, 0):
            theirs, mine = pair(net, d)
            block = pl.ds(pl.multiple_of((t + d + 4) % 4 * 128, 128), 128)
            load_rows[d] = [
                net.move(two_ref.at[theirs, :], two.at[theirs, :]),
                net.move(two_ref.at[mine, :], two.at[mine, :]),
                net.move(other_ref.at[block, :], grads.at[theirs, :]),
                net.move(own_ref.at[block, :], grads.at[mine, :]),
            ]
        load_hidden = net.move(hidden_in, hidden_ref)
        load_out = load_weights(net, w_ref, weights, STARTS[4], 0, 432)
        load_gate = [net.move(s_in, s_ref), net.move(norm_in, norm_ref), net.move(dev_in, dev_ref)]
        load_mixed = net.move(mixed_in, mixed_ref)
        net.greet(XZ_HOPS + Y_HOPS)

        def take(at, value):
            total[at, :] = value

        def keep(at, value):
            sums_out[at, :] = value

        r1 = RowSums(net, part, row_bufs, take)
        gather = gather_rows(net, mid)
        split = len(scatter_shapes(864))
        s_gu, s_d = (
            scatter_weights(net, weights, lo, hi, some, lambda at, value: keep(pl.ds(at.start - 432, at.size), value))
            for lo, hi, some in ((432, 1296, bufs[:split]), (1296, 1728, bufs[split:]))
        )
        wait_all(load_w)
        for d in (2, 1, -1, 0):
            rows = pair(net, d)
            wait_all(load_rows[d])
            gate = times_flipped(two, rows, weights, 432, 432)
            up = times_flipped(two, rows, weights, 864, 432)
            back = times_flipped(grads, rows, weights, 1296, 432)
            share = 0.5 + 0.5 * lax.erf(gate * 0.7071067811865476)
            slope = share + gate * (0.3989422804014327 * jnp.exp(-0.5 * gate * gate))
            gelu = gate * share
            put(act, rows, gelu * up)
            back_gate, back_up = (back * up * slope).astype(BF), (back * gelu).astype(BF)
            put(gate_grad, rows, back_gate)
            put(up_grad, rows, back_up)
            times_plain(((back_gate, weights, 432, 432), (back_up, weights, 864, 432)), part, rows)
            r1.side(d)
            if d == 1:
                r1.far()
        r1.near()
        weight_grad(gate_grad, two, weights, 432, 432)
        weight_grad(up_grad, two, weights, 864, 432)
        s_gu[0]()

        def down_rows(at):
            times_plain(((act[at, :], weights, 1296, 432),), down, at)

        loop(SEQ, 256, down_rows)
        stores.append(net.move(down, down_out))
        weight_grad(act, grads, weights, 1296, 432)
        s_d[0]()
        s_gu[1]()
        load_hidden.wait()
        r1.finish()
        own = c * 512 + t * 128

        def store(at, value):
            to = pl.ds(pl.multiple_of(own + at.start, 32), 32)
            whole = grads[to, :].astype(F32) + value
            grad_hidden[at, :] = whole
            mid[to, :] = whole.astype(BF)

        gain_out[...] = norm_back(lambda at: hidden_ref[at, :], gain, lambda at: total[at, :], store)
        gather[0]()
        s_d[1]()
        s_gu[2]()
        s_d[2]()
        wait_all(load_out + load_gate + [load_mixed])

        def gate_back(d):
            rows = pair(net, d)
            mask = jnp.concatenate([masked(facts, at.start, 128) for at in rows], axis=0)
            back = times_flipped(mid, rows, weights, 0, 432) * mask
            swish = of(s_ref, rows).astype(F32)
            unit = of(norm_ref, rows).astype(F32)
            share = jax.nn.sigmoid(swish)
            put(swish_grad, rows, back * unit * (share * (1.0 + swish * (1.0 - share))))
            back = back * (swish * share)
            mean = jnp.sum(back, axis=-1, keepdims=True) * (1.0 / VDIM)
            along = jnp.sum(back * unit, axis=-1, keepdims=True) * (1.0 / VDIM)
            put(ret_grad, rows, (back - mean - unit * along) * of(dev_ref, rows))

        gather[2]()
        gate_back(0)
        gather[1]()
        s_gu[3]()
        s_d[3]()
        gather[3]()
        s_d[4]()
        gather[4]()
        gate_back(1)
        s_gu[4]()
        gate_back(-1)
        gather[5]()
        gate_back(2)
        stores += [net.move(ret_grad, ret_out), net.move(swish_grad, swish_out)]
        weight_grad(mixed_ref, mid, weights, 0, 432)
        stores.append(net.move(weights.at[:, :, pl.ds(0, 432), :], out_grad_out))
        net.flush()
        wait_all(stores)

    cols = pltpu.VMEM((SEQ, VDIM), BF)
    rows = pltpu.VMEM((SEQ, D), BF)
    return call(
        kernel,
        [
            (shape(SEQ, D), False),
            (shape(128, D, kind=F32), True),
            (shape(1, D, kind=F32), True),
            (shape(1296, 128, kind=F32), True),
            (shape(SEQ, VDIM), False),
            (shape(SEQ, VDIM), False),
            (shape(4, 4, 432, 128), False),
        ],
        [
            (weights_all, False),
            (rows_two, False),
            (grad_own, False),
            (grad_other, False),
            (hidden, False),
            (mlp_gain, True),
            (s, False),
            (normed, False),
            (dev, False),
            (mixed, False),
            (facts, True),
        ],
        [pltpu.VMEM((4, 4, 1728, 128), BF)]
        + [rows] * 5
        + [cols] * 5
        + [pltpu.VMEM((128, D), F32), cols, cols, pltpu.VMEM((SEQ, 1), F32), cols, pltpu.VMEM((128, D), F32)]
        + ROW_BUFS
        + scatter_shapes(864)
        + scatter_shapes(432),
        52,
        48,
        cid,
    )


SPREAD_HOPS = tuple(dict(dt=dt, dc=dc) for dt in (0, 1, 2, -1) for dc in (0, 1) if (dt, dc) != (0, 0))
FAR_HOPS = (dict(dx=2), dict(dz=2))


def retention_back(
    weights_all, rows_one, down_part, q, k, v, mix, prior, swish_grad, ret_grad, out_grad, hidden, grad_hidden, inputs,
    attn_gain, cosine, sine, facts, mlp_gain_part, sums_mlp, cid
):

    def kernel(
        w_ref, one_in, down_in, q_in, k_in, v_in, mix_in, prior_in, swish_in, ret_in, out_grad_in, hidden_in, gh_in,
        in_ref, gain, cos_in, sin_in, facts, mlp_gain_ref, sums_mlp_ref,
        out_ref, in_grad, gains_out, sums_out, sums_got, mlp_got,
        weights, sums_ref, one, part, down, q_ref, k_ref, v_ref, mix_ref, prior_ref, swish_grad, ret_grad, hidden_ref,
        gh_ref, cos_ref, sin_ref, q_grad, k_grad, v_grad, score_grad, total, by_group, by_x, by_z,
        *rest,
    ):
        first_bufs, second_bufs, bufs, sems = rest[:5], rest[5:10], rest[10:-3], rest[-3:]
        net = Net(*sems)
        c, t = net.c, net.t
        load_score = [
            net.move(a, b)
            for a, b in (
                (ret_in, ret_grad), (v_in, v_ref), (k_in, k_ref), (prior_in, prior_ref), (cos_in, cos_ref),
                (sin_in, sin_ref),
            )
        ]
        load_rest = [net.move(a, b) for a, b in ((q_in, q_ref), (mix_in, mix_ref), (swish_in, swish_grad))]
        load_down = net.move(down_in.at[pl.ds(pl.multiple_of(c * HALF, HALF), HALF), :], down)
        load_w = []
        for lo, to, n in ((STARTS[3], 0, 432), (STARTS[2], 432, 432), (0, 864, 512)):
            load_w += load_weights(net, w_ref, weights, lo, to, n)
        load_out = net.move(out_grad_in, sums_ref.at[:, :, pl.ds(0, 432), :])
        load_one = net.move(one_in, one)
        load_last = [net.move(hidden_in, hidden_ref), net.move(gh_in, gh_ref)]
        net.greet(XZ_HOPS + FAR_HOPS + SPREAD_HOPS)
        send_mlp = net.copy(sums_mlp_ref, mlp_got, dc=1)

        def take_out(at, value):
            out_ref[at, :] = (hidden_ref[at, :] + value).astype(BF)

        def take(at, value):
            total[at, :] = value

        def keep(at, value):
            sums_out[at, :] = value

        r1 = RowSums(net, down, first_bufs, take_out, source=down_in, first=0)
        r2 = RowSums(net, part, second_bufs, take)
        sums, at = [], 0
        for lo, hi in ((0, 432), (432, 864), (864, 1296), (1296, 1808)):
            n = len(scatter_shapes(hi - lo))
            sums.append(scatter_weights(net, sums_ref, lo, hi, bufs[at : at + n], keep))
            at += n
        s_o, s_s, s_v, s_qk = sums
        decay = facts[0:1, 0:1]
        far = lax.broadcasted_iota(jnp.int32, (HALF, 1), 0).astype(F32)
        tail = jnp.exp((HALF - 1.0 - far) * decay)

        def turn_back(at, raw):
            cs, sn = cos_ref[at, :], sin_ref[at, :]
            former, latter = raw[:, :128], raw[:, 128:]
            return (former * cs + latter * sn).astype(BF), (latter * cs - former * sn).astype(BF)

        wait_all(load_score)
        for stretch in range(2):
            keys = slice(stretch * HALF, stretch * HALF + HALF)

            def score_rows(rows, stretch=stretch, keys=keys):
                at = pl.ds(pl.multiple_of(stretch * HALF + rows.start, rows.size), rows.size)
                fade, head = fades(decay, rows.start, rows.size)
                scores = (dot(ret_grad[at, :], v_ref[keys, :], NT) * fade).astype(BF)
                score_grad[at, :] = scores
                raw = dot(scores, k_ref[keys, :], NN) + dot(ret_grad[at, :], prior_ref[stretch], NT) * head
                q_grad[at, :128], q_grad[at, 128:] = turn_back(at, raw)

            loop(HALF, 128, score_rows)
        wait_all(load_rest)
        ahead = (q_ref[HALF:, :].astype(F32) * jnp.exp((far + 1.0) * decay)).astype(BF)
        grad_local = dot(ahead, ret_grad[HALF:, :], TN).astype(BF)
        for stretch in range(2):
            keys = slice(stretch * HALF, stretch * HALF + HALF)
            raw = dot(score_grad[keys, :], q_ref[keys, :], TN)
            value = dot(mix_ref[keys, :], ret_grad[keys, :], TN)
            if stretch == 0:
                raw = raw + dot(v_ref[keys, :], grad_local, NT) * tail
                value = value + dot(k_ref[keys, :], grad_local, NN) * tail
            k_grad[keys, :128], k_grad[keys, 128:] = turn_back(keys, raw)
            v_grad[keys, :] = (value * masked(facts, stretch * HALF, HALF)).astype(BF)
        load_out.wait()
        s_o[0]()

        def back_rows(d):
            rows = pair(net, d)
            terms = (
                (of(swish_grad, rows), weights, 0, 432),
                (of(v_grad, rows), weights, 432, 432),
                (of(q_grad, rows), weights, 864, 256),
                (of(k_grad, rows), weights, 1120, 256),
            )
            times_plain(terms, part, rows)
            r2.side(d)

        wait_all(load_w)
        back_rows(2)
        load_one.wait()
        weight_grad(v_grad, one, sums_ref, 864, 432)
        s_v[0]()
        r2.far()
        back_rows(1)
        back_rows(-1)
        s_o[1]()
        back_rows(0)
        weight_grad(q_grad, one, sums_ref, 1296, 256)
        weight_grad(k_grad, one, sums_ref, 1552, 256)
        s_qk[0]()
        r2.near()
        weight_grad(swish_grad, one, sums_ref, 432, 432)
        s_s[0]()
        send_mlp.start()
        for d in (2, 1, -1, 0):
            r1.side(d)
        s_o[2]()
        s_v[1]()
        load_down.wait()
        r1.far()
        s_qk[1]()
        s_s[1]()
        s_v[2]()
        r1.near()
        r2.finish()

        wait_all(load_last)

        def store(at, value):
            in_grad[at, :] = gh_ref[at, :] + value

        first = norm_back(lambda at: in_ref[at, :].astype(F32), gain, lambda at: total[at, :], store)

        by_group[t * 2 + c, 0:1, :] = first
        by_group[t * 2 + c, 1:2, :] = mlp_gain_ref[...]

        def spread(ref, place, hops):
            copies = [net.copy(ref.at[place], ref.at[place], **hop) for hop in hops]
            for copy in copies:
                copy.start()
            return copies

        def gathered(ref, copies, count):
            for copy in copies:
                copy.wait_recv()
            value = ref[0]
            for k in range(1, count):
                value = value + ref[k]
            return value

        near = spread(by_group, t * 2 + c, SPREAD_HOPS)
        s_o[3]()
        s_s[2]()
        s_v[3]()
        s_qk[2]()
        by_x[net.x] = gathered(by_group, near, 8)
        near = spread(by_x, net.x, (dict(dx=1), dict(dx=-1), dict(dx=2)))
        s_o[4]()
        s_s[3]()
        s_qk[3]()
        s_v[4]()
        by_z[net.z] = gathered(by_x, near, 4)
        near = spread(by_z, net.z, (dict(dz=1), dict(dz=-1), dict(dz=2)))
        s_s[4]()
        early = net.copy(sums_out.at[pl.ds(0, 1296), :], sums_got.at[pl.ds(0, 1296), :], dc=1)
        early.start()
        s_qk[4]()
        late = net.copy(sums_out.at[pl.ds(1296, 512), :], sums_got.at[pl.ds(1296, 512), :], dc=1)
        late.start()
        r1.finish()
        gains_out[...] = gathered(by_z, near, 4)
        send_mlp.wait_recv()
        early.wait_recv()
        late.wait_recv()
        net.flush()

    cols = pltpu.VMEM((SEQ, VDIM), BF)
    keys = pltpu.VMEM((SEQ, KDIM), BF)
    rows = pltpu.VMEM((SEQ, D), BF)
    own = pltpu.VMEM((128, D), F32)
    return call(
        kernel,
        [
            (shape(128, D), True),
            (shape(128, D, kind=F32), True),
            (shape(2, D, kind=F32), True),
            (shape(1808, 128, kind=F32), True),
            (shape(1808, 128, kind=F32), True),
            (shape(1296, 128, kind=F32), False),
        ],
        [
            (weights_all, False),
            (rows_one, False),
            (down_part, False),
            (q, False),
            (k, False),
            (v, False),
            (mix, False),
            (prior, False),
            (swish_grad, False),
            (ret_grad, False),
            (out_grad, False),
            (hidden, False),
            (grad_hidden, False),
            (inputs, True),
            (attn_gain, True),
            (cosine, False),
            (sine, False),
            (facts, True),
            (mlp_gain_part, True),
            (sums_mlp, False),
        ],
        [
            pltpu.VMEM((4, 4, 1376, 128), BF),
            pltpu.VMEM((4, 4, 1808, 128), BF),
            rows,
            rows,
            pltpu.VMEM((HALF, D), BF),
            keys,
            keys,
            cols,
            pltpu.VMEM((SEQ, HALF), BF),
            pltpu.VMEM((2, KDIM, VDIM), BF),
            cols,
            cols,
            own,
            own,
            pltpu.VMEM((SEQ, 128), F32),
            pltpu.VMEM((SEQ, 128), F32),
            keys,
            keys,
            cols,
            pltpu.VMEM((SEQ, HALF), BF),
            own,
            pltpu.VMEM((8, 2, D), F32),
            pltpu.VMEM((4, 2, D), F32),
            pltpu.VMEM((4, 2, D), F32),
        ]
        + ROW_BUFS
        + ROW_BUFS
        + scatter_shapes(432) * 3
        + scatter_shapes(512),
        100,
        48,
        cid,
    )


def hand_out(outputs, input_grad, gains, sums, got, sums_mlp, got_mlp):
    places = (
        (0, 1296, 256), (0, 1552, 256), (0, 864, 432), (0, 432, 432), (0, 0, 432), (1, 0, 432), (1, 432, 432),
        (1, 864, 432),
    )

    def kernel(out_in, in_in, gains_in, sums_in, got_in, mlp_in, mlp_got_in, out_ref, in_ref, one_ref, two_ref, *refs):
        first_core = lax.axis_index("ctx") == 0
        out_ref[...] = out_in[...]
        in_ref[...] = in_in[...]
        one_ref[...] = gains_in[0:1, :]
        two_ref[...] = gains_in[1:2, :]
        for (which, lo, n), ref in zip(places, refs):
            a = (sums_in, mlp_in)[which][lo : lo + n, :]
            b = (got_in, mlp_got_in)[which][lo : lo + n, :]
            both = jnp.concatenate([jnp.where(first_core, a, b), jnp.where(first_core, b, a)], axis=0)
            both = both.T
            ref[...] = jnp.where(first_core, both[:64], both[64:])

    outs = [shape(128, D), shape(128, D, kind=F32), shape(1, D, kind=F32), shape(1, D, kind=F32)]
    for _, _, n in places:
        outs.append(shape(64, 2 * n, kind=F32))
    spec = pl.BlockSpec(memory_space=pltpu.VMEM)
    return pl.pallas_call(
        kernel,
        out_shape=outs,
        in_specs=[spec] * 7,
        out_specs=[spec] * len(outs),
        compiler_params=pltpu.CompilerParams(vmem_limit_bytes=61 * 2**20),
    )(outputs, input_grad, gains, sums, got, sums_mlp, got_mlp)


def turning_tables():
    frequency = 10000.0 ** (-np.arange(128) / 128.0)
    angles = np.arange(SEQ)[:, None] * frequency[None, :]
    return jnp.asarray(np.cos(angles), F32), jnp.asarray(np.sin(angles), F32)


def on_device(
    inputs,
    seq_lengths,
    carried_state,
    attn_gain,
    query_weight,
    key_weight,
    value_weight,
    swish_weight,
    out_weight,
    mlp_gain,
    gate_weight,
    up_weight,
    down_weight,
    output_grad,
):
    head = lax.axis_index("tp") * 2 + lax.axis_index("ctx")
    decay = -jnp.power(2.0, 5.0 - head.astype(F32)) / SEQ
    row = lax.broadcasted_iota(jnp.int32, (8, 128), 0)
    facts = jnp.where(row == 0, decay, seq_lengths[0].astype(F32))
    cosine, sine = turning_tables()
    gains = attn_gain[None, :], mlp_gain[None, :]
    shards = (
        query_weight, key_weight, value_weight, swish_weight, out_weight.T, gate_weight, up_weight, down_weight.T
    )
    weights, rows_one, rows_two, q, k, v, s, mix, normed, dev, mixed, prior, hidden, grad_other = forward(
        shards, inputs, carried_state.transpose(0, 1, 3, 2), *gains, cosine, sine, facts, output_grad, 1
    )
    down_part, grad_hidden, mlp_gain_part, sums_mlp, swish_grad, ret_grad, out_grad = mlp_back(
        weights, rows_two, output_grad, grad_other, hidden, gains[1], s, normed, dev, mixed, facts, 2
    )
    outputs, input_grad, gain_grads, sums, got_sums, got_mlp = retention_back(
        weights, rows_one, down_part, q, k, v, mix, prior, swish_grad, ret_grad, out_grad, hidden, grad_hidden, inputs,
        gains[0], cosine, sine, facts, mlp_gain_part, sums_mlp, 3
    )
    outputs, input_grad, first, second, *grads = hand_out(
        outputs, input_grad, gain_grads, sums, got_sums, sums_mlp, got_mlp
    )
    return (
        outputs,
        input_grad,
        first[0],
        grads[0],
        grads[1],
        grads[2],
        grads[3],
        grads[4].T,
        second[0],
        grads[5],
        grads[6],
        grads[7].T,
    )


def solution(mesh):
    placed = (
        P(("fsdp", "ctx", "tp"), None),
        P("fsdp"),
        P("fsdp", "tp", None, None),
        P(),
        P(("fsdp", "ctx"), "tp"),
        P(("fsdp", "ctx"), "tp"),
        P(("fsdp", "ctx"), "tp"),
        P(("fsdp", "ctx"), "tp"),
        P("tp", ("fsdp", "ctx")),
        P(),
        P(("fsdp", "ctx"), "tp"),
        P(("fsdp", "ctx"), "tp"),
        P("tp", ("fsdp", "ctx")),
        P(("fsdp", "ctx"), None),
    )
    return jax.shard_map(
        on_device,
        mesh=mesh,
        in_specs=placed,
        out_specs=(
            P(("fsdp", "ctx", "tp"), None),
            P(("fsdp", "ctx", "tp"), None),
            P(),
            P(("fsdp", "ctx"), "tp"),
            P(("fsdp", "ctx"), "tp"),
            P(("fsdp", "ctx"), "tp"),
            P(("fsdp", "ctx"), "tp"),
            P("tp", ("fsdp", "ctx")),
            P(),
            P(("fsdp", "ctx"), "tp"),
            P(("fsdp", "ctx"), "tp"),
            P("tp", ("fsdp", "ctx")),
        ),
        check_vma=False,
    )
```

```python
import jax
import jax.numpy as jnp
import numpy as np
from jax import lax
from jax.experimental import pallas as pl
from jax.experimental.pallas import tpu as pltpu
from jax.sharding import PartitionSpec as P

D = 2048
KDIM = 256
VDIM = 432
SEQ = 1024
HALF = 512
SIZES = (256, 256, 432, 432, 432, 432, 432, 432)
STARTS = (0, 256, 512, 944, 1376, 1808, 2240, 2672)
ROWS = 3104
EPSILON = 1e-05
MESH = pl.DeviceIdType.MESH
BF = jnp.bfloat16
F32 = jnp.float32


def even(rows):
    return rows // 32 * 16


class Net:
    def __init__(self, send, recv, local):
        group = lax.axis_index("fsdp")
        self.c = lax.axis_index("ctx")
        self.t = lax.axis_index("tp")
        self.x = group // 4
        self.z = group % 4
        self.send, self.recv, self.local = send, recv, local
        self.copies, self.gone, self.moves = [], [], 0

    def dev(self, dx=0, dz=0, dt=0, dc=0):
        x, z, t = ((at + d + 4) % 4 if d else at for at, d in ((self.x, dx), (self.z, dz), (self.t, dt)))
        c = 1 - self.c if dc else self.c
        return (x * 4 + z, c, t)

    def greet(self, hops):
        barrier = pltpu.get_barrier_semaphore()
        for hop in hops:
            pl.semaphore_signal(barrier, inc=1, device_id=self.dev(**hop), device_id_type=MESH)
        pl.semaphore_wait(barrier, len(hops))

    def copy(self, src, dst, **hop):
        at = len(self.copies)
        self.copies.append(
            pltpu.make_async_remote_copy(
                src_ref=src,
                dst_ref=dst,
                send_sem=self.send.at[at],
                recv_sem=self.recv.at[at],
                device_id=self.dev(**hop),
                device_id_type=MESH,
            )
        )
        return self.copies[-1]

    def move(self, src, dst):
        copy = pltpu.make_async_copy(src, dst, self.local.at[self.moves])
        self.moves += 1
        copy.start()
        return copy

    def sent(self, copies):
        for copy in copies:
            if not any(copy is other for other in self.gone):
                copy.wait_send()
                self.gone.append(copy)

    def flush(self):
        self.sent(self.copies)


XZ_HOPS = (dict(dx=1), dict(dx=-1), dict(dz=1), dict(dz=-1))
Y_HOPS = (dict(dt=1), dict(dt=-1), dict(dc=1))


def ring_views(net, axis):
    x, z = net.x, net.z
    along_x = lambda ref, d, rows: ref.at[(x + d + 4) % 4, z, rows, :]
    along_z = lambda ref, d, rows: ref.at[x, (z + d + 4) % 4, rows, :]
    all_z = lambda ref, d, rows: ref.at[(x + d + 4) % 4, :, rows, :]
    all_x = lambda ref, d, rows: ref.at[:, (z + d + 4) % 4, rows, :]
    if axis == "x":
        return along_x, all_x, "dx", "dz"
    return along_z, all_z, "dz", "dx"


def gather_weights(net, ref, start, stop):
    cut = start + even(stop - start)
    plans = []
    for axis, lo, hi in (("z", start, cut), ("x", cut, stop)):
        mid = lo + even(hi - lo)
        whole, head, tail = pl.ds(lo, hi - lo), pl.ds(lo, mid - lo), pl.ds(mid, hi - mid)
        first, second, hop_a, hop_b = ring_views(net, axis)
        plan = []
        for view, hop in ((first, hop_a), (second, hop_b)):
            mine = view(ref, 0, whole)
            plan.append(
                (
                    net.copy(mine, mine, **{hop: 1}),
                    net.copy(mine, mine, **{hop: -1}),
                    net.copy(view(ref, -1, head), view(ref, -1, head), **{hop: 1}),
                    net.copy(view(ref, 1, tail), view(ref, 1, tail), **{hop: -1}),
                )
            )
        plans.append(plan)

    def near(phase):
        for plan in plans:
            plan[phase][0].start()
            plan[phase][1].start()

    def far(phase):
        for k in (0, 1):
            for plan in plans:
                plan[phase][k].wait_recv()
                plan[phase][2 + k].start()

    def land(phase):
        for plan in plans:
            plan[phase][2].wait_recv()
            plan[phase][3].wait_recv()

    return [
        lambda: near(0),
        lambda: far(0),
        lambda: (land(0), near(1)),
        lambda: far(1),
        lambda: land(1),
        lambda: net.sent([copy for plan in plans for phase in plan for copy in phase]),
    ]


def add_rows(refs, out, count):
    step = 16

    def body(i, carry):
        at = pl.ds(pl.multiple_of(i * step, step), step)
        total = refs[0](at).astype(F32)
        for ref in refs[1:]:
            total = total + ref(at).astype(F32)
        out(at, total)
        return carry

    lax.fori_loop(0, count // step, body, 0)


def scatter_shapes(rows):
    shapes = []
    cut = even(rows)
    for axis, count in (("z", cut), ("x", rows - cut)):
        head = even(count)
        for pieces in ((4,), ()):
            for n in (head, count - head, count, count):
                shapes.append(pltpu.VMEM((*pieces, n, 128), BF))
    return shapes


def scatter_weights(net, ref, start, stop, bufs, out):
    cut = start + even(stop - start)
    plans = []
    bufs = list(bufs)
    for axis, lo, hi in (("z", start, cut), ("x", cut, stop)):
        mid = lo + even(hi - lo)
        parts = (lo, mid - lo), (mid, hi - mid), (lo, hi - lo)
        head, tail, whole = (pl.ds(*part) for part in parts)
        plan = []
        _, wide, hop_b, hop_a = ring_views(net, "x" if axis == "z" else "z")
        thin = ring_views(net, "z" if axis == "x" else "x")[0]
        for view, hop in ((wide, hop_a), (thin, hop_b)):
            fa, fb, ma, mb = bufs[:4]
            bufs = bufs[4:]
            plan.append(
                dict(
                    view=view,
                    bufs=(fa, fb, ma, mb),
                    copies=(
                        net.copy(view(ref, 2, head), fa, **{hop: 1}),
                        net.copy(view(ref, 2, tail), fb, **{hop: -1}),
                        net.copy(view(ref, 1, whole), ma, **{hop: 1}),
                        net.copy(view(ref, -1, whole), mb, **{hop: -1}),
                    ),
                )
            )
        plans.append((plan, parts))

    def at_rows(view, d, lo):
        def read(at):
            return view(ref, d, pl.ds(lo + at.start, at.size))[...]

        def write(at, value):
            view(ref, d, pl.ds(lo + at.start, at.size))[...] = value.astype(BF)

        return read, write

    def buf_rows(buf):
        if len(buf.shape) == 3:
            return lambda at: buf[:, at, :]
        return lambda at: buf[at, :]

    def far(phase):
        for plan, _ in plans:
            plan[phase]["copies"][0].start()
            plan[phase]["copies"][1].start()

    def near(phase):
        for k, d in ((0, 1), (1, -1)):
            for plan, parts in plans:
                step = plan[phase]
                lo, count = parts[k]
                step["copies"][k].wait_recv()
                read, write = at_rows(step["view"], d, lo)
                add_rows((read, buf_rows(step["bufs"][k])), write, count)
                step["copies"][2 + k].start()

    def total(phase, last):
        for plan, parts in plans:
            step = plan[phase]
            lo, count = parts[2]
            step["copies"][2].wait_recv()
            step["copies"][3].wait_recv()
            read, write = at_rows(step["view"], 0, lo)
            if last:
                write = lambda at, value, lo=lo: out(pl.ds(lo + at.start, at.size), value)
            add_rows((read, buf_rows(step["bufs"][2]), buf_rows(step["bufs"][3])), write, count)

    return [
        lambda: far(0),
        lambda: near(0),
        lambda: (total(0, False), far(1)),
        lambda: near(1),
        lambda: total(1, True),
    ]


def gather_rows(net, ref, first=0, count=128):
    def block(c, t, lo=0, n=count):
        return ref.at[pl.ds(pl.multiple_of(c * 512 + t * 128 + first + lo, 16), n), :]

    c, t = net.c, net.t
    half = count // 2
    before, after, across = (t + 3) % 4, (t + 1) % 4, (t + 2) % 4
    own = block(c, t)
    up = net.copy(own, own, dt=1)
    down = net.copy(own, own, dt=-1)
    side = net.copy(own, own, dc=1)
    fore = net.copy(block(c, before, 0, half), block(c, before, 0, half), dt=1)
    back = net.copy(block(c, after, half, half), block(c, after, half, half), dt=-1)
    over = [
        net.copy(block(c, before), block(c, before), dc=1),
        net.copy(block(c, after), block(c, after), dc=1),
        net.copy(block(c, across, 0, half), block(c, across, 0, half), dc=1),
        net.copy(block(c, across, half, half), block(c, across, half, half), dc=1),
    ]

    def start():
        up.start()
        down.start()
        side.start()

    def forward():
        up.wait_recv()
        fore.start()
        over[0].start()
        down.wait_recv()
        back.start()
        over[1].start()

    def beside():
        side.wait_recv()

    def near():
        over[0].wait_recv()
        over[1].wait_recv()

    def far():
        fore.wait_recv()
        over[2].start()
        back.wait_recv()
        over[3].start()

    def last():
        over[2].wait_recv()
        over[3].wait_recv()

    def sent():
        net.sent((up, down, side, fore, back, *over))

    return start, forward, beside, near, far, last, sent


ROW_BUFS = [
    pltpu.VMEM((512, D), BF),
    pltpu.VMEM((64, D), BF),
    pltpu.VMEM((64, D), BF),
    pltpu.VMEM((128, D), BF),
    pltpu.VMEM((128, D), BF),
]


class RowSums:
    def __init__(self, net, ref, bufs, out, lo=0, count=128, source=None, first=None):
        c, t = net.c, net.t
        self.net, self.t, self.ref, self.out, self.lo, self.count = net, t, ref, out, lo, count
        self.first = c * HALF if first is None else first
        self.half = count // 2
        other, far_a, far_b, near_a, near_b = bufs
        self.other = other
        self.far_a, self.far_b = (far.at[pl.ds(lo // 2, self.half), :] for far in (far_a, far_b))
        self.near_a, self.near_b = (near.at[pl.ds(lo, count), :] for near in (near_a, near_b))
        source = ref if source is None else source
        self.sides = {}
        for d in (2, 1, -1, 0):
            row = self.row(d)
            self.sides[d] = net.copy(
                source.at[pl.ds(pl.multiple_of((1 - c) * HALF + row, 64), count), :],
                other.at[pl.ds(pl.multiple_of(row, 64), count), :],
                dc=1,
            )
        self.hops = (
            net.copy(self.block(2, 0, self.half), self.far_a, dt=1),
            net.copy(self.block(2, self.half, self.half), self.far_b, dt=-1),
            net.copy(self.block(1), self.near_a, dt=1),
            net.copy(self.block(-1), self.near_b, dt=-1),
        )

    def row(self, d, lo=0):
        return (self.t + d + 4) % 4 * 128 + self.lo + lo

    def block(self, d, lo=0, n=None):
        return self.ref.at[pl.ds(pl.multiple_of(self.first + self.row(d, lo), 16), n or self.count), :]

    def mine(self, d, lo=0):
        return self.read(self.ref, self.first + self.row(d, lo)), self.read(self.other, self.row(d, lo))

    @staticmethod
    def read(source, base):
        return lambda at: source[pl.ds(pl.multiple_of(base + at.start, 16), at.size), :]

    def keep(self, d, lo=0):
        base = self.first + self.row(d, lo)

        def store(at, value):
            self.ref[pl.ds(pl.multiple_of(base + at.start, 16), at.size), :] = value.astype(BF)

        return store

    def side(self, d):
        self.sides[d].start()

    def far(self):
        self.sides[2].wait_recv()
        for k in (0, 1):
            add_rows(self.mine(2, k * self.half), self.keep(2, k * self.half), self.half)
            self.hops[k].start()

    def near(self):
        for k, d, buf in ((0, 1, self.far_a), (1, -1, self.far_b)):
            lo, rest = k * self.half, (1 - k) * self.half
            self.sides[d].wait_recv()
            add_rows(self.mine(d, rest), self.keep(d, rest), self.half)
            self.hops[k].wait_recv()
            add_rows((*self.mine(d, lo), self.read(buf, 0)), self.keep(d, lo), self.half)
            self.hops[2 + k].start()

    def finish(self):
        self.sides[0].wait_recv()
        self.hops[2].wait_recv()
        self.hops[3].wait_recv()
        add_rows((*self.mine(0), self.read(self.near_a, 0), self.read(self.near_b, 0)), self.out, self.count)

    def sent(self):
        self.net.sent([*self.sides.values(), *self.hops])


def call(kernel, outs, ins, scratch, copies, moves, cid):
    any_spec = pl.BlockSpec(memory_space=pl.ANY)
    vmem_spec = pl.BlockSpec(memory_space=pltpu.VMEM)
    return pl.pallas_call(
        kernel,
        out_shape=[shape for shape, _ in outs],
        in_specs=[vmem_spec if v else any_spec for _, v in ins],
        out_specs=[vmem_spec if v else any_spec for _, v in outs],
        scratch_shapes=list(scratch)
        + [
            pltpu.SemaphoreType.DMA((copies,)),
            pltpu.SemaphoreType.DMA((copies,)),
            pltpu.SemaphoreType.DMA((moves,)),
        ],
        compiler_params=pltpu.CompilerParams(
            collective_id=cid, has_side_effects=True, vmem_limit_bytes=61 * 2**20
        ),
    )(*[array for array, _ in ins])


def shape(*dims, kind=BF):
    return jax.ShapeDtypeStruct(dims, kind)


def dot(a, b, dims):
    return lax.dot_general(a, b, (dims, ((), ())), preferred_element_type=F32)


NN = ((1,), (0,))
NT = ((1,), (1,))
TN = ((0,), (0,))


def normal(rows, width):
    centred = rows - jnp.sum(rows, axis=-1, keepdims=True) * (1.0 / width)
    spread = jnp.sum(centred * centred, axis=-1, keepdims=True) * (1.0 / width)
    return centred, lax.rsqrt(spread + EPSILON)


def loop(count, step, body):
    def turn(i, carry):
        body(pl.ds(pl.multiple_of(i * step, step), step))
        return carry

    lax.fori_loop(0, count // step, turn, 0)


def pair(net, d):
    lo = (net.t + d + 4) % 4 * 128
    return tuple(pl.ds(pl.multiple_of(c * HALF + lo, 128), 128) for c in (1 - net.c, net.c))


def tile(net, ds, half):
    rows = []
    for d in ds:
        lo = (net.t + d + 4) % 4 * 128 + half * 64
        rows += [pl.ds(pl.multiple_of(c * HALF + lo, 64), 64) for c in (1 - net.c, net.c)]
    return tuple(rows)


def of(ref, rows, cols=slice(None)):
    if isinstance(rows, tuple):
        return jnp.concatenate([ref[at, cols] for at in rows], axis=0)
    return ref[rows, cols]


def put(ref, rows, value, cols=slice(None)):
    if isinstance(rows, tuple):
        for k, at in enumerate(rows):
            ref[at, cols] = value[k * at.size : (k + 1) * at.size].astype(ref.dtype)
    else:
        ref[rows, cols] = value.astype(ref.dtype)


def wide(weights, x, start, count):
    return jnp.concatenate([weights[x, z, start : start + count, :] for z in range(4)], axis=1)


def times_flipped(ref, rows, weights, start, count):
    total = None
    for x in range(4):
        part = dot(of(ref, rows, slice(x * 512, x * 512 + 512)), wide(weights, x, start, count), NT)
        total = part if total is None else total + part
    return total


def times_plain(terms, out, rows):
    for x in range(4):
        total = None
        for value, weights, start, count in terms:
            part = dot(value, wide(weights, x, start, count), NN)
            total = part if total is None else total + part
        put(out, rows, total, slice(x * 512, x * 512 + 512))


def weight_grad(cols, rows, out, start, count):
    for x in range(4):
        grad = dot(cols[...], rows[:, x * 512 : x * 512 + 512], TN).astype(BF)
        for z in range(4):
            out[x, z, start : start + count, :] = grad[:, z * 128 : z * 128 + 128]


def wait_all(copies):
    for copy in copies:
        copy.wait()


def masked(facts, start, rows):
    place = lax.broadcasted_iota(jnp.int32, (rows, 1), 0) + start
    return jnp.where(place.astype(F32) < facts[1:2, 0:1], 1.0, 0.0)


def mask_of(facts, rows):
    return jnp.concatenate([masked(facts, at.start, at.size) for at in rows], axis=0)


def fades(decay, start, rows):
    n = lax.broadcasted_iota(jnp.int32, (rows, HALF), 0) + start
    distance = (n - lax.broadcasted_iota(jnp.int32, (rows, HALF), 1)).astype(F32)
    fade = jnp.where(distance >= 0.0, jnp.exp(jnp.maximum(distance, 0.0) * decay), 0.0)
    ahead = lax.broadcasted_iota(jnp.int32, (rows, 1), 0) + start + 1
    return fade, jnp.exp(ahead.astype(F32) * decay)


def norm_back(source, gain, grad, out, lo=0, count=128):
    def body(i, total):
        at = pl.ds(pl.multiple_of(lo + i * 32, 32), 32)
        centred, dev = normal(source(at), D)
        normed = centred * dev
        back = grad(at)
        scaled = back * gain[...]
        mean = jnp.sum(scaled, axis=-1, keepdims=True) * (1.0 / D)
        along = jnp.sum(scaled * normed, axis=-1, keepdims=True) * (1.0 / D)
        out(at, dev * (scaled - mean - normed * along))
        return total + jnp.sum(back * normed, axis=0, keepdims=True)

    return lax.fori_loop(0, count // 32, body, jnp.zeros((1, D), F32))


def load_weights(net, source, weights, lo, to, rows):
    return [net.move(source.at[:, :, pl.ds(lo, rows), :], weights.at[:, :, pl.ds(to, rows), :])]


ORDER = (
    "y1.0", "sw.qk", "j.qk", "qk.0", "sw.v", "j.v", "sw.s", "v.0", "qk.1", "cs.gs", "j.s", "s.0", "v.1", "qk.2",
    "y1.1", "sw.ogud", "s.1", "v.2", "j.ogud", "y1.2", "o.0", "qk.3", "cw.gs", "y1.3", "v.3", "qk.4", "y1.4",
    "s.2", "o.1", "v.4", "y1.5", "Pqk", "o.2", "Pv", "st", "mix", "s.3", "ret", "o.3", "s.4", "gate", "o.4",
    "oA0", "ra0.2", "g.0", "u.0", "oB0", "oA1", "ra0.far", "ra1.2", "ra1.1", "u.1", "ra0.-1", "d.0", "ra0.1",
    "oB1", "ra1.-1", "ra1.far", "d.1", "ra0.0", "g.1", "ra0.near", "u.2", "d.2", "g.2", "ra1.near", "ra1.0",
    "ra0.fin", "ln0", "yb0.0", "ra1.fin", "g.3", "ln1", "yb1.0", "yb0.1", "u.3", "g.4", "yb0.3", "d.3", "yb0.4",
    "yb1.1", "yb0.2", "yb0.5", "u.4", "d.4", "mA0", "rb0.1", "rb0.2", "yb1.3", "yb1.2", "yb1.4", "mB0", "rb0.-1",
    "rb0.far", "yb1.5", "rb0.0", "mA1", "rb1.2", "rb0.near", "rb1.1", "rb1.far", "mB1", "wgu", "rb1.-1", "wgg",
    "SG.0", "rb1.near", "rb1.0", "down", "wgd", "SD.0", "rb0.fin", "lnb0", "yc0.0", "SG.1", "rb1.fin", "lnb1",
    "yc1.0", "yc0.1", "SD.1", "yc1.1", "SG.2", "yc0.4", "yc1.3", "SD.2", "yc1.2", "yc0.2", "yc0.3", "yc0.5",
    "gA0", "yc1.4", "SG.3", "gB0", "SD.3", "yc1.5", "gA1", "gB1", "wgo", "SG.4", "SD.4",
)


def forward_and_mlp_back(
    shards, inputs, carried_state, attn_gain, mlp_gain, cosine, sine, facts, output_grad, cid
):
    def kernel(
        wq, wk, wv, ws, wo, wg, wu, wd, in_ref, carried_in, gain_one, gain_two, cos_in, sin_in, facts, grad_ref,
        weights_out, one_out, q_out, k_out, v_out, mix_out, prior_out, hidden_out, down_out, grad_hidden, gain_out,
        sums_out, swish_out, ret_out, out_grad_out,
        weights, one, two, part, grads, packs, got, carried, cos_ref, sin_ref,
        q_ref, k_ref, v_ref, mix_ref, prior_ref, hidden_ref, s_ref, norm_ref, dev_ref, mixed_ref, gate_grad, up_grad,
        total,
        *rest,
    ):
        row_bufs, bufs, sems = rest[:5], rest[5:-3], rest[-3:]
        net = Net(*sems)
        c, t = net.c, net.t
        mid, act, swish_grad, ret_grad = one, v_ref, v_ref, gate_grad
        load_cos, load_sin = net.move(cos_in, cos_ref), net.move(sin_in, sin_ref)
        load_state = net.move(carried_in.at[0, c], carried)
        mine = pl.ds(pl.multiple_of(c * HALF, HALF), HALF)
        load_grad = net.move(grad_ref, grads.at[mine, :])
        own = c * 512 + t * 128
        stores, early = [], []

        def norm_rows(source, gain, rows_ref, lo, count):
            def body(rows):
                at = pl.ds(pl.multiple_of(lo + rows.start, rows.size), rows.size)
                centred, dev = normal(source[at, :].astype(F32), D)
                to = pl.ds(pl.multiple_of(own + at.start, 16), at.size)
                rows_ref[to, :] = (centred * dev * gain[...]).astype(BF)

            loop(count, 32, body)

        norm_rows(in_ref, gain_one, one, 0, 128)
        spot = lax.broadcasted_iota(jnp.int32, (64, 128), 0) + c * 64
        place = jnp.where(spot == lax.broadcasted_iota(jnp.int32, (64, 128), 1), 1.0, 0.0).astype(BF)
        for k, ref in enumerate((wq, wk, wv, ws, wo, wg, wu, wd)):
            flat = dot(ref[...], place, TN).astype(BF)
            for core in range(2):
                packs[core, STARTS[k] : STARTS[k] + SIZES[k], :] = flat[core * SIZES[k] : (core + 1) * SIZES[k]]

        net.greet(XZ_HOPS + Y_HOPS)
        steps = {}

        def add(name, stages):
            for k, stage in enumerate(stages):
                steps[f"{name}.{k}"] = stage

        names = ("qk", "v", "s", "o", "g", "u", "d")
        bounds = dict(zip(names, ((0, 512), (512, 944), (944, 1376), (1376, 1808), (1808, 2240), (2240, 2672), (2672, 3104))))
        leave = {}

        def keep_weights(lo, hi):
            rows = pl.ds(lo, hi - lo)
            early.append(net.move(weights.at[:, :, rows, :], weights_out.at[:, :, rows, :]))

        for name in names:
            stages = gather_weights(net, weights, *bounds[name])
            leave[name] = stages[5]
            add(name, stages[:5])
            if name in ("qk", "v", "s"):
                steps[name + ".4"] = lambda last=stages[4], at=bounds[name]: (last(), keep_weights(*at))

        def join(swap, lo, hi):
            swap.wait_recv()
            step = 256 if hi == 512 else 432
            for at in range(lo, hi, step):
                weights[net.x, net.z, at : at + step, :] = packs[c, at : at + step, :] + got[at : at + step, :]

        for name, lo, hi in (("qk", 0, 512), ("v", 512, 944), ("s", 944, 1376), ("ogud", 1376, ROWS)):
            swap = net.copy(packs.at[1 - c, pl.ds(lo, hi - lo), :], got.at[pl.ds(lo, hi - lo), :], dc=1)
            steps["sw." + name] = swap.start
            steps["j." + name] = lambda swap=swap, lo=lo, hi=hi: join(swap, lo, hi)
        grad_swap = net.copy(grad_ref, grads.at[mine, :], dc=1)
        steps["cs.gs"] = grad_swap.start
        steps["cw.gs"] = lambda: (grad_swap.wait_recv(), load_grad.wait())

        *first_gather, first_sent = gather_rows(net, one)
        add("y1", first_gather)
        decay = facts[0:1, 0:1]

        def project_qk():
            wait_all([load_cos, load_sin])

            def body(at):
                cs, sn = cos_ref[at, :], sin_ref[at, :]
                for k, ref in ((0, q_ref), (1, k_ref)):
                    raw = times_flipped(one, at, weights, STARTS[k], SIZES[k])
                    former, latter = raw[:, :128], raw[:, 128:]
                    ref[at, :128] = (former * cs - latter * sn).astype(BF)
                    ref[at, 128:] = (former * sn + latter * cs).astype(BF)

            loop(SEQ, 256, body)
            early.append(net.move(one, one_out))
            stores.extend([net.move(q_ref, q_out), net.move(k_ref, k_out)])

        def project_v():
            def body(at):
                value = times_flipped(one, at, weights, STARTS[2], VDIM)
                v_ref[at, :] = (value * masked(facts, at.start, at.size)).astype(BF)

            loop(SEQ, 256, body)
            early.append(net.move(v_ref, v_out))

        def mix():
            for stretch in range(2):

                def body(rows, stretch=stretch):
                    at = pl.ds(pl.multiple_of(stretch * HALF + rows.start, rows.size), rows.size)
                    fade, _ = fades(decay, rows.start, rows.size)
                    keys = k_ref[stretch * HALF : stretch * HALF + HALF, :]
                    mix_ref[at, :] = (dot(q_ref[at, :], keys, NT) * fade).astype(BF)

                loop(HALF, 128, body)
            stores.append(net.move(mix_ref, mix_out))

        def states():
            load_state.wait()
            before = carried[...].T
            prior_ref[0] = before.astype(BF)
            far = lax.broadcasted_iota(jnp.int32, (HALF, 1), 0).astype(F32)
            tail = jnp.exp((HALF - 1.0 - far) * decay)
            local_state = dot((k_ref[:HALF, :].astype(F32) * tail).astype(BF), v_ref[:HALF, :], TN)
            prior_ref[1] = (jnp.exp(HALF * decay) * before + local_state).astype(BF)
            stores.append(net.move(prior_ref, prior_out))

        def retain():
            for stretch in range(2):

                def body(rows, stretch=stretch):
                    at = pl.ds(pl.multiple_of(stretch * HALF + rows.start, rows.size), rows.size)
                    _, head = fades(decay, rows.start, rows.size)
                    values = v_ref[stretch * HALF : stretch * HALF + HALF, :]
                    retained = dot(mix_ref[at, :], values, NN) + dot(q_ref[at, :], prior_ref[stretch], NN) * head
                    centred, dev = normal(retained, VDIM)
                    norm_ref[at, :] = (centred * dev).astype(BF)
                    dev_ref[at, :] = dev

                loop(HALF, 128, body)

        def gate():
            def body(at):
                swish = times_flipped(one, at, weights, STARTS[3], VDIM)
                s_ref[at, :] = swish.astype(BF)
                share = masked(facts, at.start, at.size) * (swish * jax.nn.sigmoid(swish))
                mixed_ref[at, :] = (share * norm_ref[at, :].astype(F32)).astype(BF)

            loop(SEQ, 256, body)
            wait_all(early)
            first_sent()

        steps.update(Pqk=project_qk, Pv=project_v, mix=mix, st=states, ret=retain, gate=gate)

        def hidden_rows(lo):
            def take(rows, value):
                at = pl.ds(pl.multiple_of(lo + rows.start, rows.size), rows.size)
                hidden_ref[at, :] = in_ref[at, :].astype(F32) + value

            return take

        def grad_rows(lo):
            def take(rows, value):
                total[pl.ds(pl.multiple_of(lo + rows.start, rows.size), rows.size), :] = value

            return take

        def out_rows(rows):
            times_plain(((of(mixed_ref, rows), weights, STARTS[4], VDIM),), part, rows)

        def mlp_rows(rows):
            gate = times_flipped(two, rows, weights, STARTS[5], VDIM)
            up = times_flipped(two, rows, weights, STARTS[6], VDIM)
            back = times_flipped(grads, rows, weights, STARTS[7], VDIM)
            share = 0.5 + 0.5 * lax.erf(gate * 0.7071067811865476)
            slope = share + gate * (0.3989422804014327 * jnp.exp(-0.5 * gate * gate))
            gelu = gate * share
            put(act, rows, gelu * up)
            back_gate, back_up = (back * up * slope).astype(BF), (back * gelu).astype(BF)
            put(gate_grad, rows, back_gate)
            put(up_grad, rows, back_up)
            times_plain(((back_gate, weights, STARTS[5], VDIM), (back_up, weights, STARTS[6], VDIM)), part, rows)

        def gate_back(rows):
            back = times_flipped(mid, rows, weights, STARTS[4], VDIM) * mask_of(facts, rows)
            swish = of(s_ref, rows).astype(F32)
            unit = of(norm_ref, rows).astype(F32)
            share = jax.nn.sigmoid(swish)
            put(swish_grad, rows, back * unit * (share * (1.0 + swish * (1.0 - share))))
            back = back * (swish * share)
            mean = jnp.sum(back, axis=-1, keepdims=True) * (1.0 / VDIM)
            along = jnp.sum(back * unit, axis=-1, keepdims=True) * (1.0 / VDIM)
            put(ret_grad, rows, (back - mean - unit * along) * of(dev_ref, rows))

        def norm_two(lo):
            norm_rows(hidden_ref, gain_two, two, lo, 64)

        def norm_two_back(lo):
            def store(at, value):
                to = pl.ds(pl.multiple_of(own + at.start, 32), 32)
                whole = grads[to, :].astype(F32) + value
                grad_hidden[at, :] = whole
                mid[to, :] = whole.astype(BF)

            some = norm_back(lambda at: hidden_ref[at, :], gain_two, lambda at: total[at, :], store, lo, 64)
            gain_out[...] = some if lo == 0 else gain_out[...] + some

        first_sums, second_sums = (
            [RowSums(net, part, row_bufs, rows(lo), lo, 64) for lo in (0, 64)] for rows in (hidden_rows, grad_rows)
        )
        for h in (0, 1):
            for name, sums in (("ra", first_sums[h]), ("rb", second_sums[h])):
                for d in (2, 1, -1, 0):
                    steps[f"{name}{h}.{d}"] = lambda sums=sums, d=d: sums.side(d)
                steps.update({f"{name}{h}.far": sums.far, f"{name}{h}.near": sums.near, f"{name}{h}.fin": sums.finish})
            add(f"yb{h}", gather_rows(net, two, h * 64, 64)[:6])
            add(f"yc{h}", gather_rows(net, mid, h * 64, 64)[:6])
            steps[f"ln{h}"] = lambda h=h: norm_two(h * 64)
            steps[f"lnb{h}"] = lambda h=h: norm_two_back(h * 64)
            for which, ds in (("A", (2, 1)), ("B", (-1, 0))):
                rows = tile(net, ds, h)
                steps[f"o{which}{h}"] = lambda rows=rows: out_rows(rows)
                steps[f"m{which}{h}"] = lambda rows=rows: mlp_rows(rows)
                steps[f"g{which}{h}"] = lambda rows=rows: gate_back(rows)
        first_tile = steps["mA0"]
        steps["mA0"] = lambda: (first_sums[0].sent(), first_sums[1].sent(), first_tile())

        def keep(at, value):
            sums_out[pl.ds(at.start - STARTS[5], at.size), :] = value

        split = len(scatter_shapes(864))
        add("SG", scatter_weights(net, weights, STARTS[5], STARTS[7], bufs[:split], keep))
        add("SD", scatter_weights(net, weights, STARTS[7], ROWS, bufs[split:], keep))

        def grad_of(name, cols, rows, k):
            leave[name]()
            weight_grad(cols, rows, weights, STARTS[k], VDIM)

        def down_rows():
            for name in ("qk", "v", "s"):
                leave[name]()

            def body(at):
                for x in range(4):
                    value = dot(act[at, :], wide(weights, x, STARTS[7], VDIM), NN).astype(BF)
                    for z in range(4):
                        weights[x, z, at, :] = value[:, z * 128 : z * 128 + 128]

            loop(SEQ, 256, body)
            for x in range(4):
                for z in range(4):
                    cols = pl.ds(x * 512 + z * 128, 128)
                    stores.append(net.move(weights.at[x, z, pl.ds(0, SEQ), :], down_out.at[:, cols]))

        def out_grad():
            grad_of("o", mixed_ref, mid, 4)
            stores.append(net.move(weights.at[:, :, pl.ds(STARTS[4], VDIM), :], out_grad_out))

        steps.update(
            wgg=lambda: grad_of("g", gate_grad, two, 5),
            wgu=lambda: grad_of("u", up_grad, two, 6),
            wgd=lambda: grad_of("d", act, grads, 7),
            wgo=out_grad,
            down=down_rows,
        )
        for name in ORDER:
            steps.pop(name)()
            if name == "ra1.fin":
                stores.append(net.move(hidden_ref, hidden_out))
        assert not steps
        stores += [net.move(ret_grad, ret_out), net.move(swish_grad, swish_out)]
        net.flush()
        wait_all(stores)

    cols = pltpu.VMEM((SEQ, VDIM), BF)
    rows = pltpu.VMEM((SEQ, D), BF)
    keys = pltpu.VMEM((SEQ, KDIM), BF)
    own = pltpu.VMEM((128, D), F32)
    return call(
        kernel,
        [
            (shape(4, 4, STARTS[4], 128), False),
            (shape(SEQ, D), False),
            (shape(SEQ, KDIM), False),
            (shape(SEQ, KDIM), False),
            (shape(SEQ, VDIM), False),
            (shape(SEQ, HALF), False),
            (shape(2, KDIM, VDIM), False),
            (shape(128, D, kind=F32), False),
            (shape(SEQ, D), False),
            (shape(128, D, kind=F32), True),
            (shape(1, D, kind=F32), True),
            (shape(1296, 128, kind=F32), True),
            (shape(SEQ, VDIM), False),
            (shape(SEQ, VDIM), False),
            (shape(4, 4, 432, 128), False),
        ],
        [(shard, True) for shard in shards]
        + [
            (inputs, True),
            (carried_state, False),
            (attn_gain, True),
            (mlp_gain, True),
            (cosine, False),
            (sine, False),
            (facts, True),
            (output_grad, False),
        ],
        [
            pltpu.VMEM((4, 4, ROWS, 128), BF),
            rows,
            rows,
            rows,
            rows,
            pltpu.VMEM((2, ROWS, 128), BF),
            pltpu.VMEM((ROWS, 128), BF),
            pltpu.VMEM((VDIM, KDIM), F32),
            pltpu.VMEM((SEQ, 128), F32),
            pltpu.VMEM((SEQ, 128), F32),
            keys,
            keys,
            cols,
            pltpu.VMEM((SEQ, HALF), BF),
            pltpu.VMEM((2, KDIM, VDIM), BF),
            own,
            cols,
            cols,
            pltpu.VMEM((SEQ, 1), F32),
            cols,
            cols,
            cols,
            own,
        ]
        + ROW_BUFS
        + scatter_shapes(864)
        + scatter_shapes(432),
        228,
        48,
        cid,
    )


SPREAD_HOPS = tuple(dict(dt=dt, dc=dc) for dt in (0, 1, 2, -1) for dc in (0, 1) if (dt, dc) != (0, 0))
FAR_HOPS = (dict(dx=2), dict(dz=2))


def retention_back(
    weights_all, rows_one, down_part, q, k, v, mix, prior, swish_grad, ret_grad, out_grad, hidden, grad_hidden, inputs,
    attn_gain, cosine, sine, facts, mlp_gain_part, sums_mlp, cid
):

    def kernel(
        w_ref, one_in, down_in, q_in, k_in, v_in, mix_in, prior_in, swish_in, ret_in, out_grad_in, hidden_in, gh_in,
        in_ref, gain, cos_in, sin_in, facts, mlp_gain_ref, sums_mlp_ref,
        out_ref, in_grad, gains_out, sums_out, sums_got, mlp_got,
        weights, sums_ref, one, part, down, q_ref, k_ref, v_ref, mix_ref, prior_ref, swish_grad, ret_grad, hidden_ref,
        gh_ref, cos_ref, sin_ref, q_grad, k_grad, v_grad, score_grad, total, by_group, by_x, by_z,
        *rest,
    ):
        first_bufs, second_bufs, bufs, sems = rest[:5], rest[5:10], rest[10:-3], rest[-3:]
        net = Net(*sems)
        c, t = net.c, net.t
        load_score = [
            net.move(a, b)
            for a, b in (
                (ret_in, ret_grad), (v_in, v_ref), (k_in, k_ref), (prior_in, prior_ref), (cos_in, cos_ref),
                (sin_in, sin_ref),
            )
        ]
        load_rest = [net.move(a, b) for a, b in ((q_in, q_ref), (mix_in, mix_ref), (swish_in, swish_grad))]
        load_down = net.move(down_in.at[pl.ds(pl.multiple_of(c * HALF, HALF), HALF), :], down)
        load_w = []
        for lo, to, n in ((STARTS[3], 0, 432), (STARTS[2], 432, 432), (0, 864, 512)):
            load_w += load_weights(net, w_ref, weights, lo, to, n)
        load_out = net.move(out_grad_in, sums_ref.at[:, :, pl.ds(0, 432), :])
        load_one = net.move(one_in, one)
        load_last = [net.move(hidden_in, hidden_ref), net.move(gh_in, gh_ref)]
        net.greet(XZ_HOPS + FAR_HOPS + SPREAD_HOPS)
        send_mlp = net.copy(sums_mlp_ref, mlp_got, dc=1)

        def take_out(at, value):
            out_ref[at, :] = (hidden_ref[at, :] + value).astype(BF)

        def take(at, value):
            total[at, :] = value

        def keep(at, value):
            sums_out[at, :] = value

        r1 = RowSums(net, down, first_bufs, take_out, source=down_in, first=0)
        r2 = RowSums(net, part, second_bufs, take)
        sums, at = [], 0
        for lo, hi in ((0, 432), (432, 864), (864, 1296), (1296, 1808)):
            n = len(scatter_shapes(hi - lo))
            sums.append(scatter_weights(net, sums_ref, lo, hi, bufs[at : at + n], keep))
            at += n
        s_o, s_s, s_v, s_qk = sums
        decay = facts[0:1, 0:1]
        far = lax.broadcasted_iota(jnp.int32, (HALF, 1), 0).astype(F32)
        tail = jnp.exp((HALF - 1.0 - far) * decay)

        def turn_back(at, raw):
            cs, sn = cos_ref[at, :], sin_ref[at, :]
            former, latter = raw[:, :128], raw[:, 128:]
            return (former * cs + latter * sn).astype(BF), (latter * cs - former * sn).astype(BF)

        wait_all(load_score)
        for stretch in range(2):
            keys = slice(stretch * HALF, stretch * HALF + HALF)

            def score_rows(rows, stretch=stretch, keys=keys):
                at = pl.ds(pl.multiple_of(stretch * HALF + rows.start, rows.size), rows.size)
                fade, head = fades(decay, rows.start, rows.size)
                scores = (dot(ret_grad[at, :], v_ref[keys, :], NT) * fade).astype(BF)
                score_grad[at, :] = scores
                raw = dot(scores, k_ref[keys, :], NN) + dot(ret_grad[at, :], prior_ref[stretch], NT) * head
                q_grad[at, :128], q_grad[at, 128:] = turn_back(at, raw)

            loop(HALF, 128, score_rows)
        wait_all(load_rest)
        ahead = (q_ref[HALF:, :].astype(F32) * jnp.exp((far + 1.0) * decay)).astype(BF)
        grad_local = dot(ahead, ret_grad[HALF:, :], TN).astype(BF)
        for stretch in range(2):
            keys = slice(stretch * HALF, stretch * HALF + HALF)
            raw = dot(score_grad[keys, :], q_ref[keys, :], TN)
            value = dot(mix_ref[keys, :], ret_grad[keys, :], TN)
            if stretch == 0:
                raw = raw + dot(v_ref[keys, :], grad_local, NT) * tail
                value = value + dot(k_ref[keys, :], grad_local, NN) * tail
            k_grad[keys, :128], k_grad[keys, 128:] = turn_back(keys, raw)
            v_grad[keys, :] = (value * masked(facts, stretch * HALF, HALF)).astype(BF)
        load_out.wait()
        s_o[0]()

        def back_rows(d):
            rows = pair(net, d)
            terms = (
                (of(swish_grad, rows), weights, 0, 432),
                (of(v_grad, rows), weights, 432, 432),
                (of(q_grad, rows), weights, 864, 256),
                (of(k_grad, rows), weights, 1120, 256),
            )
            times_plain(terms, part, rows)
            r2.side(d)

        wait_all(load_w)
        back_rows(2)
        load_one.wait()
        weight_grad(v_grad, one, sums_ref, 864, 432)
        s_v[0]()
        r2.far()
        back_rows(1)
        back_rows(-1)
        s_o[1]()
        back_rows(0)
        weight_grad(q_grad, one, sums_ref, 1296, 256)
        weight_grad(k_grad, one, sums_ref, 1552, 256)
        s_qk[0]()
        r2.near()
        weight_grad(swish_grad, one, sums_ref, 432, 432)
        s_s[0]()
        send_mlp.start()
        for d in (2, 1, -1, 0):
            r1.side(d)
        s_o[2]()
        s_v[1]()
        load_down.wait()
        r1.far()
        s_qk[1]()
        s_s[1]()
        s_v[2]()
        r1.near()
        r2.finish()

        wait_all(load_last)

        def store(at, value):
            in_grad[at, :] = gh_ref[at, :] + value

        first = norm_back(lambda at: in_ref[at, :].astype(F32), gain, lambda at: total[at, :], store)

        by_group[t * 2 + c, 0:1, :] = first
        by_group[t * 2 + c, 1:2, :] = mlp_gain_ref[...]

        def spread(ref, place, hops):
            copies = [net.copy(ref.at[place], ref.at[place], **hop) for hop in hops]
            for copy in copies:
                copy.start()
            return copies

        def gathered(ref, copies, count):
            for copy in copies:
                copy.wait_recv()
            value = ref[0]
            for k in range(1, count):
                value = value + ref[k]
            return value

        near = spread(by_group, t * 2 + c, SPREAD_HOPS)
        s_o[3]()
        s_s[2]()
        s_v[3]()
        s_qk[2]()
        by_x[net.x] = gathered(by_group, near, 8)
        near = spread(by_x, net.x, (dict(dx=1), dict(dx=-1), dict(dx=2)))
        s_o[4]()
        s_s[3]()
        s_qk[3]()
        s_v[4]()
        by_z[net.z] = gathered(by_x, near, 4)
        near = spread(by_z, net.z, (dict(dz=1), dict(dz=-1), dict(dz=2)))
        s_s[4]()
        early = net.copy(sums_out.at[pl.ds(0, 1296), :], sums_got.at[pl.ds(0, 1296), :], dc=1)
        early.start()
        s_qk[4]()
        late = net.copy(sums_out.at[pl.ds(1296, 512), :], sums_got.at[pl.ds(1296, 512), :], dc=1)
        late.start()
        r1.finish()
        gains_out[...] = gathered(by_z, near, 4)
        send_mlp.wait_recv()
        early.wait_recv()
        late.wait_recv()
        net.flush()

    cols = pltpu.VMEM((SEQ, VDIM), BF)
    keys = pltpu.VMEM((SEQ, KDIM), BF)
    rows = pltpu.VMEM((SEQ, D), BF)
    own = pltpu.VMEM((128, D), F32)
    return call(
        kernel,
        [
            (shape(128, D), True),
            (shape(128, D, kind=F32), True),
            (shape(2, D, kind=F32), True),
            (shape(1808, 128, kind=F32), True),
            (shape(1808, 128, kind=F32), True),
            (shape(1296, 128, kind=F32), False),
        ],
        [
            (weights_all, False),
            (rows_one, False),
            (down_part, False),
            (q, False),
            (k, False),
            (v, False),
            (mix, False),
            (prior, False),
            (swish_grad, False),
            (ret_grad, False),
            (out_grad, False),
            (hidden, False),
            (grad_hidden, False),
            (inputs, True),
            (attn_gain, True),
            (cosine, False),
            (sine, False),
            (facts, True),
            (mlp_gain_part, True),
            (sums_mlp, False),
        ],
        [
            pltpu.VMEM((4, 4, 1376, 128), BF),
            pltpu.VMEM((4, 4, 1808, 128), BF),
            rows,
            rows,
            pltpu.VMEM((HALF, D), BF),
            keys,
            keys,
            cols,
            pltpu.VMEM((SEQ, HALF), BF),
            pltpu.VMEM((2, KDIM, VDIM), BF),
            cols,
            cols,
            own,
            own,
            pltpu.VMEM((SEQ, 128), F32),
            pltpu.VMEM((SEQ, 128), F32),
            keys,
            keys,
            cols,
            pltpu.VMEM((SEQ, HALF), BF),
            own,
            pltpu.VMEM((8, 2, D), F32),
            pltpu.VMEM((4, 2, D), F32),
            pltpu.VMEM((4, 2, D), F32),
        ]
        + ROW_BUFS
        + ROW_BUFS
        + scatter_shapes(432) * 3
        + scatter_shapes(512),
        100,
        48,
        cid,
    )


def hand_out(outputs, input_grad, gains, sums, got, sums_mlp, got_mlp):
    places = (
        (0, 1296, 256), (0, 1552, 256), (0, 864, 432), (0, 432, 432), (0, 0, 432), (1, 0, 432), (1, 432, 432),
        (1, 864, 432),
    )

    def kernel(out_in, in_in, gains_in, sums_in, got_in, mlp_in, mlp_got_in, out_ref, in_ref, one_ref, two_ref, *refs):
        first_core = lax.axis_index("ctx") == 0
        out_ref[...] = out_in[...]
        in_ref[...] = in_in[...]
        one_ref[...] = gains_in[0:1, :]
        two_ref[...] = gains_in[1:2, :]
        for (which, lo, n), ref in zip(places, refs):
            a = (sums_in, mlp_in)[which][lo : lo + n, :]
            b = (got_in, mlp_got_in)[which][lo : lo + n, :]
            both = jnp.concatenate([jnp.where(first_core, a, b), jnp.where(first_core, b, a)], axis=0)
            both = both.T
            ref[...] = jnp.where(first_core, both[:64], both[64:])

    outs = [shape(128, D), shape(128, D, kind=F32), shape(1, D, kind=F32), shape(1, D, kind=F32)]
    for _, _, n in places:
        outs.append(shape(64, 2 * n, kind=F32))
    spec = pl.BlockSpec(memory_space=pltpu.VMEM)
    return pl.pallas_call(
        kernel,
        out_shape=outs,
        in_specs=[spec] * 7,
        out_specs=[spec] * len(outs),
        compiler_params=pltpu.CompilerParams(vmem_limit_bytes=61 * 2**20),
    )(outputs, input_grad, gains, sums, got, sums_mlp, got_mlp)


def turning_tables():
    frequency = 10000.0 ** (-np.arange(128) / 128.0)
    angles = np.arange(SEQ)[:, None] * frequency[None, :]
    return jnp.asarray(np.cos(angles), F32), jnp.asarray(np.sin(angles), F32)


def on_device(
    inputs,
    seq_lengths,
    carried_state,
    attn_gain,
    query_weight,
    key_weight,
    value_weight,
    swish_weight,
    out_weight,
    mlp_gain,
    gate_weight,
    up_weight,
    down_weight,
    output_grad,
):
    head = lax.axis_index("tp") * 2 + lax.axis_index("ctx")
    decay = -jnp.power(2.0, 5.0 - head.astype(F32)) / SEQ
    row = lax.broadcasted_iota(jnp.int32, (8, 128), 0)
    facts = jnp.where(row == 0, decay, seq_lengths[0].astype(F32))
    cosine, sine = turning_tables()
    gains = attn_gain[None, :], mlp_gain[None, :]
    shards = (
        query_weight, key_weight, value_weight, swish_weight, out_weight.T, gate_weight, up_weight, down_weight.T
    )
    (
        weights, rows_one, q, k, v, mix, prior, hidden, down_part, grad_hidden, mlp_gain_part, sums_mlp, swish_grad,
        ret_grad, out_grad
    ) = forward_and_mlp_back(
        shards, inputs, carried_state.transpose(0, 1, 3, 2), *gains, cosine, sine, facts, output_grad, 1
    )
    outputs, input_grad, gain_grads, sums, got_sums, got_mlp = retention_back(
        weights, rows_one, down_part, q, k, v, mix, prior, swish_grad, ret_grad, out_grad, hidden, grad_hidden, inputs,
        gains[0], cosine, sine, facts, mlp_gain_part, sums_mlp, 2
    )
    outputs, input_grad, first, second, *grads = hand_out(
        outputs, input_grad, gain_grads, sums, got_sums, sums_mlp, got_mlp
    )
    return (
        outputs,
        input_grad,
        first[0],
        grads[0],
        grads[1],
        grads[2],
        grads[3],
        grads[4].T,
        second[0],
        grads[5],
        grads[6],
        grads[7].T,
    )


def solution(mesh):
    placed = (
        P(("fsdp", "ctx", "tp"), None),
        P("fsdp"),
        P("fsdp", "tp", None, None),
        P(),
        P(("fsdp", "ctx"), "tp"),
        P(("fsdp", "ctx"), "tp"),
        P(("fsdp", "ctx"), "tp"),
        P(("fsdp", "ctx"), "tp"),
        P("tp", ("fsdp", "ctx")),
        P(),
        P(("fsdp", "ctx"), "tp"),
        P(("fsdp", "ctx"), "tp"),
        P("tp", ("fsdp", "ctx")),
        P(("fsdp", "ctx"), None),
    )
    return jax.shard_map(
        on_device,
        mesh=mesh,
        in_specs=placed,
        out_specs=(
            P(("fsdp", "ctx", "tp"), None),
            P(("fsdp", "ctx", "tp"), None),
            P(),
            P(("fsdp", "ctx"), "tp"),
            P(("fsdp", "ctx"), "tp"),
            P(("fsdp", "ctx"), "tp"),
            P(("fsdp", "ctx"), "tp"),
            P("tp", ("fsdp", "ctx")),
            P(),
            P(("fsdp", "ctx"), "tp"),
            P(("fsdp", "ctx"), "tp"),
            P("tp", ("fsdp", "ctx")),
        ),
        check_vma=False,
    )
```

```python
import jax
import jax.numpy as jnp
import numpy as np
from jax import lax
from jax.experimental import pallas as pl
from jax.experimental.pallas import tpu as pltpu
from jax.sharding import PartitionSpec as P

D = 2048
KDIM = 256
VDIM = 432
SEQ = 1024
HALF = 512
SIZES = (256, 256, 432, 432, 432, 432, 432, 432)
STARTS = (0, 256, 512, 944, 1376, 1808, 2240, 2672)
ROWS = 3104
EPSILON = 1e-05
MESH = pl.DeviceIdType.MESH
BF = jnp.bfloat16
F32 = jnp.float32


def even(rows):
    return rows // 32 * 16


class Net:
    def __init__(self, send, recv, local):
        group = lax.axis_index("fsdp")
        self.c = lax.axis_index("ctx")
        self.t = lax.axis_index("tp")
        self.x = group // 4
        self.z = group % 4
        self.send, self.recv, self.local = send, recv, local
        self.copies, self.gone, self.moves = [], [], 0

    def dev(self, dx=0, dz=0, dt=0, dc=0):
        x, z, t = ((at + d + 4) % 4 if d else at for at, d in ((self.x, dx), (self.z, dz), (self.t, dt)))
        c = 1 - self.c if dc else self.c
        return (x * 4 + z, c, t)

    def greet(self, hops):
        self.greeted = len(hops)
        for hop in hops:
            pl.semaphore_signal(
                pltpu.get_barrier_semaphore(), inc=1, device_id=self.dev(**hop), device_id_type=MESH
            )

    def met(self):
        pl.semaphore_wait(pltpu.get_barrier_semaphore(), self.greeted)

    def copy(self, src, dst, **hop):
        at = len(self.copies)
        self.copies.append(
            pltpu.make_async_remote_copy(
                src_ref=src,
                dst_ref=dst,
                send_sem=self.send.at[at],
                recv_sem=self.recv.at[at],
                device_id=self.dev(**hop),
                device_id_type=MESH,
            )
        )
        return self.copies[-1]

    def move(self, src, dst):
        copy = pltpu.make_async_copy(src, dst, self.local.at[self.moves])
        self.moves += 1
        copy.start()
        return copy

    def sent(self, copies):
        for copy in copies:
            if not any(copy is other for other in self.gone):
                copy.wait_send()
                self.gone.append(copy)

    def flush(self):
        self.sent(self.copies)


XZ_HOPS = (dict(dx=1), dict(dx=-1), dict(dz=1), dict(dz=-1))
Y_HOPS = (dict(dt=1), dict(dt=-1), dict(dc=1))


def ring_views(net, axis):
    x, z = net.x, net.z
    along_x = lambda ref, d, rows: ref.at[(x + d + 4) % 4, z, rows, :]
    along_z = lambda ref, d, rows: ref.at[x, (z + d + 4) % 4, rows, :]
    all_z = lambda ref, d, rows: ref.at[(x + d + 4) % 4, :, rows, :]
    all_x = lambda ref, d, rows: ref.at[:, (z + d + 4) % 4, rows, :]
    if axis == "x":
        return along_x, all_x, "dx", "dz"
    return along_z, all_z, "dz", "dx"


def gather_weights(net, ref, start, stop):
    cut = start + even(stop - start)
    plans = []
    for axis, lo, hi in (("z", start, cut), ("x", cut, stop)):
        mid = lo + even(hi - lo)
        whole, head, tail = pl.ds(lo, hi - lo), pl.ds(lo, mid - lo), pl.ds(mid, hi - mid)
        first, second, hop_a, hop_b = ring_views(net, axis)
        plan = []
        for view, hop in ((first, hop_a), (second, hop_b)):
            mine = view(ref, 0, whole)
            plan.append(
                (
                    net.copy(mine, mine, **{hop: 1}),
                    net.copy(mine, mine, **{hop: -1}),
                    net.copy(view(ref, -1, head), view(ref, -1, head), **{hop: 1}),
                    net.copy(view(ref, 1, tail), view(ref, 1, tail), **{hop: -1}),
                )
            )
        plans.append(plan)

    def near(phase):
        for plan in plans:
            plan[phase][0].start()
            plan[phase][1].start()

    def far(phase):
        for k in (0, 1):
            for plan in plans:
                plan[phase][k].wait_recv()
                plan[phase][2 + k].start()

    def land(phase):
        for plan in plans:
            plan[phase][2].wait_recv()
            plan[phase][3].wait_recv()

    return [
        lambda: near(0),
        lambda: far(0),
        lambda: (land(0), near(1)),
        lambda: far(1),
        lambda: land(1),
        lambda: net.sent([copy for plan in plans for phase in plan for copy in phase]),
    ]


def add_rows(refs, out, count):
    step = 16

    def body(i, carry):
        at = pl.ds(pl.multiple_of(i * step, step), step)
        total = refs[0](at).astype(F32)
        for ref in refs[1:]:
            total = total + ref(at).astype(F32)
        out(at, total)
        return carry

    lax.fori_loop(0, count // step, body, 0)


def scatter_shapes(rows):
    shapes = []
    cut = even(rows)
    for axis, count in (("z", cut), ("x", rows - cut)):
        head = even(count)
        for pieces in ((4,), ()):
            for n in (head, count - head, count, count):
                shapes.append(pltpu.VMEM((*pieces, n, 128), BF))
    return shapes


def scatter_weights(net, ref, start, stop, bufs, out):
    cut = start + even(stop - start)
    plans = []
    bufs = list(bufs)
    for axis, lo, hi in (("z", start, cut), ("x", cut, stop)):
        mid = lo + even(hi - lo)
        parts = (lo, mid - lo), (mid, hi - mid), (lo, hi - lo)
        head, tail, whole = (pl.ds(*part) for part in parts)
        plan = []
        _, wide, hop_b, hop_a = ring_views(net, "x" if axis == "z" else "z")
        thin = ring_views(net, "z" if axis == "x" else "x")[0]
        for view, hop in ((wide, hop_a), (thin, hop_b)):
            fa, fb, ma, mb = bufs[:4]
            bufs = bufs[4:]
            plan.append(
                dict(
                    view=view,
                    bufs=(fa, fb, ma, mb),
                    copies=(
                        net.copy(view(ref, 2, head), fa, **{hop: 1}),
                        net.copy(view(ref, 2, tail), fb, **{hop: -1}),
                        net.copy(view(ref, 1, whole), ma, **{hop: 1}),
                        net.copy(view(ref, -1, whole), mb, **{hop: -1}),
                    ),
                )
            )
        plans.append((plan, parts))

    def at_rows(view, d, lo):
        def read(at):
            return view(ref, d, pl.ds(lo + at.start, at.size))[...]

        def write(at, value):
            view(ref, d, pl.ds(lo + at.start, at.size))[...] = value.astype(BF)

        return read, write

    def buf_rows(buf):
        if len(buf.shape) == 3:
            return lambda at: buf[:, at, :]
        return lambda at: buf[at, :]

    def far(phase):
        for plan, _ in plans:
            plan[phase]["copies"][0].start()
            plan[phase]["copies"][1].start()

    def near(phase):
        for k, d in ((0, 1), (1, -1)):
            for plan, parts in plans:
                step = plan[phase]
                lo, count = parts[k]
                step["copies"][k].wait_recv()
                read, write = at_rows(step["view"], d, lo)
                add_rows((read, buf_rows(step["bufs"][k])), write, count)
                step["copies"][2 + k].start()

    def total(phase, last):
        for plan, parts in plans:
            step = plan[phase]
            lo, count = parts[2]
            step["copies"][2].wait_recv()
            step["copies"][3].wait_recv()
            read, write = at_rows(step["view"], 0, lo)
            if last:
                write = lambda at, value, lo=lo: out(pl.ds(lo + at.start, at.size), value)
            add_rows((read, buf_rows(step["bufs"][2]), buf_rows(step["bufs"][3])), write, count)

    return [
        lambda: far(0),
        lambda: near(0),
        lambda: (total(0, False), far(1)),
        lambda: near(1),
        lambda: total(1, True),
    ]


def gather_rows(net, ref, first=0, count=128):
    def block(c, t, lo=0, n=count):
        return ref.at[pl.ds(pl.multiple_of(c * 512 + t * 128 + first + lo, 16), n), :]

    c, t = net.c, net.t
    half = count // 2
    before, after, across = (t + 3) % 4, (t + 1) % 4, (t + 2) % 4
    own = block(c, t)
    up = net.copy(own, own, dt=1)
    down = net.copy(own, own, dt=-1)
    side = net.copy(own, own, dc=1)
    fore = net.copy(block(c, before, 0, half), block(c, before, 0, half), dt=1)
    back = net.copy(block(c, after, half, half), block(c, after, half, half), dt=-1)
    over = [
        net.copy(block(c, before), block(c, before), dc=1),
        net.copy(block(c, after), block(c, after), dc=1),
        net.copy(block(c, across, 0, half), block(c, across, 0, half), dc=1),
        net.copy(block(c, across, half, half), block(c, across, half, half), dc=1),
    ]

    def start():
        up.start()
        down.start()
        side.start()

    def forward():
        up.wait_recv()
        fore.start()
        over[0].start()
        down.wait_recv()
        back.start()
        over[1].start()

    def beside():
        side.wait_recv()

    def near():
        over[0].wait_recv()
        over[1].wait_recv()

    def far():
        fore.wait_recv()
        over[2].start()
        back.wait_recv()
        over[3].start()

    def last():
        over[2].wait_recv()
        over[3].wait_recv()

    def sent():
        net.sent((up, down, side, fore, back, *over))

    return start, forward, beside, near, far, last, sent


ROW_BUFS = [
    pltpu.VMEM((512, D), BF),
    pltpu.VMEM((64, D), BF),
    pltpu.VMEM((64, D), BF),
    pltpu.VMEM((128, D), BF),
    pltpu.VMEM((128, D), BF),
]


class RowSums:
    def __init__(self, net, ref, bufs, out, lo=0, count=128, source=None, first=None):
        c, t = net.c, net.t
        self.net, self.t, self.ref, self.out, self.lo, self.count = net, t, ref, out, lo, count
        self.first = c * HALF if first is None else first
        self.half = count // 2
        other, far_a, far_b, near_a, near_b = bufs
        self.other = other
        self.far_a, self.far_b = (far.at[pl.ds(lo // 2, self.half), :] for far in (far_a, far_b))
        self.near_a, self.near_b = (near.at[pl.ds(lo, count), :] for near in (near_a, near_b))
        source = ref if source is None else source
        self.sides = {}
        for d in (2, 1, -1, 0):
            row = self.row(d)
            self.sides[d] = net.copy(
                source.at[pl.ds(pl.multiple_of((1 - c) * HALF + row, 64), count), :],
                other.at[pl.ds(pl.multiple_of(row, 64), count), :],
                dc=1,
            )
        self.hops = (
            net.copy(self.block(2, 0, self.half), self.far_a, dt=1),
            net.copy(self.block(2, self.half, self.half), self.far_b, dt=-1),
            net.copy(self.block(1), self.near_a, dt=1),
            net.copy(self.block(-1), self.near_b, dt=-1),
        )

    def row(self, d, lo=0):
        return (self.t + d + 4) % 4 * 128 + self.lo + lo

    def block(self, d, lo=0, n=None):
        return self.ref.at[pl.ds(pl.multiple_of(self.first + self.row(d, lo), 16), n or self.count), :]

    def mine(self, d, lo=0):
        return self.read(self.ref, self.first + self.row(d, lo)), self.read(self.other, self.row(d, lo))

    @staticmethod
    def read(source, base):
        return lambda at: source[pl.ds(pl.multiple_of(base + at.start, 16), at.size), :]

    def keep(self, d, lo=0):
        base = self.first + self.row(d, lo)

        def store(at, value):
            self.ref[pl.ds(pl.multiple_of(base + at.start, 16), at.size), :] = value.astype(BF)

        return store

    def side(self, d):
        self.sides[d].start()

    def far(self):
        self.sides[2].wait_recv()
        for k in (0, 1):
            add_rows(self.mine(2, k * self.half), self.keep(2, k * self.half), self.half)
            self.hops[k].start()

    def near(self):
        for k, d, buf in ((0, 1, self.far_a), (1, -1, self.far_b)):
            lo, rest = k * self.half, (1 - k) * self.half
            self.sides[d].wait_recv()
            add_rows(self.mine(d, rest), self.keep(d, rest), self.half)
            self.hops[k].wait_recv()
            add_rows((*self.mine(d, lo), self.read(buf, 0)), self.keep(d, lo), self.half)
            self.hops[2 + k].start()

    def finish(self):
        self.sides[0].wait_recv()
        self.hops[2].wait_recv()
        self.hops[3].wait_recv()
        add_rows((*self.mine(0), self.read(self.near_a, 0), self.read(self.near_b, 0)), self.out, self.count)

    def sent(self):
        self.net.sent([*self.sides.values(), *self.hops])


SMEM = pl.BlockSpec(memory_space=pltpu.SMEM)


def call(kernel, outs, ins, scratch, copies, moves, cid):
    any_spec = pl.BlockSpec(memory_space=pl.ANY)
    vmem_spec = pl.BlockSpec(memory_space=pltpu.VMEM)
    return pl.pallas_call(
        kernel,
        out_shape=[shape for shape, _ in outs],
        in_specs=[SMEM if v is SMEM else vmem_spec if v else any_spec for _, v in ins],
        out_specs=[vmem_spec if v else any_spec for _, v in outs],
        scratch_shapes=list(scratch)
        + [
            pltpu.SemaphoreType.DMA((copies,)),
            pltpu.SemaphoreType.DMA((copies,)),
            pltpu.SemaphoreType.DMA((moves,)),
        ],
        compiler_params=pltpu.CompilerParams(
            collective_id=cid, has_side_effects=True, vmem_limit_bytes=61 * 2**20
        ),
    )(*[array for array, _ in ins])


def shape(*dims, kind=BF):
    return jax.ShapeDtypeStruct(dims, kind)


def dot(a, b, dims):
    return lax.dot_general(a, b, (dims, ((), ())), preferred_element_type=F32)


NN = ((1,), (0,))
NT = ((1,), (1,))
TN = ((0,), (0,))


def normal(rows, width):
    centred = rows - jnp.sum(rows, axis=-1, keepdims=True) * (1.0 / width)
    spread = jnp.sum(centred * centred, axis=-1, keepdims=True) * (1.0 / width)
    return centred, lax.rsqrt(spread + EPSILON)


def loop(count, step, body):
    def turn(i, carry):
        body(pl.ds(pl.multiple_of(i * step, step), step))
        return carry

    lax.fori_loop(0, count // step, turn, 0)


def pair(net, d):
    lo = (net.t + d + 4) % 4 * 128
    return tuple(pl.ds(pl.multiple_of(c * HALF + lo, 128), 128) for c in (1 - net.c, net.c))


def tile(net, ds, half):
    rows = []
    for d in ds:
        lo = (net.t + d + 4) % 4 * 128 + half * 64
        rows += [pl.ds(pl.multiple_of(c * HALF + lo, 64), 64) for c in (1 - net.c, net.c)]
    return tuple(rows)


def of(ref, rows, cols=slice(None)):
    if isinstance(rows, tuple):
        return jnp.concatenate([ref[at, cols] for at in rows], axis=0)
    return ref[rows, cols]


def put(ref, rows, value, cols=slice(None)):
    if isinstance(rows, tuple):
        for k, at in enumerate(rows):
            ref[at, cols] = value[k * at.size : (k + 1) * at.size].astype(ref.dtype)
    else:
        ref[rows, cols] = value.astype(ref.dtype)


def wide(weights, x, start, count):
    return jnp.concatenate([weights[x, z, start : start + count, :] for z in range(4)], axis=1)


def times_flipped(ref, rows, weights, start, count):
    total = None
    for x in range(4):
        part = dot(of(ref, rows, slice(x * 512, x * 512 + 512)), wide(weights, x, start, count), NT)
        total = part if total is None else total + part
    return total


def times_plain(terms, out, rows):
    for x in range(4):
        total = None
        for value, weights, start, count in terms:
            part = dot(value, wide(weights, x, start, count), NN)
            total = part if total is None else total + part
        put(out, rows, total, slice(x * 512, x * 512 + 512))


def weight_grad(cols, rows, out, start, count):
    for x in range(4):
        grad = dot(cols[...], rows[:, x * 512 : x * 512 + 512], TN).astype(BF)
        for z in range(4):
            out[x, z, start : start + count, :] = grad[:, z * 128 : z * 128 + 128]


def wait_all(copies):
    for copy in copies:
        copy.wait()


def masked(length, start, rows):
    place = lax.broadcasted_iota(jnp.int32, (rows, 1), 0) + start
    return jnp.where(place < length[0], 1.0, 0.0)


def mask_of(length, rows):
    return jnp.concatenate([masked(length, at.start, at.size) for at in rows], axis=0)


def decay_of(net):
    by_t = jnp.where(net.t % 2 == 1, 0.25, 1.0) * jnp.where(net.t // 2 == 1, 0.0625, 1.0)
    return jnp.where(net.c == 1, 0.5, 1.0) * by_t * (-32.0 / SEQ)


def fades(decay, start, rows):
    n = lax.broadcasted_iota(jnp.int32, (rows, HALF), 0) + start
    distance = (n - lax.broadcasted_iota(jnp.int32, (rows, HALF), 1)).astype(F32)
    fade = jnp.where(distance >= 0.0, jnp.exp(jnp.maximum(distance, 0.0) * decay), 0.0)
    ahead = lax.broadcasted_iota(jnp.int32, (rows, 1), 0) + start + 1
    return fade, jnp.exp(ahead.astype(F32) * decay)


def norm_back(source, gain, grad, out, lo=0, count=128):
    def body(i, total):
        at = pl.ds(pl.multiple_of(lo + i * 32, 32), 32)
        centred, dev = normal(source(at), D)
        normed = centred * dev
        back = grad(at)
        scaled = back * gain[...]
        mean = jnp.sum(scaled, axis=-1, keepdims=True) * (1.0 / D)
        along = jnp.sum(scaled * normed, axis=-1, keepdims=True) * (1.0 / D)
        out(at, dev * (scaled - mean - normed * along))
        return total + jnp.sum(back * normed, axis=0, keepdims=True)

    return lax.fori_loop(0, count // 32, body, jnp.zeros((1, D), F32))


def load_weights(net, source, weights, lo, to, rows):
    return [net.move(source.at[:, :, pl.ds(lo, rows), :], weights.at[:, :, pl.ds(to, rows), :])]


def forward_and_mlp_back(
    shards, inputs, carried_state, attn_gain, mlp_gain, cosine, sine, length, output_grad, cid
):
    def kernel(
        wq, wk, wv, ws, wo, wg, wu, wd, in_ref, carried_in, gain_one, gain_two, cos_in, sin_in, length, grad_ref,
        weights_out, one_out, q_out, k_out, v_out, mix_out, prior_out, hidden_out, down_out, grad_hidden, gain_out,
        sums_out, swish_out, ret_out, out_grad_out,
        weights, one, two, part, grads, packs, got, carried, cos_ref, sin_ref,
        q_ref, k_ref, v_ref, mix_ref, prior_ref, hidden_ref, s_ref, norm_ref, dev_ref, mixed_ref, gate_grad, up_grad,
        total, gh_ref,
        *rest,
    ):
        row_bufs, bufs, sems = rest[:5], rest[5:-3], rest[-3:]
        net = Net(*sems)
        c, t = net.c, net.t
        mid, act, swish_grad, ret_grad = one, v_ref, v_ref, gate_grad
        net.greet(XZ_HOPS + Y_HOPS)
        load_cos, load_sin = net.move(cos_in, cos_ref), net.move(sin_in, sin_ref)
        load_state = net.move(carried_in.at[0, c], carried)
        mine = pl.ds(pl.multiple_of(c * HALF, HALF), HALF)
        load_grad = net.move(grad_ref, grads.at[mine, :])
        own = c * 512 + t * 128
        stores, early = [], []

        def norm_rows(source, gain, rows_ref, lo, count):
            def body(rows):
                at = pl.ds(pl.multiple_of(lo + rows.start, rows.size), rows.size)
                centred, dev = normal(source[at, :].astype(F32), D)
                to = pl.ds(pl.multiple_of(own + at.start, 16), at.size)
                rows_ref[to, :] = (centred * dev * gain[...]).astype(BF)

            loop(count, 32, body)

        shard_refs = (wq, wk, wv, ws, wo, wg, wu, wd)

        def pack(first, last):
            spot = lax.broadcasted_iota(jnp.int32, (64, 128), 0) + c * 64
            place = jnp.where(spot == lax.broadcasted_iota(jnp.int32, (64, 128), 1), 1.0, 0.0).astype(BF)
            for k in range(first, last):
                flat = dot(shard_refs[k][...], place, TN).astype(BF)
                for core in range(2):
                    packs[core, STARTS[k] : STARTS[k] + SIZES[k], :] = flat[core * SIZES[k] : (core + 1) * SIZES[k]]

        def keep_weights(lo, hi):
            rows = pl.ds(lo, hi - lo)
            early.append(net.move(weights.at[:, :, rows, :], weights_out.at[:, :, rows, :]))

        w_qk, w_v, w_s, w_o, w_g, w_u, w_d = (
            gather_weights(net, weights, lo, hi)
            for lo, hi in ((0, 512), (512, 944), (944, 1376), (1376, 1808), (1808, 2240), (2240, 2672), (2672, 3104))
        )

        def join(swap, lo, hi):
            swap.wait_recv()
            step = 256 if hi == 512 else 432
            for at in range(lo, hi, step):
                weights[net.x, net.z, at : at + step, :] = packs[c, at : at + step, :] + got[at : at + step, :]

        swap_qk, swap_v, swap_s, swap_rest = (
            net.copy(packs.at[1 - c, pl.ds(lo, hi - lo), :], got.at[pl.ds(lo, hi - lo), :], dc=1)
            for lo, hi in ((0, 512), (512, 944), (944, 1376), (1376, ROWS))
        )
        grad_swap = net.copy(grad_ref, grads.at[mine, :], dc=1)

        y1 = gather_rows(net, one)
        decay = decay_of(net)

        def project_qk():
            wait_all([load_cos, load_sin])

            def body(at):
                cs, sn = cos_ref[at, :], sin_ref[at, :]
                for k, ref in ((0, q_ref), (1, k_ref)):
                    raw = times_flipped(one, at, weights, STARTS[k], SIZES[k])
                    former, latter = raw[:, :128], raw[:, 128:]
                    ref[at, :128] = (former * cs - latter * sn).astype(BF)
                    ref[at, 128:] = (former * sn + latter * cs).astype(BF)

            loop(SEQ, 256, body)
            early.append(net.move(one, one_out))
            stores.extend([net.move(q_ref, q_out), net.move(k_ref, k_out)])

        def project_v():
            def body(at):
                value = times_flipped(one, at, weights, STARTS[2], VDIM)
                v_ref[at, :] = (value * masked(length, at.start, at.size)).astype(BF)

            loop(SEQ, 256, body)
            early.append(net.move(v_ref, v_out))

        def mix():
            for stretch in range(2):

                def body(rows, stretch=stretch):
                    at = pl.ds(pl.multiple_of(stretch * HALF + rows.start, rows.size), rows.size)
                    fade, _ = fades(decay, rows.start, rows.size)
                    keys = k_ref[stretch * HALF : stretch * HALF + HALF, :]
                    mix_ref[at, :] = (dot(q_ref[at, :], keys, NT) * fade).astype(BF)

                loop(HALF, 128, body)
            stores.append(net.move(mix_ref, mix_out))

        def states():
            load_state.wait()
            before = carried[...].T
            prior_ref[0] = before.astype(BF)
            far = lax.broadcasted_iota(jnp.int32, (HALF, 1), 0).astype(F32)
            tail = jnp.exp((HALF - 1.0 - far) * decay)
            local_state = dot((k_ref[:HALF, :].astype(F32) * tail).astype(BF), v_ref[:HALF, :], TN)
            prior_ref[1] = (jnp.exp(HALF * decay) * before + local_state).astype(BF)
            stores.append(net.move(prior_ref, prior_out))

        def retain():
            for stretch in range(2):

                def body(rows, stretch=stretch):
                    at = pl.ds(pl.multiple_of(stretch * HALF + rows.start, rows.size), rows.size)
                    _, head = fades(decay, rows.start, rows.size)
                    values = v_ref[stretch * HALF : stretch * HALF + HALF, :]
                    retained = dot(mix_ref[at, :], values, NN) + dot(q_ref[at, :], prior_ref[stretch], NN) * head
                    centred, dev = normal(retained, VDIM)
                    norm_ref[at, :] = (centred * dev).astype(BF)
                    dev_ref[at, :] = dev

                loop(HALF, 128, body)

        def gate():
            def body(at):
                swish = times_flipped(one, at, weights, STARTS[3], VDIM)
                s_ref[at, :] = swish.astype(BF)
                share = masked(length, at.start, at.size) * (swish * jax.nn.sigmoid(swish))
                mixed_ref[at, :] = (share * norm_ref[at, :].astype(F32)).astype(BF)

            loop(SEQ, 256, body)
            wait_all(early)
            y1[6]()

        def hidden_rows(lo):
            def take(rows, value):
                at = pl.ds(pl.multiple_of(lo + rows.start, rows.size), rows.size)
                hidden_ref[at, :] = in_ref[at, :].astype(F32) + value

            return take

        def grad_rows(lo):
            def take(rows, value):
                total[pl.ds(pl.multiple_of(lo + rows.start, rows.size), rows.size), :] = value

            return take

        def out_rows(rows):
            times_plain(((of(mixed_ref, rows), weights, STARTS[4], VDIM),), part, rows)

        def mlp_rows(rows):
            gate = times_flipped(two, rows, weights, STARTS[5], VDIM)
            up = times_flipped(two, rows, weights, STARTS[6], VDIM)
            back = times_flipped(grads, rows, weights, STARTS[7], VDIM)
            share = 0.5 + 0.5 * lax.erf(gate * 0.7071067811865476)
            slope = share + gate * (0.3989422804014327 * jnp.exp(-0.5 * gate * gate))
            gelu = gate * share
            put(act, rows, gelu * up)
            back_gate, back_up = (back * up * slope).astype(BF), (back * gelu).astype(BF)
            put(gate_grad, rows, back_gate)
            put(up_grad, rows, back_up)
            times_plain(((back_gate, weights, STARTS[5], VDIM), (back_up, weights, STARTS[6], VDIM)), part, rows)

        def gate_back(rows):
            back = times_flipped(mid, rows, weights, STARTS[4], VDIM) * mask_of(length, rows)
            swish = of(s_ref, rows).astype(F32)
            unit = of(norm_ref, rows).astype(F32)
            share = jax.nn.sigmoid(swish)
            put(swish_grad, rows, back * unit * (share * (1.0 + swish * (1.0 - share))))
            back = back * (swish * share)
            mean = jnp.sum(back, axis=-1, keepdims=True) * (1.0 / VDIM)
            along = jnp.sum(back * unit, axis=-1, keepdims=True) * (1.0 / VDIM)
            put(ret_grad, rows, (back - mean - unit * along) * of(dev_ref, rows))

        def norm_two(lo):
            norm_rows(hidden_ref, gain_two, two, lo, 64)

        def norm_two_back(lo):
            def store(at, value):
                to = pl.ds(pl.multiple_of(own + at.start, 32), 32)
                whole = grads[to, :].astype(F32) + value
                gh_ref[at, :] = whole
                mid[to, :] = whole.astype(BF)

            some = norm_back(lambda at: hidden_ref[at, :], gain_two, lambda at: total[at, :], store, lo, 64)
            gain_out[...] = some if lo == 0 else gain_out[...] + some

        ra0, ra1 = (RowSums(net, part, row_bufs, hidden_rows(lo), lo, 64) for lo in (0, 64))
        rb0, rb1 = (RowSums(net, part, row_bufs, grad_rows(lo), lo, 64) for lo in (0, 64))
        yb0, yb1 = (gather_rows(net, two, lo, 64) for lo in (0, 64))
        yc0, yc1 = (gather_rows(net, mid, lo, 64) for lo in (0, 64))
        rows_a0, rows_b0, rows_a1, rows_b1 = (tile(net, ds, half) for half in (0, 1) for ds in ((2, 1), (-1, 0)))

        def keep(at, value):
            sums_out[pl.ds(at.start - STARTS[5], at.size), :] = value

        split = len(scatter_shapes(864))
        sum_gu = scatter_weights(net, weights, STARTS[5], STARTS[7], bufs[:split], keep)
        sum_d = scatter_weights(net, weights, STARTS[7], ROWS, bufs[split:], keep)

        def grad_of(gathered, cols, rows, k):
            gathered[5]()
            weight_grad(cols, rows, weights, STARTS[k], VDIM)

        def down_rows():
            for gathered in (w_qk, w_v, w_s):
                gathered[5]()

            def body(at):
                values = [dot(act[at, :], wide(weights, x, STARTS[7], VDIM), NN).astype(BF) for x in range(4)]
                for x in range(4):
                    for z in range(4):
                        weights[x, z, at, :] = values[x][:, z * 128 : z * 128 + 128]

            loop(SEQ, 256, body)
            for x in range(4):
                for z in range(4):
                    cols = pl.ds(x * 512 + z * 128, 128)
                    stores.append(net.move(weights.at[x, z, pl.ds(0, SEQ), :], down_out.at[:, cols]))

        def out_grad():
            grad_of(w_o, mixed_ref, mid, 4)
            stores.append(net.move(weights.at[:, :, pl.ds(STARTS[4], VDIM), :], out_grad_out))

        pack(4, 8)
        pack(0, 2)
        net.met()
        swap_qk.start()
        pack(2, 3)
        swap_rest.start()
        pack(3, 4)
        join(swap_qk, 0, 512)
        swap_v.start()
        w_qk[0]()
        norm_rows(in_ref, gain_one, one, 0, 128)
        join(swap_rest, 1376, ROWS)
        swap_s.start()
        w_o[0]()
        y1[0]()
        join(swap_s, 944, 1376)
        w_s[0]()
        w_qk[1]()
        w_o[1]()
        y1[2]()
        join(swap_v, 512, 944)
        w_v[0]()
        w_qk[2]()
        w_v[1]()
        w_v[2]()
        y1[1]()
        w_qk[3]()
        w_s[1]()
        y1[3]()
        w_s[2]()
        y1[4]()
        w_v[3]()
        w_qk[4]()
        keep_weights(0, 512)
        y1[5]()
        project_qk()
        w_o[2]()
        mix()
        w_v[4]()
        keep_weights(512, 944)
        project_v()
        w_s[3]()
        states()
        retain()
        w_o[3]()
        w_s[4]()
        keep_weights(944, 1376)
        gate()
        w_d[0]()
        w_o[4]()
        out_rows(rows_a0)
        ra0.side(2)
        out_rows(rows_b0)
        w_u[0]()
        ra0.far()
        ra0.side(1)
        out_rows(rows_a1)
        ra1.side(2)
        w_u[1]()
        w_d[1]()
        ra1.far()
        ra1.side(1)
        ra0.side(-1)
        ra0.near()
        w_g[0]()
        out_rows(rows_b1)
        w_u[2]()
        ra1.side(-1)
        w_g[1]()
        ra1.near()
        ra0.side(0)
        w_d[2]()
        w_u[3]()
        ra0.finish()
        norm_two(0)
        ra1.side(0)
        yb0[0]()
        ra1.finish()
        stores.append(net.move(hidden_ref, hidden_out))
        w_d[3]()
        w_g[2]()
        norm_two(64)
        grad_swap.start()
        yb1[0]()
        grad_swap.wait_recv()
        load_grad.wait()
        yb0[1]()
        w_d[4]()
        w_g[3]()
        yb0[2]()
        yb1[2]()
        yb0[3]()
        yb1[1]()
        yb0[4]()
        yb0[5]()
        yb1[3]()
        w_g[4]()
        w_u[4]()
        ra0.sent()
        ra1.sent()
        mlp_rows(rows_a0)
        yb1[4]()
        mlp_rows(rows_b0)
        rb0.side(2)
        yb1[5]()
        rb0.side(-1)
        rb0.side(1)
        mlp_rows(rows_a1)
        rb1.side(2)
        rb0.far()
        mlp_rows(rows_b1)
        rb1.far()
        rb1.side(-1)
        grad_of(w_u, up_grad, two, 6)
        rb0.near()
        rb1.side(0)
        grad_of(w_g, gate_grad, two, 5)
        rb0.side(0)
        rb1.side(1)
        sum_gu[0]()
        rb1.near()
        down_rows()
        sum_gu[1]()
        grad_of(w_d, act, grads, 7)
        rb0.finish()
        norm_two_back(0)
        yc0[0]()
        sum_d[0]()
        rb1.finish()
        norm_two_back(64)
        stores.append(net.move(gh_ref, grad_hidden))
        yc1[0]()
        sum_d[1]()
        yc0[1]()
        yc0[3]()
        sum_gu[2]()
        yc1[1]()
        yc1[2]()
        sum_d[2]()
        yc0[2]()
        yc0[4]()
        sum_gu[3]()
        yc0[5]()
        yc1[3]()
        gate_back(rows_a0)
        yc1[4]()
        gate_back(rows_b0)
        sum_d[3]()
        yc1[5]()
        gate_back(rows_a1)
        gate_back(rows_b1)
        stores += [net.move(ret_grad, ret_out), net.move(swish_grad, swish_out)]
        out_grad()
        sum_gu[4]()
        sum_d[4]()
        net.flush()
        wait_all(stores)

    cols = pltpu.VMEM((SEQ, VDIM), BF)
    rows = pltpu.VMEM((SEQ, D), BF)
    keys = pltpu.VMEM((SEQ, KDIM), BF)
    own = pltpu.VMEM((128, D), F32)
    return call(
        kernel,
        [
            (shape(4, 4, STARTS[4], 128), False),
            (shape(SEQ, D), False),
            (shape(SEQ, KDIM), False),
            (shape(SEQ, KDIM), False),
            (shape(SEQ, VDIM), False),
            (shape(SEQ, HALF), False),
            (shape(2, KDIM, VDIM), False),
            (shape(128, D, kind=F32), False),
            (shape(SEQ, D), False),
            (shape(128, D, kind=F32), False),
            (shape(1, D, kind=F32), True),
            (shape(1296, 128, kind=F32), True),
            (shape(SEQ, VDIM), False),
            (shape(SEQ, VDIM), False),
            (shape(4, 4, 432, 128), False),
        ],
        [(shard, True) for shard in shards]
        + [
            (inputs, True),
            (carried_state, False),
            (attn_gain, True),
            (mlp_gain, True),
            (cosine, False),
            (sine, False),
            (length, SMEM),
            (output_grad, False),
        ],
        [
            pltpu.VMEM((4, 4, ROWS, 128), BF),
            rows,
            rows,
            rows,
            rows,
            pltpu.VMEM((2, ROWS, 128), BF),
            pltpu.VMEM((ROWS, 128), BF),
            pltpu.VMEM((VDIM, KDIM), F32),
            pltpu.VMEM((SEQ, 128), F32),
            pltpu.VMEM((SEQ, 128), F32),
            keys,
            keys,
            cols,
            pltpu.VMEM((SEQ, HALF), BF),
            pltpu.VMEM((2, KDIM, VDIM), BF),
            own,
            cols,
            cols,
            pltpu.VMEM((SEQ, 1), F32),
            cols,
            cols,
            cols,
            own,
            own,
        ]
        + ROW_BUFS
        + scatter_shapes(864)
        + scatter_shapes(432),
        228,
        48,
        cid,
    )


SPREAD_HOPS = tuple(dict(dt=dt, dc=dc) for dt in (0, 1, 2, -1) for dc in (0, 1) if (dt, dc) != (0, 0))
FAR_HOPS = (dict(dx=2), dict(dz=2))


def retention_back(
    weights_all, rows_one, down_part, q, k, v, mix, prior, swish_grad, ret_grad, out_grad, hidden, grad_hidden, inputs,
    attn_gain, cosine, sine, length, mlp_gain_part, sums_mlp, cid
):

    def kernel(
        w_ref, one_in, down_in, q_in, k_in, v_in, mix_in, prior_in, swish_in, ret_in, out_grad_in, hidden_in, gh_in,
        in_ref, gain, cos_in, sin_in, length, mlp_gain_ref, sums_mlp_ref,
        out_out, in_grad_out, gains_out, sums_all, sums_got, mlp_got,
        out_ref, in_grad, sums_out, weights, sums_ref, one, part, down, q_ref, k_ref, v_ref, mix_ref, prior_ref, swish_grad, ret_grad, hidden_ref,
        gh_ref, cos_ref, sin_ref, q_grad, k_grad, v_grad, score_grad, total, gain_sum, by_group, by_x, by_z,
        *rest,
    ):
        first_bufs, second_bufs, bufs, sems = rest[:5], rest[5:10], rest[10:-3], rest[-3:]
        net = Net(*sems)
        c, t = net.c, net.t
        net.greet(XZ_HOPS + FAR_HOPS + SPREAD_HOPS)

        def moves(*pairs):
            return [net.move(a, b) for a, b in pairs]

        load_out = moves((out_grad_in, sums_ref.at[:, :, pl.ds(0, 432), :]))
        load_score = moves(
            (ret_in, ret_grad), (v_in, v_ref), (k_in, k_ref), (prior_in, prior_ref), (cos_in, cos_ref), (sin_in, sin_ref)
        )
        load_kv = moves((q_in, q_ref), (mix_in, mix_ref))
        load_w = moves((swish_in, swish_grad))
        for lo, to, n in ((STARTS[3], 0, 432), (STARTS[2], 432, 432), (0, 864, 512)):
            load_w += load_weights(net, w_ref, weights, lo, to, n)
        load_one = moves((one_in, one))
        load_down = moves((down_in.at[pl.ds(pl.multiple_of(c * HALF, HALF), HALF), :], down))
        load_last = moves((hidden_in, hidden_ref), (gh_in, gh_ref))
        stores = []
        decay = decay_of(net)

        def turn_back(at, raw):
            cs, sn = cos_ref[at, :], sin_ref[at, :]
            former, latter = raw[:, :128], raw[:, 128:]
            return (former * cs + latter * sn).astype(BF), (latter * cs - former * sn).astype(BF)

        def score():
            wait_all(load_score)
            for stretch in range(2):
                keys = slice(stretch * HALF, stretch * HALF + HALF)

                def body(rows, stretch=stretch, keys=keys):
                    at = pl.ds(pl.multiple_of(stretch * HALF + rows.start, rows.size), rows.size)
                    fade, head = fades(decay, rows.start, rows.size)
                    scores = (dot(ret_grad[at, :], v_ref[keys, :], NT) * fade).astype(BF)
                    score_grad[at, :] = scores
                    raw = dot(scores, k_ref[keys, :], NN) + dot(ret_grad[at, :], prior_ref[stretch], NT) * head
                    q_grad[at, :128], q_grad[at, 128:] = turn_back(at, raw)

                loop(HALF, 128, body)

        def keys_and_values():
            wait_all(load_kv)
            far = lax.broadcasted_iota(jnp.int32, (HALF, 1), 0).astype(F32)
            tail = jnp.exp((HALF - 1.0 - far) * decay)
            ahead = (q_ref[HALF:, :].astype(F32) * jnp.exp((far + 1.0) * decay)).astype(BF)
            grad_local = dot(ahead, ret_grad[HALF:, :], TN).astype(BF)
            for stretch in range(2):
                keys = slice(stretch * HALF, stretch * HALF + HALF)
                raw = dot(score_grad[keys, :], q_ref[keys, :], TN)
                value = dot(mix_ref[keys, :], ret_grad[keys, :], TN)
                if stretch == 0:
                    raw = raw + dot(v_ref[keys, :], grad_local, NT) * tail
                    value = value + dot(k_ref[keys, :], grad_local, NN) * tail
                k_grad[keys, :128], k_grad[keys, 128:] = turn_back(keys, raw)
                v_grad[keys, :] = (value * masked(length, stretch * HALF, HALF)).astype(BF)

        def back_rows(rows):
            terms = (
                (of(swish_grad, rows), weights, 0, 432),
                (of(v_grad, rows), weights, 432, 432),
                (of(q_grad, rows), weights, 864, 256),
                (of(k_grad, rows), weights, 1120, 256),
            )
            times_plain(terms, part, rows)

        def gain_rows(rows):
            for x in range(4):
                at = slice(x * 512, x * 512 + 512)
                along = of(part, rows, at).astype(F32) * of(one, rows, at).astype(F32)
                gain_sum[:, at] = gain_sum[:, at] + jnp.sum(along, axis=0, keepdims=True)

        def output_rows(lo):
            def take(rows, value):
                at = pl.ds(pl.multiple_of(lo + rows.start, rows.size), rows.size)
                out_ref[at, :] = (hidden_ref[at, :] + value).astype(BF)

            return take

        def grad_rows(lo):
            def take(rows, value):
                total[pl.ds(pl.multiple_of(lo + rows.start, rows.size), rows.size), :] = value

            return take

        def norm_one_back(lo):
            def store(at, value):
                in_grad[at, :] = gh_ref[at, :] + value

            norm_back(lambda at: in_ref[at, :].astype(F32), gain, lambda at: total[at, :], store, lo, 64)

        gain_sum[...] = jnp.zeros_like(gain_sum)
        ra0, ra1 = (RowSums(net, down, first_bufs, output_rows(lo), lo, 64, down_in, 0) for lo in (0, 64))
        rb0, rb1 = (RowSums(net, part, second_bufs, grad_rows(lo), lo, 64) for lo in (0, 64))
        rows_a0, rows_b0, rows_a1, rows_b1 = (tile(net, ds, half) for half in (0, 1) for ds in ((2, 1), (-1, 0)))

        def keep(at, value):
            sums_out[at, :] = value

        sums, at = [], 0
        for lo, hi in ((0, 432), (432, 864), (864, 1296), (1296, 1808)):
            n = len(scatter_shapes(hi - lo))
            sums.append(scatter_weights(net, sums_ref, lo, hi, bufs[at : at + n], keep))
            at += n
        sum_o, sum_s, sum_v, sum_qk = sums

        def keys_grad():
            weight_grad(q_grad, one, sums_ref, 1296, 256)
            weight_grad(k_grad, one, sums_ref, 1552, 256)

        def spread(ref, place, hops):
            return [net.copy(ref.at[place], ref.at[place], **hop) for hop in hops]

        def gathered(ref, copies):
            for copy in copies:
                copy.wait_recv()
            value = ref[0]
            for k in range(1, ref.shape[0]):
                value = value + ref[k]
            return value

        def begin():
            by_group[t * 2 + c, 0:1, :] = gain_sum[...] / gain[...]
            by_group[t * 2 + c, 1:2, :] = mlp_gain_ref[...]
            for copy in in_group:
                copy.start()

        def along_x():
            by_x[net.x] = gathered(by_group, in_group)
            for copy in in_x:
                copy.start()

        def along_z():
            by_z[net.z] = gathered(by_x, in_x)
            for copy in in_z:
                copy.start()

        def all_gains():
            gains_out[...] = gathered(by_z, in_z)

        in_group = spread(by_group, t * 2 + c, SPREAD_HOPS)
        in_x = spread(by_x, net.x, (dict(dx=1), dict(dx=-1), dict(dx=2)))
        in_z = spread(by_z, net.z, (dict(dz=1), dict(dz=-1), dict(dz=2)))
        def keep_sums(lo, n):
            stores.append(net.move(sums_out.at[pl.ds(lo, n), :], sums_all.at[pl.ds(lo, n), :]))

        swap_mlp = net.copy(sums_mlp_ref, mlp_got, dc=1)
        swap_o, swap_s, swap_v, swap_qk = (
            net.copy(sums_out.at[pl.ds(lo, n), :], sums_got.at[pl.ds(lo, n), :], dc=1)
            for lo, n in ((0, 432), (432, 432), (864, 432), (1296, 512))
        )
        net.met()
        ra0.side(2)
        ra0.side(1)
        wait_all(load_out)
        sum_o[0]()
        score()
        sum_o[1]()
        keys_and_values()
        wait_all(load_w)
        back_rows(rows_a0)
        ra0.side(-1)
        ra1.side(2)
        wait_all(load_down)
        ra0.far()
        wait_all(load_one)
        gain_rows(rows_a0)
        weight_grad(v_grad, one, sums_ref, 864, 432)
        rb0.side(2)
        sum_v[0]()
        ra1.far()
        keys_grad()
        rb0.far()
        sum_qk[0]()
        rb0.side(1)
        back_rows(rows_b0)
        ra0.near()
        sum_v[1]()
        ra1.side(0)
        sum_o[2]()
        gain_rows(rows_b0)
        back_rows(rows_a1)
        swap_mlp.start()
        rb0.side(-1)
        back_rows(rows_b1)
        rb0.side(0)
        sum_qk[1]()
        rb1.side(2)
        gain_rows(rows_b1)
        ra1.side(-1)
        gain_rows(rows_a1)
        rb0.near()
        ra1.side(1)
        weight_grad(swish_grad, one, sums_ref, 432, 432)
        rb1.side(-1)
        sum_s[0]()
        sum_v[2]()
        ra1.near()
        rb1.side(1)
        rb1.far()
        begin()
        sum_v[3]()
        rb1.side(0)
        sum_s[1]()
        along_x()
        sum_v[4]()
        keep_sums(864, 432)
        ra0.side(0)
        wait_all(load_last)
        ra0.finish()
        swap_v.start()
        sum_qk[2]()
        rb1.near()
        sum_o[3]()
        sum_s[2]()
        sum_qk[3]()
        along_z()
        sum_s[3]()
        sum_o[4]()
        keep_sums(0, 432)
        rb0.finish()
        sum_qk[4]()
        keep_sums(1296, 512)
        swap_qk.start()
        swap_o.start()
        ra1.finish()
        stores.append(net.move(out_ref, out_out))
        norm_one_back(0)
        sum_s[4]()
        keep_sums(432, 432)
        swap_s.start()
        all_gains()
        rb1.finish()
        norm_one_back(64)
        stores.append(net.move(in_grad, in_grad_out))
        for swap in (swap_mlp, swap_o, swap_s, swap_v, swap_qk):
            swap.wait_recv()
        net.flush()
        wait_all(stores)

    cols = pltpu.VMEM((SEQ, VDIM), BF)
    keys = pltpu.VMEM((SEQ, KDIM), BF)
    rows = pltpu.VMEM((SEQ, D), BF)
    own = pltpu.VMEM((128, D), F32)
    return call(
        kernel,
        [
            (shape(128, D), False),
            (shape(128, D, kind=F32), False),
            (shape(2, D, kind=F32), True),
            (shape(1808, 128, kind=F32), False),
            (shape(1808, 128, kind=F32), False),
            (shape(1296, 128, kind=F32), False),
        ],
        [
            (weights_all, False),
            (rows_one, False),
            (down_part, False),
            (q, False),
            (k, False),
            (v, False),
            (mix, False),
            (prior, False),
            (swish_grad, False),
            (ret_grad, False),
            (out_grad, False),
            (hidden, False),
            (grad_hidden, False),
            (inputs, True),
            (attn_gain, True),
            (cosine, False),
            (sine, False),
            (length, SMEM),
            (mlp_gain_part, True),
            (sums_mlp, False),
        ],
        [
            pltpu.VMEM((128, D), BF),
            own,
            pltpu.VMEM((1808, 128), F32),
            pltpu.VMEM((4, 4, 1376, 128), BF),
            pltpu.VMEM((4, 4, 1808, 128), BF),
            rows,
            rows,
            pltpu.VMEM((HALF, D), BF),
            keys,
            keys,
            cols,
            pltpu.VMEM((SEQ, HALF), BF),
            pltpu.VMEM((2, KDIM, VDIM), BF),
            cols,
            cols,
            own,
            own,
            pltpu.VMEM((SEQ, 128), F32),
            pltpu.VMEM((SEQ, 128), F32),
            keys,
            keys,
            cols,
            pltpu.VMEM((SEQ, HALF), BF),
            own,
            pltpu.VMEM((1, D), F32),
            pltpu.VMEM((8, 2, D), F32),
            pltpu.VMEM((4, 2, D), F32),
            pltpu.VMEM((4, 2, D), F32),
        ]
        + ROW_BUFS
        + ROW_BUFS
        + scatter_shapes(432) * 3
        + scatter_shapes(512),
        120,
        48,
        cid,
    )


def hand_out(outputs, input_grad, gains, sums, got, sums_mlp, got_mlp):
    places = (
        (0, 1296, 256), (0, 1552, 256), (0, 864, 432), (0, 432, 432), (0, 0, 432), (1, 0, 432), (1, 432, 432),
        (1, 864, 432),
    )

    def kernel(*refs):
        n = len(outs)
        ins, results, held, made, loads, stores = (
            refs[:7], refs[7 : 7 + n], refs[7 + n : 14 + n], refs[14 + n : 14 + 2 * n], refs[-2], refs[-1]
        )
        arrive = [pltpu.make_async_copy(ins[k], held[k], loads.at[k]) for k in range(7)]
        leave = [pltpu.make_async_copy(made[k], results[k], stores.at[k]) for k in range(n)]
        for k in (5, 6, 3, 4, 1, 0, 2):
            arrive[k].start()
        first_core = lax.axis_index("ctx") == 0
        wait_all([arrive[5], arrive[6]])
        waited = False
        for k in (5, 6, 7, 4, 3, 2, 0, 1):
            which, lo, rows = places[k]
            if which == 0 and not waited:
                wait_all([arrive[3], arrive[4]])
                waited = True
            a, b = (held[at][lo : lo + rows, :] for at in ((3, 4), (5, 6))[which])
            both = jnp.concatenate([jnp.where(first_core, a, b), jnp.where(first_core, b, a)], axis=0).T
            made[4 + k][...] = jnp.where(first_core, both[:64], both[64:])
            leave[4 + k].start()
        wait_all([arrive[0], arrive[1], arrive[2]])
        made[1][...] = held[1][...]
        leave[1].start()
        made[0][...] = held[0][...]
        made[2][...] = held[2][0:1, :]
        made[3][...] = held[2][1:2, :]
        for k in (0, 2, 3):
            leave[k].start()
        wait_all(leave)

    outs = [shape(128, D), shape(128, D, kind=F32), shape(1, D, kind=F32), shape(1, D, kind=F32)]
    for _, _, n in places:
        outs.append(shape(64, 2 * n, kind=F32))
    ins = (outputs, input_grad, gains, sums, got, sums_mlp, got_mlp)
    spec = pl.BlockSpec(memory_space=pl.ANY)
    return pl.pallas_call(
        kernel,
        out_shape=outs,
        in_specs=[spec] * len(ins),
        out_specs=[spec] * len(outs),
        scratch_shapes=[pltpu.VMEM(a.shape, a.dtype) for a in (*ins, *outs)]
        + [pltpu.SemaphoreType.DMA((len(ins),)), pltpu.SemaphoreType.DMA((len(outs),))],
        compiler_params=pltpu.CompilerParams(vmem_limit_bytes=61 * 2**20),
    )(*ins)


def turning_tables():
    frequency = 10000.0 ** (-np.arange(128) / 128.0)
    angles = np.arange(SEQ)[:, None] * frequency[None, :]
    return jnp.asarray(np.cos(angles), F32), jnp.asarray(np.sin(angles), F32)


def on_device(
    inputs,
    seq_lengths,
    carried_state,
    attn_gain,
    query_weight,
    key_weight,
    value_weight,
    swish_weight,
    out_weight,
    mlp_gain,
    gate_weight,
    up_weight,
    down_weight,
    output_grad,
):
    cosine, sine = turning_tables()
    gains = attn_gain[None, :], mlp_gain[None, :]
    shards = (
        query_weight, key_weight, value_weight, swish_weight, out_weight.T, gate_weight, up_weight, down_weight.T
    )
    (
        weights, rows_one, q, k, v, mix, prior, hidden, down_part, grad_hidden, mlp_gain_part, sums_mlp, swish_grad,
        ret_grad, out_grad
    ) = forward_and_mlp_back(
        shards, inputs, carried_state.transpose(0, 1, 3, 2), *gains, cosine, sine, seq_lengths, output_grad, 1
    )
    outputs, input_grad, gain_grads, sums, got_sums, got_mlp = retention_back(
        weights, rows_one, down_part, q, k, v, mix, prior, swish_grad, ret_grad, out_grad, hidden, grad_hidden, inputs,
        gains[0], cosine, sine, seq_lengths, mlp_gain_part, sums_mlp, 2
    )
    outputs, input_grad, first, second, *grads = hand_out(
        outputs, input_grad, gain_grads, sums, got_sums, sums_mlp, got_mlp
    )
    return (
        outputs,
        input_grad,
        first[0],
        grads[0],
        grads[1],
        grads[2],
        grads[3],
        grads[4].T,
        second[0],
        grads[5],
        grads[6],
        grads[7].T,
    )


def solution(mesh):
    placed = (
        P(("fsdp", "ctx", "tp"), None),
        P("fsdp"),
        P("fsdp", "tp", None, None),
        P(),
        P(("fsdp", "ctx"), "tp"),
        P(("fsdp", "ctx"), "tp"),
        P(("fsdp", "ctx"), "tp"),
        P(("fsdp", "ctx"), "tp"),
        P("tp", ("fsdp", "ctx")),
        P(),
        P(("fsdp", "ctx"), "tp"),
        P(("fsdp", "ctx"), "tp"),
        P("tp", ("fsdp", "ctx")),
        P(("fsdp", "ctx"), None),
    )
    return jax.shard_map(
        on_device,
        mesh=mesh,
        in_specs=placed,
        out_specs=(
            P(("fsdp", "ctx", "tp"), None),
            P(("fsdp", "ctx", "tp"), None),
            P(),
            P(("fsdp", "ctx"), "tp"),
            P(("fsdp", "ctx"), "tp"),
            P(("fsdp", "ctx"), "tp"),
            P(("fsdp", "ctx"), "tp"),
            P("tp", ("fsdp", "ctx")),
            P(),
            P(("fsdp", "ctx"), "tp"),
            P(("fsdp", "ctx"), "tp"),
            P("tp", ("fsdp", "ctx")),
        ),
        check_vma=False,
    )
```

```python
import jax
import jax.numpy as jnp
import numpy as np
from jax import lax
from jax.experimental import pallas as pl
from jax.experimental.pallas import tpu as pltpu
from jax.sharding import PartitionSpec as P

D = 2048
KDIM = 256
VDIM = 432
SEQ = 1024
HALF = 512
SIZES = (256, 256, 432, 432, 432, 432, 432, 432)
STARTS = (0, 256, 512, 944, 1376, 1808, 2240, 2672)
ROWS = 3104
EPSILON = 1e-05
MESH = pl.DeviceIdType.MESH
BF = jnp.bfloat16
F32 = jnp.float32


def even(rows):
    return rows // 32 * 16


class Net:
    def __init__(self, send, recv, local):
        group = lax.axis_index("fsdp")
        self.c = lax.axis_index("ctx")
        self.t = lax.axis_index("tp")
        self.x = group // 4
        self.z = group % 4
        self.send, self.recv, self.local = send, recv, local
        self.copies, self.gone, self.moves = [], [], 0

    def dev(self, dx=0, dz=0, dt=0, dc=0):
        x, z, t = ((at + d + 4) % 4 if d else at for at, d in ((self.x, dx), (self.z, dz), (self.t, dt)))
        c = 1 - self.c if dc else self.c
        return (x * 4 + z, c, t)

    def greet(self, hops):
        self.greeted = len(hops)
        for hop in hops:
            pl.semaphore_signal(
                pltpu.get_barrier_semaphore(), inc=1, device_id=self.dev(**hop), device_id_type=MESH
            )

    def met(self):
        pl.semaphore_wait(pltpu.get_barrier_semaphore(), self.greeted)

    def copy(self, src, dst, **hop):
        at = len(self.copies)
        self.copies.append(
            pltpu.make_async_remote_copy(
                src_ref=src,
                dst_ref=dst,
                send_sem=self.send.at[at],
                recv_sem=self.recv.at[at],
                device_id=self.dev(**hop),
                device_id_type=MESH,
            )
        )
        return self.copies[-1]

    def move(self, src, dst):
        copy = pltpu.make_async_copy(src, dst, self.local.at[self.moves])
        self.moves += 1
        copy.start()
        return copy

    def sent(self, copies):
        for copy in copies:
            if not any(copy is other for other in self.gone):
                copy.wait_send()
                self.gone.append(copy)

    def flush(self):
        self.sent(self.copies)


XZ_HOPS = (dict(dx=1), dict(dx=-1), dict(dz=1), dict(dz=-1))
Y_HOPS = (dict(dt=1), dict(dt=-1), dict(dc=1))


def ring_views(net, axis):
    x, z = net.x, net.z
    along_x = lambda ref, d, rows: ref.at[(x + d + 4) % 4, z, rows, :]
    along_z = lambda ref, d, rows: ref.at[x, (z + d + 4) % 4, rows, :]
    all_z = lambda ref, d, rows: ref.at[(x + d + 4) % 4, :, rows, :]
    all_x = lambda ref, d, rows: ref.at[:, (z + d + 4) % 4, rows, :]
    if axis == "x":
        return along_x, all_x, "dx", "dz"
    return along_z, all_z, "dz", "dx"


def gather_weights(net, ref, start, stop):
    cut = start + even(stop - start)
    plans = []
    for axis, lo, hi in (("z", start, cut), ("x", cut, stop)):
        mid = lo + even(hi - lo)
        whole, head, tail = pl.ds(lo, hi - lo), pl.ds(lo, mid - lo), pl.ds(mid, hi - mid)
        first, second, hop_a, hop_b = ring_views(net, axis)
        plan = []
        for view, hop in ((first, hop_a), (second, hop_b)):
            mine = view(ref, 0, whole)
            plan.append(
                (
                    net.copy(mine, mine, **{hop: 1}),
                    net.copy(mine, mine, **{hop: -1}),
                    net.copy(view(ref, -1, head), view(ref, -1, head), **{hop: 1}),
                    net.copy(view(ref, 1, tail), view(ref, 1, tail), **{hop: -1}),
                )
            )
        plans.append(plan)

    def near(phase):
        for plan in plans:
            plan[phase][0].start()
            plan[phase][1].start()

    def far(phase):
        for k in (0, 1):
            for plan in plans:
                plan[phase][k].wait_recv()
                plan[phase][2 + k].start()

    def land(phase):
        for plan in plans:
            plan[phase][2].wait_recv()
            plan[phase][3].wait_recv()

    return [
        lambda: near(0),
        lambda: far(0),
        lambda: (land(0), near(1)),
        lambda: far(1),
        lambda: land(1),
        lambda: net.sent([copy for plan in plans for phase in plan for copy in phase]),
    ]


def add_rows(refs, out, count):
    step = 16

    def body(i, carry):
        at = pl.ds(pl.multiple_of(i * step, step), step)
        total = refs[0](at).astype(F32)
        for ref in refs[1:]:
            total = total + ref(at).astype(F32)
        out(at, total)
        return carry

    lax.fori_loop(0, count // step, body, 0)


def scatter_shapes(rows):
    shapes = []
    cut = even(rows)
    for axis, count in (("z", cut), ("x", rows - cut)):
        head = even(count)
        for pieces in ((4,), ()):
            for n in (head, count - head, count, count):
                shapes.append(pltpu.VMEM((*pieces, n, 128), BF))
    return shapes


def scatter_weights(net, ref, start, stop, bufs, out):
    cut = start + even(stop - start)
    plans = []
    bufs = list(bufs)
    for axis, lo, hi in (("z", start, cut), ("x", cut, stop)):
        mid = lo + even(hi - lo)
        parts = (lo, mid - lo), (mid, hi - mid), (lo, hi - lo)
        head, tail, whole = (pl.ds(*part) for part in parts)
        plan = []
        _, wide, hop_b, hop_a = ring_views(net, "x" if axis == "z" else "z")
        thin = ring_views(net, "z" if axis == "x" else "x")[0]
        for view, hop in ((wide, hop_a), (thin, hop_b)):
            fa, fb, ma, mb = bufs[:4]
            bufs = bufs[4:]
            plan.append(
                dict(
                    view=view,
                    bufs=(fa, fb, ma, mb),
                    copies=(
                        net.copy(view(ref, 2, head), fa, **{hop: 1}),
                        net.copy(view(ref, 2, tail), fb, **{hop: -1}),
                        net.copy(view(ref, 1, whole), ma, **{hop: 1}),
                        net.copy(view(ref, -1, whole), mb, **{hop: -1}),
                    ),
                )
            )
        plans.append((plan, parts))

    def at_rows(view, d, lo):
        def read(at):
            return view(ref, d, pl.ds(lo + at.start, at.size))[...]

        def write(at, value):
            view(ref, d, pl.ds(lo + at.start, at.size))[...] = value.astype(BF)

        return read, write

    def buf_rows(buf):
        if len(buf.shape) == 3:
            return lambda at: buf[:, at, :]
        return lambda at: buf[at, :]

    def far(phase):
        for plan, _ in plans:
            plan[phase]["copies"][0].start()
            plan[phase]["copies"][1].start()

    def near(phase):
        for k, d in ((0, 1), (1, -1)):
            for plan, parts in plans:
                step = plan[phase]
                lo, count = parts[k]
                step["copies"][k].wait_recv()
                read, write = at_rows(step["view"], d, lo)
                add_rows((read, buf_rows(step["bufs"][k])), write, count)
                step["copies"][2 + k].start()

    def total(phase, last):
        for plan, parts in plans:
            step = plan[phase]
            lo, count = parts[2]
            step["copies"][2].wait_recv()
            step["copies"][3].wait_recv()
            read, write = at_rows(step["view"], 0, lo)
            if last:
                write = lambda at, value, lo=lo: out(pl.ds(lo + at.start, at.size), value)
            add_rows((read, buf_rows(step["bufs"][2]), buf_rows(step["bufs"][3])), write, count)

    return [
        lambda: far(0),
        lambda: near(0),
        lambda: (total(0, False), far(1)),
        lambda: near(1),
        lambda: total(1, True),
    ]


def gather_rows(net, ref, first=0, count=128):
    def block(c, t, lo=0, n=count):
        return ref.at[pl.ds(pl.multiple_of(c * 512 + t * 128 + first + lo, 16), n), :]

    c, t = net.c, net.t
    half = count // 2
    before, after, across = (t + 3) % 4, (t + 1) % 4, (t + 2) % 4
    own = block(c, t)
    up = net.copy(own, own, dt=1)
    down = net.copy(own, own, dt=-1)
    side = net.copy(own, own, dc=1)
    fore = net.copy(block(c, before, 0, half), block(c, before, 0, half), dt=1)
    back = net.copy(block(c, after, half, half), block(c, after, half, half), dt=-1)
    over = [
        net.copy(block(c, before), block(c, before), dc=1),
        net.copy(block(c, after), block(c, after), dc=1),
        net.copy(block(c, across, 0, half), block(c, across, 0, half), dc=1),
        net.copy(block(c, across, half, half), block(c, across, half, half), dc=1),
    ]

    def start():
        up.start()
        down.start()
        side.start()

    def forward():
        up.wait_recv()
        fore.start()
        over[0].start()
        down.wait_recv()
        back.start()
        over[1].start()

    def beside():
        side.wait_recv()

    def near():
        over[0].wait_recv()
        over[1].wait_recv()

    def far():
        fore.wait_recv()
        over[2].start()
        back.wait_recv()
        over[3].start()

    def last():
        over[2].wait_recv()
        over[3].wait_recv()

    def sent():
        net.sent((up, down, side, fore, back, *over))

    return start, forward, beside, near, far, last, sent


ROW_BUFS = [
    pltpu.VMEM((512, D), BF),
    pltpu.VMEM((64, D), BF),
    pltpu.VMEM((64, D), BF),
    pltpu.VMEM((128, D), BF),
    pltpu.VMEM((128, D), BF),
]


class RowSums:
    def __init__(self, net, ref, bufs, out, lo=0, count=128, source=None, first=None):
        c, t = net.c, net.t
        self.net, self.t, self.ref, self.out, self.lo, self.count = net, t, ref, out, lo, count
        self.first = c * HALF if first is None else first
        self.half = count // 2
        other, far_a, far_b, near_a, near_b = bufs
        self.other = other
        self.far_a, self.far_b = (far.at[pl.ds(lo // 2, self.half), :] for far in (far_a, far_b))
        self.near_a, self.near_b = (near.at[pl.ds(lo, count), :] for near in (near_a, near_b))
        source = ref if source is None else source
        self.sides = {}
        for d in (2, 1, -1, 0):
            row = self.row(d)
            self.sides[d] = net.copy(
                source.at[pl.ds(pl.multiple_of((1 - c) * HALF + row, 64), count), :],
                other.at[pl.ds(pl.multiple_of(row, 64), count), :],
                dc=1,
            )
        self.hops = (
            net.copy(self.block(2, 0, self.half), self.far_a, dt=1),
            net.copy(self.block(2, self.half, self.half), self.far_b, dt=-1),
            net.copy(self.block(1), self.near_a, dt=1),
            net.copy(self.block(-1), self.near_b, dt=-1),
        )

    def row(self, d, lo=0):
        return (self.t + d + 4) % 4 * 128 + self.lo + lo

    def block(self, d, lo=0, n=None):
        return self.ref.at[pl.ds(pl.multiple_of(self.first + self.row(d, lo), 16), n or self.count), :]

    def mine(self, d, lo=0):
        return self.read(self.ref, self.first + self.row(d, lo)), self.read(self.other, self.row(d, lo))

    @staticmethod
    def read(source, base):
        return lambda at: source[pl.ds(pl.multiple_of(base + at.start, 16), at.size), :]

    def keep(self, d, lo=0):
        base = self.first + self.row(d, lo)

        def store(at, value):
            self.ref[pl.ds(pl.multiple_of(base + at.start, 16), at.size), :] = value.astype(BF)

        return store

    def side(self, d):
        self.sides[d].start()

    def far(self):
        self.sides[2].wait_recv()
        for k in (0, 1):
            add_rows(self.mine(2, k * self.half), self.keep(2, k * self.half), self.half)
            self.hops[k].start()

    def near(self):
        for k, d, buf in ((0, 1, self.far_a), (1, -1, self.far_b)):
            lo, rest = k * self.half, (1 - k) * self.half
            self.sides[d].wait_recv()
            add_rows(self.mine(d, rest), self.keep(d, rest), self.half)
            self.hops[k].wait_recv()
            add_rows((*self.mine(d, lo), self.read(buf, 0)), self.keep(d, lo), self.half)
            self.hops[2 + k].start()

    def finish(self):
        self.sides[0].wait_recv()
        self.hops[2].wait_recv()
        self.hops[3].wait_recv()
        add_rows((*self.mine(0), self.read(self.near_a, 0), self.read(self.near_b, 0)), self.out, self.count)

    def sent(self):
        self.net.sent([*self.sides.values(), *self.hops])


SMEM = pl.BlockSpec(memory_space=pltpu.SMEM)


def call(kernel, outs, ins, scratch, copies, moves, cid):
    any_spec = pl.BlockSpec(memory_space=pl.ANY)
    vmem_spec = pl.BlockSpec(memory_space=pltpu.VMEM)
    return pl.pallas_call(
        kernel,
        out_shape=[shape for shape, _ in outs],
        in_specs=[SMEM if v is SMEM else vmem_spec if v else any_spec for _, v in ins],
        out_specs=[vmem_spec if v else any_spec for _, v in outs],
        scratch_shapes=list(scratch)
        + [
            pltpu.SemaphoreType.DMA((copies,)),
            pltpu.SemaphoreType.DMA((copies,)),
            pltpu.SemaphoreType.DMA((moves,)),
        ],
        compiler_params=pltpu.CompilerParams(
            collective_id=cid, has_side_effects=True, vmem_limit_bytes=61 * 2**20
        ),
    )(*[array for array, _ in ins])


def shape(*dims, kind=BF):
    return jax.ShapeDtypeStruct(dims, kind)


def dot(a, b, dims):
    return lax.dot_general(a, b, (dims, ((), ())), preferred_element_type=F32)


NN = ((1,), (0,))
NT = ((1,), (1,))
TN = ((0,), (0,))


def normal(rows, width):
    centred = rows - jnp.sum(rows, axis=-1, keepdims=True) * (1.0 / width)
    spread = jnp.sum(centred * centred, axis=-1, keepdims=True) * (1.0 / width)
    return centred, lax.rsqrt(spread + EPSILON)


def loop(count, step, body):
    def turn(i, carry):
        body(pl.ds(pl.multiple_of(i * step, step), step))
        return carry

    lax.fori_loop(0, count // step, turn, 0)


def pair(net, d):
    lo = (net.t + d + 4) % 4 * 128
    return tuple(pl.ds(pl.multiple_of(c * HALF + lo, 128), 128) for c in (1 - net.c, net.c))


def tile(net, ds, half):
    rows = []
    for d in ds:
        lo = (net.t + d + 4) % 4 * 128 + half * 64
        rows += [pl.ds(pl.multiple_of(c * HALF + lo, 64), 64) for c in (1 - net.c, net.c)]
    return tuple(rows)


def of(ref, rows, cols=slice(None)):
    if isinstance(rows, tuple):
        return jnp.concatenate([ref[at, cols] for at in rows], axis=0)
    return ref[rows, cols]


def put(ref, rows, value, cols=slice(None)):
    if isinstance(rows, tuple):
        for k, at in enumerate(rows):
            ref[at, cols] = value[k * at.size : (k + 1) * at.size].astype(ref.dtype)
    else:
        ref[rows, cols] = value.astype(ref.dtype)


def wide(weights, x, start, count):
    return jnp.concatenate([weights[x, z, start : start + count, :] for z in range(4)], axis=1)


def times_flipped(ref, rows, weights, start, count):
    total = None
    for x in range(4):
        part = dot(of(ref, rows, slice(x * 512, x * 512 + 512)), wide(weights, x, start, count), NT)
        total = part if total is None else total + part
    return total


def times_plain(terms, out, rows):
    for x in range(4):
        total = None
        for value, weights, start, count in terms:
            part = dot(value, wide(weights, x, start, count), NN)
            total = part if total is None else total + part
        put(out, rows, total, slice(x * 512, x * 512 + 512))


def weight_grad(cols, rows, out, start, count, then=lambda x: None):
    for x in range(4):
        grad = dot(cols[...], rows[:, x * 512 : x * 512 + 512], TN).astype(BF)
        for z in range(4):
            out[x, z, start : start + count, :] = grad[:, z * 128 : z * 128 + 128]
        then(x)


def wait_all(copies):
    for copy in copies:
        copy.wait()


def masked(length, start, rows):
    place = lax.broadcasted_iota(jnp.int32, (rows, 1), 0) + start
    return jnp.where(place < length[0], 1.0, 0.0)


def mask_of(length, rows):
    return jnp.concatenate([masked(length, at.start, at.size) for at in rows], axis=0)


def decay_of(net):
    by_t = jnp.where(net.t % 2 == 1, 0.25, 1.0) * jnp.where(net.t // 2 == 1, 0.0625, 1.0)
    return jnp.where(net.c == 1, 0.5, 1.0) * by_t * (-32.0 / SEQ)


def fades(decay, start, rows, keys):
    n = lax.broadcasted_iota(jnp.int32, (rows, keys), 0) + start
    distance = (n - lax.broadcasted_iota(jnp.int32, (rows, keys), 1)).astype(F32)
    return jnp.where(distance >= 0.0, jnp.exp(jnp.maximum(distance, 0.0) * decay), 0.0)


def heads(decay, start, rows):
    ahead = lax.broadcasted_iota(jnp.int32, (rows, 1), 0) + start + 1
    return jnp.exp(ahead.astype(F32) * decay)


def causal():
    for lo in range(0, HALF, 128):
        for base in (0, HALF):
            yield lo, 128, lo + 128, base


def norm_back(source, gain, grad, out, lo=0, count=128):
    def body(i, total):
        at = pl.ds(pl.multiple_of(lo + i * 32, 32), 32)
        centred, dev = normal(source(at), D)
        normed = centred * dev
        back = grad(at)
        scaled = back * gain[...]
        mean = jnp.sum(scaled, axis=-1, keepdims=True) * (1.0 / D)
        along = jnp.sum(scaled * normed, axis=-1, keepdims=True) * (1.0 / D)
        out(at, dev * (scaled - mean - normed * along))
        return total + jnp.sum(back * normed, axis=0, keepdims=True)

    return lax.fori_loop(0, count // 32, body, jnp.zeros((1, D), F32))


def load_weights(net, source, weights, lo, to, rows):
    return [net.move(source.at[:, :, pl.ds(lo, rows), :], weights.at[:, :, pl.ds(to, rows), :])]


def forward_and_mlp_back(
    shards, inputs, carried_state, attn_gain, mlp_gain, cosine, sine, length, output_grad, cid
):
    def kernel(
        wq, wk, wv, ws, wo, wg, wu, wd, in_in, carried_in, gain_one, gain_two, cos_in, sin_in, length, grad_ref,
        weights_out, one_out, q_out, k_out, v_out, mix_out, prior_out, hidden_out, down_out, grad_hidden, gain_out,
        sums_out, swish_out, ret_out, out_grad_out,
        weights, one, two, part, grads, packs, got, carried, cos_ref, sin_ref,
        q_ref, k_ref, v_ref, mix_ref, prior_ref, hidden_ref, s_ref, norm_ref, dev_ref, mixed_ref, gate_grad, up_grad,
        total, gh_ref, in_ref,
        *rest,
    ):
        held, row_bufs, bufs, sems = rest[:8], rest[8:13], rest[13:-3], rest[-3:]
        net = Net(*sems)
        c, t = net.c, net.t
        mid, act, swish_grad, ret_grad = one, v_ref, v_ref, gate_grad
        net.greet(XZ_HOPS + Y_HOPS)
        load_in = net.move(in_in, in_ref)
        load_shards = [net.move(a, b) for a, b in zip((wq, wk, wv, ws, wo, wg, wu, wd), held)]
        load_cos, load_sin = net.move(cos_in, cos_ref), net.move(sin_in, sin_ref)
        load_state = net.move(carried_in.at[0, c], carried)
        mine = pl.ds(pl.multiple_of(c * HALF, HALF), HALF)
        load_grad = net.move(grad_ref, grads.at[mine, :])
        own = c * 512 + t * 128
        stores, early = [], []

        def norm_rows(source, gain, rows_ref, lo, count):
            def body(rows):
                at = pl.ds(pl.multiple_of(lo + rows.start, rows.size), rows.size)
                centred, dev = normal(source[at, :].astype(F32), D)
                to = pl.ds(pl.multiple_of(own + at.start, 16), at.size)
                rows_ref[to, :] = (centred * dev * gain[...]).astype(BF)

            loop(count, 32, body)

        def pack(first, last):
            spot = lax.broadcasted_iota(jnp.int32, (64, 128), 0) + c * 64
            place = jnp.where(spot == lax.broadcasted_iota(jnp.int32, (64, 128), 1), 1.0, 0.0).astype(BF)
            for k in range(first, last):
                load_shards[k].wait()
                flat = dot(held[k][...], place, TN).astype(BF)
                for core in range(2):
                    packs[core, STARTS[k] : STARTS[k] + SIZES[k], :] = flat[core * SIZES[k] : (core + 1) * SIZES[k]]

        def keep_weights(lo, hi):
            rows = pl.ds(lo, hi - lo)
            early.append(net.move(weights.at[:, :, rows, :], weights_out.at[:, :, rows, :]))

        w_qk, w_v, w_s, w_o, w_g, w_u, w_d = (
            gather_weights(net, weights, lo, hi)
            for lo, hi in ((0, 512), (512, 944), (944, 1376), (1376, 1808), (1808, 2240), (2240, 2672), (2672, 3104))
        )

        def join(swap, lo, hi):
            swap.wait_recv()
            step = 256 if hi == 512 else 432
            for at in range(lo, hi, step):
                weights[net.x, net.z, at : at + step, :] = packs[c, at : at + step, :] + got[at : at + step, :]

        swap_qk, swap_v, swap_s, swap_rest = (
            net.copy(packs.at[1 - c, pl.ds(lo, hi - lo), :], got.at[pl.ds(lo, hi - lo), :], dc=1)
            for lo, hi in ((0, 512), (512, 944), (944, 1376), (1376, ROWS))
        )
        grad_swap = net.copy(grad_ref, grads.at[mine, :], dc=1)

        y1 = gather_rows(net, one)
        decay = decay_of(net)

        def project_qk():
            wait_all([load_cos, load_sin])

            def body(at):
                cs, sn = cos_ref[at, :], sin_ref[at, :]
                for k, ref in ((0, q_ref), (1, k_ref)):
                    raw = times_flipped(one, at, weights, STARTS[k], SIZES[k])
                    former, latter = raw[:, :128], raw[:, 128:]
                    ref[at, :128] = (former * cs - latter * sn).astype(BF)
                    ref[at, 128:] = (former * sn + latter * cs).astype(BF)

            loop(SEQ, 256, body)
            early.append(net.move(one, one_out))
            stores.extend([net.move(q_ref, q_out), net.move(k_ref, k_out)])

        def project_v():
            def body(at):
                value = times_flipped(one, at, weights, STARTS[2], VDIM)
                v_ref[at, :] = (value * masked(length, at.start, at.size)).astype(BF)

            loop(SEQ, 256, body)
            early.append(net.move(v_ref, v_out))

        def mix():
            fade = {}
            for lo, n, seen, base in causal():
                if lo not in fade:
                    fade[lo] = fades(decay, lo, n, seen)
                at = slice(base + lo, base + lo + n)
                scores = dot(q_ref[at, :], k_ref[base : base + seen, :], NT)
                mix_ref[at, :seen] = (scores * fade[lo]).astype(BF)
                if seen < HALF:
                    mix_ref[at, seen:] = jnp.zeros((n, HALF - seen), BF)
            stores.append(net.move(mix_ref, mix_out))

        def states():
            load_state.wait()
            before = carried[...].T
            prior_ref[0] = before.astype(BF)
            far = lax.broadcasted_iota(jnp.int32, (HALF, 1), 0).astype(F32)
            tail = jnp.exp((HALF - 1.0 - far) * decay)
            local_state = dot((k_ref[:HALF, :].astype(F32) * tail).astype(BF), v_ref[:HALF, :], TN)
            prior_ref[1] = (jnp.exp(HALF * decay) * before + local_state).astype(BF)
            stores.append(net.move(prior_ref, prior_out))

        def retain():
            for lo, n, seen, base in causal():
                at = slice(base + lo, base + lo + n)
                inner = dot(mix_ref[at, :seen], v_ref[base : base + seen, :], NN)
                cross = dot(q_ref[at, :], prior_ref[base // HALF], NN) * heads(decay, lo, n)
                centred, dev = normal(inner + cross, VDIM)
                norm_ref[at, :] = (centred * dev).astype(BF)
                dev_ref[at, :] = dev

        def gate():
            def body(at):
                swish = times_flipped(one, at, weights, STARTS[3], VDIM)
                s_ref[at, :] = swish.astype(BF)
                share = masked(length, at.start, at.size) * (swish * jax.nn.sigmoid(swish))
                mixed_ref[at, :] = (share * norm_ref[at, :].astype(F32)).astype(BF)

            loop(SEQ, 256, body)
            wait_all(early)
            y1[6]()

        def hidden_rows(lo):
            def take(rows, value):
                at = pl.ds(pl.multiple_of(lo + rows.start, rows.size), rows.size)
                hidden_ref[at, :] = in_ref[at, :].astype(F32) + value

            return take

        def grad_rows(lo):
            def take(rows, value):
                total[pl.ds(pl.multiple_of(lo + rows.start, rows.size), rows.size), :] = value

            return take

        def out_rows(rows):
            times_plain(((of(mixed_ref, rows), weights, STARTS[4], VDIM),), part, rows)

        def act_grad_rows(at):
            up_grad[at, :] = times_flipped(grads, at, weights, STARTS[7], VDIM).astype(BF)

        def mlp_rows(rows):
            gate = times_flipped(two, rows, weights, STARTS[5], VDIM)
            up = times_flipped(two, rows, weights, STARTS[6], VDIM)
            back = of(up_grad, rows).astype(F32)
            share = 0.5 + 0.5 * lax.erf(gate * 0.7071067811865476)
            slope = share + gate * (0.3989422804014327 * jnp.exp(-0.5 * gate * gate))
            gelu = gate * share
            put(act, rows, gelu * up)
            back_gate, back_up = (back * up * slope).astype(BF), (back * gelu).astype(BF)
            put(gate_grad, rows, back_gate)
            put(up_grad, rows, back_up)
            times_plain(((back_gate, weights, STARTS[5], VDIM), (back_up, weights, STARTS[6], VDIM)), part, rows)

        def gate_back(rows):
            back = times_flipped(mid, rows, weights, STARTS[4], VDIM) * mask_of(length, rows)
            swish = of(s_ref, rows).astype(F32)
            unit = of(norm_ref, rows).astype(F32)
            share = jax.nn.sigmoid(swish)
            put(swish_grad, rows, back * unit * (share * (1.0 + swish * (1.0 - share))))
            back = back * (swish * share)
            mean = jnp.sum(back, axis=-1, keepdims=True) * (1.0 / VDIM)
            along = jnp.sum(back * unit, axis=-1, keepdims=True) * (1.0 / VDIM)
            put(ret_grad, rows, (back - mean - unit * along) * of(dev_ref, rows))

        def norm_two(lo):
            norm_rows(hidden_ref, gain_two, two, lo, 64)

        def norm_two_back(lo):
            def store(at, value):
                to = pl.ds(pl.multiple_of(own + at.start, 32), 32)
                whole = grads[to, :].astype(F32) + value
                gh_ref[at, :] = whole
                mid[to, :] = whole.astype(BF)

            some = norm_back(lambda at: hidden_ref[at, :], gain_two, lambda at: total[at, :], store, lo, 64)
            gain_out[...] = some if lo == 0 else gain_out[...] + some

        ra0, ra1 = (RowSums(net, part, row_bufs, hidden_rows(lo), lo, 64) for lo in (0, 64))
        rb0, rb1 = (RowSums(net, part, row_bufs, grad_rows(lo), lo, 64) for lo in (0, 64))
        yb0, yb1 = (gather_rows(net, two, lo, 64) for lo in (0, 64))
        yc0, yc1 = (gather_rows(net, mid, lo, 64) for lo in (0, 64))
        rows_a0, rows_b0, rows_a1, rows_b1 = (tile(net, ds, half) for half in (0, 1) for ds in ((2, 1), (-1, 0)))

        def keep(at, value):
            sums_out[pl.ds(at.start - STARTS[5], at.size), :] = value

        split = len(scatter_shapes(864))
        sum_gu = scatter_weights(net, weights, STARTS[5], STARTS[7], bufs[:split], keep)
        sum_d = scatter_weights(net, weights, STARTS[7], ROWS, bufs[split:], keep)

        def grad_of(gathered, cols, rows, k):
            gathered[5]()
            weight_grad(cols, rows, weights, STARTS[k], VDIM)

        def down_rows():
            for gathered in (w_qk, w_v, w_s):
                gathered[5]()

            def body(at):
                values = [dot(act[at, :], wide(weights, x, STARTS[7], VDIM), NN).astype(BF) for x in range(4)]
                for x in range(4):
                    for z in range(4):
                        weights[x, z, at, :] = values[x][:, z * 128 : z * 128 + 128]

            loop(SEQ, 256, body)
            for x in range(4):
                for z in range(4):
                    cols = pl.ds(x * 512 + z * 128, 128)
                    stores.append(net.move(weights.at[x, z, pl.ds(0, SEQ), :], down_out.at[:, cols]))

        def out_grad():
            def keep_piece(x):
                stores.append(net.move(weights.at[x, :, pl.ds(STARTS[4], VDIM), :], out_grad_out.at[x]))

            w_o[5]()
            weight_grad(mixed_ref, mid, weights, STARTS[4], VDIM, keep_piece)

        pack(4, 8)
        pack(0, 2)
        net.met()
        swap_qk.start()
        pack(3, 4)
        swap_s.start()
        join(swap_qk, 0, 512)
        w_qk[0]()
        grad_swap.start()
        pack(2, 3)
        swap_rest.start()
        load_in.wait()
        norm_rows(in_ref, gain_one, one, 0, 128)
        swap_v.start()
        join(swap_s, 944, 1376)
        w_s[0]()
        join(swap_v, 512, 944)
        w_v[0]()
        y1[0]()
        w_qk[1]()
        join(swap_rest, 1376, ROWS)
        w_s[1]()
        w_o[0]()
        w_v[1]()
        w_qk[2]()
        w_v[2]()
        y1[1]()
        w_o[1]()
        w_qk[3]()
        y1[2]()
        w_v[3]()
        w_s[2]()
        y1[4]()
        y1[5]()
        w_o[2]()
        w_qk[4]()
        keep_weights(0, 512)
        y1[3]()
        project_qk()
        mix()
        w_v[4]()
        keep_weights(512, 944)
        project_v()
        states()
        w_s[3]()
        retain()
        w_o[3]()
        w_s[4]()
        keep_weights(944, 1376)
        gate()
        w_d[0]()
        w_o[4]()
        out_rows(rows_a0)
        ra0.side(2)
        out_rows(rows_b0)
        ra0.far()
        ra0.side(1)
        ra0.side(0)
        out_rows(rows_a1)
        w_g[0]()
        ra0.side(-1)
        ra1.side(2)
        w_d[1]()
        ra1.far()
        out_rows(rows_b1)
        ra1.side(-1)
        w_d[2]()
        ra0.near()
        w_g[1]()
        ra1.side(1)
        grad_swap.wait_recv()
        load_grad.wait()
        w_g[2]()
        w_u[0]()
        ra1.near()
        ra0.finish()
        w_d[3]()
        norm_two(0)
        w_u[1]()
        ra1.side(0)
        yb0[0]()
        w_u[2]()
        ra1.finish()
        stores.append(net.move(hidden_ref, hidden_out))
        norm_two(64)
        yb1[0]()
        w_u[3]()
        yb0[1]()
        yb1[2]()
        yb0[2]()
        w_d[4]()
        loop(SEQ, 256, act_grad_rows)
        w_g[3]()
        yb0[3]()
        yb1[1]()
        yb0[4]()
        yb0[5]()
        w_u[4]()
        w_g[4]()
        ra0.sent()
        ra1.sent()
        mlp_rows(rows_a0)
        rb0.side(1)
        yb1[4]()
        rb0.side(2)
        mlp_rows(rows_b0)
        yb1[5]()
        yb1[3]()
        rb0.side(-1)
        rb0.far()
        mlp_rows(rows_a1)
        rb1.side(2)
        rb1.far()
        mlp_rows(rows_b1)
        rb0.near()
        grad_of(w_g, gate_grad, two, 5)
        rb1.side(-1)
        rb1.side(1)
        grad_of(w_u, up_grad, two, 6)
        rb1.near()
        sum_gu[0]()
        rb0.side(0)
        down_rows()
        grad_of(w_d, act, grads, 7)
        sum_d[0]()
        rb0.finish()
        norm_two_back(0)
        yc0[0]()
        sum_gu[1]()
        yc0[2]()
        rb1.side(0)
        rb1.finish()
        sum_d[1]()
        norm_two_back(64)
        stores.append(net.move(gh_ref, grad_hidden))
        yc1[0]()
        yc1[1]()
        sum_d[2]()
        yc1[2]()
        yc0[1]()
        sum_gu[2]()
        yc1[4]()
        sum_d[3]()
        yc1[5]()
        yc1[3]()
        gate_back(rows_a1)
        yc0[4]()
        sum_gu[3]()
        gate_back(rows_b1)
        sum_d[4]()
        yc0[3]()
        yc0[5]()
        gate_back(rows_a0)
        gate_back(rows_b0)
        stores += [net.move(ret_grad, ret_out), net.move(swish_grad, swish_out)]
        out_grad()
        sum_gu[4]()
        net.flush()
        wait_all(stores)

    cols = pltpu.VMEM((SEQ, VDIM), BF)
    rows = pltpu.VMEM((SEQ, D), BF)
    keys = pltpu.VMEM((SEQ, KDIM), BF)
    own = pltpu.VMEM((128, D), F32)
    return call(
        kernel,
        [
            (shape(4, 4, STARTS[4], 128), False),
            (shape(SEQ, D), False),
            (shape(SEQ, KDIM), False),
            (shape(SEQ, KDIM), False),
            (shape(SEQ, VDIM), False),
            (shape(SEQ, HALF), False),
            (shape(2, KDIM, VDIM), False),
            (shape(128, D, kind=F32), False),
            (shape(SEQ, D), False),
            (shape(128, D, kind=F32), False),
            (shape(1, D, kind=F32), True),
            (shape(1296, 128, kind=F32), True),
            (shape(SEQ, VDIM), False),
            (shape(SEQ, VDIM), False),
            (shape(4, 4, 432, 128), False),
        ],
        [(shard, False) for shard in shards]
        + [
            (inputs, False),
            (carried_state, False),
            (attn_gain, True),
            (mlp_gain, True),
            (cosine, False),
            (sine, False),
            (length, SMEM),
            (output_grad, False),
        ],
        [
            pltpu.VMEM((4, 4, ROWS, 128), BF),
            rows,
            rows,
            rows,
            rows,
            pltpu.VMEM((2, ROWS, 128), BF),
            pltpu.VMEM((ROWS, 128), BF),
            pltpu.VMEM((VDIM, KDIM), F32),
            pltpu.VMEM((SEQ, 128), F32),
            pltpu.VMEM((SEQ, 128), F32),
            keys,
            keys,
            cols,
            pltpu.VMEM((SEQ, HALF), BF),
            pltpu.VMEM((2, KDIM, VDIM), BF),
            own,
            cols,
            cols,
            pltpu.VMEM((SEQ, 1), F32),
            cols,
            cols,
            cols,
            own,
            own,
            pltpu.VMEM((128, D), BF),
        ]
        + [pltpu.VMEM(shard.shape, BF) for shard in shards]
        + ROW_BUFS
        + scatter_shapes(864)
        + scatter_shapes(432),
        228,
        64,
        cid,
    )


SPREAD_HOPS = tuple(dict(dt=dt, dc=dc) for dt in (0, 1, 2, -1) for dc in (0, 1) if (dt, dc) != (0, 0))
FAR_HOPS = (dict(dx=2), dict(dz=2))


def retention_back(
    weights_all, rows_one, down_part, q, k, v, mix, prior, swish_grad, ret_grad, out_grad, hidden, grad_hidden, inputs,
    attn_gain, cosine, sine, length, mlp_gain_part, sums_mlp, cid
):

    def kernel(
        w_ref, one_in, down_in, q_in, k_in, v_in, mix_in, prior_in, swish_in, ret_in, out_grad_in, hidden_in, gh_in,
        in_ref, gain, cos_in, sin_in, length, mlp_gain_ref, sums_mlp_ref,
        out_out, in_grad_out, gains_out, sums_all, sums_got, mlp_got,
        out_ref, in_grad, sums_out, weights, sums_ref, one, part, down, q_ref, k_ref, v_ref, mix_ref, prior_ref, swish_grad, ret_grad, hidden_ref,
        gh_ref, cos_ref, sin_ref, q_grad, k_grad, v_grad, score_grad, total, gain_sum, by_group, by_x, by_z,
        *rest,
    ):
        first_bufs, second_bufs, bufs, sems = rest[:5], rest[5:10], rest[10:-3], rest[-3:]
        net = Net(*sems)
        c, t = net.c, net.t
        net.greet(XZ_HOPS + FAR_HOPS + SPREAD_HOPS)

        def moves(*pairs):
            return [net.move(a, b) for a, b in pairs]

        load_score = moves(
            (ret_in, ret_grad), (v_in, v_ref), (k_in, k_ref), (prior_in, prior_ref), (cos_in, cos_ref), (sin_in, sin_ref)
        )
        load_out = moves((out_grad_in, sums_ref.at[:, :, pl.ds(0, 432), :]))
        load_kv = moves((q_in, q_ref), (mix_in, mix_ref))
        load_w = moves((swish_in, swish_grad))
        for lo, to, n in ((STARTS[3], 0, 432), (STARTS[2], 432, 432), (0, 864, 512)):
            load_w += load_weights(net, w_ref, weights, lo, to, n)
        load_one = moves((one_in, one))
        load_down = moves((down_in.at[pl.ds(pl.multiple_of(c * HALF, HALF), HALF), :], down))
        load_last = moves((hidden_in, hidden_ref), (gh_in, gh_ref))
        stores = []
        decay = decay_of(net)

        def turn_back(at, raw):
            cs, sn = cos_ref[at, :], sin_ref[at, :]
            former, latter = raw[:, :128], raw[:, 128:]
            return (former * cs + latter * sn).astype(BF), (latter * cs - former * sn).astype(BF)

        def score():
            wait_all(load_score)
            fade = {}
            for lo, n, seen, base in causal():
                if lo not in fade:
                    fade[lo] = fades(decay, lo, n, seen)
                at, keys = slice(base + lo, base + lo + n), slice(base, base + seen)
                scores = (dot(ret_grad[at, :], v_ref[keys, :], NT) * fade[lo]).astype(BF)
                score_grad[at, :seen] = scores
                if seen < HALF:
                    score_grad[at, seen:] = jnp.zeros((n, HALF - seen), BF)
                cross = dot(ret_grad[at, :], prior_ref[base // HALF], NT) * heads(decay, lo, n)
                q_grad[at, :128], q_grad[at, 128:] = turn_back(at, dot(scores, k_ref[keys, :], NN) + cross)

        def keys_and_values():
            wait_all(load_kv)
            far = lax.broadcasted_iota(jnp.int32, (HALF, 1), 0).astype(F32)
            tail = jnp.exp((HALF - 1.0 - far) * decay)
            ahead = (q_ref[HALF:, :].astype(F32) * jnp.exp((far + 1.0) * decay)).astype(BF)
            grad_local = dot(ahead, ret_grad[HALF:, :], TN).astype(BF)
            for stretch in range(2):
                keys = slice(stretch * HALF, stretch * HALF + HALF)
                raw = dot(score_grad[keys, :], q_ref[keys, :], TN)
                value = dot(mix_ref[keys, :], ret_grad[keys, :], TN)
                if stretch == 0:
                    raw = raw + dot(v_ref[keys, :], grad_local, NT) * tail
                    value = value + dot(k_ref[keys, :], grad_local, NN) * tail
                k_grad[keys, :128], k_grad[keys, 128:] = turn_back(keys, raw)
                v_grad[keys, :] = (value * masked(length, stretch * HALF, HALF)).astype(BF)

        def back_rows(rows):
            terms = (
                (of(swish_grad, rows), weights, 0, 432),
                (of(v_grad, rows), weights, 432, 432),
                (of(q_grad, rows), weights, 864, 256),
                (of(k_grad, rows), weights, 1120, 256),
            )
            times_plain(terms, part, rows)

        def gain_rows(rows):
            for x in range(4):
                at = slice(x * 512, x * 512 + 512)
                along = of(part, rows, at).astype(F32) * of(one, rows, at).astype(F32)
                gain_sum[:, at] = gain_sum[:, at] + jnp.sum(along, axis=0, keepdims=True)

        def output_rows(lo):
            def take(rows, value):
                at = pl.ds(pl.multiple_of(lo + rows.start, rows.size), rows.size)
                out_ref[at, :] = (hidden_ref[at, :] + value).astype(BF)

            return take

        def grad_rows(lo):
            def take(rows, value):
                total[pl.ds(pl.multiple_of(lo + rows.start, rows.size), rows.size), :] = value

            return take

        def norm_one_back(lo):
            def store(at, value):
                in_grad[at, :] = gh_ref[at, :] + value

            norm_back(lambda at: in_ref[at, :].astype(F32), gain, lambda at: total[at, :], store, lo, 64)

        gain_sum[...] = jnp.zeros_like(gain_sum)
        ra0, ra1 = (RowSums(net, down, first_bufs, output_rows(lo), lo, 64, down_in, 0) for lo in (0, 64))
        rb0, rb1 = (RowSums(net, part, second_bufs, grad_rows(lo), lo, 64) for lo in (0, 64))
        rows_a0, rows_b0, rows_a1, rows_b1 = (tile(net, ds, half) for half in (0, 1) for ds in ((2, 1), (-1, 0)))

        def keep(at, value):
            sums_out[at, :] = value

        sums, at = [], 0
        for lo, hi in ((0, 432), (432, 864), (864, 1296), (1296, 1808)):
            n = len(scatter_shapes(hi - lo))
            sums.append(scatter_weights(net, sums_ref, lo, hi, bufs[at : at + n], keep))
            at += n
        sum_o, sum_s, sum_v, sum_qk = sums

        def keys_grad():
            weight_grad(q_grad, one, sums_ref, 1296, 256)
            weight_grad(k_grad, one, sums_ref, 1552, 256)

        def spread(ref, place, hops):
            return [net.copy(ref.at[place], ref.at[place], **hop) for hop in hops]

        def gathered(ref, copies):
            for copy in copies:
                copy.wait_recv()
            value = ref[0]
            for k in range(1, ref.shape[0]):
                value = value + ref[k]
            return value

        def begin():
            by_group[t * 2 + c, 0:1, :] = gain_sum[...] / gain[...]
            by_group[t * 2 + c, 1:2, :] = mlp_gain_ref[...]
            for copy in in_group:
                copy.start()

        def along_x():
            by_x[net.x] = gathered(by_group, in_group)
            for copy in in_x:
                copy.start()

        def along_z():
            by_z[net.z] = gathered(by_x, in_x)
            for copy in in_z:
                copy.start()

        def all_gains():
            gains_out[...] = gathered(by_z, in_z)

        in_group = spread(by_group, t * 2 + c, SPREAD_HOPS)
        in_x = spread(by_x, net.x, (dict(dx=1), dict(dx=-1), dict(dx=2)))
        in_z = spread(by_z, net.z, (dict(dz=1), dict(dz=-1), dict(dz=2)))
        def keep_sums(lo, n):
            stores.append(net.move(sums_out.at[pl.ds(lo, n), :], sums_all.at[pl.ds(lo, n), :]))

        swap_mlp = net.copy(sums_mlp_ref, mlp_got, dc=1)
        swap_o, swap_s, swap_v, swap_qk = (
            net.copy(sums_out.at[pl.ds(lo, n), :], sums_got.at[pl.ds(lo, n), :], dc=1)
            for lo, n in ((0, 432), (432, 432), (864, 432), (1296, 512))
        )
        net.met()
        wait_all(load_out)
        sum_o[0]()
        ra1.side(2)
        ra0.side(-1)
        score()
        keys_and_values()
        ra0.side(1)
        sum_o[1]()
        ra0.side(2)
        wait_all(load_w)
        back_rows(rows_a0)
        wait_all(load_down)
        ra0.far()
        rb0.side(2)
        wait_all(load_one)
        gain_rows(rows_a0)
        weight_grad(v_grad, one, sums_ref, 864, 432)
        swap_mlp.start()
        sum_v[0]()
        rb0.far()
        keys_grad()
        sum_qk[0]()
        ra0.near()
        back_rows(rows_b0)
        rb0.side(1)
        sum_v[1]()
        ra1.side(0)
        ra1.far()
        ra0.side(0)
        rb0.side(-1)
        weight_grad(swish_grad, one, sums_ref, 432, 432)
        back_rows(rows_a1)
        rb1.side(2)
        sum_qk[1]()
        gain_rows(rows_a1)
        rb1.far()
        ra1.side(-1)
        gain_rows(rows_b0)
        sum_s[0]()
        ra1.side(1)
        rb0.near()
        rb1.side(1)
        back_rows(rows_b1)
        gain_rows(rows_b1)
        sum_s[1]()
        rb1.side(-1)
        sum_o[2]()
        rb1.near()
        begin()
        sum_qk[2]()
        sum_qk[3]()
        sum_v[2]()
        ra1.near()
        rb0.side(0)
        wait_all(load_last)
        ra0.finish()
        along_x()
        sum_s[2]()
        sum_o[3]()
        rb1.side(0)
        sum_v[3]()
        rb0.finish()
        sum_qk[4]()
        keep_sums(1296, 512)
        sum_s[3]()
        sum_o[4]()
        keep_sums(0, 432)
        along_z()
        swap_o.start()
        norm_one_back(0)
        rb1.finish()
        sum_v[4]()
        keep_sums(864, 432)
        swap_v.start()
        swap_qk.start()
        norm_one_back(64)
        stores.append(net.move(in_grad, in_grad_out))
        sum_s[4]()
        keep_sums(432, 432)
        swap_s.start()
        all_gains()
        ra1.finish()
        stores.append(net.move(out_ref, out_out))
        for swap in (swap_mlp, swap_o, swap_s, swap_v, swap_qk):
            swap.wait_recv()
        net.flush()
        wait_all(stores)

    cols = pltpu.VMEM((SEQ, VDIM), BF)
    keys = pltpu.VMEM((SEQ, KDIM), BF)
    rows = pltpu.VMEM((SEQ, D), BF)
    own = pltpu.VMEM((128, D), F32)
    return call(
        kernel,
        [
            (shape(128, D), False),
            (shape(128, D, kind=F32), False),
            (shape(2, D, kind=F32), True),
            (shape(1808, 128, kind=F32), False),
            (shape(1808, 128, kind=F32), False),
            (shape(1296, 128, kind=F32), False),
        ],
        [
            (weights_all, False),
            (rows_one, False),
            (down_part, False),
            (q, False),
            (k, False),
            (v, False),
            (mix, False),
            (prior, False),
            (swish_grad, False),
            (ret_grad, False),
            (out_grad, False),
            (hidden, False),
            (grad_hidden, False),
            (inputs, True),
            (attn_gain, True),
            (cosine, False),
            (sine, False),
            (length, SMEM),
            (mlp_gain_part, True),
            (sums_mlp, False),
        ],
        [
            pltpu.VMEM((128, D), BF),
            own,
            pltpu.VMEM((1808, 128), F32),
            pltpu.VMEM((4, 4, 1376, 128), BF),
            pltpu.VMEM((4, 4, 1808, 128), BF),
            rows,
            rows,
            pltpu.VMEM((HALF, D), BF),
            keys,
            keys,
            cols,
            pltpu.VMEM((SEQ, HALF), BF),
            pltpu.VMEM((2, KDIM, VDIM), BF),
            cols,
            cols,
            own,
            own,
            pltpu.VMEM((SEQ, 128), F32),
            pltpu.VMEM((SEQ, 128), F32),
            keys,
            keys,
            cols,
            pltpu.VMEM((SEQ, HALF), BF),
            own,
            pltpu.VMEM((1, D), F32),
            pltpu.VMEM((8, 2, D), F32),
            pltpu.VMEM((4, 2, D), F32),
            pltpu.VMEM((4, 2, D), F32),
        ]
        + ROW_BUFS
        + ROW_BUFS
        + scatter_shapes(432) * 3
        + scatter_shapes(512),
        120,
        48,
        cid,
    )


def hand_out(outputs, input_grad, gains, sums, got, sums_mlp, got_mlp):
    places = (
        (0, 1296, 256), (0, 1552, 256), (0, 864, 432), (0, 432, 432), (0, 0, 432), (1, 0, 432), (1, 432, 432),
        (1, 864, 432),
    )

    def kernel(*refs):
        n = len(outs)
        ins, results, held, made, loads, stores = (
            refs[:7], refs[7 : 7 + n], refs[7 + n : 14 + n], refs[14 + n : 14 + 2 * n], refs[-2], refs[-1]
        )
        arrive = [pltpu.make_async_copy(ins[k], held[k], loads.at[k]) for k in range(7)]
        leave = [pltpu.make_async_copy(made[k], results[k], stores.at[k]) for k in range(n)]
        for k in (5, 6, 3, 4, 1, 0, 2):
            arrive[k].start()
        first_core = lax.axis_index("ctx") == 0
        wait_all([arrive[5], arrive[6]])
        waited = False
        for k in (5, 6, 7, 4, 3, 2, 0, 1):
            which, lo, rows = places[k]
            if which == 0 and not waited:
                wait_all([arrive[3], arrive[4]])
                waited = True
            a, b = (held[at][lo : lo + rows, :] for at in ((3, 4), (5, 6))[which])
            both = jnp.concatenate([jnp.where(first_core, a, b), jnp.where(first_core, b, a)], axis=0).T
            made[4 + k][...] = jnp.where(first_core, both[:64], both[64:])
            leave[4 + k].start()
        wait_all([arrive[0], arrive[1], arrive[2]])
        made[1][...] = held[1][...]
        leave[1].start()
        made[0][...] = held[0][...]
        made[2][...] = held[2][0:1, :]
        made[3][...] = held[2][1:2, :]
        for k in (0, 2, 3):
            leave[k].start()
        wait_all(leave)

    outs = [shape(128, D), shape(128, D, kind=F32), shape(1, D, kind=F32), shape(1, D, kind=F32)]
    for _, _, n in places:
        outs.append(shape(64, 2 * n, kind=F32))
    ins = (outputs, input_grad, gains, sums, got, sums_mlp, got_mlp)
    spec = pl.BlockSpec(memory_space=pl.ANY)
    return pl.pallas_call(
        kernel,
        out_shape=outs,
        in_specs=[spec] * len(ins),
        out_specs=[spec] * len(outs),
        scratch_shapes=[pltpu.VMEM(a.shape, a.dtype) for a in (*ins, *outs)]
        + [pltpu.SemaphoreType.DMA((len(ins),)), pltpu.SemaphoreType.DMA((len(outs),))],
        compiler_params=pltpu.CompilerParams(vmem_limit_bytes=61 * 2**20),
    )(*ins)


def turning_tables():
    frequency = 10000.0 ** (-np.arange(128) / 128.0)
    angles = np.arange(SEQ)[:, None] * frequency[None, :]
    return jnp.asarray(np.cos(angles), F32), jnp.asarray(np.sin(angles), F32)


def on_device(
    inputs,
    seq_lengths,
    carried_state,
    attn_gain,
    query_weight,
    key_weight,
    value_weight,
    swish_weight,
    out_weight,
    mlp_gain,
    gate_weight,
    up_weight,
    down_weight,
    output_grad,
):
    cosine, sine = turning_tables()
    gains = attn_gain[None, :], mlp_gain[None, :]
    shards = (
        query_weight, key_weight, value_weight, swish_weight, out_weight.T, gate_weight, up_weight, down_weight.T
    )
    (
        weights, rows_one, q, k, v, mix, prior, hidden, down_part, grad_hidden, mlp_gain_part, sums_mlp, swish_grad,
        ret_grad, out_grad
    ) = forward_and_mlp_back(
        shards, inputs, carried_state.transpose(0, 1, 3, 2), *gains, cosine, sine, seq_lengths, output_grad, 1
    )
    outputs, input_grad, gain_grads, sums, got_sums, got_mlp = retention_back(
        weights, rows_one, down_part, q, k, v, mix, prior, swish_grad, ret_grad, out_grad, hidden, grad_hidden, inputs,
        gains[0], cosine, sine, seq_lengths, mlp_gain_part, sums_mlp, 2
    )
    outputs, input_grad, first, second, *grads = hand_out(
        outputs, input_grad, gain_grads, sums, got_sums, sums_mlp, got_mlp
    )
    return (
        outputs,
        input_grad,
        first[0],
        grads[0],
        grads[1],
        grads[2],
        grads[3],
        grads[4].T,
        second[0],
        grads[5],
        grads[6],
        grads[7].T,
    )


def solution(mesh):
    placed = (
        P(("fsdp", "ctx", "tp"), None),
        P("fsdp"),
        P("fsdp", "tp", None, None),
        P(),
        P(("fsdp", "ctx"), "tp"),
        P(("fsdp", "ctx"), "tp"),
        P(("fsdp", "ctx"), "tp"),
        P(("fsdp", "ctx"), "tp"),
        P("tp", ("fsdp", "ctx")),
        P(),
        P(("fsdp", "ctx"), "tp"),
        P(("fsdp", "ctx"), "tp"),
        P("tp", ("fsdp", "ctx")),
        P(("fsdp", "ctx"), None),
    )
    return jax.shard_map(
        on_device,
        mesh=mesh,
        in_specs=placed,
        out_specs=(
            P(("fsdp", "ctx", "tp"), None),
            P(("fsdp", "ctx", "tp"), None),
            P(),
            P(("fsdp", "ctx"), "tp"),
            P(("fsdp", "ctx"), "tp"),
            P(("fsdp", "ctx"), "tp"),
            P(("fsdp", "ctx"), "tp"),
            P("tp", ("fsdp", "ctx")),
            P(),
            P(("fsdp", "ctx"), "tp"),
            P(("fsdp", "ctx"), "tp"),
            P("tp", ("fsdp", "ctx")),
        ),
        check_vma=False,
    )
```

```python
import jax
import jax.numpy as jnp
import numpy as np
from jax import lax
from jax.experimental import pallas as pl
from jax.experimental.pallas import tpu as pltpu
from jax.sharding import PartitionSpec as P

D = 2048
KDIM = 256
VDIM = 432
SEQ = 1024
HALF = 512
SIZES = (256, 256, 432, 432, 432, 432, 432, 432)
STARTS = (0, 256, 512, 944, 1376, 1808, 2240, 2672)
ROWS = 3104
EPSILON = 1e-05
MESH = pl.DeviceIdType.MESH
BF = jnp.bfloat16
F32 = jnp.float32


def even(rows):
    return rows // 32 * 16


class Net:
    def __init__(self, send, recv, local):
        group = lax.axis_index("fsdp")
        self.c = lax.axis_index("ctx")
        self.t = lax.axis_index("tp")
        self.x = group // 4
        self.z = group % 4
        self.send, self.recv, self.local = send, recv, local
        self.copies, self.gone, self.moves = [], [], 0

    def dev(self, dx=0, dz=0, dt=0, dc=0):
        x, z, t = ((at + d + 4) % 4 if d else at for at, d in ((self.x, dx), (self.z, dz), (self.t, dt)))
        c = 1 - self.c if dc else self.c
        return (x * 4 + z, c, t)

    def greet(self, hops):
        self.greeted = len(hops)
        for hop in hops:
            pl.semaphore_signal(
                pltpu.get_barrier_semaphore(), inc=1, device_id=self.dev(**hop), device_id_type=MESH
            )

    def met(self):
        pl.semaphore_wait(pltpu.get_barrier_semaphore(), self.greeted)

    def copy(self, src, dst, **hop):
        at = len(self.copies)
        self.copies.append(
            pltpu.make_async_remote_copy(
                src_ref=src,
                dst_ref=dst,
                send_sem=self.send.at[at],
                recv_sem=self.recv.at[at],
                device_id=self.dev(**hop),
                device_id_type=MESH,
            )
        )
        return self.copies[-1]

    def move(self, src, dst):
        copy = pltpu.make_async_copy(src, dst, self.local.at[self.moves])
        self.moves += 1
        copy.start()
        return copy

    def sent(self, copies):
        for copy in copies:
            if not any(copy is other for other in self.gone):
                copy.wait_send()
                self.gone.append(copy)

    def flush(self):
        self.sent(self.copies)


XZ_HOPS = (dict(dx=1), dict(dx=-1), dict(dz=1), dict(dz=-1))
Y_HOPS = (dict(dt=1), dict(dt=-1), dict(dc=1))


def ring_views(net, axis):
    x, z = net.x, net.z
    along_x = lambda ref, d, rows: ref.at[(x + d + 4) % 4, z, rows, :]
    along_z = lambda ref, d, rows: ref.at[x, (z + d + 4) % 4, rows, :]
    all_z = lambda ref, d, rows: ref.at[(x + d + 4) % 4, :, rows, :]
    all_x = lambda ref, d, rows: ref.at[:, (z + d + 4) % 4, rows, :]
    if axis == "x":
        return along_x, all_x, "dx", "dz"
    return along_z, all_z, "dz", "dx"


def gather_weights(net, ref, start, stop):
    cut = start + even(stop - start)
    plans = []
    for axis, lo, hi in (("z", start, cut), ("x", cut, stop)):
        mid = lo + even(hi - lo)
        whole, head, tail = pl.ds(lo, hi - lo), pl.ds(lo, mid - lo), pl.ds(mid, hi - mid)
        first, second, hop_a, hop_b = ring_views(net, axis)
        plan = []
        for view, hop in ((first, hop_a), (second, hop_b)):
            mine = view(ref, 0, whole)
            plan.append(
                (
                    net.copy(mine, mine, **{hop: 1}),
                    net.copy(mine, mine, **{hop: -1}),
                    net.copy(view(ref, -1, head), view(ref, -1, head), **{hop: 1}),
                    net.copy(view(ref, 1, tail), view(ref, 1, tail), **{hop: -1}),
                )
            )
        plans.append(plan)

    def near(phase):
        for plan in plans:
            plan[phase][0].start()
            plan[phase][1].start()

    def far(phase):
        for k in (0, 1):
            for plan in plans:
                plan[phase][k].wait_recv()
                plan[phase][2 + k].start()

    def land(phase):
        for plan in plans:
            plan[phase][2].wait_recv()
            plan[phase][3].wait_recv()

    return [
        lambda: near(0),
        lambda: far(0),
        lambda: (land(0), near(1)),
        lambda: far(1),
        lambda: land(1),
        lambda: net.sent([copy for plan in plans for phase in plan for copy in phase]),
    ]


def add_rows(refs, out, count):
    step = 16

    def body(i, carry):
        at = pl.ds(pl.multiple_of(i * step, step), step)
        total = refs[0](at).astype(F32)
        for ref in refs[1:]:
            total = total + ref(at).astype(F32)
        out(at, total)
        return carry

    lax.fori_loop(0, count // step, body, 0)


def scatter_shapes(rows):
    shapes = []
    cut = even(rows)
    for axis, count in (("z", cut), ("x", rows - cut)):
        head = even(count)
        for pieces in ((4,), ()):
            for n in (head, count - head, count, count):
                shapes.append(pltpu.VMEM((*pieces, n, 128), BF))
    return shapes


def scatter_weights(net, ref, start, stop, bufs, out):
    cut = start + even(stop - start)
    plans = []
    bufs = list(bufs)
    for axis, lo, hi in (("z", start, cut), ("x", cut, stop)):
        mid = lo + even(hi - lo)
        parts = (lo, mid - lo), (mid, hi - mid), (lo, hi - lo)
        head, tail, whole = (pl.ds(*part) for part in parts)
        plan = []
        _, wide, hop_b, hop_a = ring_views(net, "x" if axis == "z" else "z")
        thin = ring_views(net, "z" if axis == "x" else "x")[0]
        for view, hop in ((wide, hop_a), (thin, hop_b)):
            fa, fb, ma, mb = bufs[:4]
            bufs = bufs[4:]
            plan.append(
                dict(
                    view=view,
                    bufs=(fa, fb, ma, mb),
                    copies=(
                        net.copy(view(ref, 2, head), fa, **{hop: 1}),
                        net.copy(view(ref, 2, tail), fb, **{hop: -1}),
                        net.copy(view(ref, 1, whole), ma, **{hop: 1}),
                        net.copy(view(ref, -1, whole), mb, **{hop: -1}),
                    ),
                )
            )
        plans.append((plan, parts))

    def at_rows(view, d, lo):
        def read(at):
            return view(ref, d, pl.ds(lo + at.start, at.size))[...]

        def write(at, value):
            view(ref, d, pl.ds(lo + at.start, at.size))[...] = value.astype(BF)

        return read, write

    def buf_rows(buf):
        if len(buf.shape) == 3:
            return lambda at: buf[:, at, :]
        return lambda at: buf[at, :]

    def far(phase):
        for plan, _ in plans:
            plan[phase]["copies"][0].start()
            plan[phase]["copies"][1].start()

    def near(phase):
        for k, d in ((0, 1), (1, -1)):
            for plan, parts in plans:
                step = plan[phase]
                lo, count = parts[k]
                step["copies"][k].wait_recv()
                read, write = at_rows(step["view"], d, lo)
                add_rows((read, buf_rows(step["bufs"][k])), write, count)
                step["copies"][2 + k].start()

    def total(phase, last):
        for plan, parts in plans:
            step = plan[phase]
            lo, count = parts[2]
            step["copies"][2].wait_recv()
            step["copies"][3].wait_recv()
            read, write = at_rows(step["view"], 0, lo)
            if last:
                write = lambda at, value, lo=lo: out(pl.ds(lo + at.start, at.size), value)
            add_rows((read, buf_rows(step["bufs"][2]), buf_rows(step["bufs"][3])), write, count)

    return [
        lambda: far(0),
        lambda: near(0),
        lambda: (total(0, False), far(1)),
        lambda: near(1),
        lambda: total(1, True),
    ]


def gather_rows(net, ref, first=0, count=128):
    def block(c, t, lo=0, n=count):
        return ref.at[pl.ds(pl.multiple_of(c * 512 + t * 128 + first + lo, 16), n), :]

    c, t = net.c, net.t
    half = count // 2
    before, after, across = (t + 3) % 4, (t + 1) % 4, (t + 2) % 4
    own = block(c, t)
    up = net.copy(own, own, dt=1)
    down = net.copy(own, own, dt=-1)
    side = net.copy(own, own, dc=1)
    fore = net.copy(block(c, before, 0, half), block(c, before, 0, half), dt=1)
    back = net.copy(block(c, after, half, half), block(c, after, half, half), dt=-1)
    over = [
        net.copy(block(c, before), block(c, before), dc=1),
        net.copy(block(c, after), block(c, after), dc=1),
        net.copy(block(c, across, 0, half), block(c, across, 0, half), dc=1),
        net.copy(block(c, across, half, half), block(c, across, half, half), dc=1),
    ]

    def start():
        up.start()
        down.start()
        side.start()

    def forward():
        up.wait_recv()
        fore.start()
        over[0].start()
        down.wait_recv()
        back.start()
        over[1].start()

    def beside():
        side.wait_recv()

    def near():
        over[0].wait_recv()
        over[1].wait_recv()

    def far():
        fore.wait_recv()
        over[2].start()
        back.wait_recv()
        over[3].start()

    def last():
        over[2].wait_recv()
        over[3].wait_recv()

    def sent():
        net.sent((up, down, side, fore, back, *over))

    return start, forward, beside, near, far, last, sent


ROW_BUFS = [
    pltpu.VMEM((512, D), BF),
    pltpu.VMEM((64, D), BF),
    pltpu.VMEM((64, D), BF),
    pltpu.VMEM((128, D), BF),
    pltpu.VMEM((128, D), BF),
]


class RowSums:
    def __init__(self, net, ref, bufs, out, lo=0, count=128, source=None, first=None):
        c, t = net.c, net.t
        self.net, self.t, self.ref, self.out, self.lo, self.count = net, t, ref, out, lo, count
        self.first = c * HALF if first is None else first
        self.half = count // 2
        other, far_a, far_b, near_a, near_b = bufs
        self.other = other
        self.far_a, self.far_b = (far.at[pl.ds(lo // 2, self.half), :] for far in (far_a, far_b))
        self.near_a, self.near_b = (near.at[pl.ds(lo, count), :] for near in (near_a, near_b))
        source = ref if source is None else source
        self.sides = {}
        for d in (2, 1, -1, 0):
            row = self.row(d)
            self.sides[d] = net.copy(
                source.at[pl.ds(pl.multiple_of((1 - c) * HALF + row, 64), count), :],
                other.at[pl.ds(pl.multiple_of(row, 64), count), :],
                dc=1,
            )
        self.hops = (
            net.copy(self.block(2, 0, self.half), self.far_a, dt=1),
            net.copy(self.block(2, self.half, self.half), self.far_b, dt=-1),
            net.copy(self.block(1), self.near_a, dt=1),
            net.copy(self.block(-1), self.near_b, dt=-1),
        )

    def row(self, d, lo=0):
        return (self.t + d + 4) % 4 * 128 + self.lo + lo

    def block(self, d, lo=0, n=None):
        return self.ref.at[pl.ds(pl.multiple_of(self.first + self.row(d, lo), 16), n or self.count), :]

    def mine(self, d, lo=0):
        return self.read(self.ref, self.first + self.row(d, lo)), self.read(self.other, self.row(d, lo))

    @staticmethod
    def read(source, base):
        return lambda at: source[pl.ds(pl.multiple_of(base + at.start, 16), at.size), :]

    def keep(self, d, lo=0):
        base = self.first + self.row(d, lo)

        def store(at, value):
            self.ref[pl.ds(pl.multiple_of(base + at.start, 16), at.size), :] = value.astype(BF)

        return store

    def side(self, d):
        self.sides[d].start()

    def far(self):
        self.sides[2].wait_recv()
        for k in (0, 1):
            add_rows(self.mine(2, k * self.half), self.keep(2, k * self.half), self.half)
            self.hops[k].start()

    def near(self):
        for k, d, buf in ((0, 1, self.far_a), (1, -1, self.far_b)):
            lo, rest = k * self.half, (1 - k) * self.half
            self.sides[d].wait_recv()
            add_rows(self.mine(d, rest), self.keep(d, rest), self.half)
            self.hops[k].wait_recv()
            add_rows((*self.mine(d, lo), self.read(buf, 0)), self.keep(d, lo), self.half)
            self.hops[2 + k].start()

    def finish(self):
        self.sides[0].wait_recv()
        self.hops[2].wait_recv()
        self.hops[3].wait_recv()
        add_rows((*self.mine(0), self.read(self.near_a, 0), self.read(self.near_b, 0)), self.out, self.count)

    def sent(self):
        self.net.sent([*self.sides.values(), *self.hops])


SMEM = pl.BlockSpec(memory_space=pltpu.SMEM)


def call(kernel, outs, ins, scratch, copies, moves, cid):
    any_spec = pl.BlockSpec(memory_space=pl.ANY)
    vmem_spec = pl.BlockSpec(memory_space=pltpu.VMEM)
    return pl.pallas_call(
        kernel,
        out_shape=[shape for shape, _ in outs],
        in_specs=[SMEM if v is SMEM else vmem_spec if v else any_spec for _, v in ins],
        out_specs=[vmem_spec if v else any_spec for _, v in outs],
        scratch_shapes=list(scratch)
        + [
            pltpu.SemaphoreType.DMA((copies,)),
            pltpu.SemaphoreType.DMA((copies,)),
            pltpu.SemaphoreType.DMA((moves,)),
        ],
        compiler_params=pltpu.CompilerParams(
            collective_id=cid, has_side_effects=True, vmem_limit_bytes=61 * 2**20
        ),
    )(*[array for array, _ in ins])


def shape(*dims, kind=BF):
    return jax.ShapeDtypeStruct(dims, kind)


def dot(a, b, dims):
    return lax.dot_general(a, b, (dims, ((), ())), preferred_element_type=F32)


NN = ((1,), (0,))
NT = ((1,), (1,))
TN = ((0,), (0,))


def normal(rows, width):
    centred = rows - jnp.sum(rows, axis=-1, keepdims=True) * (1.0 / width)
    spread = jnp.sum(centred * centred, axis=-1, keepdims=True) * (1.0 / width)
    return centred, lax.rsqrt(spread + EPSILON)


def loop(count, step, body):
    def turn(i, carry):
        body(pl.ds(pl.multiple_of(i * step, step), step))
        return carry

    lax.fori_loop(0, count // step, turn, 0)


def pair(net, d):
    lo = (net.t + d + 4) % 4 * 128
    return tuple(pl.ds(pl.multiple_of(c * HALF + lo, 128), 128) for c in (1 - net.c, net.c))


def tile(net, ds, half):
    rows = []
    for d in ds:
        lo = (net.t + d + 4) % 4 * 128 + half * 64
        rows += [pl.ds(pl.multiple_of(c * HALF + lo, 64), 64) for c in (1 - net.c, net.c)]
    return tuple(rows)


def of(ref, rows, cols=slice(None)):
    if isinstance(rows, tuple):
        return jnp.concatenate([ref[at, cols] for at in rows], axis=0)
    return ref[rows, cols]


def put(ref, rows, value, cols=slice(None)):
    if isinstance(rows, tuple):
        for k, at in enumerate(rows):
            ref[at, cols] = value[k * at.size : (k + 1) * at.size].astype(ref.dtype)
    else:
        ref[rows, cols] = value.astype(ref.dtype)


def wide(weights, x, start, count):
    return jnp.concatenate([weights[x, z, start : start + count, :] for z in range(4)], axis=1)


def times_flipped(ref, rows, weights, start, count):
    total = None
    for x in range(4):
        part = dot(of(ref, rows, slice(x * 512, x * 512 + 512)), wide(weights, x, start, count), NT)
        total = part if total is None else total + part
    return total


def times_plain(terms, out, rows):
    for x in range(4):
        total = None
        for value, weights, start, count in terms:
            part = dot(value, wide(weights, x, start, count), NN)
            total = part if total is None else total + part
        put(out, rows, total, slice(x * 512, x * 512 + 512))


def weight_grad(cols, rows, out, start, count, then=lambda x: None):
    for x in range(4):
        grad = dot(cols[...], rows[:, x * 512 : x * 512 + 512], TN).astype(BF)
        for z in range(4):
            out[x, z, start : start + count, :] = grad[:, z * 128 : z * 128 + 128]
        then(x)


def wait_all(copies):
    for copy in copies:
        copy.wait()


def masked(length, start, rows):
    place = lax.broadcasted_iota(jnp.int32, (rows, 1), 0) + start
    return jnp.where(place < length[0], 1.0, 0.0)


def mask_of(length, rows):
    return jnp.concatenate([masked(length, at.start, at.size) for at in rows], axis=0)


def decay_of(net):
    by_t = jnp.where(net.t % 2 == 1, 0.25, 1.0) * jnp.where(net.t // 2 == 1, 0.0625, 1.0)
    return jnp.where(net.c == 1, 0.5, 1.0) * by_t * (-32.0 / SEQ)


def fades(decay, start, rows, keys):
    n = lax.broadcasted_iota(jnp.int32, (rows, keys), 0) + start
    distance = (n - lax.broadcasted_iota(jnp.int32, (rows, keys), 1)).astype(F32)
    return jnp.where(distance >= 0.0, jnp.exp(jnp.maximum(distance, 0.0) * decay), 0.0)


def heads(decay, start, rows):
    ahead = lax.broadcasted_iota(jnp.int32, (rows, 1), 0) + start + 1
    return jnp.exp(ahead.astype(F32) * decay)


def causal():
    for lo in range(0, HALF, 128):
        for base in (0, HALF):
            yield lo, 128, lo + 128, base


def norm_back(source, gain, grad, out, lo=0, count=128):
    def body(i, total):
        at = pl.ds(pl.multiple_of(lo + i * 32, 32), 32)
        centred, dev = normal(source(at), D)
        normed = centred * dev
        back = grad(at)
        scaled = back * gain[...]
        mean = jnp.sum(scaled, axis=-1, keepdims=True) * (1.0 / D)
        along = jnp.sum(scaled * normed, axis=-1, keepdims=True) * (1.0 / D)
        out(at, dev * (scaled - mean - normed * along))
        return total + jnp.sum(back * normed, axis=0, keepdims=True)

    return lax.fori_loop(0, count // 32, body, jnp.zeros((1, D), F32))


def load_weights(net, source, weights, lo, to, rows):
    return [net.move(source.at[:, :, pl.ds(lo, rows), :], weights.at[:, :, pl.ds(to, rows), :])]


def forward_and_mlp_back(
    shards, inputs, carried_state, attn_gain, mlp_gain, cosine, sine, length, output_grad, cid
):
    def kernel(
        wq, wk, wv, ws, wo, wg, wu, wd, in_in, carried_in, gain_one, gain_two, cos_in, sin_in, length, grad_ref,
        weights_out, one_out, q_out, k_out, v_out, mix_out, prior_out, hidden_out, down_out, grad_hidden, gain_out,
        sums_out, swish_out, ret_out, out_grad_out,
        weights, one, two, part, grads, packs, got, carried, cos_ref, sin_ref,
        q_ref, k_ref, v_ref, mix_ref, prior_ref, hidden_ref, s_ref, norm_ref, dev_ref, mixed_ref, gate_grad, up_grad,
        total, gh_ref, in_ref,
        *rest,
    ):
        held, row_bufs, bufs, sems = rest[:8], rest[8:13], rest[13:-3], rest[-3:]
        net = Net(*sems)
        c, t = net.c, net.t
        mid, act, swish_grad, ret_grad = one, v_ref, v_ref, gate_grad
        net.greet(XZ_HOPS + Y_HOPS)
        load_in = net.move(in_in, in_ref)
        load_shards = [net.move(a, b) for a, b in zip((wq, wk, wv, ws, wo, wg, wu, wd), held)]
        load_cos, load_sin = net.move(cos_in, cos_ref), net.move(sin_in, sin_ref)
        load_state = net.move(carried_in.at[0, c], carried)
        mine = pl.ds(pl.multiple_of(c * HALF, HALF), HALF)
        load_grad = net.move(grad_ref, grads.at[mine, :])
        own = c * 512 + t * 128
        stores, early = [], []

        def norm_rows(source, gain, rows_ref, lo, count):
            def body(rows):
                at = pl.ds(pl.multiple_of(lo + rows.start, rows.size), rows.size)
                centred, dev = normal(source[at, :].astype(F32), D)
                to = pl.ds(pl.multiple_of(own + at.start, 16), at.size)
                rows_ref[to, :] = (centred * dev * gain[...]).astype(BF)

            loop(count, 32, body)

        def pack(first, last):
            spot = lax.broadcasted_iota(jnp.int32, (64, 128), 0) + c * 64
            place = jnp.where(spot == lax.broadcasted_iota(jnp.int32, (64, 128), 1), 1.0, 0.0).astype(BF)
            for k in range(first, last):
                load_shards[k].wait()
                flat = dot(held[k][...], place, TN).astype(BF)
                for core in range(2):
                    packs[core, STARTS[k] : STARTS[k] + SIZES[k], :] = flat[core * SIZES[k] : (core + 1) * SIZES[k]]

        def keep_weights(lo, hi):
            rows = pl.ds(lo, hi - lo)
            early.append(net.move(weights.at[:, :, rows, :], weights_out.at[:, :, rows, :]))

        w_qk, w_v, w_s, w_o, w_g, w_u, w_d = (
            gather_weights(net, weights, lo, hi)
            for lo, hi in ((0, 512), (512, 944), (944, 1376), (1376, 1808), (1808, 2240), (2240, 2672), (2672, 3104))
        )

        def join(swap, lo, hi):
            swap.wait_recv()
            step = 256 if hi == 512 else 432
            for at in range(lo, hi, step):
                weights[net.x, net.z, at : at + step, :] = packs[c, at : at + step, :] + got[at : at + step, :]

        swap_qk, swap_v, swap_s, swap_rest = (
            net.copy(packs.at[1 - c, pl.ds(lo, hi - lo), :], got.at[pl.ds(lo, hi - lo), :], dc=1)
            for lo, hi in ((0, 512), (512, 944), (944, 1376), (1376, ROWS))
        )
        grad_swap = net.copy(grad_ref, grads.at[mine, :], dc=1)

        y1 = gather_rows(net, one)
        decay = decay_of(net)

        def project_qk():
            wait_all([load_cos, load_sin])

            def body(at):
                cs, sn = cos_ref[at, :], sin_ref[at, :]
                for k, ref in ((0, q_ref), (1, k_ref)):
                    raw = times_flipped(one, at, weights, STARTS[k], SIZES[k])
                    former, latter = raw[:, :128], raw[:, 128:]
                    ref[at, :128] = (former * cs - latter * sn).astype(BF)
                    ref[at, 128:] = (former * sn + latter * cs).astype(BF)

            loop(SEQ, 256, body)
            early.append(net.move(one, one_out))
            stores.extend([net.move(q_ref, q_out), net.move(k_ref, k_out)])

        def project_v():
            def body(at):
                value = times_flipped(one, at, weights, STARTS[2], VDIM)
                v_ref[at, :] = (value * masked(length, at.start, at.size)).astype(BF)

            loop(SEQ, 256, body)
            early.append(net.move(v_ref, v_out))

        def mix():
            fade = {}
            for lo, n, seen, base in causal():
                if lo not in fade:
                    fade[lo] = fades(decay, lo, n, seen)
                at = slice(base + lo, base + lo + n)
                scores = dot(q_ref[at, :], k_ref[base : base + seen, :], NT)
                mix_ref[at, :seen] = (scores * fade[lo]).astype(BF)
                if seen < HALF:
                    mix_ref[at, seen:] = jnp.zeros((n, HALF - seen), BF)
            stores.append(net.move(mix_ref, mix_out))

        def states():
            load_state.wait()
            before = carried[...].T
            prior_ref[0] = before.astype(BF)
            far = lax.broadcasted_iota(jnp.int32, (HALF, 1), 0).astype(F32)
            tail = jnp.exp((HALF - 1.0 - far) * decay)
            local_state = dot((k_ref[:HALF, :].astype(F32) * tail).astype(BF), v_ref[:HALF, :], TN)
            prior_ref[1] = (jnp.exp(HALF * decay) * before + local_state).astype(BF)
            stores.append(net.move(prior_ref, prior_out))

        def retain():
            for lo, n, seen, base in causal():
                at = slice(base + lo, base + lo + n)
                inner = dot(mix_ref[at, :seen], v_ref[base : base + seen, :], NN)
                cross = dot(q_ref[at, :], prior_ref[base // HALF], NN) * heads(decay, lo, n)
                centred, dev = normal(inner + cross, VDIM)
                norm_ref[at, :] = (centred * dev).astype(BF)
                dev_ref[at, :] = dev

        def gate():
            def body(at):
                swish = times_flipped(one, at, weights, STARTS[3], VDIM)
                s_ref[at, :] = swish.astype(BF)
                share = masked(length, at.start, at.size) * (swish * jax.nn.sigmoid(swish))
                mixed_ref[at, :] = (share * norm_ref[at, :].astype(F32)).astype(BF)

            loop(SEQ, 256, body)
            wait_all(early)
            y1[6]()

        def hidden_rows(lo):
            def take(rows, value):
                at = pl.ds(pl.multiple_of(lo + rows.start, rows.size), rows.size)
                hidden_ref[at, :] = in_ref[at, :].astype(F32) + value

            return take

        def grad_rows(lo):
            def take(rows, value):
                total[pl.ds(pl.multiple_of(lo + rows.start, rows.size), rows.size), :] = value

            return take

        def out_rows(rows):
            times_plain(((of(mixed_ref, rows), weights, STARTS[4], VDIM),), part, rows)

        def act_grad_rows(at):
            up_grad[at, :] = times_flipped(grads, at, weights, STARTS[7], VDIM).astype(BF)

        def mlp_rows(rows):
            gate = times_flipped(two, rows, weights, STARTS[5], VDIM)
            up = times_flipped(two, rows, weights, STARTS[6], VDIM)
            back = of(up_grad, rows).astype(F32)
            share = 0.5 + 0.5 * lax.erf(gate * 0.7071067811865476)
            slope = share + gate * (0.3989422804014327 * jnp.exp(-0.5 * gate * gate))
            gelu = gate * share
            put(act, rows, gelu * up)
            back_gate, back_up = (back * up * slope).astype(BF), (back * gelu).astype(BF)
            put(gate_grad, rows, back_gate)
            put(up_grad, rows, back_up)
            times_plain(((back_gate, weights, STARTS[5], VDIM), (back_up, weights, STARTS[6], VDIM)), part, rows)

        def gate_back(rows):
            back = times_flipped(mid, rows, weights, STARTS[4], VDIM) * mask_of(length, rows)
            swish = of(s_ref, rows).astype(F32)
            unit = of(norm_ref, rows).astype(F32)
            share = jax.nn.sigmoid(swish)
            put(swish_grad, rows, back * unit * (share * (1.0 + swish * (1.0 - share))))
            back = back * (swish * share)
            mean = jnp.sum(back, axis=-1, keepdims=True) * (1.0 / VDIM)
            along = jnp.sum(back * unit, axis=-1, keepdims=True) * (1.0 / VDIM)
            put(ret_grad, rows, (back - mean - unit * along) * of(dev_ref, rows))

        def norm_two(lo):
            norm_rows(hidden_ref, gain_two, two, lo, 64)

        def norm_two_back(lo):
            def store(at, value):
                to = pl.ds(pl.multiple_of(own + at.start, 32), 32)
                whole = grads[to, :].astype(F32) + value
                gh_ref[at, :] = whole
                mid[to, :] = whole.astype(BF)

            some = norm_back(lambda at: hidden_ref[at, :], gain_two, lambda at: total[at, :], store, lo, 64)
            gain_out[...] = some if lo == 0 else gain_out[...] + some

        ra0, ra1 = (RowSums(net, part, row_bufs, hidden_rows(lo), lo, 64) for lo in (0, 64))
        rb0, rb1 = (RowSums(net, part, row_bufs, grad_rows(lo), lo, 64) for lo in (0, 64))
        yb0, yb1 = (gather_rows(net, two, lo, 64) for lo in (0, 64))
        yc0, yc1 = (gather_rows(net, mid, lo, 64) for lo in (0, 64))
        rows_a0, rows_b0, rows_a1, rows_b1 = (tile(net, ds, half) for half in (0, 1) for ds in ((2, 1), (-1, 0)))

        def keep(at, value):
            sums_out[pl.ds(at.start - STARTS[5], at.size), :] = value

        split = len(scatter_shapes(864))
        sum_gu = scatter_weights(net, weights, STARTS[5], STARTS[7], bufs[:split], keep)
        sum_d = scatter_weights(net, weights, STARTS[7], ROWS, bufs[split:], keep)

        def grad_of(gathered, cols, rows, k):
            gathered[5]()
            weight_grad(cols, rows, weights, STARTS[k], VDIM)

        def down_rows():
            for gathered in (w_qk, w_v, w_s):
                gathered[5]()

            def body(at):
                values = [dot(act[at, :], wide(weights, x, STARTS[7], VDIM), NN).astype(BF) for x in range(4)]
                for x in range(4):
                    for z in range(4):
                        weights[x, z, at, :] = values[x][:, z * 128 : z * 128 + 128]

            loop(SEQ, 256, body)
            for x in range(4):
                for z in range(4):
                    cols = pl.ds(x * 512 + z * 128, 128)
                    stores.append(net.move(weights.at[x, z, pl.ds(0, SEQ), :], down_out.at[:, cols]))

        def out_grad():
            def keep_piece(x):
                stores.append(net.move(weights.at[x, :, pl.ds(STARTS[4], VDIM), :], out_grad_out.at[x]))

            w_o[5]()
            weight_grad(mixed_ref, mid, weights, STARTS[4], VDIM, keep_piece)

        pack(3, 4)
        pack(4, 8)
        pack(0, 2)
        net.met()
        swap_qk.start()
        load_in.wait()
        norm_rows(in_ref, gain_one, one, 0, 128)
        pack(2, 3)
        swap_v.start()
        swap_s.start()
        join(swap_qk, 0, 512)
        y1[0]()
        w_qk[0]()
        join(swap_s, 944, 1376)
        join(swap_v, 512, 944)
        w_v[0]()
        w_s[0]()
        swap_rest.start()
        join(swap_rest, 1376, ROWS)
        w_qk[1]()
        w_v[1]()
        w_o[0]()
        w_qk[2]()
        y1[1]()
        w_v[2]()
        w_s[1]()
        w_s[2]()
        w_qk[3]()
        y1[4]()
        w_o[1]()
        w_v[3]()
        y1[3]()
        y1[2]()
        w_o[2]()
        y1[5]()
        w_qk[4]()
        keep_weights(0, 512)
        project_qk()
        mix()
        w_v[4]()
        keep_weights(512, 944)
        w_s[3]()
        project_v()
        w_d[0]()
        states()
        w_o[3]()
        retain()
        w_g[0]()
        w_u[0]()
        w_s[4]()
        keep_weights(944, 1376)
        gate()
        w_o[4]()
        w_d[1]()
        out_rows(rows_a0)
        ra0.side(2)
        out_rows(rows_b0)
        ra0.side(1)
        ra0.far()
        out_rows(rows_a1)
        ra1.side(2)
        w_d[2]()
        w_u[1]()
        ra0.side(0)
        w_g[1]()
        grad_swap.start()
        out_rows(rows_b1)
        ra0.side(-1)
        ra1.side(0)
        ra1.far()
        ra0.near()
        ra1.side(1)
        w_d[3]()
        w_g[2]()
        ra1.side(-1)
        ra1.near()
        ra0.finish()
        norm_two(0)
        yb0[0]()
        w_u[2]()
        yb0[2]()
        ra1.finish()
        stores.append(net.move(hidden_ref, hidden_out))
        w_d[4]()
        grad_swap.wait_recv()
        load_grad.wait()
        norm_two(64)
        yb1[0]()
        w_u[3]()
        loop(SEQ, 256, act_grad_rows)
        w_g[3]()
        yb0[1]()
        yb1[1]()
        yb1[2]()
        yb0[3]()
        yb0[4]()
        yb0[5]()
        w_g[4]()
        w_u[4]()
        ra0.sent()
        ra1.sent()
        mlp_rows(rows_a0)
        rb0.side(2)
        yb1[4]()
        mlp_rows(rows_b0)
        rb0.side(1)
        yb1[5]()
        rb0.far()
        yb1[3]()
        mlp_rows(rows_a1)
        rb1.side(2)
        rb1.far()
        rb0.side(-1)
        mlp_rows(rows_b1)
        rb0.near()
        grad_of(w_g, gate_grad, two, 5)
        rb0.side(0)
        rb1.side(0)
        rb1.side(1)
        rb1.side(-1)
        grad_of(w_u, up_grad, two, 6)
        sum_gu[0]()
        rb1.near()
        down_rows()
        grad_of(w_d, act, grads, 7)
        sum_d[0]()
        rb0.finish()
        norm_two_back(0)
        yc0[0]()
        sum_gu[1]()
        rb1.finish()
        norm_two_back(64)
        stores.append(net.move(gh_ref, grad_hidden))
        yc1[0]()
        yc0[1]()
        sum_d[1]()
        yc1[1]()
        sum_gu[2]()
        yc0[4]()
        yc0[3]()
        yc1[3]()
        yc0[2]()
        sum_d[2]()
        yc0[5]()
        gate_back(rows_a0)
        sum_gu[3]()
        yc1[4]()
        gate_back(rows_b0)
        yc1[2]()
        sum_d[3]()
        yc1[5]()
        gate_back(rows_a1)
        gate_back(rows_b1)
        stores += [net.move(ret_grad, ret_out), net.move(swish_grad, swish_out)]
        out_grad()
        sum_gu[4]()
        sum_d[4]()
        net.flush()
        wait_all(stores)

    cols = pltpu.VMEM((SEQ, VDIM), BF)
    rows = pltpu.VMEM((SEQ, D), BF)
    keys = pltpu.VMEM((SEQ, KDIM), BF)
    own = pltpu.VMEM((128, D), F32)
    return call(
        kernel,
        [
            (shape(4, 4, STARTS[4], 128), False),
            (shape(SEQ, D), False),
            (shape(SEQ, KDIM), False),
            (shape(SEQ, KDIM), False),
            (shape(SEQ, VDIM), False),
            (shape(SEQ, HALF), False),
            (shape(2, KDIM, VDIM), False),
            (shape(128, D, kind=F32), False),
            (shape(SEQ, D), False),
            (shape(128, D, kind=F32), False),
            (shape(1, D, kind=F32), True),
            (shape(1296, 128, kind=F32), True),
            (shape(SEQ, VDIM), False),
            (shape(SEQ, VDIM), False),
            (shape(4, 4, 432, 128), False),
        ],
        [(shard, False) for shard in shards]
        + [
            (inputs, False),
            (carried_state, False),
            (attn_gain, True),
            (mlp_gain, True),
            (cosine, False),
            (sine, False),
            (length, SMEM),
            (output_grad, False),
        ],
        [
            pltpu.VMEM((4, 4, ROWS, 128), BF),
            rows,
            rows,
            rows,
            rows,
            pltpu.VMEM((2, ROWS, 128), BF),
            pltpu.VMEM((ROWS, 128), BF),
            pltpu.VMEM((VDIM, KDIM), F32),
            pltpu.VMEM((SEQ, 128), F32),
            pltpu.VMEM((SEQ, 128), F32),
            keys,
            keys,
            cols,
            pltpu.VMEM((SEQ, HALF), BF),
            pltpu.VMEM((2, KDIM, VDIM), BF),
            own,
            cols,
            cols,
            pltpu.VMEM((SEQ, 1), F32),
            cols,
            cols,
            cols,
            own,
            own,
            pltpu.VMEM((128, D), BF),
        ]
        + [pltpu.VMEM(shard.shape, BF) for shard in shards]
        + ROW_BUFS
        + scatter_shapes(864)
        + scatter_shapes(432),
        228,
        64,
        cid,
    )


SPREAD_HOPS = tuple(dict(dt=dt, dc=dc) for dt in (0, 1, 2, -1) for dc in (0, 1) if (dt, dc) != (0, 0))
FAR_HOPS = (dict(dx=2), dict(dz=2))


def retention_back(
    weights_all, rows_one, down_part, q, k, v, mix, prior, swish_grad, ret_grad, out_grad, hidden, grad_hidden, inputs,
    attn_gain, cosine, sine, length, mlp_gain_part, sums_mlp, cid
):

    def kernel(
        w_ref, one_in, down_in, q_in, k_in, v_in, mix_in, prior_in, swish_in, ret_in, out_grad_in, hidden_in, gh_in,
        in_ref, gain, cos_in, sin_in, length, mlp_gain_ref, sums_mlp_ref,
        out_out, in_grad_out, gains_out, sums_all, sums_got, mlp_got,
        out_ref, in_grad, sums_out, weights, sums_ref, one, part, down, q_ref, k_ref, v_ref, mix_ref, prior_ref, swish_grad, ret_grad, hidden_ref,
        gh_ref, cos_ref, sin_ref, q_grad, k_grad, v_grad, score_grad, total, gain_sum, by_group, by_x, by_z,
        *rest,
    ):
        first_bufs, second_bufs, bufs, sems = rest[:5], rest[5:10], rest[10:-3], rest[-3:]
        net = Net(*sems)
        c, t = net.c, net.t
        net.greet(XZ_HOPS + FAR_HOPS + SPREAD_HOPS)

        def moves(*pairs):
            return [net.move(a, b) for a, b in pairs]

        load_score = moves(
            (ret_in, ret_grad), (v_in, v_ref), (k_in, k_ref), (prior_in, prior_ref), (cos_in, cos_ref), (sin_in, sin_ref)
        )
        load_out = moves((out_grad_in, sums_ref.at[:, :, pl.ds(0, 432), :]))
        load_kv = moves((q_in, q_ref), (mix_in, mix_ref))
        load_w = moves((swish_in, swish_grad))
        for lo, to, n in ((STARTS[3], 0, 432), (STARTS[2], 432, 432), (0, 864, 512)):
            load_w += load_weights(net, w_ref, weights, lo, to, n)
        load_one = moves((one_in, one))
        load_down = moves((down_in.at[pl.ds(pl.multiple_of(c * HALF, HALF), HALF), :], down))
        load_last = moves((hidden_in, hidden_ref), (gh_in, gh_ref))
        stores = []
        decay = decay_of(net)

        def turn_back(at, raw):
            cs, sn = cos_ref[at, :], sin_ref[at, :]
            former, latter = raw[:, :128], raw[:, 128:]
            return (former * cs + latter * sn).astype(BF), (latter * cs - former * sn).astype(BF)

        def score():
            wait_all(load_score)
            fade = {}
            for lo, n, seen, base in causal():
                if lo not in fade:
                    fade[lo] = fades(decay, lo, n, seen)
                at, keys = slice(base + lo, base + lo + n), slice(base, base + seen)
                scores = (dot(ret_grad[at, :], v_ref[keys, :], NT) * fade[lo]).astype(BF)
                score_grad[at, :seen] = scores
                if seen < HALF:
                    score_grad[at, seen:] = jnp.zeros((n, HALF - seen), BF)
                cross = dot(ret_grad[at, :], prior_ref[base // HALF], NT) * heads(decay, lo, n)
                q_grad[at, :128], q_grad[at, 128:] = turn_back(at, dot(scores, k_ref[keys, :], NN) + cross)

        def keys_and_values():
            wait_all(load_kv)
            far = lax.broadcasted_iota(jnp.int32, (HALF, 1), 0).astype(F32)
            tail = jnp.exp((HALF - 1.0 - far) * decay)
            ahead = (q_ref[HALF:, :].astype(F32) * jnp.exp((far + 1.0) * decay)).astype(BF)
            grad_local = dot(ahead, ret_grad[HALF:, :], TN).astype(BF)
            for stretch in range(2):
                keys = slice(stretch * HALF, stretch * HALF + HALF)
                raw = dot(score_grad[keys, :], q_ref[keys, :], TN)
                value = dot(mix_ref[keys, :], ret_grad[keys, :], TN)
                if stretch == 0:
                    raw = raw + dot(v_ref[keys, :], grad_local, NT) * tail
                    value = value + dot(k_ref[keys, :], grad_local, NN) * tail
                k_grad[keys, :128], k_grad[keys, 128:] = turn_back(keys, raw)
                v_grad[keys, :] = (value * masked(length, stretch * HALF, HALF)).astype(BF)

        def back_rows(rows):
            terms = (
                (of(swish_grad, rows), weights, 0, 432),
                (of(v_grad, rows), weights, 432, 432),
                (of(q_grad, rows), weights, 864, 256),
                (of(k_grad, rows), weights, 1120, 256),
            )
            times_plain(terms, part, rows)

        def gain_rows(rows):
            for x in range(4):
                at = slice(x * 512, x * 512 + 512)
                along = of(part, rows, at).astype(F32) * of(one, rows, at).astype(F32)
                gain_sum[:, at] = gain_sum[:, at] + jnp.sum(along, axis=0, keepdims=True)

        def output_rows(lo):
            def take(rows, value):
                at = pl.ds(pl.multiple_of(lo + rows.start, rows.size), rows.size)
                out_ref[at, :] = (hidden_ref[at, :] + value).astype(BF)

            return take

        def grad_rows(lo):
            def take(rows, value):
                total[pl.ds(pl.multiple_of(lo + rows.start, rows.size), rows.size), :] = value

            return take

        def norm_one_back(lo):
            def store(at, value):
                in_grad[at, :] = gh_ref[at, :] + value

            norm_back(lambda at: in_ref[at, :].astype(F32), gain, lambda at: total[at, :], store, lo, 64)

        gain_sum[...] = jnp.zeros_like(gain_sum)
        ra0, ra1 = (RowSums(net, down, first_bufs, output_rows(lo), lo, 64, down_in, 0) for lo in (0, 64))
        rb0, rb1 = (RowSums(net, part, second_bufs, grad_rows(lo), lo, 64) for lo in (0, 64))
        rows_a0, rows_b0, rows_a1, rows_b1 = (tile(net, ds, half) for half in (0, 1) for ds in ((2, 1), (-1, 0)))

        def keep(at, value):
            sums_out[at, :] = value

        sums, at = [], 0
        for lo, hi in ((0, 432), (432, 864), (864, 1296), (1296, 1808)):
            n = len(scatter_shapes(hi - lo))
            sums.append(scatter_weights(net, sums_ref, lo, hi, bufs[at : at + n], keep))
            at += n
        sum_o, sum_s, sum_v, sum_qk = sums

        def keys_grad():
            weight_grad(q_grad, one, sums_ref, 1296, 256)
            weight_grad(k_grad, one, sums_ref, 1552, 256)

        def spread(ref, place, hops):
            return [net.copy(ref.at[place], ref.at[place], **hop) for hop in hops]

        def gathered(ref, copies):
            for copy in copies:
                copy.wait_recv()
            value = ref[0]
            for k in range(1, ref.shape[0]):
                value = value + ref[k]
            return value

        def begin():
            by_group[t * 2 + c, 0:1, :] = gain_sum[...] / gain[...]
            by_group[t * 2 + c, 1:2, :] = mlp_gain_ref[...]
            for copy in in_group:
                copy.start()

        def along_x():
            by_x[net.x] = gathered(by_group, in_group)
            for copy in in_x:
                copy.start()

        def along_z():
            by_z[net.z] = gathered(by_x, in_x)
            for copy in in_z:
                copy.start()

        def all_gains():
            gains_out[...] = gathered(by_z, in_z)

        in_group = spread(by_group, t * 2 + c, SPREAD_HOPS)
        in_x = spread(by_x, net.x, (dict(dx=1), dict(dx=-1), dict(dx=2)))
        in_z = spread(by_z, net.z, (dict(dz=1), dict(dz=-1), dict(dz=2)))
        def keep_sums(lo, n):
            stores.append(net.move(sums_out.at[pl.ds(lo, n), :], sums_all.at[pl.ds(lo, n), :]))

        swap_mlp = net.copy(sums_mlp_ref, mlp_got, dc=1)
        swap_o, swap_s, swap_v, swap_qk = (
            net.copy(sums_out.at[pl.ds(lo, n), :], sums_got.at[pl.ds(lo, n), :], dc=1)
            for lo, n in ((0, 432), (432, 432), (864, 432), (1296, 512))
        )
        net.met()
        ra1.side(2)
        wait_all(load_out)
        sum_o[0]()
        score()
        keys_and_values()
        ra0.side(2)
        sum_o[1]()
        wait_all(load_w)
        back_rows(rows_a0)
        rb0.side(2)
        wait_all(load_one)
        gain_rows(rows_a0)
        ra1.side(1)
        ra0.side(1)
        wait_all(load_down)
        ra0.far()
        rb0.side(1)
        weight_grad(v_grad, one, sums_ref, 864, 432)
        sum_v[0]()
        rb0.far()
        keys_grad()
        sum_qk[0]()
        ra0.side(0)
        ra1.far()
        ra0.side(-1)
        back_rows(rows_b0)
        sum_o[2]()
        ra0.near()
        rb0.side(-1)
        ra1.side(-1)
        rb0.side(0)
        sum_v[1]()
        back_rows(rows_a1)
        weight_grad(swish_grad, one, sums_ref, 432, 432)
        rb1.side(2)
        gain_rows(rows_b0)
        rb1.side(1)
        sum_s[0]()
        sum_qk[1]()
        gain_rows(rows_a1)
        ra1.side(0)
        rb0.near()
        rb1.far()
        back_rows(rows_b1)
        sum_v[2]()
        sum_s[1]()
        swap_mlp.start()
        rb1.side(-1)
        gain_rows(rows_b1)
        begin()
        rb1.near()
        rb0.finish()
        sum_qk[2]()
        rb1.side(0)
        sum_o[3]()
        along_x()
        sum_s[2]()
        ra1.near()
        wait_all(load_last)
        ra0.finish()
        sum_v[3]()
        sum_qk[3]()
        sum_o[4]()
        keep_sums(0, 432)
        along_z()
        sum_s[3]()
        swap_o.start()
        rb1.finish()
        norm_one_back(64)
        sum_v[4]()
        keep_sums(864, 432)
        sum_qk[4]()
        keep_sums(1296, 512)
        swap_qk.start()
        swap_v.start()
        norm_one_back(0)
        stores.append(net.move(in_grad, in_grad_out))
        sum_s[4]()
        keep_sums(432, 432)
        swap_s.start()
        ra1.finish()
        stores.append(net.move(out_ref, out_out))
        all_gains()
        for swap in (swap_mlp, swap_o, swap_s, swap_v, swap_qk):
            swap.wait_recv()
        net.flush()
        wait_all(stores)

    cols = pltpu.VMEM((SEQ, VDIM), BF)
    keys = pltpu.VMEM((SEQ, KDIM), BF)
    rows = pltpu.VMEM((SEQ, D), BF)
    own = pltpu.VMEM((128, D), F32)
    return call(
        kernel,
        [
            (shape(128, D), False),
            (shape(128, D, kind=F32), False),
            (shape(2, D, kind=F32), True),
            (shape(1808, 128, kind=F32), False),
            (shape(1808, 128, kind=F32), False),
            (shape(1296, 128, kind=F32), False),
        ],
        [
            (weights_all, False),
            (rows_one, False),
            (down_part, False),
            (q, False),
            (k, False),
            (v, False),
            (mix, False),
            (prior, False),
            (swish_grad, False),
            (ret_grad, False),
            (out_grad, False),
            (hidden, False),
            (grad_hidden, False),
            (inputs, True),
            (attn_gain, True),
            (cosine, False),
            (sine, False),
            (length, SMEM),
            (mlp_gain_part, True),
            (sums_mlp, False),
        ],
        [
            pltpu.VMEM((128, D), BF),
            own,
            pltpu.VMEM((1808, 128), F32),
            pltpu.VMEM((4, 4, 1376, 128), BF),
            pltpu.VMEM((4, 4, 1808, 128), BF),
            rows,
            rows,
            pltpu.VMEM((HALF, D), BF),
            keys,
            keys,
            cols,
            pltpu.VMEM((SEQ, HALF), BF),
            pltpu.VMEM((2, KDIM, VDIM), BF),
            cols,
            cols,
            own,
            own,
            pltpu.VMEM((SEQ, 128), F32),
            pltpu.VMEM((SEQ, 128), F32),
            keys,
            keys,
            cols,
            pltpu.VMEM((SEQ, HALF), BF),
            own,
            pltpu.VMEM((1, D), F32),
            pltpu.VMEM((8, 2, D), F32),
            pltpu.VMEM((4, 2, D), F32),
            pltpu.VMEM((4, 2, D), F32),
        ]
        + ROW_BUFS
        + ROW_BUFS
        + scatter_shapes(432) * 3
        + scatter_shapes(512),
        120,
        48,
        cid,
    )


def hand_out(outputs, input_grad, gains, sums, got, sums_mlp, got_mlp):
    places = (
        (0, 1296, 256), (0, 1552, 256), (0, 864, 432), (0, 432, 432), (0, 0, 432), (1, 0, 432), (1, 432, 432),
        (1, 864, 432),
    )

    def kernel(*refs):
        n = len(outs)
        ins, results, held, made, loads, stores = (
            refs[:7], refs[7 : 7 + n], refs[7 + n : 14 + n], refs[14 + n : 14 + 2 * n], refs[-2], refs[-1]
        )
        arrive = [pltpu.make_async_copy(ins[k], held[k], loads.at[k]) for k in range(7)]
        leave = [pltpu.make_async_copy(made[k], results[k], stores.at[k]) for k in range(n)]
        for k in (5, 6, 3, 4, 1, 0, 2):
            arrive[k].start()
        first_core = lax.axis_index("ctx") == 0
        wait_all([arrive[5], arrive[6]])
        waited = False
        for k in (5, 6, 7, 4, 3, 2, 0, 1):
            which, lo, rows = places[k]
            if which == 0 and not waited:
                wait_all([arrive[3], arrive[4]])
                waited = True
            a, b = (held[at][lo : lo + rows, :] for at in ((3, 4), (5, 6))[which])
            both = jnp.concatenate([jnp.where(first_core, a, b), jnp.where(first_core, b, a)], axis=0).T
            made[4 + k][...] = jnp.where(first_core, both[:64], both[64:])
            leave[4 + k].start()
        wait_all([arrive[0], arrive[1], arrive[2]])
        made[1][...] = held[1][...]
        leave[1].start()
        made[0][...] = held[0][...]
        made[2][...] = held[2][0:1, :]
        made[3][...] = held[2][1:2, :]
        for k in (0, 2, 3):
            leave[k].start()
        wait_all(leave)

    outs = [shape(128, D), shape(128, D, kind=F32), shape(1, D, kind=F32), shape(1, D, kind=F32)]
    for _, _, n in places:
        outs.append(shape(64, 2 * n, kind=F32))
    ins = (outputs, input_grad, gains, sums, got, sums_mlp, got_mlp)
    spec = pl.BlockSpec(memory_space=pl.ANY)
    return pl.pallas_call(
        kernel,
        out_shape=outs,
        in_specs=[spec] * len(ins),
        out_specs=[spec] * len(outs),
        scratch_shapes=[pltpu.VMEM(a.shape, a.dtype) for a in (*ins, *outs)]
        + [pltpu.SemaphoreType.DMA((len(ins),)), pltpu.SemaphoreType.DMA((len(outs),))],
        compiler_params=pltpu.CompilerParams(vmem_limit_bytes=61 * 2**20),
    )(*ins)


def turning_tables():
    frequency = 10000.0 ** (-np.arange(128) / 128.0)
    angles = np.arange(SEQ)[:, None] * frequency[None, :]
    return jnp.asarray(np.cos(angles), F32), jnp.asarray(np.sin(angles), F32)


def on_device(
    inputs,
    seq_lengths,
    carried_state,
    attn_gain,
    query_weight,
    key_weight,
    value_weight,
    swish_weight,
    out_weight,
    mlp_gain,
    gate_weight,
    up_weight,
    down_weight,
    output_grad,
):
    cosine, sine = turning_tables()
    gains = attn_gain[None, :], mlp_gain[None, :]
    shards = (
        query_weight, key_weight, value_weight, swish_weight, out_weight.T, gate_weight, up_weight, down_weight.T
    )
    (
        weights, rows_one, q, k, v, mix, prior, hidden, down_part, grad_hidden, mlp_gain_part, sums_mlp, swish_grad,
        ret_grad, out_grad
    ) = forward_and_mlp_back(
        shards, inputs, carried_state.transpose(0, 1, 3, 2), *gains, cosine, sine, seq_lengths, output_grad, 1
    )
    outputs, input_grad, gain_grads, sums, got_sums, got_mlp = retention_back(
        weights, rows_one, down_part, q, k, v, mix, prior, swish_grad, ret_grad, out_grad, hidden, grad_hidden, inputs,
        gains[0], cosine, sine, seq_lengths, mlp_gain_part, sums_mlp, 2
    )
    outputs, input_grad, first, second, *grads = hand_out(
        outputs, input_grad, gain_grads, sums, got_sums, sums_mlp, got_mlp
    )
    return (
        outputs,
        input_grad,
        first[0],
        grads[0],
        grads[1],
        grads[2],
        grads[3],
        grads[4].T,
        second[0],
        grads[5],
        grads[6],
        grads[7].T,
    )


def solution(mesh):
    placed = (
        P(("fsdp", "ctx", "tp"), None),
        P("fsdp"),
        P("fsdp", "tp", None, None),
        P(),
        P(("fsdp", "ctx"), "tp"),
        P(("fsdp", "ctx"), "tp"),
        P(("fsdp", "ctx"), "tp"),
        P(("fsdp", "ctx"), "tp"),
        P("tp", ("fsdp", "ctx")),
        P(),
        P(("fsdp", "ctx"), "tp"),
        P(("fsdp", "ctx"), "tp"),
        P("tp", ("fsdp", "ctx")),
        P(("fsdp", "ctx"), None),
    )
    return jax.shard_map(
        on_device,
        mesh=mesh,
        in_specs=placed,
        out_specs=(
            P(("fsdp", "ctx", "tp"), None),
            P(("fsdp", "ctx", "tp"), None),
            P(),
            P(("fsdp", "ctx"), "tp"),
            P(("fsdp", "ctx"), "tp"),
            P(("fsdp", "ctx"), "tp"),
            P(("fsdp", "ctx"), "tp"),
            P("tp", ("fsdp", "ctx")),
            P(),
            P(("fsdp", "ctx"), "tp"),
            P(("fsdp", "ctx"), "tp"),
            P("tp", ("fsdp", "ctx")),
        ),
        check_vma=False,
    )
```

```python
import jax
import jax.numpy as jnp
import numpy as np
from jax import lax
from jax.experimental import pallas as pl
from jax.experimental.pallas import tpu as pltpu
from jax.sharding import PartitionSpec as P

D = 2048
KDIM = 256
VDIM = 432
SEQ = 1024
HALF = 512
SIZES = (256, 256, 432, 432, 432, 432, 432, 432)
STARTS = (0, 256, 512, 944, 1376, 1808, 2240, 2672)
ROWS = 3104
EPSILON = 1e-05
MESH = pl.DeviceIdType.MESH
BF = jnp.bfloat16
F32 = jnp.float32


def even(rows):
    return rows // 32 * 16


class Net:
    def __init__(self, send, recv, local):
        group = lax.axis_index("fsdp")
        self.c = lax.axis_index("ctx")
        self.t = lax.axis_index("tp")
        self.x = group // 4
        self.z = group % 4
        self.send, self.recv, self.local = send, recv, local
        self.copies, self.gone, self.moves = [], [], 0

    def dev(self, dx=0, dz=0, dt=0, dc=0):
        x, z, t = ((at + d + 4) % 4 if d else at for at, d in ((self.x, dx), (self.z, dz), (self.t, dt)))
        c = 1 - self.c if dc else self.c
        return (x * 4 + z, c, t)

    def greet(self, hops):
        self.greeted = len(hops)
        for hop in hops:
            pl.semaphore_signal(
                pltpu.get_barrier_semaphore(), inc=1, device_id=self.dev(**hop), device_id_type=MESH
            )

    def met(self):
        pl.semaphore_wait(pltpu.get_barrier_semaphore(), self.greeted)

    def copy(self, src, dst, **hop):
        at = len(self.copies)
        self.copies.append(
            pltpu.make_async_remote_copy(
                src_ref=src,
                dst_ref=dst,
                send_sem=self.send.at[at],
                recv_sem=self.recv.at[at],
                device_id=self.dev(**hop),
                device_id_type=MESH,
            )
        )
        return self.copies[-1]

    def move(self, src, dst):
        copy = pltpu.make_async_copy(src, dst, self.local.at[self.moves])
        self.moves += 1
        copy.start()
        return copy

    def sent(self, copies):
        for copy in copies:
            if not any(copy is other for other in self.gone):
                copy.wait_send()
                self.gone.append(copy)

    def flush(self):
        self.sent(self.copies)


XZ_HOPS = (dict(dx=1), dict(dx=-1), dict(dz=1), dict(dz=-1))
Y_HOPS = (dict(dt=1), dict(dt=-1), dict(dc=1))


def ring_views(net, axis):
    x, z = net.x, net.z
    along_x = lambda ref, d, rows: ref.at[(x + d + 4) % 4, z, rows, :]
    along_z = lambda ref, d, rows: ref.at[x, (z + d + 4) % 4, rows, :]
    all_z = lambda ref, d, rows: ref.at[(x + d + 4) % 4, :, rows, :]
    all_x = lambda ref, d, rows: ref.at[:, (z + d + 4) % 4, rows, :]
    if axis == "x":
        return along_x, all_x, "dx", "dz"
    return along_z, all_z, "dz", "dx"


def gather_weights(net, ref, start, stop):
    cut = start + even(stop - start)
    plans = []
    for axis, lo, hi in (("z", start, cut), ("x", cut, stop)):
        mid = lo + even(hi - lo)
        whole, head, tail = pl.ds(lo, hi - lo), pl.ds(lo, mid - lo), pl.ds(mid, hi - mid)
        first, second, hop_a, hop_b = ring_views(net, axis)
        plan = []
        for view, hop in ((first, hop_a), (second, hop_b)):
            mine = view(ref, 0, whole)
            plan.append(
                (
                    net.copy(mine, mine, **{hop: 1}),
                    net.copy(mine, mine, **{hop: -1}),
                    net.copy(view(ref, -1, head), view(ref, -1, head), **{hop: 1}),
                    net.copy(view(ref, 1, tail), view(ref, 1, tail), **{hop: -1}),
                )
            )
        plans.append(plan)

    def near(phase):
        for plan in plans:
            plan[phase][0].start()
            plan[phase][1].start()

    def far(phase):
        for k in (0, 1):
            for plan in plans:
                plan[phase][k].wait_recv()
                plan[phase][2 + k].start()

    def land(phase):
        for plan in plans:
            plan[phase][2].wait_recv()
            plan[phase][3].wait_recv()

    return [
        lambda: near(0),
        lambda: far(0),
        lambda: (land(0), near(1)),
        lambda: far(1),
        lambda: land(1),
        lambda: net.sent([copy for plan in plans for phase in plan for copy in phase]),
    ]


def add_rows(refs, out, count):
    step = 16

    def body(i, carry):
        at = pl.ds(pl.multiple_of(i * step, step), step)
        total = refs[0](at).astype(F32)
        for ref in refs[1:]:
            total = total + ref(at).astype(F32)
        out(at, total)
        return carry

    lax.fori_loop(0, count // step, body, 0)


def scatter_shapes(rows):
    shapes = []
    cut = even(rows)
    for axis, count in (("z", cut), ("x", rows - cut)):
        head = even(count)
        for pieces in ((4,), ()):
            for n in (head, count - head, count, count):
                shapes.append(pltpu.VMEM((*pieces, n, 128), BF))
    return shapes


def scatter_weights(net, ref, start, stop, bufs, out):
    cut = start + even(stop - start)
    plans = []
    bufs = list(bufs)
    for axis, lo, hi in (("z", start, cut), ("x", cut, stop)):
        mid = lo + even(hi - lo)
        parts = (lo, mid - lo), (mid, hi - mid), (lo, hi - lo)
        head, tail, whole = (pl.ds(*part) for part in parts)
        plan = []
        _, wide, hop_b, hop_a = ring_views(net, "x" if axis == "z" else "z")
        thin = ring_views(net, "z" if axis == "x" else "x")[0]
        for view, hop in ((wide, hop_a), (thin, hop_b)):
            fa, fb, ma, mb = bufs[:4]
            bufs = bufs[4:]
            plan.append(
                dict(
                    view=view,
                    bufs=(fa, fb, ma, mb),
                    copies=(
                        net.copy(view(ref, 2, head), fa, **{hop: 1}),
                        net.copy(view(ref, 2, tail), fb, **{hop: -1}),
                        net.copy(view(ref, 1, whole), ma, **{hop: 1}),
                        net.copy(view(ref, -1, whole), mb, **{hop: -1}),
                    ),
                )
            )
        plans.append((plan, parts))

    def at_rows(view, d, lo):
        def read(at):
            return view(ref, d, pl.ds(lo + at.start, at.size))[...]

        def write(at, value):
            view(ref, d, pl.ds(lo + at.start, at.size))[...] = value.astype(BF)

        return read, write

    def buf_rows(buf):
        if len(buf.shape) == 3:
            return lambda at: buf[:, at, :]
        return lambda at: buf[at, :]

    def far(phase):
        for plan, _ in plans:
            plan[phase]["copies"][0].start()
            plan[phase]["copies"][1].start()

    def near(phase):
        for k, d in ((0, 1), (1, -1)):
            for plan, parts in plans:
                step = plan[phase]
                lo, count = parts[k]
                step["copies"][k].wait_recv()
                read, write = at_rows(step["view"], d, lo)
                add_rows((read, buf_rows(step["bufs"][k])), write, count)
                step["copies"][2 + k].start()

    def total(phase, last):
        for plan, parts in plans:
            step = plan[phase]
            lo, count = parts[2]
            step["copies"][2].wait_recv()
            step["copies"][3].wait_recv()
            read, write = at_rows(step["view"], 0, lo)
            if last:
                write = lambda at, value, lo=lo: out(pl.ds(lo + at.start, at.size), value)
            add_rows((read, buf_rows(step["bufs"][2]), buf_rows(step["bufs"][3])), write, count)

    return [
        lambda: far(0),
        lambda: near(0),
        lambda: (total(0, False), far(1)),
        lambda: near(1),
        lambda: total(1, True),
    ]


def gather_rows(net, ref, first=0, count=128):
    def block(c, t, lo=0, n=count):
        return ref.at[pl.ds(pl.multiple_of(c * 512 + t * 128 + first + lo, 16), n), :]

    c, t = net.c, net.t
    half = count // 2
    before, after, across = (t + 3) % 4, (t + 1) % 4, (t + 2) % 4
    own = block(c, t)
    up = net.copy(own, own, dt=1)
    down = net.copy(own, own, dt=-1)
    side = net.copy(own, own, dc=1)
    fore = net.copy(block(c, before, 0, half), block(c, before, 0, half), dt=1)
    back = net.copy(block(c, after, half, half), block(c, after, half, half), dt=-1)
    over = [
        net.copy(block(c, before), block(c, before), dc=1),
        net.copy(block(c, after), block(c, after), dc=1),
        net.copy(block(c, across, 0, half), block(c, across, 0, half), dc=1),
        net.copy(block(c, across, half, half), block(c, across, half, half), dc=1),
    ]

    def start():
        up.start()
        down.start()
        side.start()

    def forward():
        up.wait_recv()
        fore.start()
        over[0].start()
        down.wait_recv()
        back.start()
        over[1].start()

    def beside():
        side.wait_recv()

    def near():
        over[0].wait_recv()
        over[1].wait_recv()

    def far():
        fore.wait_recv()
        over[2].start()
        back.wait_recv()
        over[3].start()

    def last():
        over[2].wait_recv()
        over[3].wait_recv()

    def sent():
        net.sent((up, down, side, fore, back, *over))

    return start, forward, beside, near, far, last, sent


ROW_BUFS = [
    pltpu.VMEM((512, D), BF),
    pltpu.VMEM((64, D), BF),
    pltpu.VMEM((64, D), BF),
    pltpu.VMEM((128, D), BF),
    pltpu.VMEM((128, D), BF),
]


class RowSums:
    def __init__(self, net, ref, bufs, out, lo=0, count=128, source=None, first=None):
        c, t = net.c, net.t
        self.net, self.t, self.ref, self.out, self.lo, self.count = net, t, ref, out, lo, count
        self.first = c * HALF if first is None else first
        self.half = count // 2
        other, far_a, far_b, near_a, near_b = bufs
        self.other = other
        self.far_a, self.far_b = (far.at[pl.ds(lo // 2, self.half), :] for far in (far_a, far_b))
        self.near_a, self.near_b = (near.at[pl.ds(lo, count), :] for near in (near_a, near_b))
        source = ref if source is None else source
        self.sides = {}
        for d in (2, 1, -1, 0):
            row = self.row(d)
            self.sides[d] = net.copy(
                source.at[pl.ds(pl.multiple_of((1 - c) * HALF + row, 64), count), :],
                other.at[pl.ds(pl.multiple_of(row, 64), count), :],
                dc=1,
            )
        self.hops = (
            net.copy(self.block(2, 0, self.half), self.far_a, dt=1),
            net.copy(self.block(2, self.half, self.half), self.far_b, dt=-1),
            net.copy(self.block(1), self.near_a, dt=1),
            net.copy(self.block(-1), self.near_b, dt=-1),
        )

    def row(self, d, lo=0):
        return (self.t + d + 4) % 4 * 128 + self.lo + lo

    def block(self, d, lo=0, n=None):
        return self.ref.at[pl.ds(pl.multiple_of(self.first + self.row(d, lo), 16), n or self.count), :]

    def mine(self, d, lo=0):
        return self.read(self.ref, self.first + self.row(d, lo)), self.read(self.other, self.row(d, lo))

    @staticmethod
    def read(source, base):
        return lambda at: source[pl.ds(pl.multiple_of(base + at.start, 16), at.size), :]

    def keep(self, d, lo=0):
        base = self.first + self.row(d, lo)

        def store(at, value):
            self.ref[pl.ds(pl.multiple_of(base + at.start, 16), at.size), :] = value.astype(BF)

        return store

    def side(self, d):
        self.sides[d].start()

    def far(self):
        self.sides[2].wait_recv()
        for k in (0, 1):
            add_rows(self.mine(2, k * self.half), self.keep(2, k * self.half), self.half)
            self.hops[k].start()

    def near(self):
        for k, d, buf in ((0, 1, self.far_a), (1, -1, self.far_b)):
            lo, rest = k * self.half, (1 - k) * self.half
            self.sides[d].wait_recv()
            add_rows(self.mine(d, rest), self.keep(d, rest), self.half)
            self.hops[k].wait_recv()
            add_rows((*self.mine(d, lo), self.read(buf, 0)), self.keep(d, lo), self.half)
            self.hops[2 + k].start()

    def finish(self):
        self.sides[0].wait_recv()
        self.hops[2].wait_recv()
        self.hops[3].wait_recv()
        add_rows((*self.mine(0), self.read(self.near_a, 0), self.read(self.near_b, 0)), self.out, self.count)

    def sent(self):
        self.net.sent([*self.sides.values(), *self.hops])


SMEM = pl.BlockSpec(memory_space=pltpu.SMEM)


def call(kernel, outs, ins, scratch, copies, moves, cid):
    any_spec = pl.BlockSpec(memory_space=pl.ANY)
    vmem_spec = pl.BlockSpec(memory_space=pltpu.VMEM)
    return pl.pallas_call(
        kernel,
        out_shape=[shape for shape, _ in outs],
        in_specs=[SMEM if v is SMEM else vmem_spec if v else any_spec for _, v in ins],
        out_specs=[vmem_spec if v else any_spec for _, v in outs],
        scratch_shapes=list(scratch)
        + [
            pltpu.SemaphoreType.DMA((copies,)),
            pltpu.SemaphoreType.DMA((copies,)),
            pltpu.SemaphoreType.DMA((moves,)),
        ],
        compiler_params=pltpu.CompilerParams(
            collective_id=cid, has_side_effects=True, vmem_limit_bytes=61 * 2**20
        ),
    )(*[array for array, _ in ins])


def shape(*dims, kind=BF):
    return jax.ShapeDtypeStruct(dims, kind)


def dot(a, b, dims):
    return lax.dot_general(a, b, (dims, ((), ())), preferred_element_type=F32)


NN = ((1,), (0,))
NT = ((1,), (1,))
TN = ((0,), (0,))


def normal(rows, width):
    centred = rows - jnp.sum(rows, axis=-1, keepdims=True) * (1.0 / width)
    spread = jnp.sum(centred * centred, axis=-1, keepdims=True) * (1.0 / width)
    return centred, lax.rsqrt(spread + EPSILON)


def loop(count, step, body):
    def turn(i, carry):
        body(pl.ds(pl.multiple_of(i * step, step), step))
        return carry

    lax.fori_loop(0, count // step, turn, 0)


def pair(net, d):
    lo = (net.t + d + 4) % 4 * 128
    return tuple(pl.ds(pl.multiple_of(c * HALF + lo, 128), 128) for c in (1 - net.c, net.c))


def tile(net, ds, half):
    rows = []
    for d in ds:
        lo = (net.t + d + 4) % 4 * 128 + half * 64
        rows += [pl.ds(pl.multiple_of(c * HALF + lo, 64), 64) for c in (1 - net.c, net.c)]
    return tuple(rows)


def of(ref, rows, cols=slice(None)):
    if isinstance(rows, tuple):
        return jnp.concatenate([ref[at, cols] for at in rows], axis=0)
    return ref[rows, cols]


def put(ref, rows, value, cols=slice(None)):
    if isinstance(rows, tuple):
        for k, at in enumerate(rows):
            ref[at, cols] = value[k * at.size : (k + 1) * at.size].astype(ref.dtype)
    else:
        ref[rows, cols] = value.astype(ref.dtype)


def wide(weights, x, start, count):
    return jnp.concatenate([weights[x, z, start : start + count, :] for z in range(4)], axis=1)


def times_flipped(ref, rows, weights, start, count):
    total = None
    for x in range(4):
        part = dot(of(ref, rows, slice(x * 512, x * 512 + 512)), wide(weights, x, start, count), NT)
        total = part if total is None else total + part
    return total


def times_plain(terms, out, rows):
    for x in range(4):
        total = None
        for value, weights, start, count in terms:
            part = dot(value, wide(weights, x, start, count), NN)
            total = part if total is None else total + part
        put(out, rows, total, slice(x * 512, x * 512 + 512))


def weight_grad(cols, rows, out, start, count, then=lambda x: None):
    for x in range(4):
        grad = dot(cols[...], rows[:, x * 512 : x * 512 + 512], TN).astype(BF)
        for z in range(4):
            out[x, z, start : start + count, :] = grad[:, z * 128 : z * 128 + 128]
        then(x)


def wait_all(copies):
    for copy in copies:
        copy.wait()


def masked(length, start, rows):
    place = lax.broadcasted_iota(jnp.int32, (rows, 1), 0) + start
    return jnp.where(place < length[0], 1.0, 0.0)


def mask_of(length, rows):
    return jnp.concatenate([masked(length, at.start, at.size) for at in rows], axis=0)


def decay_of(net):
    by_t = jnp.where(net.t % 2 == 1, 0.25, 1.0) * jnp.where(net.t // 2 == 1, 0.0625, 1.0)
    return jnp.where(net.c == 1, 0.5, 1.0) * by_t * (-32.0 / SEQ)


def fades(decay, start, rows, keys):
    n = lax.broadcasted_iota(jnp.int32, (rows, keys), 0) + start
    distance = (n - lax.broadcasted_iota(jnp.int32, (rows, keys), 1)).astype(F32)
    return jnp.where(distance >= 0.0, jnp.exp(jnp.maximum(distance, 0.0) * decay), 0.0)


def heads(decay, start, rows):
    ahead = lax.broadcasted_iota(jnp.int32, (rows, 1), 0) + start + 1
    return jnp.exp(ahead.astype(F32) * decay)


def causal():
    for lo in range(0, HALF, 128):
        for base in (0, HALF):
            yield lo, 128, lo + 128, base


def norm_back(source, gain, grad, out, lo=0, count=128):
    def body(i, total):
        at = pl.ds(pl.multiple_of(lo + i * 32, 32), 32)
        centred, dev = normal(source(at), D)
        normed = centred * dev
        back = grad(at)
        scaled = back * gain[...]
        mean = jnp.sum(scaled, axis=-1, keepdims=True) * (1.0 / D)
        along = jnp.sum(scaled * normed, axis=-1, keepdims=True) * (1.0 / D)
        out(at, dev * (scaled - mean - normed * along))
        return total + jnp.sum(back * normed, axis=0, keepdims=True)

    return lax.fori_loop(0, count // 32, body, jnp.zeros((1, D), F32))


def load_weights(net, source, weights, lo, to, rows):
    return [net.move(source.at[:, :, pl.ds(lo, rows), :], weights.at[:, :, pl.ds(to, rows), :])]


def forward_and_mlp_back(
    shards, inputs, carried_state, attn_gain, mlp_gain, cosine, sine, length, output_grad, cid
):
    def kernel(
        wq, wk, wv, ws, wo, wg, wu, wd, in_in, carried_in, gain_one, gain_two, cos_in, sin_in, length, grad_ref,
        weights_out, one_out, q_out, k_out, v_out, mix_out, prior_out, hidden_out, down_out, grad_hidden, gain_out,
        sums_out, swish_out, ret_out, out_grad_out,
        weights, one, two, part, grads, packs, got, carried, cos_ref, sin_ref,
        q_ref, k_ref, v_ref, mix_ref, prior_ref, hidden_ref, s_ref, norm_ref, dev_ref, mixed_ref, gate_grad, up_grad,
        total, gh_ref, in_ref,
        *rest,
    ):
        held, row_bufs, bufs, sems = rest[:8], rest[8:13], rest[13:-3], rest[-3:]
        net = Net(*sems)
        c, t = net.c, net.t
        mid, act, swish_grad, ret_grad = one, v_ref, v_ref, gate_grad
        net.greet(XZ_HOPS + Y_HOPS)
        load_in = net.move(in_in, in_ref)
        load_shards = [net.move(a, b) for a, b in zip((wq, wk, wv, ws, wo, wg, wu, wd), held)]
        load_cos, load_sin = net.move(cos_in, cos_ref), net.move(sin_in, sin_ref)
        load_state = net.move(carried_in.at[0, c], carried)
        mine = pl.ds(pl.multiple_of(c * HALF, HALF), HALF)
        load_grad = net.move(grad_ref, grads.at[mine, :])
        own = c * 512 + t * 128
        stores, early = [], []

        def norm_rows(source, gain, rows_ref, lo, count):
            def body(rows):
                at = pl.ds(pl.multiple_of(lo + rows.start, rows.size), rows.size)
                centred, dev = normal(source[at, :].astype(F32), D)
                to = pl.ds(pl.multiple_of(own + at.start, 16), at.size)
                rows_ref[to, :] = (centred * dev * gain[...]).astype(BF)

            loop(count, 32, body)

        def pack(first, last):
            spot = lax.broadcasted_iota(jnp.int32, (64, 128), 0) + c * 64
            place = jnp.where(spot == lax.broadcasted_iota(jnp.int32, (64, 128), 1), 1.0, 0.0).astype(BF)
            for k in range(first, last):
                load_shards[k].wait()
                flat = dot(held[k][...], place, TN).astype(BF)
                for core in range(2):
                    packs[core, STARTS[k] : STARTS[k] + SIZES[k], :] = flat[core * SIZES[k] : (core + 1) * SIZES[k]]

        def keep_weights(lo, hi):
            rows = pl.ds(lo, hi - lo)
            early.append(net.move(weights.at[:, :, rows, :], weights_out.at[:, :, rows, :]))

        w_qk, w_v, w_s, w_o, w_g, w_u, w_d = (
            gather_weights(net, weights, lo, hi)
            for lo, hi in ((0, 512), (512, 944), (944, 1376), (1376, 1808), (1808, 2240), (2240, 2672), (2672, 3104))
        )

        def join(swap, lo, hi):
            swap.wait_recv()
            step = 256 if hi == 512 else 432
            for at in range(lo, hi, step):
                weights[net.x, net.z, at : at + step, :] = packs[c, at : at + step, :] + got[at : at + step, :]

        swap_qk, swap_v, swap_s, swap_rest = (
            net.copy(packs.at[1 - c, pl.ds(lo, hi - lo), :], got.at[pl.ds(lo, hi - lo), :], dc=1)
            for lo, hi in ((0, 512), (512, 944), (944, 1376), (1376, ROWS))
        )
        grad_swap = net.copy(grad_ref, grads.at[mine, :], dc=1)

        y1 = gather_rows(net, one)
        decay = decay_of(net)

        def project_qk(ds):
            wait_all([load_cos, load_sin] if 0 in ds else [])
            for d in ds:
                rows = pair(net, d)
                cs, sn = of(cos_ref, rows), of(sin_ref, rows)
                for k, ref in ((0, q_ref), (1, k_ref)):
                    raw = times_flipped(one, rows, weights, STARTS[k], SIZES[k])
                    former, latter = raw[:, :128], raw[:, 128:]
                    put(ref, rows, former * cs - latter * sn, slice(0, 128))
                    put(ref, rows, former * sn + latter * cs, slice(128, 256))
            if 2 in ds:
                early.append(net.move(one, one_out))
                stores.extend([net.move(q_ref, q_out), net.move(k_ref, k_out)])

        def project_v(ds):
            for d in ds:
                rows = pair(net, d)
                value = times_flipped(one, rows, weights, STARTS[2], VDIM)
                put(v_ref, rows, value * mask_of(length, rows))
            if 2 in ds:
                early.append(net.move(v_ref, v_out))

        def mix():
            fade = {}
            for lo, n, seen, base in causal():
                if lo not in fade:
                    fade[lo] = fades(decay, lo, n, seen)
                at = slice(base + lo, base + lo + n)
                scores = dot(q_ref[at, :], k_ref[base : base + seen, :], NT)
                mix_ref[at, :seen] = (scores * fade[lo]).astype(BF)
                if seen < HALF:
                    mix_ref[at, seen:] = jnp.zeros((n, HALF - seen), BF)
            stores.append(net.move(mix_ref, mix_out))

        def states():
            load_state.wait()
            before = carried[...].T
            prior_ref[0] = before.astype(BF)
            far = lax.broadcasted_iota(jnp.int32, (HALF, 1), 0).astype(F32)
            tail = jnp.exp((HALF - 1.0 - far) * decay)
            local_state = dot((k_ref[:HALF, :].astype(F32) * tail).astype(BF), v_ref[:HALF, :], TN)
            prior_ref[1] = (jnp.exp(HALF * decay) * before + local_state).astype(BF)
            stores.append(net.move(prior_ref, prior_out))

        def retain():
            for lo, n, seen, base in causal():
                at = slice(base + lo, base + lo + n)
                inner = dot(mix_ref[at, :seen], v_ref[base : base + seen, :], NN)
                cross = dot(q_ref[at, :], prior_ref[base // HALF], NN) * heads(decay, lo, n)
                centred, dev = normal(inner + cross, VDIM)
                norm_ref[at, :] = (centred * dev).astype(BF)
                dev_ref[at, :] = dev

        def gate():
            def body(at):
                swish = times_flipped(one, at, weights, STARTS[3], VDIM)
                s_ref[at, :] = swish.astype(BF)
                share = masked(length, at.start, at.size) * (swish * jax.nn.sigmoid(swish))
                mixed_ref[at, :] = (share * norm_ref[at, :].astype(F32)).astype(BF)

            loop(SEQ, 256, body)
            wait_all(early)
            y1[6]()

        def hidden_rows(lo):
            def take(rows, value):
                at = pl.ds(pl.multiple_of(lo + rows.start, rows.size), rows.size)
                hidden_ref[at, :] = in_ref[at, :].astype(F32) + value

            return take

        def grad_rows(lo):
            def take(rows, value):
                total[pl.ds(pl.multiple_of(lo + rows.start, rows.size), rows.size), :] = value

            return take

        def out_rows(rows):
            times_plain(((of(mixed_ref, rows), weights, STARTS[4], VDIM),), part, rows)

        def act_grad_rows(at):
            up_grad[at, :] = times_flipped(grads, at, weights, STARTS[7], VDIM).astype(BF)

        def mlp_rows(rows):
            gate = times_flipped(two, rows, weights, STARTS[5], VDIM)
            up = times_flipped(two, rows, weights, STARTS[6], VDIM)
            back = of(up_grad, rows).astype(F32)
            share = 0.5 + 0.5 * lax.erf(gate * 0.7071067811865476)
            slope = share + gate * (0.3989422804014327 * jnp.exp(-0.5 * gate * gate))
            gelu = gate * share
            put(act, rows, gelu * up)
            back_gate, back_up = (back * up * slope).astype(BF), (back * gelu).astype(BF)
            put(gate_grad, rows, back_gate)
            put(up_grad, rows, back_up)
            times_plain(((back_gate, weights, STARTS[5], VDIM), (back_up, weights, STARTS[6], VDIM)), part, rows)

        def gate_back(rows):
            back = times_flipped(mid, rows, weights, STARTS[4], VDIM) * mask_of(length, rows)
            swish = of(s_ref, rows).astype(F32)
            unit = of(norm_ref, rows).astype(F32)
            share = jax.nn.sigmoid(swish)
            put(swish_grad, rows, back * unit * (share * (1.0 + swish * (1.0 - share))))
            back = back * (swish * share)
            mean = jnp.sum(back, axis=-1, keepdims=True) * (1.0 / VDIM)
            along = jnp.sum(back * unit, axis=-1, keepdims=True) * (1.0 / VDIM)
            put(ret_grad, rows, (back - mean - unit * along) * of(dev_ref, rows))

        def norm_two(lo):
            norm_rows(hidden_ref, gain_two, two, lo, 64)

        def norm_two_back(lo):
            def store(at, value):
                to = pl.ds(pl.multiple_of(own + at.start, 32), 32)
                whole = grads[to, :].astype(F32) + value
                gh_ref[at, :] = whole
                mid[to, :] = whole.astype(BF)

            some = norm_back(lambda at: hidden_ref[at, :], gain_two, lambda at: total[at, :], store, lo, 64)
            gain_out[...] = some if lo == 0 else gain_out[...] + some

        ra0, ra1 = (RowSums(net, part, row_bufs, hidden_rows(lo), lo, 64) for lo in (0, 64))
        rb0, rb1 = (RowSums(net, part, row_bufs, grad_rows(lo), lo, 64) for lo in (0, 64))
        yb0, yb1 = (gather_rows(net, two, lo, 64) for lo in (0, 64))
        yc0, yc1 = (gather_rows(net, mid, lo, 64) for lo in (0, 64))
        rows_a0, rows_b0, rows_a1, rows_b1 = (tile(net, ds, half) for half in (0, 1) for ds in ((2, 1), (-1, 0)))

        def keep(at, value):
            sums_out[pl.ds(at.start - STARTS[5], at.size), :] = value

        split = len(scatter_shapes(864))
        sum_gu = scatter_weights(net, weights, STARTS[5], STARTS[7], bufs[:split], keep)
        sum_d = scatter_weights(net, weights, STARTS[7], ROWS, bufs[split:], keep)

        def grad_of(gathered, cols, rows, k):
            gathered[5]()
            weight_grad(cols, rows, weights, STARTS[k], VDIM)

        def down_rows():
            for gathered in (w_qk, w_v, w_s):
                gathered[5]()

            def body(at):
                values = [dot(act[at, :], wide(weights, x, STARTS[7], VDIM), NN).astype(BF) for x in range(4)]
                for x in range(4):
                    for z in range(4):
                        weights[x, z, at, :] = values[x][:, z * 128 : z * 128 + 128]

            loop(SEQ, 256, body)
            for x in range(4):
                for z in range(4):
                    cols = pl.ds(x * 512 + z * 128, 128)
                    stores.append(net.move(weights.at[x, z, pl.ds(0, SEQ), :], down_out.at[:, cols]))

        def out_grad():
            def keep_piece(x):
                stores.append(net.move(weights.at[x, :, pl.ds(STARTS[4], VDIM), :], out_grad_out.at[x]))

            w_o[5]()
            weight_grad(mixed_ref, mid, weights, STARTS[4], VDIM, keep_piece)

        pack(2, 3)
        pack(3, 4)
        pack(0, 2)
        load_in.wait()
        norm_rows(in_ref, gain_one, one, 0, 128)
        net.met()
        swap_qk.start()
        join(swap_qk, 0, 512)
        w_qk[0]()
        swap_v.start()
        y1[0]()
        pack(4, 8)
        swap_s.start()
        join(swap_v, 512, 944)
        w_v[0]()
        join(swap_s, 944, 1376)
        swap_rest.start()
        y1[2]()
        w_s[0]()
        w_qk[1]()
        join(swap_rest, 1376, ROWS)
        w_o[0]()
        w_v[1]()
        w_s[1]()
        w_qk[2]()
        w_o[1]()
        y1[1]()
        w_v[2]()
        w_qk[3]()
        w_s[2]()
        y1[3]()
        w_v[3]()
        y1[4]()
        y1[5]()
        w_qk[4]()
        keep_weights(0, 512)
        w_o[2]()
        project_qk((0, 1, -1))
        project_qk((2,))
        w_v[4]()
        keep_weights(512, 944)
        mix()
        w_s[3]()
        project_v((0, 1, -1))
        project_v((2,))
        w_d[0]()
        states()
        w_o[3]()
        retain()
        w_g[0]()
        w_s[4]()
        keep_weights(944, 1376)
        gate()
        w_d[1]()
        w_u[0]()
        w_o[4]()
        out_rows(rows_a0)
        ra0.side(2)
        out_rows(rows_b0)
        ra0.far()
        out_rows(rows_a1)
        ra1.side(1)
        ra1.side(2)
        w_d[2]()
        out_rows(rows_b1)
        w_g[1]()
        ra1.side(-1)
        w_u[1]()
        ra0.side(1)
        ra0.side(-1)
        ra1.far()
        ra0.near()
        grad_swap.start()
        w_u[2]()
        grad_swap.wait_recv()
        load_grad.wait()
        ra1.side(0)
        ra1.near()
        ra0.side(0)
        w_g[2]()
        ra0.finish()
        norm_two(0)
        w_d[3]()
        w_u[3]()
        yb0[0]()
        ra1.finish()
        stores.append(net.move(hidden_ref, hidden_out))
        norm_two(64)
        yb1[0]()
        w_g[3]()
        yb1[2]()
        w_g[4]()
        w_d[4]()
        yb0[1]()
        loop(SEQ, 256, act_grad_rows)
        yb1[1]()
        yb0[4]()
        w_u[4]()
        yb0[5]()
        yb0[2]()
        yb0[3]()
        ra0.sent()
        ra1.sent()
        mlp_rows(rows_a0)
        rb0.side(2)
        yb1[3]()
        yb1[4]()
        mlp_rows(rows_b0)
        yb1[5]()
        rb0.side(1)
        rb0.far()
        mlp_rows(rows_a1)
        rb1.side(2)
        mlp_rows(rows_b1)
        rb1.far()
        rb0.side(-1)
        rb1.side(0)
        grad_of(w_u, up_grad, two, 6)
        rb0.near()
        grad_of(w_g, gate_grad, two, 5)
        rb0.side(0)
        rb1.side(-1)
        sum_gu[0]()
        rb1.side(1)
        down_rows()
        rb1.near()
        grad_of(w_d, act, grads, 7)
        sum_d[0]()
        sum_gu[1]()
        rb0.finish()
        norm_two_back(0)
        yc0[0]()
        yc0[2]()
        rb1.finish()
        norm_two_back(64)
        stores.append(net.move(gh_ref, grad_hidden))
        yc1[0]()
        yc0[1]()
        sum_d[1]()
        sum_gu[2]()
        yc1[1]()
        sum_gu[3]()
        yc0[4]()
        yc0[5]()
        yc1[2]()
        yc0[3]()
        sum_d[2]()
        gate_back(rows_a0)
        yc1[4]()
        yc1[3]()
        gate_back(rows_b0)
        sum_gu[4]()
        sum_d[3]()
        yc1[5]()
        gate_back(rows_a1)
        gate_back(rows_b1)
        stores += [net.move(ret_grad, ret_out), net.move(swish_grad, swish_out)]
        out_grad()
        sum_d[4]()
        net.flush()
        wait_all(stores)

    cols = pltpu.VMEM((SEQ, VDIM), BF)
    rows = pltpu.VMEM((SEQ, D), BF)
    keys = pltpu.VMEM((SEQ, KDIM), BF)
    own = pltpu.VMEM((128, D), F32)
    return call(
        kernel,
        [
            (shape(4, 4, STARTS[4], 128), False),
            (shape(SEQ, D), False),
            (shape(SEQ, KDIM), False),
            (shape(SEQ, KDIM), False),
            (shape(SEQ, VDIM), False),
            (shape(SEQ, HALF), False),
            (shape(2, KDIM, VDIM), False),
            (shape(128, D, kind=F32), False),
            (shape(SEQ, D), False),
            (shape(128, D, kind=F32), False),
            (shape(1, D, kind=F32), True),
            (shape(1296, 128, kind=F32), True),
            (shape(SEQ, VDIM), False),
            (shape(SEQ, VDIM), False),
            (shape(4, 4, 432, 128), False),
        ],
        [(shard, False) for shard in shards]
        + [
            (inputs, False),
            (carried_state, False),
            (attn_gain, True),
            (mlp_gain, True),
            (cosine, False),
            (sine, False),
            (length, SMEM),
            (output_grad, False),
        ],
        [
            pltpu.VMEM((4, 4, ROWS, 128), BF),
            rows,
            rows,
            rows,
            rows,
            pltpu.VMEM((2, ROWS, 128), BF),
            pltpu.VMEM((ROWS, 128), BF),
            pltpu.VMEM((VDIM, KDIM), F32),
            pltpu.VMEM((SEQ, 128), F32),
            pltpu.VMEM((SEQ, 128), F32),
            keys,
            keys,
            cols,
            pltpu.VMEM((SEQ, HALF), BF),
            pltpu.VMEM((2, KDIM, VDIM), BF),
            own,
            cols,
            cols,
            pltpu.VMEM((SEQ, 1), F32),
            cols,
            cols,
            cols,
            own,
            own,
            pltpu.VMEM((128, D), BF),
        ]
        + [pltpu.VMEM(shard.shape, BF) for shard in shards]
        + ROW_BUFS
        + scatter_shapes(864)
        + scatter_shapes(432),
        228,
        64,
        cid,
    )


SPREAD_HOPS = tuple(dict(dt=dt, dc=dc) for dt in (0, 1, 2, -1) for dc in (0, 1) if (dt, dc) != (0, 0))
FAR_HOPS = (dict(dx=2), dict(dz=2))


def retention_back(
    weights_all, rows_one, down_part, q, k, v, mix, prior, swish_grad, ret_grad, out_grad, hidden, grad_hidden, inputs,
    attn_gain, cosine, sine, length, mlp_gain_part, sums_mlp, cid
):

    def kernel(
        w_ref, one_in, down_in, q_in, k_in, v_in, mix_in, prior_in, swish_in, ret_in, out_grad_in, hidden_in, gh_in,
        in_ref, gain, cos_in, sin_in, length, mlp_gain_ref, sums_mlp_ref,
        out_out, in_grad_out, gains_out, sums_all, sums_got, mlp_got,
        out_ref, in_grad, sums_out, weights, sums_ref, one, part, down, q_ref, k_ref, v_ref, mix_ref, prior_ref, swish_grad, ret_grad, hidden_ref,
        gh_ref, cos_ref, sin_ref, q_grad, k_grad, v_grad, score_grad, total, gain_sum, by_group, by_x, by_z,
        *rest,
    ):
        first_bufs, second_bufs, bufs, sems = rest[:5], rest[5:10], rest[10:-3], rest[-3:]
        net = Net(*sems)
        c, t = net.c, net.t
        net.greet(XZ_HOPS + FAR_HOPS + SPREAD_HOPS)

        def moves(*pairs):
            return [net.move(a, b) for a, b in pairs]

        load_score = moves(
            (ret_in, ret_grad), (v_in, v_ref), (k_in, k_ref), (prior_in, prior_ref), (cos_in, cos_ref), (sin_in, sin_ref)
        )
        load_out = moves((out_grad_in, sums_ref.at[:, :, pl.ds(0, 432), :]))
        load_kv = moves((q_in, q_ref), (mix_in, mix_ref))
        load_w = moves((swish_in, swish_grad))
        for lo, to, n in ((STARTS[3], 0, 432), (STARTS[2], 432, 432), (0, 864, 512)):
            load_w += load_weights(net, w_ref, weights, lo, to, n)
        load_one = moves((one_in, one))
        load_down = moves((down_in.at[pl.ds(pl.multiple_of(c * HALF, HALF), HALF), :], down))
        load_last = moves((hidden_in, hidden_ref), (gh_in, gh_ref))
        stores = []
        decay = decay_of(net)

        def turn_back(at, raw):
            cs, sn = cos_ref[at, :], sin_ref[at, :]
            former, latter = raw[:, :128], raw[:, 128:]
            return (former * cs + latter * sn).astype(BF), (latter * cs - former * sn).astype(BF)

        def score():
            wait_all(load_score)
            fade = {}
            for lo, n, seen, base in causal():
                if lo not in fade:
                    fade[lo] = fades(decay, lo, n, seen)
                at, keys = slice(base + lo, base + lo + n), slice(base, base + seen)
                scores = (dot(ret_grad[at, :], v_ref[keys, :], NT) * fade[lo]).astype(BF)
                score_grad[at, :seen] = scores
                if seen < HALF:
                    score_grad[at, seen:] = jnp.zeros((n, HALF - seen), BF)
                cross = dot(ret_grad[at, :], prior_ref[base // HALF], NT) * heads(decay, lo, n)
                q_grad[at, :128], q_grad[at, 128:] = turn_back(at, dot(scores, k_ref[keys, :], NN) + cross)

        def keys_and_values():
            wait_all(load_kv)
            far = lax.broadcasted_iota(jnp.int32, (HALF, 1), 0).astype(F32)
            tail = jnp.exp((HALF - 1.0 - far) * decay)
            ahead = (q_ref[HALF:, :].astype(F32) * jnp.exp((far + 1.0) * decay)).astype(BF)
            grad_local = dot(ahead, ret_grad[HALF:, :], TN).astype(BF)
            for stretch in range(2):
                keys = slice(stretch * HALF, stretch * HALF + HALF)
                raw = dot(score_grad[keys, :], q_ref[keys, :], TN)
                value = dot(mix_ref[keys, :], ret_grad[keys, :], TN)
                if stretch == 0:
                    raw = raw + dot(v_ref[keys, :], grad_local, NT) * tail
                    value = value + dot(k_ref[keys, :], grad_local, NN) * tail
                k_grad[keys, :128], k_grad[keys, 128:] = turn_back(keys, raw)
                v_grad[keys, :] = (value * masked(length, stretch * HALF, HALF)).astype(BF)

        def back_rows(rows):
            terms = (
                (of(swish_grad, rows), weights, 0, 432),
                (of(v_grad, rows), weights, 432, 432),
                (of(q_grad, rows), weights, 864, 256),
                (of(k_grad, rows), weights, 1120, 256),
            )
            times_plain(terms, part, rows)

        def gain_rows(rows):
            for x in range(4):
                at = slice(x * 512, x * 512 + 512)
                along = of(part, rows, at).astype(F32) * of(one, rows, at).astype(F32)
                gain_sum[:, at] = gain_sum[:, at] + jnp.sum(along, axis=0, keepdims=True)

        def output_rows(lo):
            def take(rows, value):
                at = pl.ds(pl.multiple_of(lo + rows.start, rows.size), rows.size)
                out_ref[at, :] = (hidden_ref[at, :] + value).astype(BF)

            return take

        def grad_rows(lo):
            def take(rows, value):
                total[pl.ds(pl.multiple_of(lo + rows.start, rows.size), rows.size), :] = value

            return take

        def norm_one_back(lo):
            def store(at, value):
                in_grad[at, :] = gh_ref[at, :] + value

            norm_back(lambda at: in_ref[at, :].astype(F32), gain, lambda at: total[at, :], store, lo, 64)

        gain_sum[...] = jnp.zeros_like(gain_sum)
        ra0, ra1 = (RowSums(net, down, first_bufs, output_rows(lo), lo, 64, down_in, 0) for lo in (0, 64))
        rb0, rb1 = (RowSums(net, part, second_bufs, grad_rows(lo), lo, 64) for lo in (0, 64))
        rows_a0, rows_b0, rows_a1, rows_b1 = (tile(net, ds, half) for half in (0, 1) for ds in ((2, 1), (-1, 0)))

        def keep(at, value):
            sums_out[at, :] = value

        sums, at = [], 0
        for lo, hi in ((0, 432), (432, 864), (864, 1296), (1296, 1808)):
            n = len(scatter_shapes(hi - lo))
            sums.append(scatter_weights(net, sums_ref, lo, hi, bufs[at : at + n], keep))
            at += n
        sum_o, sum_s, sum_v, sum_qk = sums

        def keys_grad():
            weight_grad(q_grad, one, sums_ref, 1296, 256)
            weight_grad(k_grad, one, sums_ref, 1552, 256)

        def spread(ref, place, hops):
            return [net.copy(ref.at[place], ref.at[place], **hop) for hop in hops]

        def gathered(ref, copies):
            for copy in copies:
                copy.wait_recv()
            value = ref[0]
            for k in range(1, ref.shape[0]):
                value = value + ref[k]
            return value

        def begin():
            by_group[t * 2 + c, 0:1, :] = gain_sum[...] / gain[...]
            by_group[t * 2 + c, 1:2, :] = mlp_gain_ref[...]
            for copy in in_group:
                copy.start()

        def along_x():
            by_x[net.x] = gathered(by_group, in_group)
            for copy in in_x:
                copy.start()

        def along_z():
            by_z[net.z] = gathered(by_x, in_x)
            for copy in in_z:
                copy.start()

        def all_gains():
            gains_out[...] = gathered(by_z, in_z)

        in_group = spread(by_group, t * 2 + c, SPREAD_HOPS)
        in_x = spread(by_x, net.x, (dict(dx=1), dict(dx=-1), dict(dx=2)))
        in_z = spread(by_z, net.z, (dict(dz=1), dict(dz=-1), dict(dz=2)))
        def keep_sums(lo, n):
            stores.append(net.move(sums_out.at[pl.ds(lo, n), :], sums_all.at[pl.ds(lo, n), :]))

        swap_mlp = net.copy(sums_mlp_ref, mlp_got, dc=1)
        swap_o, swap_s, swap_v, swap_qk = (
            net.copy(sums_out.at[pl.ds(lo, n), :], sums_got.at[pl.ds(lo, n), :], dc=1)
            for lo, n in ((0, 432), (432, 432), (864, 432), (1296, 512))
        )
        net.met()
        ra1.side(2)
        wait_all(load_out)
        sum_o[0]()
        score()
        keys_and_values()
        ra0.side(2)
        sum_o[1]()
        wait_all(load_w)
        back_rows(rows_a0)
        rb0.side(2)
        wait_all(load_one)
        gain_rows(rows_a0)
        ra1.side(1)
        ra0.side(1)
        wait_all(load_down)
        ra0.far()
        rb0.side(1)
        weight_grad(v_grad, one, sums_ref, 864, 432)
        sum_v[0]()
        rb0.far()
        keys_grad()
        sum_qk[0]()
        ra0.side(0)
        ra1.far()
        ra0.side(-1)
        back_rows(rows_b0)
        sum_o[2]()
        ra0.near()
        rb0.side(-1)
        ra1.side(-1)
        rb0.side(0)
        sum_v[1]()
        back_rows(rows_a1)
        weight_grad(swish_grad, one, sums_ref, 432, 432)
        rb1.side(2)
        gain_rows(rows_b0)
        rb1.side(1)
        sum_s[0]()
        sum_qk[1]()
        gain_rows(rows_a1)
        ra1.side(0)
        rb0.near()
        rb1.far()
        back_rows(rows_b1)
        sum_v[2]()
        sum_s[1]()
        swap_mlp.start()
        rb1.side(-1)
        gain_rows(rows_b1)
        begin()
        rb1.near()
        rb0.finish()
        sum_qk[2]()
        rb1.side(0)
        sum_o[3]()
        along_x()
        sum_s[2]()
        ra1.near()
        wait_all(load_last)
        ra0.finish()
        sum_v[3]()
        sum_qk[3]()
        sum_o[4]()
        keep_sums(0, 432)
        along_z()
        sum_s[3]()
        swap_o.start()
        rb1.finish()
        norm_one_back(64)
        sum_v[4]()
        keep_sums(864, 432)
        sum_qk[4]()
        keep_sums(1296, 512)
        swap_qk.start()
        swap_v.start()
        norm_one_back(0)
        stores.append(net.move(in_grad, in_grad_out))
        sum_s[4]()
        keep_sums(432, 432)
        swap_s.start()
        ra1.finish()
        stores.append(net.move(out_ref, out_out))
        all_gains()
        for swap in (swap_mlp, swap_o, swap_s, swap_v, swap_qk):
            swap.wait_recv()
        net.flush()
        wait_all(stores)

    cols = pltpu.VMEM((SEQ, VDIM), BF)
    keys = pltpu.VMEM((SEQ, KDIM), BF)
    rows = pltpu.VMEM((SEQ, D), BF)
    own = pltpu.VMEM((128, D), F32)
    return call(
        kernel,
        [
            (shape(128, D), False),
            (shape(128, D, kind=F32), False),
            (shape(2, D, kind=F32), True),
            (shape(1808, 128, kind=F32), False),
            (shape(1808, 128, kind=F32), False),
            (shape(1296, 128, kind=F32), False),
        ],
        [
            (weights_all, False),
            (rows_one, False),
            (down_part, False),
            (q, False),
            (k, False),
            (v, False),
            (mix, False),
            (prior, False),
            (swish_grad, False),
            (ret_grad, False),
            (out_grad, False),
            (hidden, False),
            (grad_hidden, False),
            (inputs, True),
            (attn_gain, True),
            (cosine, False),
            (sine, False),
            (length, SMEM),
            (mlp_gain_part, True),
            (sums_mlp, False),
        ],
        [
            pltpu.VMEM((128, D), BF),
            own,
            pltpu.VMEM((1808, 128), F32),
            pltpu.VMEM((4, 4, 1376, 128), BF),
            pltpu.VMEM((4, 4, 1808, 128), BF),
            rows,
            rows,
            pltpu.VMEM((HALF, D), BF),
            keys,
            keys,
            cols,
            pltpu.VMEM((SEQ, HALF), BF),
            pltpu.VMEM((2, KDIM, VDIM), BF),
            cols,
            cols,
            own,
            own,
            pltpu.VMEM((SEQ, 128), F32),
            pltpu.VMEM((SEQ, 128), F32),
            keys,
            keys,
            cols,
            pltpu.VMEM((SEQ, HALF), BF),
            own,
            pltpu.VMEM((1, D), F32),
            pltpu.VMEM((8, 2, D), F32),
            pltpu.VMEM((4, 2, D), F32),
            pltpu.VMEM((4, 2, D), F32),
        ]
        + ROW_BUFS
        + ROW_BUFS
        + scatter_shapes(432) * 3
        + scatter_shapes(512),
        120,
        48,
        cid,
    )


def hand_out(outputs, input_grad, gains, sums, got, sums_mlp, got_mlp):
    places = (
        (0, 1296, 256), (0, 1552, 256), (0, 864, 432), (0, 432, 432), (0, 0, 432), (1, 0, 432), (1, 432, 432),
        (1, 864, 432),
    )

    def kernel(*refs):
        n = len(outs)
        ins, results, held, made, loads, stores = (
            refs[:7], refs[7 : 7 + n], refs[7 + n : 14 + n], refs[14 + n : 14 + 2 * n], refs[-2], refs[-1]
        )
        arrive = [pltpu.make_async_copy(ins[k], held[k], loads.at[k]) for k in range(7)]
        leave = [pltpu.make_async_copy(made[k], results[k], stores.at[k]) for k in range(n)]
        for k in (5, 6, 3, 4, 1, 0, 2):
            arrive[k].start()
        first_core = lax.axis_index("ctx") == 0
        wait_all([arrive[5], arrive[6]])
        waited = False
        for k in (5, 6, 7, 4, 3, 2, 0, 1):
            which, lo, rows = places[k]
            if which == 0 and not waited:
                wait_all([arrive[3], arrive[4]])
                waited = True
            a, b = (held[at][lo : lo + rows, :] for at in ((3, 4), (5, 6))[which])
            both = jnp.concatenate([jnp.where(first_core, a, b), jnp.where(first_core, b, a)], axis=0).T
            made[4 + k][...] = jnp.where(first_core, both[:64], both[64:])
            leave[4 + k].start()
        wait_all([arrive[0], arrive[1], arrive[2]])
        made[1][...] = held[1][...]
        leave[1].start()
        made[0][...] = held[0][...]
        made[2][...] = held[2][0:1, :]
        made[3][...] = held[2][1:2, :]
        for k in (0, 2, 3):
            leave[k].start()
        wait_all(leave)

    outs = [shape(128, D), shape(128, D, kind=F32), shape(1, D, kind=F32), shape(1, D, kind=F32)]
    for _, _, n in places:
        outs.append(shape(64, 2 * n, kind=F32))
    ins = (outputs, input_grad, gains, sums, got, sums_mlp, got_mlp)
    spec = pl.BlockSpec(memory_space=pl.ANY)
    return pl.pallas_call(
        kernel,
        out_shape=outs,
        in_specs=[spec] * len(ins),
        out_specs=[spec] * len(outs),
        scratch_shapes=[pltpu.VMEM(a.shape, a.dtype) for a in (*ins, *outs)]
        + [pltpu.SemaphoreType.DMA((len(ins),)), pltpu.SemaphoreType.DMA((len(outs),))],
        compiler_params=pltpu.CompilerParams(vmem_limit_bytes=61 * 2**20),
    )(*ins)


def turning_tables():
    frequency = 10000.0 ** (-np.arange(128) / 128.0)
    angles = np.arange(SEQ)[:, None] * frequency[None, :]
    return jnp.asarray(np.cos(angles), F32), jnp.asarray(np.sin(angles), F32)


def on_device(
    inputs,
    seq_lengths,
    carried_state,
    attn_gain,
    query_weight,
    key_weight,
    value_weight,
    swish_weight,
    out_weight,
    mlp_gain,
    gate_weight,
    up_weight,
    down_weight,
    output_grad,
):
    cosine, sine = turning_tables()
    gains = attn_gain[None, :], mlp_gain[None, :]
    shards = (
        query_weight, key_weight, value_weight, swish_weight, out_weight.T, gate_weight, up_weight, down_weight.T
    )
    (
        weights, rows_one, q, k, v, mix, prior, hidden, down_part, grad_hidden, mlp_gain_part, sums_mlp, swish_grad,
        ret_grad, out_grad
    ) = forward_and_mlp_back(
        shards, inputs, carried_state.transpose(0, 1, 3, 2), *gains, cosine, sine, seq_lengths, output_grad, 1
    )
    outputs, input_grad, gain_grads, sums, got_sums, got_mlp = retention_back(
        weights, rows_one, down_part, q, k, v, mix, prior, swish_grad, ret_grad, out_grad, hidden, grad_hidden, inputs,
        gains[0], cosine, sine, seq_lengths, mlp_gain_part, sums_mlp, 2
    )
    outputs, input_grad, first, second, *grads = hand_out(
        outputs, input_grad, gain_grads, sums, got_sums, sums_mlp, got_mlp
    )
    return (
        outputs,
        input_grad,
        first[0],
        grads[0],
        grads[1],
        grads[2],
        grads[3],
        grads[4].T,
        second[0],
        grads[5],
        grads[6],
        grads[7].T,
    )


def solution(mesh):
    placed = (
        P(("fsdp", "ctx", "tp"), None),
        P("fsdp"),
        P("fsdp", "tp", None, None),
        P(),
        P(("fsdp", "ctx"), "tp"),
        P(("fsdp", "ctx"), "tp"),
        P(("fsdp", "ctx"), "tp"),
        P(("fsdp", "ctx"), "tp"),
        P("tp", ("fsdp", "ctx")),
        P(),
        P(("fsdp", "ctx"), "tp"),
        P(("fsdp", "ctx"), "tp"),
        P("tp", ("fsdp", "ctx")),
        P(("fsdp", "ctx"), None),
    )
    return jax.shard_map(
        on_device,
        mesh=mesh,
        in_specs=placed,
        out_specs=(
            P(("fsdp", "ctx", "tp"), None),
            P(("fsdp", "ctx", "tp"), None),
            P(),
            P(("fsdp", "ctx"), "tp"),
            P(("fsdp", "ctx"), "tp"),
            P(("fsdp", "ctx"), "tp"),
            P(("fsdp", "ctx"), "tp"),
            P("tp", ("fsdp", "ctx")),
            P(),
            P(("fsdp", "ctx"), "tp"),
            P(("fsdp", "ctx"), "tp"),
            P("tp", ("fsdp", "ctx")),
        ),
        check_vma=False,
    )
```
